32 devices in a mesh: row: 4 (over y, core), col: 8 (over z, x).
Axes of the slice: x: 2, y: 2, z: 4, core: 2. Of those that a mesh axis runs over, the one named last changes fastest.
Arguments:
- alignment: bfloat16 [64, 384, 256], P('row', 'col'), may hold values from -6.5 to 6.5
- pair_features: float32 [384, 384, 128], P('row', 'col'), may hold values from -6 to 6
- query_weight: bfloat16 [256, 256], replicated, may hold values from -25 to 25
- key_weight: bfloat16 [256, 256], replicated, may hold values from -0.375 to 0.375
- value_projection: bfloat16 [256, 256], replicated, may hold values from -0.375 to 0.375
- gate_projection: bfloat16 [256, 256], replicated, may hold values from -0.375 to 0.375
- gate_bias: float32 [256], replicated, may hold values from -4 to 4
- output_projection: bfloat16 [256, 256], replicated, may hold values from -0.375 to 0.375
- left_projection: bfloat16 [256, 32], replicated, may hold values from -0.375 to 0.375
- right_projection: bfloat16 [256, 32], replicated, may hold values from -0.375 to 0.375
- outer_weight: bfloat16 [1024, 128], replicated, may hold values from -0.75 to 0.75
- outer_bias: float32 [128], replicated, may hold values from -3 to 3
- expand_weight: bfloat16 [128, 512], replicated, may hold values from -0.5 to 0.5
- shrink_weight: bfloat16 [512, 128], replicated, may hold values from -0.25 to 0.25
- cotangent: float32 [384, 384, 128], P('row', 'col'), may hold values from -6 to 6
Outputs:
- updated: bfloat16 [64, 384, 256], P('row', 'col')
- pair_out: float32 [384, 384, 128], P('row', 'col')
- grad_left: float32 [64, 12288], P('col', 'row')
- grad_right: float32 [64, 12288], P('row', 'col')
The draws below stay inside these ranges and needn't reach their ends.
All inputs are finite; a program needn't handle non-finite values.
Results may differ from the reference program's by a relative error of at most 0.017.
Values may be sent and summed in bfloat16 or wider, within the bound.
No kernel may reach another device: no remote copies, remote signals or barrier semaphores. Data moves between devices by JAX's collectives and lax.ppermute only.
A program may use at most 192 MiB of HBM per device.

```python
import jax
import jax.numpy as jnp
from jax import lax

ENTRY_FEATURES = 256
ATTENTION_HEADS = 8
HEAD_WIDTH = 32
FACTOR_WIDTH = 32
PAIR_W = 128
TRANSITION = 512
SEQUENCE_COUNT = 64
RESIDUE_COUNT = 384


def shared_base(key):
    base_random_key = jax.random.normal(jax.random.fold_in(key, 7), (ENTRY_FEATURES, ATTENTION_HEADS * HEAD_WIDTH), jnp.float32)
    return jnp.clip(base_random_key, -6.0, 6.0) * ENTRY_FEATURES ** (-0.5)


def draw_key_weight(key, part):
    return shared_base(key).astype(jnp.bfloat16)


def draw_query_weight(key, part):
    fresh_random_sample = jax.random.normal(jax.random.fold_in(key, 8), (ENTRY_FEATURES, ATTENTION_HEADS * HEAD_WIDTH), jnp.float32)
    fresh_random_sample = jnp.clip(fresh_random_sample, -6.0, 6.0) * ENTRY_FEATURES ** (-0.5)
    return fresh_random_sample.astype(jnp.bfloat16)


def draw_alignment(key, part):
    value_rows = jnp.clip(jax.random.normal(jax.random.fold_in(key, 5), (SEQUENCE_COUNT, RESIDUE_COUNT, ENTRY_FEATURES), jnp.float32), -6.0, 6.0)
    return value_rows.astype(jnp.bfloat16)


def block_levels(rng, dims, split, smallest, high):
    def one(dim, blocks):
        steps = jax.random.uniform(jax.random.fold_in(jax.random.fold_in(rng, 6), dim), (blocks,), jnp.float32, smallest / len(split), high / len(split))
        return jnp.repeat(jnp.exp(steps), dims[dim] // blocks).reshape((-1,) + (1,) * (len(dims) - dim - 1))

    level = one(*split[0])
    for cut in split[1:]:
        level = level * one(*cut)
    return level


def gaussian(own_key, dims, scale, bound, pieces=(), held_as=jnp.bfloat16):
    entries = jax.random.normal(own_key, dims, jnp.float32) * scale
    if len(pieces) > 0:
        entries = block_levels(own_key, dims, pieces, -0.22, 0.18) * entries
    return jnp.clip(entries, min=-bound, max=bound).astype(held_as)


def setup_inputs(seed: int = 0) -> dict:
    splits = jax.random.split(jax.random.key(seed), 16)
    return {
        "alignment": draw_alignment(jax.random.fold_in(splits[15], 71), 0),
        "pair_features": gaussian(splits[1], (RESIDUE_COUNT, RESIDUE_COUNT, PAIR_W), 1.0, 6.0, ((0, 4), (1, 8)), jnp.float32),
        "query_weight": draw_query_weight(jax.random.fold_in(splits[15], 71), 0),
        "key_weight": draw_key_weight(jax.random.fold_in(splits[15], 71), 0),
        "value_projection": gaussian(splits[4], (ENTRY_FEATURES, ATTENTION_HEADS * HEAD_WIDTH), ENTRY_FEATURES ** -0.5, 0.375),
        "gate_projection": gaussian(splits[5], (ENTRY_FEATURES, ATTENTION_HEADS * HEAD_WIDTH), ENTRY_FEATURES ** -0.5, 0.375),
        "gate_bias": gaussian(splits[6], (ATTENTION_HEADS * HEAD_WIDTH,), 1.0, 4.0, (), jnp.float32),
        "output_projection": gaussian(splits[7], (ATTENTION_HEADS * HEAD_WIDTH, ENTRY_FEATURES), (ATTENTION_HEADS * HEAD_WIDTH) ** -0.5, 0.375),
        "left_projection": gaussian(splits[8], (ENTRY_FEATURES, FACTOR_WIDTH), ENTRY_FEATURES ** -0.5, 0.375),
        "right_projection": gaussian(splits[9], (ENTRY_FEATURES, FACTOR_WIDTH), ENTRY_FEATURES ** -0.5, 0.375),
        "outer_weight": gaussian(splits[10], (FACTOR_WIDTH * FACTOR_WIDTH, PAIR_W), (2 * FACTOR_WIDTH) ** -0.5, 0.75),
        "outer_bias": gaussian(splits[11], (PAIR_W,), 0.5, 3.0, (), jnp.float32),
        "expand_weight": gaussian(splits[12], (PAIR_W, TRANSITION), PAIR_W ** -0.5, 0.5),
        "shrink_weight": gaussian(splits[13], (TRANSITION, PAIR_W), TRANSITION ** -0.5, 0.25),
        "cotangent": gaussian(splits[14], (RESIDUE_COUNT, RESIDUE_COUNT, PAIR_W), 1.0, 6.0, ((0, 4), (1, 8)), jnp.float32),
    }


epsilon = 1e-05

def layer_normalise(value_rows):
    value_rows = value_rows.astype(jnp.float32)
    average = lax.optimization_barrier(jnp.mean(value_rows, axis=-1, keepdims=True))
    centred = value_rows - average
    variance = lax.optimization_barrier(jnp.mean(centred * centred, axis=-1, keepdims=True))
    return centred * lax.rsqrt(variance + epsilon)

def gelu_value(before):
    return 0.5 * before * (1.0 + lax.erf(before * 0.7071067811865476))

def gelu_slope(before):
    return 0.5 * (1.0 + lax.erf(before * 0.7071067811865476)) + before * jnp.exp(-0.5 * before * before) * 0.3989422804014327

def dot_last(left_side, right_side):
    return lax.dot_general(left_side, right_side, (((1,), (1,)), ((), ())), preferred_element_type=jnp.float32)

def transition(middle, cotangent, expand_weight, shrink_weight):
    average = lax.optimization_barrier(jnp.mean(middle, axis=-1, keepdims=True))
    centred = middle - average
    variance = lax.optimization_barrier(jnp.mean(centred * centred, axis=-1, keepdims=True))
    inverse = lax.rsqrt(variance + epsilon)
    spread = centred * inverse
    before = jnp.dot(spread.astype(jnp.bfloat16), expand_weight, preferred_element_type=jnp.float32)
    hidden = gelu_value(before).astype(jnp.bfloat16)
    result = middle + jnp.dot(hidden, shrink_weight, preferred_element_type=jnp.float32)
    back_hidden = dot_last(cotangent.astype(jnp.bfloat16), shrink_weight)
    back_before = (back_hidden * gelu_slope(before)).astype(jnp.bfloat16)
    back_spread = dot_last(back_before, expand_weight)
    centre_term = lax.optimization_barrier(jnp.mean(back_spread, axis=-1, keepdims=True))
    slope_term = lax.optimization_barrier(jnp.mean(back_spread * spread, axis=-1, keepdims=True))
    back_middle = cotangent + inverse * (back_spread - centre_term - spread * slope_term)
    return (result, back_middle)

def column_attend(column_block, query_weight, key_weight, value_projection, gate_projection, gate_bias, output_projection):
    seq_count, res_count, feat_width = column_block.shape
    flat_rows = layer_normalise(column_block).astype(jnp.bfloat16).reshape(seq_count * res_count, feat_width)
    head_shape = (seq_count, res_count, ATTENTION_HEADS, HEAD_WIDTH)
    query_proj = jnp.dot(flat_rows, query_weight, preferred_element_type=jnp.float32).astype(jnp.bfloat16).reshape(head_shape)
    key_proj = jnp.dot(flat_rows, key_weight, preferred_element_type=jnp.float32).astype(jnp.bfloat16).reshape(head_shape)
    value_proj = jnp.dot(flat_rows, value_projection, preferred_element_type=jnp.float32).astype(jnp.bfloat16).reshape(head_shape)
    gating = jax.nn.sigmoid(jnp.dot(flat_rows, gate_projection, preferred_element_type=jnp.float32) + gate_bias).reshape(head_shape)
    scores = jnp.einsum('srhc,trhc->rhst', query_proj.astype(jnp.float32), key_proj.astype(jnp.float32)) * HEAD_WIDTH ** (-0.5)
    highest = lax.optimization_barrier(jnp.max(scores, axis=-1, keepdims=True))
    raised = jnp.exp(scores - highest)
    totals = lax.optimization_barrier(jnp.sum(raised, axis=-1))
    rounded = lax.optimization_barrier(raised.astype(jnp.bfloat16)).astype(jnp.float32)
    blended = jnp.einsum('rhst,trhc->srhc', rounded, value_proj.astype(jnp.float32))
    blended = blended / jnp.transpose(totals, (2, 0, 1))[..., None]
    gated_out = (gating * blended).astype(jnp.bfloat16).reshape(seq_count * res_count, ATTENTION_HEADS * HEAD_WIDTH)
    update = jnp.dot(gated_out, output_projection, preferred_element_type=jnp.float32).reshape(column_block.shape)
    return (column_block.astype(jnp.float32) + update).astype(jnp.bfloat16)

def reference(alignment, pair_features, query_weight, key_weight, value_projection, gate_projection, gate_bias, output_projection, left_projection, right_projection, outer_weight, outer_bias, expand_weight, shrink_weight, cotangent):
    width_of_block = 16
    count_of_blocks = RESIDUE_COUNT // width_of_block
    split_into_blocks = jnp.transpose(alignment.reshape(SEQUENCE_COUNT, count_of_blocks, width_of_block, ENTRY_FEATURES), (1, 0, 2, 3))

    def attend_block(column_block):
        return column_attend(column_block, query_weight, key_weight, value_projection, gate_projection, gate_bias, output_projection)
    attended_rows = lax.map(attend_block, split_into_blocks)
    updated = jnp.transpose(attended_rows, (1, 0, 2, 3)).reshape(SEQUENCE_COUNT, RESIDUE_COUNT, ENTRY_FEATURES)
    factor_row_matrix = layer_normalise(updated).astype(jnp.bfloat16).reshape(SEQUENCE_COUNT * RESIDUE_COUNT, ENTRY_FEATURES)
    left_factors = jnp.dot(factor_row_matrix, left_projection, preferred_element_type=jnp.float32).astype(jnp.bfloat16).reshape(SEQUENCE_COUNT, RESIDUE_COUNT, FACTOR_WIDTH)
    right_factors = jnp.dot(factor_row_matrix, right_projection, preferred_element_type=jnp.float32).astype(jnp.bfloat16).reshape(SEQUENCE_COUNT, RESIDUE_COUNT, FACTOR_WIDTH)
    right_wide = right_factors.astype(jnp.float32)
    scaling = 1.0 / SEQUENCE_COUNT

    def one_block(carried, block_index):
        left_part = lax.dynamic_slice_in_dim(left_factors, block_index * width_of_block, width_of_block, 1).astype(jnp.float32)
        pair_part = lax.dynamic_slice_in_dim(pair_features, block_index * width_of_block, width_of_block, 0)
        cot_part = lax.dynamic_slice_in_dim(cotangent, block_index * width_of_block, width_of_block, 0)
        outer_tile = (jnp.einsum('sic,sje->ijce', left_part, right_wide) * scaling).astype(jnp.bfloat16)
        outer_tile = outer_tile.reshape(width_of_block * RESIDUE_COUNT, FACTOR_WIDTH * FACTOR_WIDTH)
        middle = pair_part.reshape(width_of_block * RESIDUE_COUNT, PAIR_W) + jnp.dot(outer_tile, outer_weight, preferred_element_type=jnp.float32) + outer_bias
        result, back_middle = transition(middle, cot_part.reshape(width_of_block * RESIDUE_COUNT, PAIR_W), expand_weight, shrink_weight)
        back_outer = dot_last(back_middle.astype(jnp.bfloat16), outer_weight).astype(jnp.bfloat16)
        back_outer = back_outer.reshape(width_of_block, RESIDUE_COUNT, FACTOR_WIDTH, FACTOR_WIDTH).astype(jnp.float32)
        grad_part = jnp.einsum('ijce,sje->sic', back_outer, right_wide).reshape(SEQUENCE_COUNT, width_of_block * FACTOR_WIDTH) * scaling
        carried = carried + jnp.einsum('ijce,sic->sje', back_outer, left_part).reshape(SEQUENCE_COUNT, RESIDUE_COUNT * FACTOR_WIDTH) * scaling
        return (carried, (result.reshape(width_of_block, RESIDUE_COUNT, PAIR_W), grad_part))
    indices = jnp.arange(count_of_blocks, dtype=jnp.int32)
    start_grad = jnp.zeros((SEQUENCE_COUNT, RESIDUE_COUNT * FACTOR_WIDTH), jnp.float32)
    grad_right, (pair_blocks, grad_blocks) = lax.scan(one_block, start_grad, indices)
    pair_out = pair_blocks.reshape(RESIDUE_COUNT, RESIDUE_COUNT, PAIR_W)
    grad_left = jnp.transpose(grad_blocks, (1, 0, 2)).reshape(SEQUENCE_COUNT, RESIDUE_COUNT * FACTOR_WIDTH)
    return (updated, pair_out, grad_left, grad_right)
```

```python
import functools

import jax
import jax.numpy as jnp
from jax import lax
from jax.experimental import pallas as pl
from jax.experimental.pallas import tpu as pltpu
from jax.sharding import PartitionSpec as P

ATTENTION_HEADS = 8
HEAD_WIDTH = 32
FACTOR_WIDTH = 32
PAIR_W = 128
EPSILON = 1e-05

LANES = 128
MXU_SIDE = 256
HALF = 64


def dot_nn(a, b):
    return lax.dot_general(a, b, (((1,), (0,)), ((), ())), preferred_element_type=jnp.float32)


def dot_nt(a, b):
    return lax.dot_general(a, b, (((1,), (1,)), ((), ())), preferred_element_type=jnp.float32)


def layer_normalise(rows):
    rows = rows.astype(jnp.float32)
    average = jnp.mean(rows, axis=-1, keepdims=True)
    centred = rows - average
    variance = jnp.mean(centred * centred, axis=-1, keepdims=True)
    return centred * lax.rsqrt(variance + EPSILON)


def attend_kernel(
    x_ref, wq_ref, wk_ref, wv_ref, wg_ref, bias_ref, wo_ref, wl_ref, wr_ref,
    upd_ref, left_ref, right_ref,
    q_s, k_s, v_s, g_s, a_s,
):
    parts, residues, part_seqs, width = x_ref.shape
    seqs = parts * part_seqs
    x = jnp.concatenate([x_ref[s, r] for r in range(residues) for s in range(parts)], axis=0)
    normed = layer_normalise(x).astype(jnp.bfloat16)
    q_s[...] = dot_nn(normed, wq_ref[...]).astype(jnp.bfloat16)
    k_s[...] = dot_nn(normed, wk_ref[...]).astype(jnp.bfloat16)
    v_s[...] = dot_nn(normed, wv_ref[...]).astype(jnp.bfloat16)
    g_s[...] = jax.nn.sigmoid(dot_nn(normed, wg_ref[...]) + bias_ref[...])

    head_of = lax.broadcasted_iota(jnp.int32, (1, width), 1) // HEAD_WIDTH
    masks = [(head_of == h).astype(jnp.float32) for h in range(ATTENTION_HEADS)]
    masks_low = [m.astype(jnp.bfloat16) for m in masks]

    def one_residue(r, carry):
        rows = pl.ds(pl.multiple_of(r * seqs, seqs), seqs)
        query = q_s[rows, :]
        spread_query = jnp.concatenate([query * m for m in masks_low], axis=0)
        scores = dot_nt(spread_query, k_s[rows, :]) * HEAD_WIDTH ** (-0.5)
        raised = jnp.exp(scores - jnp.max(scores, axis=-1, keepdims=True))
        inverse = 1.0 / jnp.sum(raised, axis=-1, keepdims=True)
        blended = dot_nn(raised.astype(jnp.bfloat16), v_s[rows, :]) * inverse
        total = blended[:seqs] * masks[0]
        for h in range(1, ATTENTION_HEADS):
            total = total + blended[h * seqs:(h + 1) * seqs] * masks[h]
        a_s[rows, :] = (g_s[rows, :] * total).astype(jnp.bfloat16)
        return carry

    lax.fori_loop(0, residues, one_residue, 0, unroll=2)

    updated = (x.astype(jnp.float32) + dot_nn(a_s[...], wo_ref[...])).astype(jnp.bfloat16)
    for r in range(residues):
        for s in range(parts):
            begin = r * seqs + s * part_seqs
            upd_ref[s, r] = updated[begin:begin + part_seqs]
    factor_norm = layer_normalise(updated).astype(jnp.bfloat16)
    project = jnp.concatenate([wl_ref[...], wr_ref[...]], axis=1).astype(jnp.float32).T.astype(jnp.bfloat16)
    for p in range(residues // 2):
        both = dot_nt(project, factor_norm[p * 2 * seqs:(p + 1) * 2 * seqs]).astype(jnp.bfloat16)
        left_ref[p] = both[:FACTOR_WIDTH]
        right_ref[p] = both[FACTOR_WIDTH:]


def attend(x, wq, wk, wv, wg, gate_bias, wo, wl, wr):
    parts, residues, part_seqs, width = x.shape
    seqs = parts * part_seqs
    rows = residues * seqs
    factor = jax.ShapeDtypeStruct((residues // 2, FACTOR_WIDTH, 2 * seqs), jnp.bfloat16)
    return pl.pallas_call(
        attend_kernel,
        out_shape=(jax.ShapeDtypeStruct(x.shape, jnp.bfloat16), factor, factor),
        in_specs=[pl.BlockSpec(memory_space=pltpu.VMEM)] * 9,
        out_specs=[pl.BlockSpec(memory_space=pltpu.VMEM)] * 3,
        scratch_shapes=[
            pltpu.VMEM((rows, width), jnp.bfloat16),
            pltpu.VMEM((rows, width), jnp.bfloat16),
            pltpu.VMEM((rows, width), jnp.bfloat16),
            pltpu.VMEM((rows, width), jnp.float32),
            pltpu.VMEM((rows, width), jnp.bfloat16),
        ],
        compiler_params=pltpu.CompilerParams(vmem_limit_bytes=32 * 1024 * 1024),
        name="column_attention",
    )(x, wq, wk, wv, wg, gate_bias.reshape(1, -1), wo, wl, wr)


def pair_kernel(
    left_ref, right_ref, pair_ref, cot_ref, w_ref, bias_ref, expand_ref, shrink_ref,
    out_ref, gl_ref, gr_ref,
    outer_s, rbd_s, l_s, lt_s, stage_s, wec_s, wt_s, glacc_s,
    *, seqs, cols, fold, per_step,
):
    step = pl.program_id(0)
    groups = l_s.shape[0] // FACTOR_WIDTH
    wide = fold * HALF
    scaling = 1.0 / seqs
    stage_lanes = stage_s.shape[1]
    low_half = lax.broadcasted_iota(jnp.int32, (1, LANES), 1) < HALF

    @pl.when(step == 0)
    def _prologue():
        stage_s[:FACTOR_WIDTH * FACTOR_WIDTH, :LANES] = w_ref[...].astype(jnp.float32)
        for e in range(FACTOR_WIDTH):
            piece = stage_s[pl.ds(e, FACTOR_WIDTH, stride=FACTOR_WIDTH), :LANES]
            wec_s[e * FACTOR_WIDTH:(e + 1) * FACTOR_WIDTH, :] = piece.astype(jnp.bfloat16)
        for b in range(FACTOR_WIDTH * FACTOR_WIDTH // LANES):
            block = wec_s[b * LANES:(b + 1) * LANES, :].astype(jnp.float32)
            wt_s[:, b * LANES:(b + 1) * LANES] = block.T.astype(jnp.bfloat16)

        pairs = fold // 2
        for g in range(groups):
            for p in range(pairs):
                l_s[g * FACTOR_WIDTH:(g + 1) * FACTOR_WIDTH, p * 2 * seqs:(p + 1) * 2 * seqs] = left_ref[
                    g * pairs + p
                ]
        for b in range(l_s.shape[0] // LANES):
            block = l_s[b * LANES:(b + 1) * LANES, :].astype(jnp.float32)
            lt_s[:, b * LANES:(b + 1) * LANES] = block.T.astype(jnp.bfloat16)

        for p in range(cols // 2):
            block = right_ref[p].astype(jnp.float32)
            first = 2 * p * FACTOR_WIDTH
            second = first + FACTOR_WIDTH
            if seqs % LANES == 0:
                stage_s[first:first + FACTOR_WIDTH, :] = block[:, :seqs]
                stage_s[second:second + FACTOR_WIDTH, :] = block[:, seqs:]
            else:
                stage_s[first:first + FACTOR_WIDTH, :] = block
                stage_s[second:second + FACTOR_WIDTH, :] = pltpu.roll(block, HALF, axis=1)

        blank = jnp.zeros((seqs, LANES), jnp.bfloat16)
        pad = jnp.zeros((HALF - cols, stage_lanes), jnp.float32)
        for e in range(0, FACTOR_WIDTH, 2):
            even = stage_s[pl.ds(e, cols, stride=FACTOR_WIDTH), :]
            odd = stage_s[pl.ds(e + 1, cols, stride=FACTOR_WIDTH), :]
            turned = jnp.concatenate([even, pad, odd, pad], axis=0).T[:seqs]
            rolled = pltpu.roll(turned, HALF, axis=1)
            for at, low, high in ((e, turned, rolled), (e + 1, rolled, turned)):
                low = jnp.where(low_half, low, 0.0).astype(jnp.bfloat16)
                high = jnp.where(low_half, 0.0, high).astype(jnp.bfloat16)
                for k in range(fold):
                    for v in range(wide // LANES):
                        value = blank if v != k // 2 else (low if k % 2 == 0 else high)
                        rbd_s[at, k * seqs:(k + 1) * seqs, v * LANES:(v + 1) * LANES] = value

        def one_outer(e, carry):
            outer_s[e] = (dot_nn(l_s[...], rbd_s[e]) * scaling).astype(jnp.bfloat16)
            return carry

        lax.fori_loop(0, FACTOR_WIDTH, one_outer, 0)

    per_group = fold * cols
    rows = per_step * per_group
    gap = jnp.zeros((HALF - cols, PAIR_W), jnp.bfloat16)
    pieces = []
    for u in range(per_step):
        at = pl.ds(pl.multiple_of((step * per_step + u) * FACTOR_WIDTH, FACTOR_WIDTH), FACTOR_WIDTH)
        outer = outer_s[:, at, :].reshape(FACTOR_WIDTH * FACTOR_WIDTH, wide)
        product = dot_nn(wt_s[...], outer).T
        for k in range(fold):
            pieces.append(product[k * HALF:k * HALF + cols])
    projected = jnp.concatenate(pieces, axis=0)
    middle = pair_ref[...].reshape(rows, PAIR_W) + projected + bias_ref[...]
    cotangent = cot_ref[...].reshape(rows, PAIR_W)

    average = jnp.mean(middle, axis=-1, keepdims=True)
    centred = middle - average
    variance = jnp.mean(centred * centred, axis=-1, keepdims=True)
    inverse = lax.rsqrt(variance + EPSILON)
    spread = centred * inverse
    before = dot_nn(spread.astype(jnp.bfloat16), expand_ref[...])
    phi = 0.5 * (1.0 + lax.erf(before * 0.7071067811865476))
    slope = phi + before * jnp.exp(-0.5 * before * before) * 0.3989422804014327
    hidden = (before * phi).astype(jnp.bfloat16)
    out_ref[...] = (middle + dot_nn(hidden, shrink_ref[...])).reshape(out_ref.shape)
    back_hidden = dot_nt(cotangent.astype(jnp.bfloat16), shrink_ref[...])
    back_before = (back_hidden * slope).astype(jnp.bfloat16)
    back_spread = dot_nt(back_before, expand_ref[...])
    centre_term = jnp.mean(back_spread, axis=-1, keepdims=True)
    slope_term = jnp.mean(back_spread * spread, axis=-1, keepdims=True)
    back_middle = cotangent + inverse * (back_spread - centre_term - spread * slope_term)
    back_middle = back_middle.astype(jnp.bfloat16)
    for u in range(per_step):
        parts = []
        for k in range(fold):
            begin = u * per_group + k * cols
            parts += [back_middle[begin:begin + cols], gap]
        padded = jnp.concatenate(parts, axis=0)
        back_outer = dot_nt(wec_s[...], padded).astype(jnp.bfloat16)
        at = pl.ds(pl.multiple_of((step * per_step + u) * FACTOR_WIDTH, FACTOR_WIDTH), FACTOR_WIDTH)
        outer_s[:, at, :] = back_outer.reshape(FACTOR_WIDTH, FACTOR_WIDTH, wide)

    @pl.when(step == pl.num_programs(0) - 1)
    def _epilogue():
        glacc_s[...] = jnp.zeros_like(glacc_s)
        batch = 2
        empty = jnp.zeros((LANES - seqs % LANES, LANES), jnp.float32) if seqs % LANES else None

        def some(n, carry):
            base = n * batch
            backs = [outer_s[base + u] for u in range(batch)]
            glacc_s[...] += dot_nt(
                jnp.concatenate([rbd_s[base + u] for u in range(batch)], axis=1),
                jnp.concatenate(backs, axis=1),
            )
            lows, highs = [], []
            for u in range(batch):
                full = dot_nn(lt_s[...], backs[u])
                low = high = None
                for k in range(fold):
                    v = k // 2
                    block = full[k * seqs:(k + 1) * seqs, v * LANES:(v + 1) * LANES]
                    if k % 2 == 0:
                        low = block if low is None else low + block
                    else:
                        high = block if high is None else high + block
                lows.append(low)
                highs.append(high)
            for u in range(0, batch, 2):
                both = jnp.where(low_half, lows[u], highs[u + 1]) + pltpu.roll(
                    jnp.where(low_half, lows[u + 1], highs[u]), HALF, axis=1
                )
                if empty is not None:
                    both = jnp.concatenate([both, empty], axis=0)
                turned = both.T
                stage_s[pl.ds(base + u, cols, stride=FACTOR_WIDTH), :] = turned[:cols]
                stage_s[pl.ds(base + u + 1, cols, stride=FACTOR_WIDTH), :] = turned[HALF:HALF + cols]
            return carry

        lax.fori_loop(0, FACTOR_WIDTH // batch, some, 0)
        for b in range(cols * FACTOR_WIDTH // LANES):
            block = stage_s[b * LANES:(b + 1) * LANES, :].T[:seqs]
            gr_ref[:, b * LANES:(b + 1) * LANES] = (block * scaling).astype(jnp.bfloat16)
        span = groups * FACTOR_WIDTH
        for k in range(fold):
            gl_ref[:, k * span:(k + 1) * span] = (
                glacc_s[k * seqs:(k + 1) * seqs, :] * scaling
            ).astype(jnp.bfloat16)


def pair_tile(left, right, pair_features, cotangent, outer_weight, outer_bias, expand_weight, shrink_weight):
    seqs = left.shape[2] // 2
    rows, cols, _ = pair_features.shape
    fold = MXU_SIDE // HALF
    groups = rows // fold
    per_step = 2 if groups % 2 == 0 else 1
    wide = fold * HALF
    channels = FACTOR_WIDTH * FACTOR_WIDTH
    stage_lanes = max(seqs, LANES)
    block = pl.BlockSpec((per_step * fold, cols, PAIR_W), lambda n: (n, 0, 0))
    whole = pl.BlockSpec(memory_space=pltpu.VMEM)
    return pl.pallas_call(
        functools.partial(pair_kernel, seqs=seqs, cols=cols, fold=fold, per_step=per_step),
        grid=(groups // per_step,),
        out_shape=(
            jax.ShapeDtypeStruct(pair_features.shape, jnp.float32),
            jax.ShapeDtypeStruct((seqs, rows * FACTOR_WIDTH), jnp.bfloat16),
            jax.ShapeDtypeStruct((seqs, cols * FACTOR_WIDTH), jnp.bfloat16),
        ),
        in_specs=[whole, whole, block, block, whole, whole, whole, whole],
        out_specs=[block, whole, whole],
        scratch_shapes=[
            pltpu.VMEM((FACTOR_WIDTH, groups * FACTOR_WIDTH, wide), jnp.bfloat16),
            pltpu.VMEM((FACTOR_WIDTH, fold * seqs, wide), jnp.bfloat16),
            pltpu.VMEM((groups * FACTOR_WIDTH, fold * seqs), jnp.bfloat16),
            pltpu.VMEM((fold * seqs, groups * FACTOR_WIDTH), jnp.bfloat16),
            pltpu.VMEM((max(cols * FACTOR_WIDTH, channels), stage_lanes), jnp.float32),
            pltpu.VMEM((channels, PAIR_W), jnp.bfloat16),
            pltpu.VMEM((PAIR_W, channels), jnp.bfloat16),
            pltpu.VMEM((fold * seqs, groups * FACTOR_WIDTH), jnp.float32),
        ],
        compiler_params=pltpu.CompilerParams(
            dimension_semantics=("arbitrary",), vmem_limit_bytes=56 * 1024 * 1024
        ),
        name="pair_tile",
    )(left, right, pair_features, cotangent, outer_weight, outer_bias.reshape(1, -1), expand_weight, shrink_weight)


def local(
    alignment,
    pair_features,
    query_weight,
    key_weight,
    value_projection,
    gate_projection,
    gate_bias,
    output_projection,
    left_projection,
    right_projection,
    outer_weight,
    outer_bias,
    expand_weight,
    shrink_weight,
    cotangent,
):
    part_seqs, res_count, width = alignment.shape
    row_parts = lax.axis_size("row")
    col_parts = lax.axis_size("col")
    residues = res_count // row_parts
    own = jnp.transpose(alignment, (1, 0, 2)).reshape(row_parts, residues, part_seqs, width)
    columns = lax.all_to_all(own, "row", split_axis=0, concat_axis=0, tiled=True)
    attended, left, right = attend(
        columns, query_weight, key_weight, value_projection, gate_projection, gate_bias,
        output_projection, left_projection, right_projection,
    )
    ratio = col_parts // row_parts
    moves = [
        (r * col_parts + c, (c // ratio) * col_parts + (c % ratio) * row_parts + r)
        for r in range(row_parts)
        for c in range(col_parts)
    ]
    left = lax.ppermute(left, ("row", "col"), moves)
    left_rows = lax.all_gather(left, "col", axis=0, tiled=True)
    right_cols = lax.all_gather(right, "row", axis=0, tiled=True)
    returned = lax.all_to_all(attended, "row", split_axis=0, concat_axis=0, tiled=True)
    updated = jnp.transpose(returned.reshape(res_count, part_seqs, width), (1, 0, 2))

    pair_out, gl, gr = pair_tile(
        left_rows, right_cols, pair_features, cotangent, outer_weight, outer_bias, expand_weight, shrink_weight
    )
    seqs, gl_width = gl.shape
    fold = MXU_SIDE // HALF
    gl_parts = lax.all_to_all(
        gl.reshape(col_parts, seqs // col_parts, gl_width), "col", split_axis=0, concat_axis=0, tiled=True
    )
    grad_left = jnp.sum(gl_parts.astype(jnp.float32), axis=0)
    grad_left = jnp.transpose(
        grad_left.reshape(seqs // col_parts, fold, gl_width // fold // FACTOR_WIDTH, FACTOR_WIDTH), (0, 2, 1, 3)
    ).reshape(seqs // col_parts, gl_width)
    gr_parts = lax.all_to_all(
        gr.reshape(row_parts, seqs // row_parts, gr.shape[1]), "row", split_axis=0, concat_axis=0, tiled=True
    )
    grad_right = jnp.sum(gr_parts.astype(jnp.float32), axis=0)
    return (updated, pair_out, grad_left, grad_right)


def solution(mesh):
    return jax.shard_map(
        local,
        mesh=mesh,
        in_specs=(P("row", "col", None), P("row", "col", None)) + (P(),) * 12 + (P("row", "col", None),),
        out_specs=(P("row", "col", None), P("row", "col", None), P("col", "row"), P("row", "col")),
        check_vma=False,
    )
```

```python
import functools

import jax
import jax.numpy as jnp
from jax import lax
from jax.experimental import pallas as pl
from jax.experimental.pallas import tpu as pltpu
from jax.sharding import PartitionSpec as P

ATTENTION_HEADS = 8
HEAD_WIDTH = 32
FACTOR_WIDTH = 32
PAIR_W = 128
EPSILON = 1e-05

LANES = 128
MXU_SIDE = 256
HALF = 64
CHUNKS = 2


def dot_nn(a, b):
    return lax.dot_general(a, b, (((1,), (0,)), ((), ())), preferred_element_type=jnp.float32)


def dot_nt(a, b):
    return lax.dot_general(a, b, (((1,), (1,)), ((), ())), preferred_element_type=jnp.float32)


def layer_normalise(rows):
    rows = rows.astype(jnp.float32)
    average = jnp.mean(rows, axis=-1, keepdims=True)
    centred = rows - average
    variance = jnp.mean(centred * centred, axis=-1, keepdims=True)
    return centred * lax.rsqrt(variance + EPSILON)


def attend_kernel(
    x_ref, wq_ref, wk_ref, wv_ref, wg_ref, bias_ref, wo_ref, wl_ref, wr_ref,
    upd_ref, left_ref, right_ref,
    q_s, k_s, v_s, g_s, a_s,
):
    parts, residues, part_seqs, width = x_ref.shape
    seqs = parts * part_seqs
    x = jnp.concatenate([x_ref[s, r] for r in range(residues) for s in range(parts)], axis=0)
    normed = layer_normalise(x).astype(jnp.bfloat16)
    q_s[...] = dot_nn(normed, wq_ref[...]).astype(jnp.bfloat16)
    k_s[...] = dot_nn(normed, wk_ref[...]).astype(jnp.bfloat16)
    v_s[...] = dot_nn(normed, wv_ref[...]).astype(jnp.bfloat16)
    g_s[...] = jax.nn.sigmoid(dot_nn(normed, wg_ref[...]) + bias_ref[...])

    head_of = lax.broadcasted_iota(jnp.int32, (1, width), 1) // HEAD_WIDTH
    masks = [(head_of == h).astype(jnp.float32) for h in range(ATTENTION_HEADS)]
    masks_low = [m.astype(jnp.bfloat16) for m in masks]

    def one_residue(r, carry):
        rows = pl.ds(pl.multiple_of(r * seqs, seqs), seqs)
        query = q_s[rows, :]
        spread_query = jnp.concatenate([query * m for m in masks_low], axis=0)
        scores = dot_nt(spread_query, k_s[rows, :]) * HEAD_WIDTH ** (-0.5)
        raised = jnp.exp(scores - jnp.max(scores, axis=-1, keepdims=True))
        inverse = 1.0 / jnp.sum(raised, axis=-1, keepdims=True)
        blended = dot_nn(raised.astype(jnp.bfloat16), v_s[rows, :]) * inverse
        total = blended[:seqs] * masks[0]
        for h in range(1, ATTENTION_HEADS):
            total = total + blended[h * seqs:(h + 1) * seqs] * masks[h]
        a_s[rows, :] = (g_s[rows, :] * total).astype(jnp.bfloat16)
        return carry

    lax.fori_loop(0, residues, one_residue, 0, unroll=2)

    updated = (x.astype(jnp.float32) + dot_nn(a_s[...], wo_ref[...])).astype(jnp.bfloat16)
    for r in range(residues):
        for s in range(parts):
            begin = r * seqs + s * part_seqs
            upd_ref[s, r] = updated[begin:begin + part_seqs]
    factor_norm = layer_normalise(updated).astype(jnp.bfloat16)
    project = jnp.concatenate([wl_ref[...], wr_ref[...]], axis=0)
    for p in range(residues // 2):
        both = dot_nt(project, factor_norm[p * 2 * seqs:(p + 1) * 2 * seqs]).astype(jnp.bfloat16)
        left_ref[p] = both[:FACTOR_WIDTH]
        right_ref[p] = both[FACTOR_WIDTH:]


def whole_block(shape):
    return pl.BlockSpec(shape, lambda *_: (0,) * len(shape))


def attend(x, wq, wk, wv, wg, gate_bias, wo, wl, wr):
    parts, residues, part_seqs, width = x.shape
    seqs = parts * part_seqs
    rows = residues * seqs
    factor = jax.ShapeDtypeStruct((residues // 2, FACTOR_WIDTH, 2 * seqs), jnp.bfloat16)
    operands = (x, wq, wk, wv, wg, gate_bias.reshape(1, -1), wo, wl.T, wr.T)
    results = (jax.ShapeDtypeStruct(x.shape, jnp.bfloat16), factor, factor)
    macs = rows * width * (5 * width + 2 * FACTOR_WIDTH) + 2 * rows * ATTENTION_HEADS * width * seqs
    return pl.pallas_call(
        attend_kernel,
        grid=(1,),
        out_shape=results,
        in_specs=[whole_block(v.shape) for v in operands],
        out_specs=[whole_block(v.shape) for v in results],
        scratch_shapes=[
            pltpu.VMEM((rows, width), jnp.bfloat16),
            pltpu.VMEM((rows, width), jnp.bfloat16),
            pltpu.VMEM((rows, width), jnp.bfloat16),
            pltpu.VMEM((rows, width), jnp.float32),
            pltpu.VMEM((rows, width), jnp.bfloat16),
        ],
        compiler_params=pltpu.CompilerParams(
            dimension_semantics=("arbitrary",), vmem_limit_bytes=32 * 1024 * 1024
        ),
        cost_estimate=pl.CostEstimate(flops=2 * macs, bytes_accessed=4 * x.size * 2, transcendentals=rows * width),
        name="column_attention",
    )(*operands)


def pair_kernel(
    place_ref, *refs, seqs, cols, fold, per_step, left_blocks, right_blocks, first, last,
):
    refs = list(refs)

    def take(count):
        taken = refs[:count]
        del refs[:count]
        return taken

    lefts, rights = take(left_blocks), take(right_blocks)
    pair_ref, cot_ref, w_ref, bias_ref, expand_ref, shrink_ref = take(6)
    grprev_ref = None if first else take(2)[1]
    out_ref, gl_ref, gr_ref = take(3)
    outer_s, rbd_s, l_s, lt_s, stage_s, wec_s, wt_s, glacc_s, lblk_s, rblk_s = refs
    step = pl.program_id(0)
    groups = l_s.shape[0] // FACTOR_WIDTH
    wide = fold * HALF
    scaling = 1.0 / seqs
    stage_lanes = stage_s.shape[1]
    low_half = lax.broadcasted_iota(jnp.int32, (1, LANES), 1) < HALF

    @pl.when(step == 0)
    def _prologue():
        stage_s[:FACTOR_WIDTH * FACTOR_WIDTH, :LANES] = w_ref[...].astype(jnp.float32)
        for e in range(FACTOR_WIDTH):
            piece = stage_s[pl.ds(e, FACTOR_WIDTH, stride=FACTOR_WIDTH), :LANES]
            wec_s[e * FACTOR_WIDTH:(e + 1) * FACTOR_WIDTH, :] = piece.astype(jnp.bfloat16)
        for b in range(FACTOR_WIDTH * FACTOR_WIDTH // LANES):
            block = wec_s[b * LANES:(b + 1) * LANES, :].astype(jnp.float32)
            wt_s[:, b * LANES:(b + 1) * LANES] = block.T.astype(jnp.bfloat16)

        for n, ref in enumerate(lefts):
            lblk_s[place_ref[1 + n]] = ref[...]
        for n, ref in enumerate(rights):
            rblk_s[place_ref[1 + left_blocks + n]] = ref[...]

        pairs = fold // 2
        left_each, right_each = lblk_s.shape[1], rblk_s.shape[1]
        for g in range(groups):
            for p in range(pairs):
                l_s[g * FACTOR_WIDTH:(g + 1) * FACTOR_WIDTH, p * 2 * seqs:(p + 1) * 2 * seqs] = lblk_s[
                    (g * pairs + p) // left_each, (g * pairs + p) % left_each
                ]
        for b in range(l_s.shape[0] // LANES):
            block = l_s[b * LANES:(b + 1) * LANES, :].astype(jnp.float32)
            lt_s[:, b * LANES:(b + 1) * LANES] = block.T.astype(jnp.bfloat16)

        for p in range(cols // 2):
            block = rblk_s[p // right_each, p % right_each].astype(jnp.float32)
            even = 2 * p * FACTOR_WIDTH
            odd = even + FACTOR_WIDTH
            if seqs % LANES == 0:
                stage_s[even:even + FACTOR_WIDTH, :] = block[:, :seqs]
                stage_s[odd:odd + FACTOR_WIDTH, :] = block[:, seqs:]
            else:
                stage_s[even:even + FACTOR_WIDTH, :] = block
                stage_s[odd:odd + FACTOR_WIDTH, :] = pltpu.roll(block, HALF, axis=1)

        blank = jnp.zeros((seqs, LANES), jnp.bfloat16)
        pad = jnp.zeros((HALF - cols, stage_lanes), jnp.float32)
        for e in range(0, FACTOR_WIDTH, 2):
            even = stage_s[pl.ds(e, cols, stride=FACTOR_WIDTH), :]
            odd = stage_s[pl.ds(e + 1, cols, stride=FACTOR_WIDTH), :]
            turned = jnp.concatenate([even, pad, odd, pad], axis=0).T[:seqs]
            rolled = pltpu.roll(turned, HALF, axis=1)
            for at, low, high in ((e, turned, rolled), (e + 1, rolled, turned)):
                low = jnp.where(low_half, low, 0.0).astype(jnp.bfloat16)
                high = jnp.where(low_half, 0.0, high).astype(jnp.bfloat16)
                for k in range(fold):
                    for v in range(wide // LANES):
                        value = blank if v != k // 2 else (low if k % 2 == 0 else high)
                        rbd_s[at, k * seqs:(k + 1) * seqs, v * LANES:(v + 1) * LANES] = value

        def one_outer(e, carry):
            outer_s[e] = (dot_nn(l_s[...], rbd_s[e]) * scaling).astype(jnp.bfloat16)
            return carry

        lax.fori_loop(0, FACTOR_WIDTH, one_outer, 0)

    per_group = fold * cols
    rows = per_step * per_group
    gap = jnp.zeros((HALF - cols, PAIR_W), jnp.bfloat16)
    pieces = []
    for u in range(per_step):
        at = pl.ds(pl.multiple_of((step * per_step + u) * FACTOR_WIDTH, FACTOR_WIDTH), FACTOR_WIDTH)
        outer = outer_s[:, at, :].reshape(FACTOR_WIDTH * FACTOR_WIDTH, wide)
        product = dot_nn(wt_s[...], outer).T
        for k in range(fold):
            pieces.append(product[k * HALF:k * HALF + cols])
    projected = jnp.concatenate(pieces, axis=0)
    middle = pair_ref[...].reshape(rows, PAIR_W) + projected + bias_ref[...]
    cotangent = cot_ref[...].reshape(rows, PAIR_W)

    average = jnp.mean(middle, axis=-1, keepdims=True)
    centred = middle - average
    variance = jnp.mean(centred * centred, axis=-1, keepdims=True)
    inverse = lax.rsqrt(variance + EPSILON)
    spread = centred * inverse
    before = dot_nn(spread.astype(jnp.bfloat16), expand_ref[...])
    phi = 0.5 * (1.0 + lax.erf(before * 0.7071067811865476))
    slope = phi + before * jnp.exp(-0.5 * before * before) * 0.3989422804014327
    hidden = (before * phi).astype(jnp.bfloat16)
    out_ref[...] = (middle + dot_nn(hidden, shrink_ref[...])).reshape(out_ref.shape)
    back_hidden = dot_nt(cotangent.astype(jnp.bfloat16), shrink_ref[...])
    back_before = (back_hidden * slope).astype(jnp.bfloat16)
    back_spread = dot_nt(back_before, expand_ref[...])
    centre_term = jnp.mean(back_spread, axis=-1, keepdims=True)
    slope_term = jnp.mean(back_spread * spread, axis=-1, keepdims=True)
    back_middle = cotangent + inverse * (back_spread - centre_term - spread * slope_term)
    back_middle = back_middle.astype(jnp.bfloat16)
    for u in range(per_step):
        parts = []
        for k in range(fold):
            begin = u * per_group + k * cols
            parts += [back_middle[begin:begin + cols], gap]
        padded = jnp.concatenate(parts, axis=0)
        back_outer = dot_nt(wec_s[...], padded).astype(jnp.bfloat16)
        at = pl.ds(pl.multiple_of((step * per_step + u) * FACTOR_WIDTH, FACTOR_WIDTH), FACTOR_WIDTH)
        outer_s[:, at, :] = back_outer.reshape(FACTOR_WIDTH, FACTOR_WIDTH, wide)

    @pl.when(step == pl.num_programs(0) - 1)
    def _epilogue():
        glacc_s[...] = jnp.zeros_like(glacc_s)
        batch = 2
        empty = jnp.zeros((LANES - seqs % LANES, LANES), jnp.float32) if seqs % LANES else None

        def some(n, carry):
            base = n * batch
            backs = [outer_s[base + u] for u in range(batch)]
            glacc_s[...] += dot_nt(
                jnp.concatenate([rbd_s[base + u] for u in range(batch)], axis=1),
                jnp.concatenate(backs, axis=1),
            )
            lows, highs = [], []
            for u in range(batch):
                full = dot_nn(lt_s[...], backs[u])
                low = high = None
                for k in range(fold):
                    v = k // 2
                    block = full[k * seqs:(k + 1) * seqs, v * LANES:(v + 1) * LANES]
                    if k % 2 == 0:
                        low = block if low is None else low + block
                    else:
                        high = block if high is None else high + block
                lows.append(low)
                highs.append(high)
            for u in range(0, batch, 2):
                both = jnp.where(low_half, lows[u], highs[u + 1]) + pltpu.roll(
                    jnp.where(low_half, lows[u + 1], highs[u]), HALF, axis=1
                )
                if empty is not None:
                    both = jnp.concatenate([both, empty], axis=0)
                turned = both.T
                stage_s[pl.ds(base + u, cols, stride=FACTOR_WIDTH), :] = turned[:cols]
                stage_s[pl.ds(base + u + 1, cols, stride=FACTOR_WIDTH), :] = turned[HALF:HALF + cols]
            return carry

        lax.fori_loop(0, FACTOR_WIDTH // batch, some, 0)
        for b in range(cols * FACTOR_WIDTH // LANES):
            block = stage_s[b * LANES:(b + 1) * LANES, :].T[:seqs]
            block = block * scaling
            if not first:
                block = block + grprev_ref[:, b * LANES:(b + 1) * LANES]
            gr_ref[:, b * LANES:(b + 1) * LANES] = block.astype(gr_ref.dtype)
        span = groups * FACTOR_WIDTH
        for k in range(fold):
            gl_ref[:, k * span:(k + 1) * span] = (
                glacc_s[k * seqs:(k + 1) * seqs, :] * scaling
            ).astype(jnp.bfloat16)


def pair_tile(
    place, lefts, rights, pair_features, cotangent, outer_weight, outer_bias, expand_weight, shrink_weight,
    before, chunks,
):
    seqs = lefts[0].shape[2] // 2
    rows, cols, _ = pair_features.shape
    fold = MXU_SIDE // HALF
    groups = rows // chunks // fold
    per_step = 2 if groups % 2 == 0 else 1
    steps = groups // per_step
    wide = fold * HALF
    channels = FACTOR_WIDTH * FACTOR_WIDTH
    stage_lanes = max(seqs, LANES)
    first = before is None
    last = chunks == 1 or not first
    block = pl.BlockSpec((per_step * fold, cols, PAIR_W), lambda n, place: (place[0] * steps + n, 0, 0))
    operands = (
        *lefts, *rights, pair_features, cotangent, outer_weight, outer_bias.reshape(1, -1), expand_weight,
        shrink_weight,
    )
    n_blocks = len(lefts) + len(rights)
    in_specs = [
        block if n in (n_blocks, n_blocks + 1) else whole_block(v.shape) for n, v in enumerate(operands)
    ]
    aliases = {}
    if not first:
        aliases = {1 + len(operands): 0}
        operands += tuple(before)
        in_specs += [pl.BlockSpec(memory_space=pl.ANY), whole_block(before[1].shape)]
    results = (
        jax.ShapeDtypeStruct(pair_features.shape, jnp.float32),
        jax.ShapeDtypeStruct((seqs, rows // chunks * FACTOR_WIDTH), jnp.bfloat16),
        jax.ShapeDtypeStruct((seqs, cols * FACTOR_WIDTH), jnp.bfloat16 if last else jnp.float32),
    )
    span = groups * FACTOR_WIDTH
    padded = groups * fold * HALF
    macs = 3 * FACTOR_WIDTH * span * fold * seqs * wide + padded * (2 * channels * MXU_SIDE + 8 * MXU_SIDE * MXU_SIDE)
    return pl.pallas_call(
        functools.partial(
            pair_kernel, seqs=seqs, cols=cols, fold=fold, per_step=per_step, left_blocks=len(lefts),
            right_blocks=len(rights), first=first, last=last,
        ),
        grid_spec=pltpu.PrefetchScalarGridSpec(
            num_scalar_prefetch=1,
            grid=(steps,),
            in_specs=in_specs,
            out_specs=[block, whole_block(results[1].shape), whole_block(results[2].shape)],
            scratch_shapes=[
                pltpu.VMEM((FACTOR_WIDTH, span, wide), jnp.bfloat16),
                pltpu.VMEM((FACTOR_WIDTH, fold * seqs, wide), jnp.bfloat16),
                pltpu.VMEM((span, fold * seqs), jnp.bfloat16),
                pltpu.VMEM((fold * seqs, span), jnp.bfloat16),
                pltpu.VMEM((max(cols * FACTOR_WIDTH, channels), stage_lanes), jnp.float32),
                pltpu.VMEM((channels, PAIR_W), jnp.bfloat16),
                pltpu.VMEM((PAIR_W, channels), jnp.bfloat16),
                pltpu.VMEM((fold * seqs, span), jnp.float32),
                pltpu.VMEM((len(lefts),) + lefts[0].shape, jnp.bfloat16),
                pltpu.VMEM((len(rights),) + rights[0].shape, jnp.bfloat16),
            ],
        ),
        out_shape=results,
        input_output_aliases=aliases,
        compiler_params=pltpu.CompilerParams(
            dimension_semantics=("arbitrary",), vmem_limit_bytes=48 * 1024 * 1024
        ),
        cost_estimate=pl.CostEstimate(
            flops=4 * macs, bytes_accessed=3 * pair_features.size * 4 // chunks, transcendentals=0
        ),
        name="pair_tile_%d_of_%d" % (1 if first else 2, chunks),
    )(place, *operands)


def local(
    alignment,
    pair_features,
    query_weight,
    key_weight,
    value_projection,
    gate_projection,
    gate_bias,
    output_projection,
    left_projection,
    right_projection,
    outer_weight,
    outer_bias,
    expand_weight,
    shrink_weight,
    cotangent,
):
    part_seqs, res_count, width = alignment.shape
    row_parts = lax.axis_size("row")
    col_parts = lax.axis_size("col")
    residues = res_count // row_parts
    own = jnp.transpose(alignment, (1, 0, 2)).reshape(row_parts, residues, part_seqs, width)
    columns = lax.all_to_all(own, "row", split_axis=0, concat_axis=0, tiled=True)
    attended, left, right = attend(
        columns, query_weight, key_weight, value_projection, gate_projection, gate_bias,
        output_projection, left_projection, right_projection,
    )
    ratio = col_parts // row_parts
    row, col = lax.axis_index("row"), lax.axis_index("col")

    def exchange_left(value, k):
        moves = [
            (r * col_parts + c, (c // ratio) * col_parts + (((c % ratio) * row_parts + r) ^ k))
            for r in range(row_parts)
            for c in range(col_parts)
        ]
        return lax.ppermute(value, ("row", "col"), moves)

    def exchange_right(value, k):
        return lax.ppermute(value, "row", [(r, r ^ k) for r in range(row_parts)])

    rights = [right] + [exchange_right(right, k) for k in range(1, row_parts)]
    right_places = [row ^ k for k in range(row_parts)]
    each = col_parts // CHUNKS
    shared = (outer_weight, outer_bias, expand_weight, shrink_weight)
    gl_parts, before = [], None
    for n in range(CHUNKS):
        lefts = [exchange_left(left, k) for k in range(n * each, (n + 1) * each)]
        left_places = [(col ^ k) % each for k in range(n * each, (n + 1) * each)]
        place = jnp.stack([(col // each) ^ n] + left_places + right_places).astype(jnp.int32)
        pair_out, gl, gr = pair_tile(place, lefts, rights, pair_features, cotangent, *shared, before, CHUNKS)
        before = (pair_out, gr)
        seqs, gl_width = gl.shape
        gl_parts.append(
            lax.all_to_all(
                gl.reshape(col_parts, seqs // col_parts, gl_width), "col", split_axis=0, concat_axis=0, tiled=True
            )
        )
        if n + 1 < CHUNKS:
            left = lax.optimization_barrier((left, *lefts))[0]
    returned = lax.all_to_all(attended, "row", split_axis=0, concat_axis=0, tiled=True)
    updated = jnp.transpose(returned.reshape(res_count, part_seqs, width), (1, 0, 2))

    halves = []
    for h in range(CHUNKS):
        half = 0.0
        for n in range(CHUNKS):
            owners = (h ^ n) * each
            half = half + jnp.sum(gl_parts[n][owners:owners + each].astype(jnp.float32), axis=0)
        fold = MXU_SIDE // HALF
        half = half.reshape(half.shape[0], fold, half.shape[1] // fold // FACTOR_WIDTH, FACTOR_WIDTH)
        halves.append(jnp.transpose(half, (0, 2, 1, 3)).reshape(half.shape[0], -1))
    grad_left = jnp.concatenate(halves, axis=1)
    gr_parts = lax.all_to_all(
        gr.reshape(row_parts, seqs // row_parts, gr.shape[1]), "row", split_axis=0, concat_axis=0, tiled=True
    )
    grad_right = jnp.sum(gr_parts.astype(jnp.float32), axis=0)
    return (updated, pair_out, grad_left, grad_right)


def solution(mesh):
    return jax.shard_map(
        local,
        mesh=mesh,
        in_specs=(P("row", "col", None), P("row", "col", None)) + (P(),) * 12 + (P("row", "col", None),),
        out_specs=(P("row", "col", None), P("row", "col", None), P("col", "row"), P("row", "col")),
        check_vma=False,
    )
```

```python
import functools

import jax
import jax.numpy as jnp
from jax import lax
from jax.experimental import pallas as pl
from jax.experimental.pallas import tpu as pltpu
from jax.sharding import PartitionSpec as P

ATTENTION_HEADS = 8
HEAD_WIDTH = 32
FACTOR_WIDTH = 32
PAIR_W = 128
EPSILON = 1e-05

LANES = 128
MXU_SIDE = 256
HALF = 64


def dot_nn(a, b):
    return lax.dot_general(a, b, (((1,), (0,)), ((), ())), preferred_element_type=jnp.float32)


def dot_nt(a, b):
    return lax.dot_general(a, b, (((1,), (1,)), ((), ())), preferred_element_type=jnp.float32)


def layer_normalise(rows):
    rows = rows.astype(jnp.float32)
    average = jnp.mean(rows, axis=-1, keepdims=True)
    centred = rows - average
    variance = jnp.mean(centred * centred, axis=-1, keepdims=True)
    return centred * lax.rsqrt(variance + EPSILON)


def attend_kernel(
    x_ref, bias_ref, wl_ref, wr_ref, *refs,
):
    square_refs, refs = refs[:5], refs[5:]
    upd_ref, left_ref, right_ref, q_s, k_s, v_s, g_s, a_s, w_s, sems = refs
    parts, residues, part_seqs, width = x_ref.shape
    seqs = parts * part_seqs
    copies = [pltpu.make_async_copy(ref, w_s.at[n], sems.at[n]) for n, ref in enumerate(square_refs)]
    for copy in copies:
        copy.start()
    x = jnp.concatenate([x_ref[s, r] for r in range(residues) for s in range(parts)], axis=0)
    normed = layer_normalise(x).astype(jnp.bfloat16)
    for n, ref in enumerate((q_s, k_s, v_s)):
        copies[n].wait()
        ref[...] = dot_nn(normed, w_s[n]).astype(jnp.bfloat16)
    copies[3].wait()
    g_s[...] = jax.nn.sigmoid(dot_nn(normed, w_s[3]) + bias_ref[...])

    head_of = lax.broadcasted_iota(jnp.int32, (1, width), 1) // HEAD_WIDTH
    masks = [(head_of == h).astype(jnp.float32) for h in range(ATTENTION_HEADS)]
    masks_low = [m.astype(jnp.bfloat16) for m in masks]

    def one_residue(r, carry):
        rows = pl.ds(pl.multiple_of(r * seqs, seqs), seqs)
        query = q_s[rows, :]
        spread_query = jnp.concatenate([query * m for m in masks_low], axis=0)
        scores = dot_nt(spread_query, k_s[rows, :]) * HEAD_WIDTH ** (-0.5)
        raised = jnp.exp(scores - jnp.max(scores, axis=-1, keepdims=True))
        inverse = 1.0 / jnp.sum(raised, axis=-1, keepdims=True)
        blended = dot_nn(raised.astype(jnp.bfloat16), v_s[rows, :]) * inverse
        total = blended[:seqs] * masks[0]
        for h in range(1, ATTENTION_HEADS):
            total = total + blended[h * seqs:(h + 1) * seqs] * masks[h]
        a_s[rows, :] = (g_s[rows, :] * total).astype(jnp.bfloat16)
        return carry

    lax.fori_loop(0, residues, one_residue, 0, unroll=2)

    copies[4].wait()
    updated = (x.astype(jnp.float32) + dot_nn(a_s[...], w_s[4])).astype(jnp.bfloat16)
    for r in range(residues):
        for s in range(parts):
            begin = r * seqs + s * part_seqs
            upd_ref[s, :, r * width:(r + 1) * width] = updated[begin:begin + part_seqs]
    factor_norm = layer_normalise(updated).astype(jnp.bfloat16)
    project = jnp.concatenate([wl_ref[...], wr_ref[...]], axis=0)
    for p in range(residues // 2):
        both = dot_nt(project, factor_norm[p * 2 * seqs:(p + 1) * 2 * seqs]).astype(jnp.bfloat16)
        for n in range(left_ref.shape[0]):
            left_ref[n, p] = both[:FACTOR_WIDTH]
        right_ref[p] = both[FACTOR_WIDTH:]


def whole_block(shape):
    return pl.BlockSpec(shape, lambda *_: (0,) * len(shape))


def attend(x, wq, wk, wv, wg, gate_bias, wo, wl, wr, copies):
    parts, residues, part_seqs, width = x.shape
    seqs = parts * part_seqs
    rows = residues * seqs
    factor = (residues // 2, FACTOR_WIDTH, 2 * seqs)
    operands = (x, gate_bias.reshape(1, -1), wl.T, wr.T)
    squares = (wq, wk, wv, wg, wo)
    results = (
        jax.ShapeDtypeStruct((parts, part_seqs, residues * width), jnp.bfloat16),
        jax.ShapeDtypeStruct((copies,) + factor, jnp.bfloat16),
        jax.ShapeDtypeStruct(factor, jnp.bfloat16),
    )
    macs = rows * width * (5 * width + 2 * FACTOR_WIDTH) + 2 * rows * ATTENTION_HEADS * width * seqs
    return pl.pallas_call(
        attend_kernel,
        grid=(1,),
        out_shape=results,
        in_specs=[whole_block(v.shape) for v in operands] + [pl.BlockSpec(memory_space=pltpu.HBM)] * len(squares),
        out_specs=[whole_block(v.shape) for v in results],
        scratch_shapes=[
            pltpu.VMEM((rows, width), jnp.bfloat16),
            pltpu.VMEM((rows, width), jnp.bfloat16),
            pltpu.VMEM((rows, width), jnp.bfloat16),
            pltpu.VMEM((rows, width), jnp.float32),
            pltpu.VMEM((rows, width), jnp.bfloat16),
            pltpu.VMEM((len(squares),) + wq.shape, jnp.bfloat16),
            pltpu.SemaphoreType.DMA((len(squares),)),
        ],
        compiler_params=pltpu.CompilerParams(
            dimension_semantics=("arbitrary",), vmem_limit_bytes=60 * 1024 * 1024
        ),
        cost_estimate=pl.CostEstimate(flops=2 * macs, bytes_accessed=4 * x.size * 2, transcendentals=rows * width),
        name="column_attention",
    )(*operands, *squares)


def pair_kernel(
    factor_ref, returned_ref, pair_ref, cot_ref, w_ref, bias_ref, expand_ref, shrink_ref,
    out_ref, gl_ref, both_ref,
    outer_s, rbd_s, l_s, lt_s, stage_s, wec_s, wt_s, glacc_s,
    *, seqs, cols, fold, unit, units,
):
    step = pl.program_id(0)
    row_parts, blocks, each = factor_ref.shape[:3]
    span = l_s.shape[0]
    groups = span // FACTOR_WIDTH
    wide = fold * HALF
    scaling = 1.0 / seqs
    stage_lanes = stage_s.shape[1]
    low_half = lax.broadcasted_iota(jnp.int32, (1, LANES), 1) < HALF

    @pl.when(step == 0)
    def _prologue():
        stage_s[:FACTOR_WIDTH * FACTOR_WIDTH, :LANES] = w_ref[...].astype(jnp.float32)
        for e in range(FACTOR_WIDTH):
            piece = stage_s[pl.ds(e, FACTOR_WIDTH, stride=FACTOR_WIDTH), :LANES]
            wec_s[e * FACTOR_WIDTH:(e + 1) * FACTOR_WIDTH, :] = piece.astype(jnp.bfloat16)
        for b in range(FACTOR_WIDTH * FACTOR_WIDTH // LANES):
            block = wec_s[b * LANES:(b + 1) * LANES, :].astype(jnp.float32)
            wt_s[:, b * LANES:(b + 1) * LANES] = block.T.astype(jnp.bfloat16)

        pairs = fold // 2
        for p in range(groups * pairs):
            column, inside = divmod(p, row_parts * each)
            block = factor_ref[inside // each, column, inside % each]
            g, at = p // pairs, p % pairs * 2 * seqs
            l_s[g * FACTOR_WIDTH:(g + 1) * FACTOR_WIDTH, at:at + 2 * seqs] = (
                block.astype(jnp.float32) * scaling
            ).astype(jnp.bfloat16)
        for b in range(span // LANES):
            block = l_s[b * LANES:(b + 1) * LANES, :].astype(jnp.float32)
            lt_s[:, b * LANES:(b + 1) * LANES] = block.T.astype(jnp.bfloat16)

        for p in range(cols // 2):
            block = factor_ref[p // each, blocks - 1, p % each].astype(jnp.float32)
            even = 2 * p * FACTOR_WIDTH
            odd = even + FACTOR_WIDTH
            if seqs % LANES == 0:
                stage_s[even:even + FACTOR_WIDTH, :] = block[:, :seqs]
                stage_s[odd:odd + FACTOR_WIDTH, :] = block[:, seqs:]
            else:
                stage_s[even:even + FACTOR_WIDTH, :] = block
                stage_s[odd:odd + FACTOR_WIDTH, :] = pltpu.roll(block, HALF, axis=1)

        blank = jnp.zeros((seqs, LANES), jnp.bfloat16)
        pad = jnp.zeros((HALF - cols, stage_lanes), jnp.float32)
        for e in range(0, FACTOR_WIDTH, 2):
            even = stage_s[pl.ds(e, cols, stride=FACTOR_WIDTH), :]
            odd = stage_s[pl.ds(e + 1, cols, stride=FACTOR_WIDTH), :]
            turned = jnp.concatenate([even, pad, odd, pad], axis=0).T[:seqs]
            rolled = pltpu.roll(turned, HALF, axis=1)
            for at, low, high in ((e, turned, rolled), (e + 1, rolled, turned)):
                low = jnp.where(low_half, low, 0.0).astype(jnp.bfloat16)
                high = jnp.where(low_half, 0.0, high).astype(jnp.bfloat16)
                for k in range(fold):
                    for v in range(wide // LANES):
                        value = blank if v != k // 2 else (low if k % 2 == 0 else high)
                        rbd_s[at, k * seqs:(k + 1) * seqs, v * LANES:(v + 1) * LANES] = value

        def one_outer(e, carry):
            outer_s[e] = dot_nn(l_s[...], rbd_s[e]).astype(jnp.bfloat16)
            return carry

        lax.fori_loop(0, FACTOR_WIDTH, one_outer, 0, unroll=4)

    per_group = fold * cols
    gap = jnp.zeros((HALF - cols, PAIR_W), jnp.bfloat16)

    def group_rows(u, n):
        g = (step * units + u) * unit + n
        return pl.ds(pl.multiple_of(g * FACTOR_WIDTH, FACTOR_WIDTH), FACTOR_WIDTH)

    def forward(u):
        pieces = []
        for n in range(unit):
            outer = outer_s[:, group_rows(u, n), :].reshape(FACTOR_WIDTH * FACTOR_WIDTH, wide)
            product = dot_nn(wt_s[...], outer).T
            pieces += [product[k * HALF:k * HALF + cols] for k in range(fold)]
        own = slice(u * unit * fold, (u + 1) * unit * fold)
        middle = pair_ref[own].reshape(-1, PAIR_W) + jnp.concatenate(pieces, axis=0) + bias_ref[...]
        average = jnp.mean(middle, axis=-1, keepdims=True)
        centred = middle - average
        variance = jnp.mean(centred * centred, axis=-1, keepdims=True)
        inverse = lax.rsqrt(variance + EPSILON)
        spread = centred * inverse
        before = dot_nn(spread.astype(jnp.bfloat16), expand_ref[...])
        cotangent = cot_ref[own].reshape(-1, PAIR_W)
        back_hidden = dot_nt(cotangent.astype(jnp.bfloat16), shrink_ref[...])
        return middle, inverse, spread, before, cotangent, back_hidden

    def backward(u, middle, inverse, spread, before, cotangent, back_hidden):
        own = slice(u * unit * fold, (u + 1) * unit * fold)
        phi = 0.5 * (1.0 + lax.erf(before * 0.7071067811865476))
        slope = phi + before * jnp.exp(-0.5 * before * before) * 0.3989422804014327
        hidden = (before * phi).astype(jnp.bfloat16)
        back_before = (back_hidden * slope).astype(jnp.bfloat16)
        back_spread = dot_nt(back_before, expand_ref[...])
        out_ref[own] = (middle + dot_nn(hidden, shrink_ref[...])).reshape(unit * fold, cols, PAIR_W)
        centre_term = jnp.mean(back_spread, axis=-1, keepdims=True)
        slope_term = jnp.mean(back_spread * spread, axis=-1, keepdims=True)
        back_middle = cotangent + inverse * (back_spread - centre_term - spread * slope_term)
        back_middle = back_middle.astype(jnp.bfloat16)
        for n in range(unit):
            parts = []
            for k in range(fold):
                begin = n * per_group + k * cols
                parts += [back_middle[begin:begin + cols], gap]
            back_outer = dot_nt(wec_s[...], jnp.concatenate(parts, axis=0)).astype(jnp.bfloat16)
            outer_s[:, group_rows(u, n), :] = back_outer.reshape(FACTOR_WIDTH, FACTOR_WIDTH, wide)

    held = forward(0)
    for u in range(units):
        ahead = forward(u + 1) if u + 1 < units else None
        backward(u, *held)
        held = ahead

    @pl.when(step == pl.num_programs(0) - 1)
    def _epilogue():
        glacc_s[...] = jnp.zeros_like(glacc_s)
        batch = 4
        empty = jnp.zeros((LANES - seqs % LANES, LANES), jnp.float32) if seqs % LANES else None

        def some(n, carry):
            base = n * batch
            backs = [outer_s[base + u] for u in range(batch)]
            glacc_s[...] += dot_nt(
                jnp.concatenate([rbd_s[base + u] for u in range(batch)], axis=1),
                jnp.concatenate(backs, axis=1),
            )
            lows, highs = [], []
            for u in range(batch):
                full = dot_nn(lt_s[...], backs[u])
                low = high = None
                for k in range(fold):
                    v = k // 2
                    block = full[k * seqs:(k + 1) * seqs, v * LANES:(v + 1) * LANES]
                    if k % 2 == 0:
                        low = block if low is None else low + block
                    else:
                        high = block if high is None else high + block
                lows.append(low)
                highs.append(high)
            for u in range(0, batch, 2):
                both = jnp.where(low_half, lows[u], highs[u + 1]) + pltpu.roll(
                    jnp.where(low_half, lows[u + 1], highs[u]), HALF, axis=1
                )
                if empty is not None:
                    both = jnp.concatenate([both, empty], axis=0)
                turned = both.T
                stage_s[pl.ds(base + u, cols, stride=FACTOR_WIDTH), :] = turned[:cols]
                stage_s[pl.ds(base + u + 1, cols, stride=FACTOR_WIDTH), :] = turned[HALF:HALF + cols]
            return carry

        lax.fori_loop(0, FACTOR_WIDTH // batch, some, 0, unroll=2)
        part_seqs, width = returned_ref.shape[1:]
        both_ref[:, :, :width] = returned_ref[...]
        for b in range(cols * FACTOR_WIDTH // LANES):
            block = stage_s[b * LANES:(b + 1) * LANES, :].T[:seqs].astype(jnp.bfloat16)
            both_ref[:, :, width + b * LANES:width + (b + 1) * LANES] = block.reshape(row_parts, part_seqs, LANES)
        for k in range(fold):
            gl_ref[:, k * span:(k + 1) * span] = (
                glacc_s[k * seqs:(k + 1) * seqs, :] * scaling
            ).astype(jnp.bfloat16)


def pair_tile(factors, returned, pair_features, cotangent, outer_weight, outer_bias, expand_weight, shrink_weight):
    seqs = factors.shape[-1] // 2
    rows, cols, _ = pair_features.shape
    fold = MXU_SIDE // HALF
    groups = rows // fold
    unit = 2 if groups % 2 == 0 else 1
    units = 2 if groups % (2 * unit) == 0 else 1
    steps = groups // unit // units
    wide = fold * HALF
    span = groups * FACTOR_WIDTH
    channels = FACTOR_WIDTH * FACTOR_WIDTH
    stage_lanes = max(seqs, LANES)
    block = pl.BlockSpec((unit * units * fold, cols, PAIR_W), lambda n: (n, 0, 0))
    operands = (
        factors, returned, pair_features, cotangent, outer_weight, outer_bias.reshape(1, -1), expand_weight,
        shrink_weight,
    )
    results = (
        jax.ShapeDtypeStruct(pair_features.shape, jnp.float32),
        jax.ShapeDtypeStruct((seqs, rows * FACTOR_WIDTH), jnp.bfloat16),
        jax.ShapeDtypeStruct(returned.shape[:2] + (returned.shape[2] + cols * FACTOR_WIDTH,), jnp.bfloat16),
    )
    padded = groups * wide
    macs = 3 * FACTOR_WIDTH * span * fold * seqs * wide + padded * (2 * channels * MXU_SIDE + 8 * MXU_SIDE * MXU_SIDE)
    return pl.pallas_call(
        functools.partial(pair_kernel, seqs=seqs, cols=cols, fold=fold, unit=unit, units=units),
        grid=(steps,),
        out_shape=results,
        in_specs=[block if n in (2, 3) else whole_block(v.shape) for n, v in enumerate(operands)],
        out_specs=[block, whole_block(results[1].shape), whole_block(results[2].shape)],
        scratch_shapes=[
            pltpu.VMEM((FACTOR_WIDTH, span, wide), jnp.bfloat16),
            pltpu.VMEM((FACTOR_WIDTH, fold * seqs, wide), jnp.bfloat16),
            pltpu.VMEM((span, fold * seqs), jnp.bfloat16),
            pltpu.VMEM((fold * seqs, span), jnp.bfloat16),
            pltpu.VMEM((max(cols * FACTOR_WIDTH, channels), stage_lanes), jnp.float32),
            pltpu.VMEM((channels, PAIR_W), jnp.bfloat16),
            pltpu.VMEM((PAIR_W, channels), jnp.bfloat16),
            pltpu.VMEM((fold * seqs, span), jnp.float32),
        ],
        compiler_params=pltpu.CompilerParams(
            dimension_semantics=("arbitrary",), vmem_limit_bytes=52 * 1024 * 1024
        ),
        cost_estimate=pl.CostEstimate(
            flops=2 * macs, bytes_accessed=3 * pair_features.size * 4, transcendentals=0
        ),
        name="pair_tile",
    )(*operands)


def local(
    alignment,
    pair_features,
    query_weight,
    key_weight,
    value_projection,
    gate_projection,
    gate_bias,
    output_projection,
    left_projection,
    right_projection,
    outer_weight,
    outer_bias,
    expand_weight,
    shrink_weight,
    cotangent,
):
    part_seqs, res_count, width = alignment.shape
    row_parts = lax.axis_size("row")
    col_parts = lax.axis_size("col")
    residues = res_count // row_parts
    own = jnp.transpose(alignment, (1, 0, 2)).reshape(row_parts, residues, part_seqs, width)
    columns = lax.all_to_all(own, "row", split_axis=0, concat_axis=0, tiled=True)
    attended, left, right = attend(
        columns, query_weight, key_weight, value_projection, gate_projection, gate_bias,
        output_projection, left_projection, right_projection, col_parts,
    )
    everyone = lax.all_to_all(left, "col", split_axis=0, concat_axis=0, tiled=True)
    ratio = col_parts // row_parts
    everyone = everyone.reshape((row_parts, ratio) + right.shape)
    with_right = jnp.concatenate(
        [everyone, jnp.broadcast_to(right, (row_parts, 1) + right.shape)], axis=1
    )
    factors = lax.all_to_all(with_right, "row", split_axis=0, concat_axis=0, tiled=True)
    pair_out, gl, both = pair_tile(
        factors, attended, pair_features, cotangent, outer_weight, outer_bias, expand_weight, shrink_weight
    )
    seqs, gl_width = gl.shape
    own_seqs = seqs // col_parts
    fold = MXU_SIDE // HALF
    both = lax.all_to_all(both, "row", split_axis=0, concat_axis=0, tiled=True)
    gl = lax.all_to_all(gl.reshape(col_parts, own_seqs, gl_width), "col", split_axis=0, concat_axis=0, tiled=True)
    returned = both[:, :, :residues * width].reshape(row_parts, part_seqs, residues, width)
    updated = jnp.transpose(returned, (1, 0, 2, 3)).reshape(part_seqs, res_count, width)
    grad_right = jnp.sum(both[:, :, residues * width:].astype(jnp.float32), axis=0)
    grad_left = jnp.sum(gl.astype(jnp.float32), axis=0)
    grad_left = grad_left.reshape(own_seqs, fold, gl_width // fold // FACTOR_WIDTH, FACTOR_WIDTH)
    grad_left = jnp.transpose(grad_left, (0, 2, 1, 3)).reshape(own_seqs, gl_width)
    return (updated, pair_out, grad_left, grad_right)


def solution(mesh):
    return jax.shard_map(
        local,
        mesh=mesh,
        in_specs=(P("row", "col", None), P("row", "col", None)) + (P(),) * 12 + (P("row", "col", None),),
        out_specs=(P("row", "col", None), P("row", "col", None), P("col", "row"), P("row", "col")),
        check_vma=False,
    )
```

```python
import functools

import jax
import jax.numpy as jnp
from jax import lax
from jax.experimental import pallas as pl
from jax.experimental.pallas import tpu as pltpu
from jax.sharding import PartitionSpec as P

ATTENTION_HEADS = 8
HEAD_WIDTH = 32
FACTOR_WIDTH = 32
PAIR_W = 128
EPSILON = 1e-05

LANES = 128
MXU_SIDE = 256
HALF = 64


def dot_nn(a, b):
    return lax.dot_general(a, b, (((1,), (0,)), ((), ())), preferred_element_type=jnp.float32)


def dot_nt(a, b):
    return lax.dot_general(a, b, (((1,), (1,)), ((), ())), preferred_element_type=jnp.float32)


def layer_normalise(rows):
    rows = rows.astype(jnp.float32)
    average = jnp.mean(rows, axis=-1, keepdims=True)
    centred = rows - average
    variance = jnp.mean(centred * centred, axis=-1, keepdims=True)
    return centred * lax.rsqrt(variance + EPSILON)


def attend_kernel(
    x_ref, bias_ref, wl_ref, wr_ref, *refs,
):
    square_refs, refs = refs[:5], refs[5:]
    upd_ref, factor_ref, q_s, k_s, v_s, g_s, a_s, w_s, sems = refs
    parts, residues, part_seqs, width = x_ref.shape
    seqs = parts * part_seqs
    copies = [pltpu.make_async_copy(ref, w_s.at[n], sems.at[n]) for n, ref in enumerate(square_refs)]
    for copy in copies:
        copy.start()
    x = jnp.concatenate([x_ref[s, r] for r in range(residues) for s in range(parts)], axis=0)
    normed = layer_normalise(x).astype(jnp.bfloat16)
    for n, ref in enumerate((q_s, k_s, v_s)):
        copies[n].wait()
        ref[...] = dot_nn(normed, w_s[n]).astype(jnp.bfloat16)
    copies[3].wait()
    g_s[...] = jax.nn.sigmoid(dot_nn(normed, w_s[3]) + bias_ref[...])

    head_of = lax.broadcasted_iota(jnp.int32, (1, width), 1) // HEAD_WIDTH
    masks = [(head_of == h).astype(jnp.float32) for h in range(ATTENTION_HEADS)]
    masks_low = [m.astype(jnp.bfloat16) for m in masks]

    def one_residue(r, carry):
        rows = pl.ds(pl.multiple_of(r * seqs, seqs), seqs)
        query = q_s[rows, :]
        spread_query = jnp.concatenate([query * m for m in masks_low], axis=0)
        scores = dot_nt(spread_query, k_s[rows, :]) * HEAD_WIDTH ** (-0.5)
        raised = jnp.exp(scores - jnp.max(scores, axis=-1, keepdims=True))
        inverse = 1.0 / jnp.sum(raised, axis=-1, keepdims=True)
        blended = dot_nn(raised.astype(jnp.bfloat16), v_s[rows, :]) * inverse
        total = blended[:seqs] * masks[0]
        for h in range(1, ATTENTION_HEADS):
            total = total + blended[h * seqs:(h + 1) * seqs] * masks[h]
        a_s[rows, :] = (g_s[rows, :] * total).astype(jnp.bfloat16)
        return carry

    lax.fori_loop(0, residues, one_residue, 0, unroll=2)

    copies[4].wait()
    updated = (x.astype(jnp.float32) + dot_nn(a_s[...], w_s[4])).astype(jnp.bfloat16)
    for r in range(residues):
        for s in range(parts):
            begin = r * seqs + s * part_seqs
            upd_ref[s, :, r * width:(r + 1) * width] = updated[begin:begin + part_seqs]
    factor_norm = layer_normalise(updated).astype(jnp.bfloat16)
    project = jnp.concatenate([wl_ref[...], wr_ref[...]], axis=0)
    for p in range(residues // 2):
        both = dot_nt(project, factor_norm[p * 2 * seqs:(p + 1) * 2 * seqs]).astype(jnp.bfloat16)
        for n in range(parts):
            factor_ref[n, 0, p] = both[:FACTOR_WIDTH]
            factor_ref[n, 1, p] = both[FACTOR_WIDTH:]


def whole_block(shape):
    return pl.BlockSpec(shape, lambda *_: (0,) * len(shape))


def in_hbm(*arrays):
    return [pltpu.with_memory_space_constraint(v, pltpu.HBM) for v in arrays]


def attend(x, wq, wk, wv, wg, gate_bias, wo, wl, wr):
    parts, residues, part_seqs, width = x.shape
    seqs = parts * part_seqs
    rows = residues * seqs
    operands = (x, *in_hbm(gate_bias.reshape(1, -1), wl.T, wr.T))
    squares = in_hbm(wq, wk, wv, wg, wo)
    results = (
        jax.ShapeDtypeStruct((parts, part_seqs, residues * width), jnp.bfloat16),
        jax.ShapeDtypeStruct((parts, 2, residues // 2, FACTOR_WIDTH, 2 * seqs), jnp.bfloat16),
    )
    macs = rows * width * (5 * width + 2 * FACTOR_WIDTH) + 2 * rows * ATTENTION_HEADS * width * seqs
    return pl.pallas_call(
        attend_kernel,
        grid=(1,),
        out_shape=results,
        in_specs=[whole_block(v.shape) for v in operands] + [pl.BlockSpec(memory_space=pltpu.HBM)] * len(squares),
        out_specs=[whole_block(v.shape) for v in results],
        scratch_shapes=[
            pltpu.VMEM((rows, width), jnp.bfloat16),
            pltpu.VMEM((rows, width), jnp.bfloat16),
            pltpu.VMEM((rows, width), jnp.bfloat16),
            pltpu.VMEM((rows, width), jnp.float32),
            pltpu.VMEM((rows, width), jnp.bfloat16),
            pltpu.VMEM((len(squares),) + wq.shape, jnp.bfloat16),
            pltpu.SemaphoreType.DMA((len(squares),)),
        ],
        compiler_params=pltpu.CompilerParams(
            dimension_semantics=("arbitrary",), vmem_limit_bytes=32 * 1024 * 1024
        ),
        cost_estimate=pl.CostEstimate(flops=2 * macs, bytes_accessed=4 * x.size * 2, transcendentals=rows * width),
        name="column_attention",
    )(*operands, *squares)


def right_kernel(factor_ref, w_ref, rbd_ref, wec_ref, wt_ref, stage_s, *, seqs, cols, fold):
    each = factor_ref.shape[2]
    wide = fold * HALF
    stage_lanes = stage_s.shape[1]
    low_half = lax.broadcasted_iota(jnp.int32, (1, LANES), 1) < HALF

    stage_s[:FACTOR_WIDTH * FACTOR_WIDTH, :LANES] = w_ref[...].astype(jnp.float32)
    for e in range(FACTOR_WIDTH):
        piece = stage_s[pl.ds(e, FACTOR_WIDTH, stride=FACTOR_WIDTH), :LANES]
        wec_ref[e * FACTOR_WIDTH:(e + 1) * FACTOR_WIDTH, :] = piece.astype(jnp.bfloat16)
    for b in range(FACTOR_WIDTH * FACTOR_WIDTH // LANES):
        block = wec_ref[b * LANES:(b + 1) * LANES, :].astype(jnp.float32)
        wt_ref[:, b * LANES:(b + 1) * LANES] = block.T.astype(jnp.bfloat16)

    for p in range(cols // 2):
        block = factor_ref[p // each, 1, p % each].astype(jnp.float32)
        even = 2 * p * FACTOR_WIDTH
        odd = even + FACTOR_WIDTH
        if seqs % LANES == 0:
            stage_s[even:even + FACTOR_WIDTH, :] = block[:, :seqs]
            stage_s[odd:odd + FACTOR_WIDTH, :] = block[:, seqs:]
        else:
            stage_s[even:even + FACTOR_WIDTH, :] = block
            stage_s[odd:odd + FACTOR_WIDTH, :] = pltpu.roll(block, HALF, axis=1)

    blank = jnp.zeros((seqs, LANES), jnp.bfloat16)
    pad = jnp.zeros((HALF - cols, stage_lanes), jnp.float32)
    for e in range(0, FACTOR_WIDTH, 2):
        even = stage_s[pl.ds(e, cols, stride=FACTOR_WIDTH), :]
        odd = stage_s[pl.ds(e + 1, cols, stride=FACTOR_WIDTH), :]
        turned = jnp.concatenate([even, pad, odd, pad], axis=0).T[:seqs]
        rolled = pltpu.roll(turned, HALF, axis=1)
        for at, low, high in ((e, turned, rolled), (e + 1, rolled, turned)):
            low = jnp.where(low_half, low, 0.0).astype(jnp.bfloat16)
            high = jnp.where(low_half, 0.0, high).astype(jnp.bfloat16)
            for k in range(fold):
                for v in range(wide // LANES):
                    value = blank if v != k // 2 else (low if k % 2 == 0 else high)
                    rbd_ref[at, k * seqs:(k + 1) * seqs, v * LANES:(v + 1) * LANES] = value


def right_matrices(factors, outer_weight):
    row_parts, _, each, _, lanes = factors.shape
    seqs, cols = lanes // 2, 2 * each * row_parts
    fold = MXU_SIDE // HALF
    channels, width = outer_weight.shape
    results = (
        jax.ShapeDtypeStruct((FACTOR_WIDTH, fold * seqs, fold * HALF), jnp.bfloat16),
        jax.ShapeDtypeStruct((channels, width), jnp.bfloat16),
        jax.ShapeDtypeStruct((width, channels), jnp.bfloat16),
    )
    resident = pl.BlockSpec(memory_space=pltpu.VMEM)
    return pl.pallas_call(
        functools.partial(right_kernel, seqs=seqs, cols=cols, fold=fold),
        out_shape=results,
        in_specs=[resident] * 2,
        out_specs=[resident] * 3,
        scratch_shapes=[pltpu.VMEM((max(cols * FACTOR_WIDTH, channels), max(seqs, LANES)), jnp.float32)],
        compiler_params=pltpu.CompilerParams(vmem_limit_bytes=16 * 1024 * 1024),
        cost_estimate=pl.CostEstimate(flops=6 * 10**9, bytes_accessed=4 * results[0].size, transcendentals=0),
        name="right_matrices",
    )(factors, outer_weight)


def pair_kernel(
    place_ref, *refs, seqs, cols, fold, unit, units, blocks,
):
    left_refs, refs = refs[:blocks], refs[blocks:]
    rbd_s, wec_s, wt_s, returned_ref, pair_ref, cot_ref, bias_ref, expand_ref, shrink_ref = refs[:9]
    out_ref, gl_ref, both_ref, outer_s, l_s, lt_s, stage_s, glacc_s, lblk_s = refs[9:]
    step = pl.program_id(0)
    row_parts, each = left_refs[0].shape[:2]
    span = l_s.shape[0]
    groups = span // FACTOR_WIDTH
    wide = fold * HALF
    scaling = 1.0 / seqs
    low_half = lax.broadcasted_iota(jnp.int32, (1, LANES), 1) < HALF

    @pl.when(step == 0)
    def _prologue():
        for n, ref in enumerate(left_refs):
            lblk_s[place_ref[n]] = ref[...]
        pairs = fold // 2
        for p in range(groups * pairs):
            column, inside = divmod(p, row_parts * each)
            block = lblk_s[column, inside // each, inside % each]
            g, at = p // pairs, p % pairs * 2 * seqs
            l_s[g * FACTOR_WIDTH:(g + 1) * FACTOR_WIDTH, at:at + 2 * seqs] = (
                block.astype(jnp.float32) * scaling
            ).astype(jnp.bfloat16)
        for b in range(span // LANES):
            block = l_s[b * LANES:(b + 1) * LANES, :].astype(jnp.float32)
            lt_s[:, b * LANES:(b + 1) * LANES] = block.T.astype(jnp.bfloat16)

        def one_outer(e, carry):
            outer_s[e] = dot_nn(l_s[...], rbd_s[e]).astype(jnp.bfloat16)
            return carry

        lax.fori_loop(0, FACTOR_WIDTH, one_outer, 0, unroll=4)

    per_group = fold * cols
    gap = jnp.zeros((HALF - cols, PAIR_W), jnp.bfloat16)

    def group_rows(u, n):
        g = (step * units + u) * unit + n
        return pl.ds(pl.multiple_of(g * FACTOR_WIDTH, FACTOR_WIDTH), FACTOR_WIDTH)

    def forward(u):
        pieces = []
        for n in range(unit):
            outer = outer_s[:, group_rows(u, n), :].reshape(FACTOR_WIDTH * FACTOR_WIDTH, wide)
            product = dot_nn(wt_s[...], outer).T
            pieces += [product[k * HALF:k * HALF + cols] for k in range(fold)]
        own = slice(u * unit * fold, (u + 1) * unit * fold)
        middle = pair_ref[own].reshape(-1, PAIR_W) + jnp.concatenate(pieces, axis=0) + bias_ref[...]
        average = jnp.mean(middle, axis=-1, keepdims=True)
        centred = middle - average
        variance = jnp.mean(centred * centred, axis=-1, keepdims=True)
        inverse = lax.rsqrt(variance + EPSILON)
        spread = centred * inverse
        before = dot_nn(spread.astype(jnp.bfloat16), expand_ref[...])
        cotangent = cot_ref[own].reshape(-1, PAIR_W)
        back_hidden = dot_nt(cotangent.astype(jnp.bfloat16), shrink_ref[...])
        return middle, inverse, spread, before, cotangent, back_hidden

    def backward(u, middle, inverse, spread, before, cotangent, back_hidden):
        own = slice(u * unit * fold, (u + 1) * unit * fold)
        phi = 0.5 * (1.0 + lax.erf(before * 0.7071067811865476))
        slope = phi + before * jnp.exp(-0.5 * before * before) * 0.3989422804014327
        hidden = (before * phi).astype(jnp.bfloat16)
        back_before = (back_hidden * slope).astype(jnp.bfloat16)
        back_spread = dot_nt(back_before, expand_ref[...])
        out_ref[own] = (middle + dot_nn(hidden, shrink_ref[...])).reshape(unit * fold, cols, PAIR_W)
        centre_term = jnp.mean(back_spread, axis=-1, keepdims=True)
        slope_term = jnp.mean(back_spread * spread, axis=-1, keepdims=True)
        back_middle = cotangent + inverse * (back_spread - centre_term - spread * slope_term)
        back_middle = back_middle.astype(jnp.bfloat16)
        for n in range(unit):
            parts = []
            for k in range(fold):
                begin = n * per_group + k * cols
                parts += [back_middle[begin:begin + cols], gap]
            back_outer = dot_nt(wec_s[...], jnp.concatenate(parts, axis=0)).astype(jnp.bfloat16)
            outer_s[:, group_rows(u, n), :] = back_outer.reshape(FACTOR_WIDTH, FACTOR_WIDTH, wide)

    held = forward(0)
    for u in range(units):
        ahead = forward(u + 1) if u + 1 < units else None
        backward(u, *held)
        held = ahead

    @pl.when(step == pl.num_programs(0) - 1)
    def _epilogue():
        glacc_s[...] = jnp.zeros_like(glacc_s)
        batch = 4
        empty = jnp.zeros((LANES - seqs % LANES, LANES), jnp.float32) if seqs % LANES else None

        def some(n, carry):
            base = n * batch
            backs = [outer_s[base + u] for u in range(batch)]
            glacc_s[...] += dot_nt(
                jnp.concatenate([rbd_s[base + u] for u in range(batch)], axis=1),
                jnp.concatenate(backs, axis=1),
            )
            lows, highs = [], []
            for u in range(batch):
                full = dot_nn(lt_s[...], backs[u])
                low = high = None
                for k in range(fold):
                    v = k // 2
                    block = full[k * seqs:(k + 1) * seqs, v * LANES:(v + 1) * LANES]
                    if k % 2 == 0:
                        low = block if low is None else low + block
                    else:
                        high = block if high is None else high + block
                lows.append(low)
                highs.append(high)
            for u in range(0, batch, 2):
                both = jnp.where(low_half, lows[u], highs[u + 1]) + pltpu.roll(
                    jnp.where(low_half, lows[u + 1], highs[u]), HALF, axis=1
                )
                if empty is not None:
                    both = jnp.concatenate([both, empty], axis=0)
                turned = both.T
                stage_s[pl.ds(base + u, cols, stride=FACTOR_WIDTH), :] = turned[:cols]
                stage_s[pl.ds(base + u + 1, cols, stride=FACTOR_WIDTH), :] = turned[HALF:HALF + cols]
            return carry

        lax.fori_loop(0, FACTOR_WIDTH // batch, some, 0, unroll=2)
        part_seqs, width = returned_ref.shape[1:]
        both_ref[:, :, :width] = returned_ref[...]
        for b in range(cols * FACTOR_WIDTH // LANES):
            block = stage_s[b * LANES:(b + 1) * LANES, :].T[:seqs].astype(jnp.bfloat16)
            both_ref[:, :, width + b * LANES:width + (b + 1) * LANES] = block.reshape(row_parts, part_seqs, LANES)
        for k in range(fold):
            gl_ref[:, k * span:(k + 1) * span] = (
                glacc_s[k * seqs:(k + 1) * seqs, :] * scaling
            ).astype(jnp.bfloat16)


def pair_tile(place, lefts, matrices, returned, pair_features, cotangent, outer_bias, expand_weight, shrink_weight):
    seqs = lefts[0].shape[-1] // 2
    rows, cols, _ = pair_features.shape
    fold = MXU_SIDE // HALF
    groups = rows // fold
    unit = 2 if groups % 2 == 0 else 1
    units = 4 if groups % (4 * unit) == 0 else 1
    steps = groups // unit // units
    wide = fold * HALF
    span = groups * FACTOR_WIDTH
    channels = FACTOR_WIDTH * FACTOR_WIDTH
    block = pl.BlockSpec((unit * units * fold, cols, PAIR_W), lambda n, place: (n, 0, 0))
    resident = pl.BlockSpec(memory_space=pltpu.VMEM)
    operands = (
        *lefts, *matrices, returned, pair_features, cotangent, outer_bias.reshape(1, -1), expand_weight,
        shrink_weight,
    )
    results = (
        jax.ShapeDtypeStruct(pair_features.shape, jnp.float32),
        jax.ShapeDtypeStruct((seqs, rows * FACTOR_WIDTH), jnp.bfloat16),
        jax.ShapeDtypeStruct(returned.shape[:2] + (returned.shape[2] + cols * FACTOR_WIDTH,), jnp.bfloat16),
    )
    padded = groups * wide
    macs = 3 * FACTOR_WIDTH * span * fold * seqs * wide + padded * (2 * channels * MXU_SIDE + 8 * MXU_SIDE * MXU_SIDE)
    return pl.pallas_call(
        functools.partial(
            pair_kernel, seqs=seqs, cols=cols, fold=fold, unit=unit, units=units, blocks=len(lefts)
        ),
        grid_spec=pltpu.PrefetchScalarGridSpec(
            num_scalar_prefetch=1,
            grid=(steps,),
            in_specs=[block if v is pair_features or v is cotangent else resident for v in operands],
            out_specs=[block, resident, resident],
            scratch_shapes=[
                pltpu.VMEM((FACTOR_WIDTH, span, wide), jnp.bfloat16),
                pltpu.VMEM((span, fold * seqs), jnp.bfloat16),
                pltpu.VMEM((fold * seqs, span), jnp.bfloat16),
                pltpu.VMEM((cols * FACTOR_WIDTH, max(seqs, LANES)), jnp.float32),
                pltpu.VMEM((fold * seqs, span), jnp.float32),
                pltpu.VMEM((len(lefts),) + lefts[0].shape, jnp.bfloat16),
            ],
        ),
        out_shape=results,
        compiler_params=pltpu.CompilerParams(
            dimension_semantics=("arbitrary",), vmem_limit_bytes=40 * 1024 * 1024
        ),
        cost_estimate=pl.CostEstimate(
            flops=2 * macs, bytes_accessed=3 * pair_features.size * 4, transcendentals=0
        ),
        name="pair_tile",
    )(place, *operands)


def local(
    alignment,
    pair_features,
    query_weight,
    key_weight,
    value_projection,
    gate_projection,
    gate_bias,
    output_projection,
    left_projection,
    right_projection,
    outer_weight,
    outer_bias,
    expand_weight,
    shrink_weight,
    cotangent,
):
    part_seqs, res_count, width = alignment.shape
    row_parts = lax.axis_size("row")
    col_parts = lax.axis_size("col")
    residues = res_count // row_parts
    own = jnp.transpose(alignment, (1, 0, 2)).reshape(row_parts, residues, part_seqs, width)
    columns = lax.all_to_all(own, "row", split_axis=0, concat_axis=0, tiled=True)
    attended, factors = attend(
        columns, query_weight, key_weight, value_projection, gate_projection, gate_bias,
        output_projection, left_projection, right_projection,
    )

    factors = lax.all_to_all(factors, "row", split_axis=0, concat_axis=0, tiled=True)
    left = factors[:, 0]
    ratio = col_parts // row_parts
    lefts, place = [], []
    for m in range(ratio):
        moves = [
            (q * col_parts + ratio * r + b, r * col_parts + ratio * q + (b + m) % ratio)
            for q in range(row_parts)
            for r in range(row_parts)
            for b in range(ratio)
        ]
        lefts.append(lax.ppermute(left, ("row", "col"), moves))
        place.append((lax.axis_index("col") + ratio - m) % ratio)
    matrices = right_matrices(factors, outer_weight)
    pair_out, gl, both = pair_tile(
        jnp.stack(place).astype(jnp.int32), lefts, matrices, attended, pair_features, cotangent, outer_bias,
        expand_weight, shrink_weight,
    )
    seqs, gl_width = gl.shape
    own_seqs = seqs // col_parts
    fold = MXU_SIDE // HALF
    both = lax.all_to_all(both, "row", split_axis=0, concat_axis=0, tiled=True)
    gl = lax.all_to_all(gl.reshape(col_parts, own_seqs, gl_width), "col", split_axis=0, concat_axis=0, tiled=True)
    returned = both[:, :, :residues * width].reshape(row_parts, part_seqs, residues, width)
    updated = jnp.transpose(returned, (1, 0, 2, 3)).reshape(part_seqs, res_count, width)
    grad_right = jnp.sum(both[:, :, residues * width:].astype(jnp.float32), axis=0)
    grad_left = jnp.sum(gl.astype(jnp.float32), axis=0)
    grad_left = grad_left.reshape(own_seqs, fold, gl_width // fold // FACTOR_WIDTH, FACTOR_WIDTH)
    grad_left = jnp.transpose(grad_left, (0, 2, 1, 3)).reshape(own_seqs, gl_width)
    return (updated, pair_out, grad_left, grad_right)


def solution(mesh):
    return jax.shard_map(
        local,
        mesh=mesh,
        in_specs=(P("row", "col", None), P("row", "col", None)) + (P(),) * 12 + (P("row", "col", None),),
        out_specs=(P("row", "col", None), P("row", "col", None), P("col", "row"), P("row", "col")),
        check_vma=False,
    )
```

```python
import functools

import jax
import jax.numpy as jnp
from jax import lax
from jax.experimental import pallas as pl
from jax.experimental.pallas import tpu as pltpu
from jax.sharding import PartitionSpec as P

ATTENTION_HEADS = 8
HEAD_WIDTH = 32
FACTOR_WIDTH = 32
PAIR_W = 128
EPSILON = 1e-05

LANES = 128
MXU_SIDE = 256
HALF = 64
TILE = 32


def dot_nn(a, b):
    return lax.dot_general(a, b, (((1,), (0,)), ((), ())), preferred_element_type=jnp.float32)


def dot_nt(a, b):
    return lax.dot_general(a, b, (((1,), (1,)), ((), ())), preferred_element_type=jnp.float32)


def layer_normalise(rows):
    rows = rows.astype(jnp.float32)
    average = jnp.mean(rows, axis=-1, keepdims=True)
    centred = rows - average
    variance = jnp.mean(centred * centred, axis=-1, keepdims=True)
    return centred * lax.rsqrt(variance + EPSILON)


def attend_kernel(
    x_ref, wq_ref, wk_ref, wv_ref, wg_ref, bias_ref, wo_ref, wl_ref, wr_ref,
    upd_ref, factor_ref, q_s, k_s, v_s, g_s, a_s, w_s, bias_s, project_s, sems,
):
    parts, residues, part_seqs, width = x_ref.shape
    seqs = parts * part_seqs
    sources = (wq_ref, wk_ref, wv_ref, wg_ref, wo_ref, bias_ref, wl_ref, wr_ref)
    targets = [w_s.at[n] for n in range(5)] + [bias_s, project_s.at[0], project_s.at[1]]
    copies = [pltpu.make_async_copy(a, b, sems.at[n]) for n, (a, b) in enumerate(zip(sources, targets))]
    for copy in copies:
        copy.start()
    x = jnp.concatenate([x_ref[s, r] for r in range(residues) for s in range(parts)], axis=0)
    normed = layer_normalise(x).astype(jnp.bfloat16)
    for n, ref in enumerate((q_s, k_s, v_s)):
        copies[n].wait()
        ref[...] = dot_nn(normed, w_s[n]).astype(jnp.bfloat16)
    copies[3].wait()
    copies[5].wait()
    g_s[...] = jax.nn.sigmoid(dot_nn(normed, w_s[3]) + bias_s[...])

    head_of = lax.broadcasted_iota(jnp.int32, (1, width), 1) // HEAD_WIDTH
    masks = [(head_of == h).astype(jnp.float32) for h in range(ATTENTION_HEADS)]
    masks_low = [m.astype(jnp.bfloat16) for m in masks]

    def one_residue(r, carry):
        rows = pl.ds(pl.multiple_of(r * seqs, seqs), seqs)
        query = q_s[rows, :]
        spread_query = jnp.concatenate([query * m for m in masks_low], axis=0)
        scores = dot_nt(spread_query, k_s[rows, :]) * HEAD_WIDTH ** (-0.5)
        raised = jnp.exp(scores - jnp.max(scores, axis=-1, keepdims=True))
        inverse = 1.0 / jnp.sum(raised, axis=-1, keepdims=True)
        blended = dot_nn(raised.astype(jnp.bfloat16), v_s[rows, :]) * inverse
        total = blended[:seqs] * masks[0]
        for h in range(1, ATTENTION_HEADS):
            total = total + blended[h * seqs:(h + 1) * seqs] * masks[h]
        a_s[rows, :] = (g_s[rows, :] * total).astype(jnp.bfloat16)
        return carry

    lax.fori_loop(0, residues, one_residue, 0, unroll=4 if residues % 4 == 0 else 2)

    copies[4].wait()
    updated = (x.astype(jnp.float32) + dot_nn(a_s[...], w_s[4])).astype(jnp.bfloat16)
    for r in range(residues):
        for s in range(parts):
            begin = r * seqs + s * part_seqs
            upd_ref[s, :, r * width:(r + 1) * width] = updated[begin:begin + part_seqs]
    factor_norm = layer_normalise(updated).astype(jnp.bfloat16)
    copies[6].wait()
    copies[7].wait()
    project = project_s[...].reshape(2 * FACTOR_WIDTH, width)
    for p in range(residues // 2):
        both = dot_nt(project, factor_norm[p * 2 * seqs:(p + 1) * 2 * seqs]).astype(jnp.bfloat16)
        for n in range(parts):
            factor_ref[n, 0, p] = both[:FACTOR_WIDTH]
            factor_ref[n, 1, p] = both[FACTOR_WIDTH:]


def whole_block(shape):
    return pl.BlockSpec(shape, lambda *_: (0,) * len(shape))


def in_hbm(*arrays):
    return [pltpu.with_memory_space_constraint(v, pltpu.HBM) for v in arrays]


def attend(x, wq, wk, wv, wg, gate_bias, wo, wl, wr):
    parts, residues, part_seqs, width = x.shape
    seqs = parts * part_seqs
    rows = residues * seqs
    operands = in_hbm(wq, wk, wv, wg, gate_bias.reshape(1, -1), wo, wl.T, wr.T)
    resident = pl.BlockSpec(memory_space=pltpu.VMEM)
    results = (
        jax.ShapeDtypeStruct((parts, part_seqs, residues * width), jnp.bfloat16),
        jax.ShapeDtypeStruct((parts, 2, residues // 2, FACTOR_WIDTH, 2 * seqs), jnp.bfloat16),
    )
    macs = rows * width * (5 * width + 2 * FACTOR_WIDTH) + 2 * rows * ATTENTION_HEADS * width * seqs
    return pl.pallas_call(
        attend_kernel,
        out_shape=results,
        in_specs=[resident] + [pl.BlockSpec(memory_space=pltpu.HBM)] * len(operands),
        out_specs=[resident] * 2,
        scratch_shapes=[
            pltpu.VMEM((rows, width), jnp.bfloat16),
            pltpu.VMEM((rows, width), jnp.bfloat16),
            pltpu.VMEM((rows, width), jnp.bfloat16),
            pltpu.VMEM((rows, width), jnp.float32),
            pltpu.VMEM((rows, width), jnp.bfloat16),
            pltpu.VMEM((5,) + wq.shape, jnp.bfloat16),
            pltpu.VMEM((1, width), jnp.float32),
            pltpu.VMEM((2, FACTOR_WIDTH, width), jnp.bfloat16),
            pltpu.SemaphoreType.DMA((len(operands),)),
        ],
        compiler_params=pltpu.CompilerParams(vmem_limit_bytes=32 * 1024 * 1024),
        cost_estimate=pl.CostEstimate(flops=2 * macs, bytes_accessed=4 * x.size * 2, transcendentals=rows * width),
        name="column_attention",
    )(x, *operands)


def right_kernel(factor_ref, w_ref, rbd_ref, wec_ref, wt_ref, stage_s, *, seqs, cols, fold):
    each = factor_ref.shape[2]
    wide = fold * HALF
    stage_lanes = stage_s.shape[1]
    low_half = lax.broadcasted_iota(jnp.int32, (1, LANES), 1) < HALF

    stage_s[:FACTOR_WIDTH * FACTOR_WIDTH, :LANES] = w_ref[...].astype(jnp.float32)
    for e in range(FACTOR_WIDTH):
        piece = stage_s[pl.ds(e, FACTOR_WIDTH, stride=FACTOR_WIDTH), :LANES]
        wec_ref[e * FACTOR_WIDTH:(e + 1) * FACTOR_WIDTH, :] = piece.astype(jnp.bfloat16)
    for b in range(FACTOR_WIDTH * FACTOR_WIDTH // LANES):
        block = wec_ref[b * LANES:(b + 1) * LANES, :].astype(jnp.float32)
        wt_ref[:, b * LANES:(b + 1) * LANES] = block.T.astype(jnp.bfloat16)

    for p in range(cols // 2):
        block = factor_ref[p // each, 1, p % each].astype(jnp.float32)
        even = 2 * p * FACTOR_WIDTH
        odd = even + FACTOR_WIDTH
        if seqs % LANES == 0:
            stage_s[even:even + FACTOR_WIDTH, :] = block[:, :seqs]
            stage_s[odd:odd + FACTOR_WIDTH, :] = block[:, seqs:]
        else:
            stage_s[even:even + FACTOR_WIDTH, :] = block
            stage_s[odd:odd + FACTOR_WIDTH, :] = pltpu.roll(block, HALF, axis=1)

    blank = jnp.zeros((seqs, LANES), jnp.bfloat16)
    pad = jnp.zeros((HALF - cols, stage_lanes), jnp.float32)
    for e in range(0, FACTOR_WIDTH, 2):
        even = stage_s[pl.ds(e, cols, stride=FACTOR_WIDTH), :]
        odd = stage_s[pl.ds(e + 1, cols, stride=FACTOR_WIDTH), :]
        turned = jnp.concatenate([even, pad, odd, pad], axis=0).T[:seqs]
        rolled = pltpu.roll(turned, HALF, axis=1)
        for at, low, high in ((e, turned, rolled), (e + 1, rolled, turned)):
            low = jnp.where(low_half, low, 0.0).astype(jnp.bfloat16)
            high = jnp.where(low_half, 0.0, high).astype(jnp.bfloat16)
            for k in range(fold):
                for v in range(wide // LANES):
                    value = blank if v != k // 2 else (low if k % 2 == 0 else high)
                    rbd_ref[at, k * seqs:(k + 1) * seqs, v * LANES:(v + 1) * LANES] = value


def right_matrices(factors, outer_weight):
    row_parts, _, each, _, lanes = factors.shape
    seqs, cols = lanes // 2, 2 * each * row_parts
    fold = MXU_SIDE // HALF
    channels, width = outer_weight.shape
    results = (
        jax.ShapeDtypeStruct((FACTOR_WIDTH, fold * seqs, fold * HALF), jnp.bfloat16),
        jax.ShapeDtypeStruct((channels, width), jnp.bfloat16),
        jax.ShapeDtypeStruct((width, channels), jnp.bfloat16),
    )
    resident = pl.BlockSpec(memory_space=pltpu.VMEM)
    return pl.pallas_call(
        functools.partial(right_kernel, seqs=seqs, cols=cols, fold=fold),
        out_shape=results,
        in_specs=[resident] * 2,
        out_specs=[resident] * 3,
        scratch_shapes=[pltpu.VMEM((max(cols * FACTOR_WIDTH, channels), max(seqs, LANES)), jnp.float32)],
        compiler_params=pltpu.CompilerParams(vmem_limit_bytes=16 * 1024 * 1024),
        cost_estimate=pl.CostEstimate(flops=6 * 10**9, bytes_accessed=4 * results[0].size, transcendentals=0),
        name="right_matrices",
    )(factors, outer_weight)


def pair_kernel(
    place_ref, *refs, seqs, cols, fold, unit, units, blocks,
):
    left_refs, refs = refs[:blocks], refs[blocks:]
    rbd_s, wec_s, wt_s, returned_ref, pair_ref, cot_ref, bias_ref, expand_ref, shrink_ref = refs[:9]
    out_ref, gl_ref, both_ref, outer_s, l_s, lt_s, stage_s, glacc_s, lblk_s = refs[9:]
    step = pl.program_id(0)
    row_parts, each = left_refs[0].shape[:2]
    span = l_s.shape[0]
    groups = span // FACTOR_WIDTH
    wide = fold * HALF
    scaling = 1.0 / seqs
    low_half = lax.broadcasted_iota(jnp.int32, (1, LANES), 1) < HALF

    @pl.when(step == 0)
    def _prologue():
        for n, ref in enumerate(left_refs):
            lblk_s[place_ref[n]] = ref[...]
        pairs = fold // 2
        for p in range(groups * pairs):
            column, inside = divmod(p, row_parts * each)
            block = lblk_s[column, inside // each, inside % each]
            g, at = p // pairs, p % pairs * 2 * seqs
            l_s[g * FACTOR_WIDTH:(g + 1) * FACTOR_WIDTH, at:at + 2 * seqs] = (
                block.astype(jnp.float32) * scaling
            ).astype(jnp.bfloat16)
        for b in range(span // LANES):
            block = l_s[b * LANES:(b + 1) * LANES, :].astype(jnp.float32)
            lt_s[:, b * LANES:(b + 1) * LANES] = block.T.astype(jnp.bfloat16)

        def one_outer(e, carry):
            outer_s[e] = dot_nn(l_s[...], rbd_s[e]).astype(jnp.bfloat16)
            return carry

        lax.fori_loop(0, FACTOR_WIDTH, one_outer, 0, unroll=4)

    per_group = fold * cols
    gap = jnp.zeros((HALF - cols, PAIR_W), jnp.bfloat16)

    def group_rows(u, n):
        g = (step * units + u) * unit + n
        return pl.ds(pl.multiple_of(g * FACTOR_WIDTH, FACTOR_WIDTH), FACTOR_WIDTH)

    def forward(u):
        pieces = []
        for n in range(unit):
            outer = outer_s[:, group_rows(u, n), :].reshape(FACTOR_WIDTH * FACTOR_WIDTH, wide)
            product = dot_nn(wt_s[...], outer).T
            pieces += [product[k * HALF:k * HALF + cols] for k in range(fold)]
        own = slice(u * unit * fold, (u + 1) * unit * fold)
        projected = jnp.concatenate(pieces, axis=0)
        pair = pair_ref[own].reshape(-1, PAIR_W)
        middles, inverses, spreads = [], [], []
        for at in range(0, projected.shape[0], TILE):
            middle = pair[at:at + TILE] + projected[at:at + TILE] + bias_ref[...]
            average = jnp.mean(middle, axis=-1, keepdims=True)
            centred = middle - average
            variance = jnp.mean(centred * centred, axis=-1, keepdims=True)
            inverse = lax.rsqrt(variance + EPSILON)
            middles.append(middle)
            inverses.append(inverse)
            spreads.append(centred * inverse)
        spread_low = jnp.concatenate([v.astype(jnp.bfloat16) for v in spreads], axis=0)
        cotangent = cot_ref[own].reshape(-1, PAIR_W)
        before = dot_nn(spread_low, expand_ref[...])
        back_hidden = dot_nt(cotangent.astype(jnp.bfloat16), shrink_ref[...])
        return middles, inverses, spreads, before, cotangent, back_hidden

    def backward(u, middles, inverses, spreads, before, cotangent, back_hidden):
        own = slice(u * unit * fold, (u + 1) * unit * fold)
        rows, width = before.shape
        hidden, back_before = [], []
        for at in range(0, rows, TILE):
            hidden_parts, back_parts = [], []
            for v in range(0, width, MXU_SIDE):
                x = before[at:at + TILE, v:v + MXU_SIDE]
                phi = 0.5 * (1.0 + lax.erf(x * 0.7071067811865476))
                slope = phi + x * jnp.exp(-0.5 * x * x) * 0.3989422804014327
                hidden_parts.append((x * phi).astype(jnp.bfloat16))
                back_parts.append((back_hidden[at:at + TILE, v:v + MXU_SIDE] * slope).astype(jnp.bfloat16))
            hidden.append(jnp.concatenate(hidden_parts, axis=1))
            back_before.append(jnp.concatenate(back_parts, axis=1))
        back_spread = dot_nt(jnp.concatenate(back_before, axis=0), expand_ref[...])
        change = dot_nn(jnp.concatenate(hidden, axis=0), shrink_ref[...])
        out_ref[own] = (jnp.concatenate(middles, axis=0) + change).reshape(unit * fold, cols, PAIR_W)
        back_middle = []
        for n, at in enumerate(range(0, rows, TILE)):
            back, spread = back_spread[at:at + TILE], spreads[n]
            centre_term = jnp.mean(back, axis=-1, keepdims=True)
            slope_term = jnp.mean(back * spread, axis=-1, keepdims=True)
            back = cotangent[at:at + TILE] + inverses[n] * (back - centre_term - spread * slope_term)
            back_middle.append(back.astype(jnp.bfloat16))
        back_middle = jnp.concatenate(back_middle, axis=0)
        for n in range(unit):
            parts = []
            for k in range(fold):
                begin = n * per_group + k * cols
                parts += [back_middle[begin:begin + cols], gap]
            back_outer = dot_nt(wec_s[...], jnp.concatenate(parts, axis=0)).astype(jnp.bfloat16)
            outer_s[:, group_rows(u, n), :] = back_outer.reshape(FACTOR_WIDTH, FACTOR_WIDTH, wide)

    held = forward(0)
    for u in range(units):
        ahead = forward(u + 1) if u + 1 < units else None
        backward(u, *held)
        held = ahead

    @pl.when(step == pl.num_programs(0) - 1)
    def _epilogue():
        glacc_s[...] = jnp.zeros_like(glacc_s)
        batch = 4
        empty = jnp.zeros((LANES - seqs % LANES, LANES), jnp.float32) if seqs % LANES else None

        def some(n, carry):
            base = n * batch
            backs = [outer_s[base + u] for u in range(batch)]
            glacc_s[...] += dot_nt(
                jnp.concatenate([rbd_s[base + u] for u in range(batch)], axis=1),
                jnp.concatenate(backs, axis=1),
            )
            lows, highs = [], []
            for u in range(batch):
                full = dot_nn(lt_s[...], backs[u])
                low = high = None
                for k in range(fold):
                    v = k // 2
                    block = full[k * seqs:(k + 1) * seqs, v * LANES:(v + 1) * LANES]
                    if k % 2 == 0:
                        low = block if low is None else low + block
                    else:
                        high = block if high is None else high + block
                lows.append(low)
                highs.append(high)
            for u in range(0, batch, 2):
                both = jnp.where(low_half, lows[u], highs[u + 1]) + pltpu.roll(
                    jnp.where(low_half, lows[u + 1], highs[u]), HALF, axis=1
                )
                if empty is not None:
                    both = jnp.concatenate([both, empty], axis=0)
                turned = both.T
                stage_s[pl.ds(base + u, cols, stride=FACTOR_WIDTH), :] = turned[:cols]
                stage_s[pl.ds(base + u + 1, cols, stride=FACTOR_WIDTH), :] = turned[HALF:HALF + cols]
            return carry

        lax.fori_loop(0, FACTOR_WIDTH // batch, some, 0, unroll=2)
        part_seqs, width = returned_ref.shape[1:]
        both_ref[:, :, :width] = returned_ref[...]
        for b in range(cols * FACTOR_WIDTH // LANES):
            block = stage_s[b * LANES:(b + 1) * LANES, :].T[:seqs].astype(jnp.bfloat16)
            both_ref[:, :, width + b * LANES:width + (b + 1) * LANES] = block.reshape(row_parts, part_seqs, LANES)
        for k in range(fold):
            gl_ref[:, k * span:(k + 1) * span] = (
                glacc_s[k * seqs:(k + 1) * seqs, :] * scaling
            ).astype(jnp.bfloat16)


def pair_tile(place, lefts, matrices, returned, pair_features, cotangent, outer_bias, expand_weight, shrink_weight):
    seqs = lefts[0].shape[-1] // 2
    rows, cols, _ = pair_features.shape
    fold = MXU_SIDE // HALF
    groups = rows // fold
    unit = 2 if groups % 2 == 0 else 1
    units = 4 if groups % (4 * unit) == 0 else 1
    steps = groups // unit // units
    wide = fold * HALF
    span = groups * FACTOR_WIDTH
    channels = FACTOR_WIDTH * FACTOR_WIDTH
    block = pl.BlockSpec((unit * units * fold, cols, PAIR_W), lambda n, place: (n, 0, 0))
    resident = pl.BlockSpec(memory_space=pltpu.VMEM)
    operands = (
        *lefts, *matrices, returned, pair_features, cotangent, outer_bias.reshape(1, -1), expand_weight,
        shrink_weight,
    )
    results = (
        jax.ShapeDtypeStruct(pair_features.shape, jnp.float32),
        jax.ShapeDtypeStruct((seqs, rows * FACTOR_WIDTH), jnp.bfloat16),
        jax.ShapeDtypeStruct(returned.shape[:2] + (returned.shape[2] + cols * FACTOR_WIDTH,), jnp.bfloat16),
    )
    padded = groups * wide
    macs = 3 * FACTOR_WIDTH * span * fold * seqs * wide + padded * (2 * channels * MXU_SIDE + 8 * MXU_SIDE * MXU_SIDE)
    return pl.pallas_call(
        functools.partial(
            pair_kernel, seqs=seqs, cols=cols, fold=fold, unit=unit, units=units, blocks=len(lefts)
        ),
        grid_spec=pltpu.PrefetchScalarGridSpec(
            num_scalar_prefetch=1,
            grid=(steps,),
            in_specs=[block if v is pair_features or v is cotangent else resident for v in operands],
            out_specs=[block, resident, resident],
            scratch_shapes=[
                pltpu.VMEM((FACTOR_WIDTH, span, wide), jnp.bfloat16),
                pltpu.VMEM((span, fold * seqs), jnp.bfloat16),
                pltpu.VMEM((fold * seqs, span), jnp.bfloat16),
                pltpu.VMEM((cols * FACTOR_WIDTH, max(seqs, LANES)), jnp.float32),
                pltpu.VMEM((fold * seqs, span), jnp.float32),
                pltpu.VMEM((len(lefts),) + lefts[0].shape, jnp.bfloat16),
            ],
        ),
        out_shape=results,
        compiler_params=pltpu.CompilerParams(
            dimension_semantics=("arbitrary",), vmem_limit_bytes=40 * 1024 * 1024
        ),
        cost_estimate=pl.CostEstimate(
            flops=2 * macs, bytes_accessed=3 * pair_features.size * 4, transcendentals=0
        ),
        name="pair_tile",
    )(place, *operands)


def spread_out(q, count):
    return q if count % 2 else q % 2 * (count // 2) + q // 2


def local(
    alignment,
    pair_features,
    query_weight,
    key_weight,
    value_projection,
    gate_projection,
    gate_bias,
    output_projection,
    left_projection,
    right_projection,
    outer_weight,
    outer_bias,
    expand_weight,
    shrink_weight,
    cotangent,
):
    part_seqs, res_count, width = alignment.shape
    row_parts = lax.axis_size("row")
    col_parts = lax.axis_size("col")
    residues = res_count // row_parts
    own = jnp.transpose(alignment, (1, 0, 2)).reshape(row_parts, residues, part_seqs, width)
    columns = lax.all_to_all(own, "row", split_axis=0, concat_axis=0, tiled=True)
    attended, factors = attend(
        columns, query_weight, key_weight, value_projection, gate_projection, gate_bias,
        output_projection, left_projection, right_projection,
    )

    factors = lax.all_to_all(factors, "row", split_axis=0, concat_axis=0, tiled=True)
    left = factors[:, 0]
    ratio = col_parts // row_parts
    lefts, place = [], []
    for m in range(ratio):
        moves = [
            (q * col_parts + ratio * r + b, r * col_parts + ratio * spread_out(q, row_parts) + (b + m) % ratio)
            for q in range(row_parts)
            for r in range(row_parts)
            for b in range(ratio)
        ]
        lefts.append(lax.ppermute(left, ("row", "col"), moves))
        place.append((lax.axis_index("col") + ratio - m) % ratio)
    matrices = right_matrices(factors, outer_weight)
    pair_out, gl, both = pair_tile(
        jnp.stack(place).astype(jnp.int32), lefts, matrices, attended, pair_features, cotangent, outer_bias,
        expand_weight, shrink_weight,
    )
    seqs, gl_width = gl.shape
    own_seqs = seqs // col_parts
    fold = MXU_SIDE // HALF
    both = lax.all_to_all(both, "row", split_axis=0, concat_axis=0, tiled=True)
    gl = lax.all_to_all(gl.reshape(col_parts, own_seqs, gl_width), "col", split_axis=0, concat_axis=0, tiled=True)
    returned = both[:, :, :residues * width].reshape(row_parts, part_seqs, residues, width)
    updated = jnp.transpose(returned, (1, 0, 2, 3)).reshape(part_seqs, res_count, width)
    grad_right = jnp.sum(both[:, :, residues * width:].astype(jnp.float32), axis=0)
    grad_left = jnp.sum(gl.astype(jnp.float32), axis=0)
    grad_left = grad_left.reshape(own_seqs, fold, gl_width // fold // FACTOR_WIDTH, FACTOR_WIDTH)
    grad_left = jnp.transpose(grad_left, (0, 2, 1, 3)).reshape(own_seqs, gl_width)
    return (updated, pair_out, grad_left, grad_right)


def solution(mesh):
    return jax.shard_map(
        local,
        mesh=mesh,
        in_specs=(P("row", "col", None), P("row", "col", None)) + (P(),) * 12 + (P("row", "col", None),),
        out_specs=(P("row", "col", None), P("row", "col", None), P("col", "row"), P("row", "col")),
        check_vma=False,
    )
```

```python
import functools

import jax
import jax.numpy as jnp
from jax import lax
from jax.experimental import pallas as pl
from jax.experimental.pallas import tpu as pltpu
from jax.sharding import PartitionSpec as P

ATTENTION_HEADS = 8
HEAD_WIDTH = 32
FACTOR_WIDTH = 32
PAIR_W = 128
EPSILON = 1e-05

LANES = 128
MXU_SIDE = 256
HALF = 64
TILE = 32


def dot_nn(a, b):
    return lax.dot_general(a, b, (((1,), (0,)), ((), ())), preferred_element_type=jnp.float32)


def dot_nt(a, b):
    return lax.dot_general(a, b, (((1,), (1,)), ((), ())), preferred_element_type=jnp.float32)


def layer_normalise(rows):
    rows = rows.astype(jnp.float32)
    average = jnp.mean(rows, axis=-1, keepdims=True)
    centred = rows - average
    variance = jnp.mean(centred * centred, axis=-1, keepdims=True)
    return centred * lax.rsqrt(variance + EPSILON)


def attend_kernel(
    x_ref, wq_ref, wk_ref, wv_ref, wg_ref, bias_ref, wo_ref, wl_ref, wr_ref,
    upd_ref, factor_ref, q_s, k_s, v_s, g_s, a_s, w_s, bias_s, project_s, sems,
):
    parts, residues, part_seqs, width = x_ref.shape
    seqs = parts * part_seqs
    sources = (wq_ref, wk_ref, wv_ref, wg_ref, wo_ref, bias_ref, wl_ref, wr_ref)
    targets = [w_s.at[n] for n in range(5)] + [bias_s, project_s.at[0], project_s.at[1]]
    copies = [pltpu.make_async_copy(a, b, sems.at[n]) for n, (a, b) in enumerate(zip(sources, targets))]
    for copy in copies:
        copy.start()
    x = jnp.concatenate([x_ref[s, r] for r in range(residues) for s in range(parts)], axis=0)
    normed = layer_normalise(x).astype(jnp.bfloat16)
    for n, ref in enumerate((q_s, k_s, v_s)):
        copies[n].wait()
        ref[...] = dot_nn(normed, w_s[n]).astype(jnp.bfloat16)
    copies[3].wait()
    copies[5].wait()
    g_s[...] = jax.nn.sigmoid(dot_nn(normed, w_s[3]) + bias_s[...])

    head_of = lax.broadcasted_iota(jnp.int32, (1, width), 1) // HEAD_WIDTH
    masks = [(head_of == h).astype(jnp.float32) for h in range(ATTENTION_HEADS)]
    masks_low = [m.astype(jnp.bfloat16) for m in masks]

    def one_residue(r, carry):
        rows = pl.ds(pl.multiple_of(r * seqs, seqs), seqs)
        query = q_s[rows, :]
        spread_query = jnp.concatenate([query * m for m in masks_low], axis=0)
        scores = dot_nt(spread_query, k_s[rows, :]) * HEAD_WIDTH ** (-0.5)
        raised = jnp.exp(scores - jnp.max(scores, axis=-1, keepdims=True))
        inverse = 1.0 / jnp.sum(raised, axis=-1, keepdims=True)
        blended = dot_nn(raised.astype(jnp.bfloat16), v_s[rows, :]) * inverse
        total = blended[:seqs] * masks[0]
        for h in range(1, ATTENTION_HEADS):
            total = total + blended[h * seqs:(h + 1) * seqs] * masks[h]
        a_s[rows, :] = (g_s[rows, :] * total).astype(jnp.bfloat16)
        return carry

    lax.fori_loop(0, residues, one_residue, 0, unroll=4 if residues % 4 == 0 else 2)

    copies[4].wait()
    updated = (x.astype(jnp.float32) + dot_nn(a_s[...], w_s[4])).astype(jnp.bfloat16)
    for r in range(residues):
        for s in range(parts):
            begin = r * seqs + s * part_seqs
            upd_ref[s, :, r * width:(r + 1) * width] = updated[begin:begin + part_seqs]
    factor_norm = layer_normalise(updated).astype(jnp.bfloat16)
    copies[6].wait()
    copies[7].wait()
    project = project_s[...].reshape(2 * FACTOR_WIDTH, width)
    for p in range(residues // 2):
        both = dot_nt(project, factor_norm[p * 2 * seqs:(p + 1) * 2 * seqs]).astype(jnp.bfloat16)
        for n in range(parts):
            factor_ref[n, 0, p] = both[:FACTOR_WIDTH]
            factor_ref[n, 1, p] = both[FACTOR_WIDTH:]


def whole_block(shape):
    return pl.BlockSpec(shape, lambda *_: (0,) * len(shape))


def in_hbm(*arrays):
    return [pltpu.with_memory_space_constraint(v, pltpu.HBM) for v in arrays]


def attend(x, wq, wk, wv, wg, gate_bias, wo, wl, wr):
    parts, residues, part_seqs, width = x.shape
    seqs = parts * part_seqs
    rows = residues * seqs
    operands = in_hbm(wq, wk, wv, wg, gate_bias.reshape(1, -1), wo, wl.T, wr.T)
    resident = pl.BlockSpec(memory_space=pltpu.VMEM)
    results = (
        jax.ShapeDtypeStruct((parts, part_seqs, residues * width), jnp.bfloat16),
        jax.ShapeDtypeStruct((parts, 2, residues // 2, FACTOR_WIDTH, 2 * seqs), jnp.bfloat16),
    )
    macs = rows * width * (5 * width + 2 * FACTOR_WIDTH) + 2 * rows * ATTENTION_HEADS * width * seqs
    return pl.pallas_call(
        attend_kernel,
        out_shape=results,
        in_specs=[resident] + [pl.BlockSpec(memory_space=pltpu.HBM)] * len(operands),
        out_specs=[resident] * 2,
        scratch_shapes=[
            pltpu.VMEM((rows, width), jnp.bfloat16),
            pltpu.VMEM((rows, width), jnp.bfloat16),
            pltpu.VMEM((rows, width), jnp.bfloat16),
            pltpu.VMEM((rows, width), jnp.float32),
            pltpu.VMEM((rows, width), jnp.bfloat16),
            pltpu.VMEM((5,) + wq.shape, jnp.bfloat16),
            pltpu.VMEM((1, width), jnp.float32),
            pltpu.VMEM((2, FACTOR_WIDTH, width), jnp.bfloat16),
            pltpu.SemaphoreType.DMA((len(operands),)),
        ],
        compiler_params=pltpu.CompilerParams(vmem_limit_bytes=32 * 1024 * 1024),
        cost_estimate=pl.CostEstimate(flops=2 * macs, bytes_accessed=4 * x.size * 2, transcendentals=rows * width),
        name="column_attention",
    )(x, *operands)


def right_kernel(
    factor_ref, w_ref, expand_ref, shrink_ref, rbd_ref, rbdt_ref, wec_ref, wt_ref, et_ref, st_ref, stage_s,
    *, seqs, cols, fold,
):
    each = factor_ref.shape[2]
    wide = fold * HALF
    stage_lanes = stage_s.shape[1]
    low_half = lax.broadcasted_iota(jnp.int32, (1, LANES), 1) < HALF

    stage_s[:FACTOR_WIDTH * FACTOR_WIDTH, :LANES] = w_ref[...].astype(jnp.float32)
    for e in range(FACTOR_WIDTH):
        piece = stage_s[pl.ds(e, FACTOR_WIDTH, stride=FACTOR_WIDTH), :LANES]
        wec_ref[e * FACTOR_WIDTH:(e + 1) * FACTOR_WIDTH, :] = piece.astype(jnp.bfloat16)
    for b in range(FACTOR_WIDTH * FACTOR_WIDTH // LANES):
        block = wec_ref[b * LANES:(b + 1) * LANES, :].astype(jnp.float32)
        wt_ref[:, b * LANES:(b + 1) * LANES] = block.T.astype(jnp.bfloat16)
    et_ref[...] = expand_ref[...].astype(jnp.float32).T.astype(jnp.bfloat16)
    st_ref[...] = shrink_ref[...].astype(jnp.float32).T.astype(jnp.bfloat16)

    for p in range(cols // 2):
        block = factor_ref[p // each, 1, p % each].astype(jnp.float32)
        even = 2 * p * FACTOR_WIDTH
        odd = even + FACTOR_WIDTH
        if seqs % LANES == 0:
            stage_s[even:even + FACTOR_WIDTH, :] = block[:, :seqs]
            stage_s[odd:odd + FACTOR_WIDTH, :] = block[:, seqs:]
        else:
            stage_s[even:even + FACTOR_WIDTH, :] = block
            stage_s[odd:odd + FACTOR_WIDTH, :] = pltpu.roll(block, HALF, axis=1)

    blank = jnp.zeros((seqs, LANES), jnp.bfloat16)
    empty = jnp.zeros((HALF, stage_lanes), jnp.bfloat16)
    pad = jnp.zeros((HALF - cols, stage_lanes), jnp.float32)
    for e in range(0, FACTOR_WIDTH, 2):
        even = stage_s[pl.ds(e, cols, stride=FACTOR_WIDTH), :]
        odd = stage_s[pl.ds(e + 1, cols, stride=FACTOR_WIDTH), :]
        upright = jnp.concatenate([even, pad, odd, pad], axis=0)
        for at in (e, e + 1):
            block = upright[(at - e) * HALF:(at - e + 1) * HALF]
            if seqs % LANES == 0:
                shapes = [block.astype(jnp.bfloat16)]
            else:
                shapes = [
                    jnp.where(low_half, block, 0.0).astype(jnp.bfloat16),
                    jnp.where(low_half, 0.0, pltpu.roll(block, HALF, axis=1)).astype(jnp.bfloat16),
                ]
            for k in range(fold):
                for v in range(fold * seqs // stage_lanes):
                    value = shapes[k % len(shapes)] if v == k // len(shapes) else empty
                    rbdt_ref[at, k * HALF:(k + 1) * HALF, v * stage_lanes:(v + 1) * stage_lanes] = value
        turned = upright.T[:seqs]
        rolled = pltpu.roll(turned, HALF, axis=1)
        for at, low, high in ((e, turned, rolled), (e + 1, rolled, turned)):
            low = jnp.where(low_half, low, 0.0).astype(jnp.bfloat16)
            high = jnp.where(low_half, 0.0, high).astype(jnp.bfloat16)
            for k in range(fold):
                for v in range(wide // LANES):
                    value = blank if v != k // 2 else (low if k % 2 == 0 else high)
                    rbd_ref[at, k * seqs:(k + 1) * seqs, v * LANES:(v + 1) * LANES] = value


def right_matrices(factors, outer_weight, expand_weight, shrink_weight):
    row_parts, _, each, _, lanes = factors.shape
    seqs, cols = lanes // 2, 2 * each * row_parts
    fold = MXU_SIDE // HALF
    channels, width = outer_weight.shape
    results = (
        jax.ShapeDtypeStruct((FACTOR_WIDTH, fold * seqs, fold * HALF), jnp.bfloat16),
        jax.ShapeDtypeStruct((FACTOR_WIDTH, fold * HALF, fold * seqs), jnp.bfloat16),
        jax.ShapeDtypeStruct((channels, width), jnp.bfloat16),
        jax.ShapeDtypeStruct((width, channels), jnp.bfloat16),
        jax.ShapeDtypeStruct(expand_weight.shape[::-1], jnp.bfloat16),
        jax.ShapeDtypeStruct(shrink_weight.shape[::-1], jnp.bfloat16),
    )
    resident = pl.BlockSpec(memory_space=pltpu.VMEM)
    return pl.pallas_call(
        functools.partial(right_kernel, seqs=seqs, cols=cols, fold=fold),
        out_shape=results,
        in_specs=[resident] * 4,
        out_specs=[resident] * len(results),
        scratch_shapes=[pltpu.VMEM((max(cols * FACTOR_WIDTH, channels), max(seqs, LANES)), jnp.float32)],
        compiler_params=pltpu.CompilerParams(vmem_limit_bytes=16 * 1024 * 1024),
        cost_estimate=pl.CostEstimate(flops=6 * 10**9, bytes_accessed=4 * results[0].size, transcendentals=0),
        name="right_matrices",
    )(factors, outer_weight, expand_weight, shrink_weight)


def pair_kernel(
    place_ref, *refs, seqs, cols, fold, unit, units, blocks,
):
    left_refs, refs = refs[:blocks], refs[blocks:]
    rbd_s, rbdt_s, wec_s, wt_s, et_ref, st_ref, returned_ref, pair_ref, cot_ref = refs[:9]
    bias_ref, expand_ref, shrink_ref, out_ref, gl_ref = refs[9:14]
    both_refs, (outer_s, l_s, lt_s, stage_s, glacc_s, lblk_s, both_s) = refs[14:-7], refs[-7:]
    step = pl.program_id(0)
    row_parts, each = left_refs[0].shape[:2]
    span = l_s.shape[0]
    groups = span // FACTOR_WIDTH
    wide = fold * HALF
    scaling = 1.0 / seqs
    low_half = lax.broadcasted_iota(jnp.int32, (1, LANES), 1) < HALF

    @pl.when(step == 0)
    def _prologue():
        for n, ref in enumerate(left_refs):
            lblk_s[place_ref[n]] = ref[...]
        pairs = fold // 2
        for p in range(groups * pairs):
            column, inside = divmod(p, row_parts * each)
            block = lblk_s[column, inside // each, inside % each]
            g, at = p // pairs, p % pairs * 2 * seqs
            l_s[g * FACTOR_WIDTH:(g + 1) * FACTOR_WIDTH, at:at + 2 * seqs] = (
                block.astype(jnp.float32) * scaling
            ).astype(jnp.bfloat16)
        for b in range(span // LANES):
            block = l_s[b * LANES:(b + 1) * LANES, :].astype(jnp.float32)
            lt_s[:, b * LANES:(b + 1) * LANES] = block.T.astype(jnp.bfloat16)

        def one_outer(e, carry):
            outer_s[e] = dot_nn(l_s[...], rbd_s[e]).astype(jnp.bfloat16)
            return carry

        lax.fori_loop(0, FACTOR_WIDTH, one_outer, 0, unroll=8)

    per_group = fold * cols
    gap = jnp.zeros((HALF - cols, PAIR_W), jnp.bfloat16)

    def group_rows(u, n):
        g = (step * units + u) * unit + n
        return pl.ds(pl.multiple_of(g * FACTOR_WIDTH, FACTOR_WIDTH), FACTOR_WIDTH)

    def forward(u):
        pieces = []
        for n in range(unit):
            outer = outer_s[:, group_rows(u, n), :].reshape(FACTOR_WIDTH * FACTOR_WIDTH, wide)
            product = dot_nn(wt_s[...], outer).T
            pieces += [product[k * HALF:k * HALF + cols] for k in range(fold)]
        own = pl.ds((step * units + u) * unit * fold, unit * fold)
        projected = jnp.concatenate(pieces, axis=0)
        pair = pair_ref[own].reshape(-1, PAIR_W)
        middles, inverses, spreads = [], [], []
        for at in range(0, projected.shape[0], TILE):
            middle = pair[at:at + TILE] + projected[at:at + TILE] + bias_ref[...]
            average = jnp.mean(middle, axis=-1, keepdims=True)
            centred = middle - average
            variance = jnp.mean(centred * centred, axis=-1, keepdims=True)
            inverse = lax.rsqrt(variance + EPSILON)
            middles.append(middle)
            inverses.append(inverse)
            spreads.append(centred * inverse)
        spread_low = jnp.concatenate([v.astype(jnp.bfloat16) for v in spreads], axis=0)
        cotangent = cot_ref[own].reshape(-1, PAIR_W)
        before = dot_nn(spread_low, expand_ref[...])
        back_hidden = dot_nn(cotangent.astype(jnp.bfloat16), st_ref[...])
        return middles, inverses, spreads, before, cotangent, back_hidden

    def backward(u, middles, inverses, spreads, before, cotangent, back_hidden):
        own = slice(u * unit * fold, (u + 1) * unit * fold)
        rows, width = before.shape
        hidden, back_before = [], []
        for at in range(0, rows, TILE):
            hidden_parts, back_parts = [], []
            for v in range(0, width, MXU_SIDE):
                x = before[at:at + TILE, v:v + MXU_SIDE]
                phi = 0.5 * (1.0 + lax.erf(x * 0.7071067811865476))
                slope = phi + x * jnp.exp(-0.5 * x * x) * 0.3989422804014327
                hidden_parts.append((x * phi).astype(jnp.bfloat16))
                back_parts.append((back_hidden[at:at + TILE, v:v + MXU_SIDE] * slope).astype(jnp.bfloat16))
            hidden.append(jnp.concatenate(hidden_parts, axis=1))
            back_before.append(jnp.concatenate(back_parts, axis=1))
        back_spread = dot_nn(jnp.concatenate(back_before, axis=0), et_ref[...])
        change = dot_nn(jnp.concatenate(hidden, axis=0), shrink_ref[...])
        out_ref[own] = (jnp.concatenate(middles, axis=0) + change).reshape(unit * fold, cols, PAIR_W)
        back_middle = []
        for n, at in enumerate(range(0, rows, TILE)):
            back, spread = back_spread[at:at + TILE], spreads[n]
            centre_term = jnp.mean(back, axis=-1, keepdims=True)
            slope_term = jnp.mean(back * spread, axis=-1, keepdims=True)
            back = cotangent[at:at + TILE] + inverses[n] * (back - centre_term - spread * slope_term)
            back_middle.append(back.astype(jnp.bfloat16))
        back_middle = jnp.concatenate(back_middle, axis=0)
        for n in range(unit):
            parts = []
            for k in range(fold):
                begin = n * per_group + k * cols
                parts += [back_middle[begin:begin + cols], gap]
            back_outer = dot_nt(wec_s[...], jnp.concatenate(parts, axis=0)).astype(jnp.bfloat16)
            outer_s[:, group_rows(u, n), :] = back_outer.reshape(FACTOR_WIDTH, FACTOR_WIDTH, wide)

    held = forward(0)
    for u in range(units):
        ahead = forward(u + 1) if u + 1 < units else None
        backward(u, *held)
        held = ahead

    @pl.when(step == pl.num_programs(0) - 1)
    def _epilogue():
        glacc_s[...] = jnp.zeros_like(glacc_s)
        batch = 4
        empty = jnp.zeros((LANES - seqs % LANES, LANES), jnp.float32) if seqs % LANES else None

        def some(n, carry):
            base = n * batch
            backs = [outer_s[base + u] for u in range(batch)]
            glacc_s[...] += dot_nn(
                jnp.concatenate(backs, axis=1),
                jnp.concatenate([rbdt_s[base + u] for u in range(batch)], axis=0),
            )
            lows, highs = [], []
            for u in range(batch):
                full = dot_nn(lt_s[...], backs[u])
                low = high = None
                for k in range(fold):
                    v = k // 2
                    block = full[k * seqs:(k + 1) * seqs, v * LANES:(v + 1) * LANES]
                    if k % 2 == 0:
                        low = block if low is None else low + block
                    else:
                        high = block if high is None else high + block
                lows.append(low)
                highs.append(high)
            for u in range(0, batch, 2):
                both = jnp.where(low_half, lows[u], highs[u + 1]) + pltpu.roll(
                    jnp.where(low_half, lows[u + 1], highs[u]), HALF, axis=1
                )
                if empty is not None:
                    both = jnp.concatenate([both, empty], axis=0)
                turned = both.T
                stage_s[pl.ds(base + u, cols, stride=FACTOR_WIDTH), :] = turned[:cols]
                stage_s[pl.ds(base + u + 1, cols, stride=FACTOR_WIDTH), :] = turned[HALF:HALF + cols]
            return carry

        lax.fori_loop(0, FACTOR_WIDTH // batch, some, 0, unroll=2)
        part_seqs, width = returned_ref.shape[1:]
        both_s[:, :, :width] = returned_ref[...]
        for b in range(cols * FACTOR_WIDTH // LANES):
            block = stage_s[b * LANES:(b + 1) * LANES, :].T[:seqs].astype(jnp.bfloat16)
            both_s[:, :, width + b * LANES:width + (b + 1) * LANES] = block.reshape(row_parts, part_seqs, LANES)
        for k, ref in enumerate(both_refs):
            ref[...] = both_s[place_ref[blocks] ^ k]
        for b in range(span // LANES):
            block = glacc_s[b * LANES:(b + 1) * LANES, :].T * scaling
            for k in range(fold):
                at = k * span + b * LANES
                gl_ref[:, at:at + LANES] = block[k * seqs:(k + 1) * seqs].astype(jnp.bfloat16)


def pair_tile(place, lefts, matrices, returned, pair_features, cotangent, outer_bias, expand_weight, shrink_weight):
    seqs = lefts[0].shape[-1] // 2
    rows, cols, _ = pair_features.shape
    fold = MXU_SIDE // HALF
    groups = rows // fold
    unit = 2 if groups % 2 == 0 else 1
    units = 4 if groups % (4 * unit) == 0 else 1
    steps = groups // unit // units
    wide = fold * HALF
    span = groups * FACTOR_WIDTH
    channels = FACTOR_WIDTH * FACTOR_WIDTH
    block = pl.BlockSpec((unit * units * fold, cols, PAIR_W), lambda n, place: (n, 0, 0))
    resident = pl.BlockSpec(memory_space=pltpu.VMEM)
    operands = (
        *lefts, *matrices, returned, pair_features, cotangent, outer_bias.reshape(1, -1), expand_weight,
        shrink_weight,
    )
    results = (
        jax.ShapeDtypeStruct(pair_features.shape, jnp.float32),
        jax.ShapeDtypeStruct((seqs, rows * FACTOR_WIDTH), jnp.bfloat16),
    ) + returned.shape[0] * (
        jax.ShapeDtypeStruct((returned.shape[1], returned.shape[2] + cols * FACTOR_WIDTH), jnp.bfloat16),
    )
    padded = groups * wide
    macs = 3 * FACTOR_WIDTH * span * fold * seqs * wide + padded * (2 * channels * MXU_SIDE + 8 * MXU_SIDE * MXU_SIDE)
    return pl.pallas_call(
        functools.partial(
            pair_kernel, seqs=seqs, cols=cols, fold=fold, unit=unit, units=units, blocks=len(lefts)
        ),
        grid_spec=pltpu.PrefetchScalarGridSpec(
            num_scalar_prefetch=1,
            grid=(steps,),
            in_specs=[resident] * len(operands),
            out_specs=[block] + [resident] * (len(results) - 1),
            scratch_shapes=[
                pltpu.VMEM((FACTOR_WIDTH, span, wide), jnp.bfloat16),
                pltpu.VMEM((span, fold * seqs), jnp.bfloat16),
                pltpu.VMEM((fold * seqs, span), jnp.bfloat16),
                pltpu.VMEM((cols * FACTOR_WIDTH, max(seqs, LANES)), jnp.float32),
                pltpu.VMEM((span, fold * seqs), jnp.float32),
                pltpu.VMEM((len(lefts),) + lefts[0].shape, jnp.bfloat16),
                pltpu.VMEM(returned.shape[:1] + results[2].shape, jnp.bfloat16),
            ],
        ),
        out_shape=results,
        compiler_params=pltpu.CompilerParams(
            dimension_semantics=("arbitrary",), vmem_limit_bytes=32 * 1024 * 1024
        ),
        cost_estimate=pl.CostEstimate(
            flops=2 * macs, bytes_accessed=3 * pair_features.size * 4, transcendentals=0
        ),
        name="pair_tile",
    )(place, *operands)


def finish_kernel(place_ref, *refs, residues, fold):
    *both_refs, gl_ref, updated_ref, left_ref, right_ref, x_s = refs
    part_seqs, res_count, width = updated_ref.shape
    total = both_refs[0][:, residues * width:].astype(jnp.float32)
    for ref in both_refs[1:]:
        total = total + ref[:, residues * width:].astype(jnp.float32)
    right_ref[...] = total
    for k, ref in enumerate(both_refs):
        first = (place_ref[0] ^ k) * residues
        for r in range(residues):
            for n in range(width // LANES):
                at = r * width + n * LANES
                x_s[n, pl.ds(first + r, part_seqs, stride=res_count), :] = ref[:, at:at + LANES].astype(jnp.float32)
    for n in range(width // LANES):
        updated_ref[:, :, n * LANES:(n + 1) * LANES] = (
            x_s[n].reshape(part_seqs, res_count, LANES).astype(jnp.bfloat16)
        )
    total = gl_ref[0].astype(jnp.float32)
    for n in range(1, gl_ref.shape[0]):
        total = total + gl_ref[n].astype(jnp.float32)
    span = total.shape[1] // fold
    channel_block = lax.broadcasted_iota(jnp.int32, (1, LANES), 1) // FACTOR_WIDTH
    each = LANES // FACTOR_WIDTH
    for g in range(span // FACTOR_WIDTH):
        out = None
        for k in range(fold):
            at = k * span + g // each * LANES
            piece = total[:, at:at + LANES]
            shift = (k - g) % each * FACTOR_WIDTH
            piece = pltpu.roll(piece, shift, axis=1) if shift else piece
            out = piece if out is None else jnp.where(channel_block == k, piece, out)
        left_ref[:, g * LANES:(g + 1) * LANES] = out


def finish(place, both, gl, updated_shape):
    part_seqs, res_count, width = updated_shape
    residues = res_count // len(both)
    results = (
        jax.ShapeDtypeStruct(updated_shape, jnp.bfloat16),
        jax.ShapeDtypeStruct(gl.shape[1:], jnp.float32),
        jax.ShapeDtypeStruct((part_seqs, both[0].shape[1] - residues * width), jnp.float32),
    )
    resident = pl.BlockSpec(memory_space=pltpu.VMEM)
    return pl.pallas_call(
        functools.partial(finish_kernel, residues=residues, fold=MXU_SIDE // HALF),
        grid_spec=pltpu.PrefetchScalarGridSpec(
            num_scalar_prefetch=1,
            grid=(1,),
            in_specs=[resident] * (len(both) + 1),
            out_specs=[whole_block(v.shape) for v in results],
            scratch_shapes=[pltpu.VMEM((width // LANES, part_seqs * res_count, LANES), jnp.float32)],
        ),
        out_shape=results,
        compiler_params=pltpu.CompilerParams(
            dimension_semantics=("arbitrary",), vmem_limit_bytes=16 * 1024 * 1024
        ),
        name="finish",
    )(place, *both, gl)


def spread_out(q, count):
    return q if count % 2 else q % 2 * (count // 2) + q // 2


def local(
    alignment,
    pair_features,
    query_weight,
    key_weight,
    value_projection,
    gate_projection,
    gate_bias,
    output_projection,
    left_projection,
    right_projection,
    outer_weight,
    outer_bias,
    expand_weight,
    shrink_weight,
    cotangent,
):
    part_seqs, res_count, width = alignment.shape
    row_parts = lax.axis_size("row")
    col_parts = lax.axis_size("col")
    residues = res_count // row_parts
    own = jnp.transpose(alignment, (1, 0, 2)).reshape(row_parts, residues, part_seqs, width)
    columns = lax.all_to_all(own, "row", split_axis=0, concat_axis=0, tiled=True)
    attended, factors = attend(
        columns, query_weight, key_weight, value_projection, gate_projection, gate_bias,
        output_projection, left_projection, right_projection,
    )

    factors = lax.all_to_all(factors, "row", split_axis=0, concat_axis=0, tiled=True)
    left = factors[:, 0]
    ratio = col_parts // row_parts
    lefts, place = [], []
    for m in range(ratio):
        moves = [
            (q * col_parts + ratio * r + b, r * col_parts + ratio * spread_out(q, row_parts) + (b + m) % ratio)
            for q in range(row_parts)
            for r in range(row_parts)
            for b in range(ratio)
        ]
        lefts.append(lax.ppermute(left, ("row", "col"), moves))
        place.append((lax.axis_index("col") + ratio - m) % ratio)
    row = lax.axis_index("row")
    matrices = right_matrices(factors, outer_weight, expand_weight, shrink_weight)
    pair_out, gl, *both = pair_tile(
        jnp.stack(place + [row]).astype(jnp.int32), lefts, matrices, attended, pair_features, cotangent, outer_bias,
        expand_weight, shrink_weight,
    )
    seqs, gl_width = gl.shape
    both = both[:1] + [
        lax.ppermute(v, "row", [(r, r ^ (k + 1)) for r in range(row_parts)]) for k, v in enumerate(both[1:])
    ]
    gl = lax.all_to_all(
        gl.reshape(col_parts, seqs // col_parts, gl_width), "col", split_axis=0, concat_axis=0, tiled=True
    )
    updated, grad_left, grad_right = finish(row.astype(jnp.int32).reshape(1), both, gl, alignment.shape)
    return (updated, pair_out, grad_left, grad_right)


def solution(mesh):
    return jax.shard_map(
        local,
        mesh=mesh,
        in_specs=(P("row", "col", None), P("row", "col", None)) + (P(),) * 12 + (P("row", "col", None),),
        out_specs=(P("row", "col", None), P("row", "col", None), P("col", "row"), P("row", "col")),
        check_vma=False,
    )
```

```python
import functools

import jax
import jax.numpy as jnp
from jax import lax
from jax.experimental import pallas as pl
from jax.experimental.pallas import tpu as pltpu
from jax.sharding import PartitionSpec as P

ATTENTION_HEADS = 8
HEAD_WIDTH = 32
FACTOR_WIDTH = 32
PAIR_W = 128
EPSILON = 1e-05

LANES = 128
MXU_SIDE = 256
HALF = 64
TILE = 32


def dot_nn(a, b):
    return lax.dot_general(a, b, (((1,), (0,)), ((), ())), preferred_element_type=jnp.float32)


def dot_nt(a, b):
    return lax.dot_general(a, b, (((1,), (1,)), ((), ())), preferred_element_type=jnp.float32)


def layer_normalise(rows):
    rows = rows.astype(jnp.float32)
    average = jnp.mean(rows, axis=-1, keepdims=True)
    centred = rows - average
    variance = jnp.mean(centred * centred, axis=-1, keepdims=True)
    return centred * lax.rsqrt(variance + EPSILON)


def attend_kernel(
    x_ref, wq_ref, wk_ref, wv_ref, wg_ref, bias_ref, wo_ref, wl_ref, wr_ref,
    upd_ref, factor_ref, q_s, k_s, v_s, g_s, a_s, w_s, bias_s, project_s, sems,
):
    parts, residues, part_seqs, width = x_ref.shape
    seqs = parts * part_seqs
    sources = (wq_ref, wk_ref, wv_ref, wg_ref, wo_ref, bias_ref, wl_ref, wr_ref)
    targets = [w_s.at[n] for n in range(5)] + [bias_s, project_s.at[0], project_s.at[1]]
    copies = [pltpu.make_async_copy(a, b, sems.at[n]) for n, (a, b) in enumerate(zip(sources, targets))]
    for copy in copies:
        copy.start()
    x = jnp.concatenate([x_ref[s, r] for r in range(residues) for s in range(parts)], axis=0)
    normed = layer_normalise(x).astype(jnp.bfloat16)
    for n, ref in enumerate((q_s, k_s, v_s)):
        copies[n].wait()
        ref[...] = dot_nn(normed, w_s[n]).astype(jnp.bfloat16)
    copies[3].wait()
    copies[5].wait()
    g_s[...] = jax.nn.sigmoid(dot_nn(normed, w_s[3]) + bias_s[...])

    head_of = lax.broadcasted_iota(jnp.int32, (1, width), 1) // HEAD_WIDTH
    masks = [(head_of == h).astype(jnp.float32) for h in range(ATTENTION_HEADS)]
    masks_low = [m.astype(jnp.bfloat16) for m in masks]

    def one_residue(r, carry):
        rows = pl.ds(pl.multiple_of(r * seqs, seqs), seqs)
        query = q_s[rows, :]
        spread_query = jnp.concatenate([query * m for m in masks_low], axis=0)
        scores = dot_nt(spread_query, k_s[rows, :]) * HEAD_WIDTH ** (-0.5)
        raised = jnp.exp(scores - jnp.max(scores, axis=-1, keepdims=True))
        inverse = 1.0 / jnp.sum(raised, axis=-1, keepdims=True)
        blended = dot_nn(raised.astype(jnp.bfloat16), v_s[rows, :]) * inverse
        total = blended[:seqs] * masks[0]
        for h in range(1, ATTENTION_HEADS):
            total = total + blended[h * seqs:(h + 1) * seqs] * masks[h]
        a_s[rows, :] = (g_s[rows, :] * total).astype(jnp.bfloat16)
        return carry

    lax.fori_loop(0, residues, one_residue, 0, unroll=4 if residues % 4 == 0 else 2)

    copies[4].wait()
    updated = (x.astype(jnp.float32) + dot_nn(a_s[...], w_s[4])).astype(jnp.bfloat16)
    for r in range(residues):
        for s in range(parts):
            begin = r * seqs + s * part_seqs
            upd_ref[s, :, r * width:(r + 1) * width] = updated[begin:begin + part_seqs]
    factor_norm = layer_normalise(updated).astype(jnp.bfloat16)
    copies[6].wait()
    copies[7].wait()
    project = project_s[...].reshape(2 * FACTOR_WIDTH, width)
    for p in range(residues // 2):
        both = dot_nt(project, factor_norm[p * 2 * seqs:(p + 1) * 2 * seqs]).astype(jnp.bfloat16)
        for n in range(parts):
            factor_ref[n, 0, p] = both[:FACTOR_WIDTH]
            factor_ref[n, 1, p] = both[FACTOR_WIDTH:]


def whole_block(shape):
    return pl.BlockSpec(shape, lambda *_: (0,) * len(shape))


def in_hbm(*arrays):
    return [pltpu.with_memory_space_constraint(v, pltpu.HBM) for v in arrays]


def attend(x, wq, wk, wv, wg, gate_bias, wo, wl, wr):
    parts, residues, part_seqs, width = x.shape
    seqs = parts * part_seqs
    rows = residues * seqs
    operands = in_hbm(wq, wk, wv, wg, gate_bias.reshape(1, -1), wo, wl.T, wr.T)
    resident = pl.BlockSpec(memory_space=pltpu.VMEM)
    results = (
        jax.ShapeDtypeStruct((parts, part_seqs, residues * width), jnp.bfloat16),
        jax.ShapeDtypeStruct((parts, 2, residues // 2, FACTOR_WIDTH, 2 * seqs), jnp.bfloat16),
    )
    macs = rows * width * (5 * width + 2 * FACTOR_WIDTH) + 2 * rows * ATTENTION_HEADS * width * seqs
    return pl.pallas_call(
        attend_kernel,
        out_shape=results,
        in_specs=[resident] + [pl.BlockSpec(memory_space=pltpu.HBM)] * len(operands),
        out_specs=[resident] * 2,
        scratch_shapes=[
            pltpu.VMEM((rows, width), jnp.bfloat16),
            pltpu.VMEM((rows, width), jnp.bfloat16),
            pltpu.VMEM((rows, width), jnp.bfloat16),
            pltpu.VMEM((rows, width), jnp.float32),
            pltpu.VMEM((rows, width), jnp.bfloat16),
            pltpu.VMEM((5,) + wq.shape, jnp.bfloat16),
            pltpu.VMEM((1, width), jnp.float32),
            pltpu.VMEM((2, FACTOR_WIDTH, width), jnp.bfloat16),
            pltpu.SemaphoreType.DMA((len(operands),)),
        ],
        compiler_params=pltpu.CompilerParams(vmem_limit_bytes=32 * 1024 * 1024),
        cost_estimate=pl.CostEstimate(flops=2 * macs, bytes_accessed=4 * x.size * 2, transcendentals=rows * width),
        name="column_attention",
    )(x, *operands)


def right_kernel(
    factor_ref, w_ref, expand_ref, shrink_ref, rbd_ref, rbdt_ref, wec_ref, wt_ref, et_ref, st_ref, stage_s,
    *, seqs, cols, fold,
):
    each = factor_ref.shape[2]
    wide = fold * HALF
    stage_lanes = stage_s.shape[1]
    low_half = lax.broadcasted_iota(jnp.int32, (1, LANES), 1) < HALF

    stage_s[:FACTOR_WIDTH * FACTOR_WIDTH, :LANES] = w_ref[...].astype(jnp.float32)
    for e in range(FACTOR_WIDTH):
        piece = stage_s[pl.ds(e, FACTOR_WIDTH, stride=FACTOR_WIDTH), :LANES]
        wec_ref[e * FACTOR_WIDTH:(e + 1) * FACTOR_WIDTH, :] = piece.astype(jnp.bfloat16)
    for b in range(FACTOR_WIDTH * FACTOR_WIDTH // LANES):
        block = wec_ref[b * LANES:(b + 1) * LANES, :].astype(jnp.float32)
        wt_ref[:, b * LANES:(b + 1) * LANES] = block.T.astype(jnp.bfloat16)
    et_ref[...] = expand_ref[...].astype(jnp.float32).T.astype(jnp.bfloat16)
    st_ref[...] = shrink_ref[...].astype(jnp.float32).T.astype(jnp.bfloat16)

    for p in range(cols // 2):
        block = factor_ref[p // each, 1, p % each].astype(jnp.float32)
        even = 2 * p * FACTOR_WIDTH
        odd = even + FACTOR_WIDTH
        if seqs % LANES == 0:
            stage_s[even:even + FACTOR_WIDTH, :] = block[:, :seqs]
            stage_s[odd:odd + FACTOR_WIDTH, :] = block[:, seqs:]
        else:
            stage_s[even:even + FACTOR_WIDTH, :] = block
            stage_s[odd:odd + FACTOR_WIDTH, :] = pltpu.roll(block, HALF, axis=1)

    blank = jnp.zeros((seqs, LANES), jnp.bfloat16)
    empty = jnp.zeros((HALF, stage_lanes), jnp.bfloat16)
    pad = jnp.zeros((HALF - cols, stage_lanes), jnp.float32)
    for e in range(0, FACTOR_WIDTH, 2):
        even = stage_s[pl.ds(e, cols, stride=FACTOR_WIDTH), :]
        odd = stage_s[pl.ds(e + 1, cols, stride=FACTOR_WIDTH), :]
        upright = jnp.concatenate([even, pad, odd, pad], axis=0)
        for at in (e, e + 1):
            block = upright[(at - e) * HALF:(at - e + 1) * HALF]
            if seqs % LANES == 0:
                shapes = [block.astype(jnp.bfloat16)]
            else:
                shapes = [
                    jnp.where(low_half, block, 0.0).astype(jnp.bfloat16),
                    jnp.where(low_half, 0.0, pltpu.roll(block, HALF, axis=1)).astype(jnp.bfloat16),
                ]
            for k in range(fold):
                for v in range(fold * seqs // stage_lanes):
                    value = shapes[k % len(shapes)] if v == k // len(shapes) else empty
                    rbdt_ref[at, k * HALF:(k + 1) * HALF, v * stage_lanes:(v + 1) * stage_lanes] = value
        turned = upright.T[:seqs]
        rolled = pltpu.roll(turned, HALF, axis=1)
        for at, low, high in ((e, turned, rolled), (e + 1, rolled, turned)):
            low = jnp.where(low_half, low, 0.0).astype(jnp.bfloat16)
            high = jnp.where(low_half, 0.0, high).astype(jnp.bfloat16)
            for k in range(fold):
                for v in range(wide // LANES):
                    value = blank if v != k // 2 else (low if k % 2 == 0 else high)
                    rbd_ref[at, k * seqs:(k + 1) * seqs, v * LANES:(v + 1) * LANES] = value


def right_matrices(factors, outer_weight, expand_weight, shrink_weight):
    row_parts, _, each, _, lanes = factors.shape
    seqs, cols = lanes // 2, 2 * each * row_parts
    fold = MXU_SIDE // HALF
    channels, width = outer_weight.shape
    results = (
        jax.ShapeDtypeStruct((FACTOR_WIDTH, fold * seqs, fold * HALF), jnp.bfloat16),
        jax.ShapeDtypeStruct((FACTOR_WIDTH, fold * HALF, fold * seqs), jnp.bfloat16),
        jax.ShapeDtypeStruct((channels, width), jnp.bfloat16),
        jax.ShapeDtypeStruct((width, channels), jnp.bfloat16),
        jax.ShapeDtypeStruct(expand_weight.shape[::-1], jnp.bfloat16),
        jax.ShapeDtypeStruct(shrink_weight.shape[::-1], jnp.bfloat16),
    )
    resident = pl.BlockSpec(memory_space=pltpu.VMEM)
    return pl.pallas_call(
        functools.partial(right_kernel, seqs=seqs, cols=cols, fold=fold),
        out_shape=results,
        in_specs=[resident] * 4,
        out_specs=[resident] * len(results),
        scratch_shapes=[pltpu.VMEM((max(cols * FACTOR_WIDTH, channels), max(seqs, LANES)), jnp.float32)],
        compiler_params=pltpu.CompilerParams(vmem_limit_bytes=16 * 1024 * 1024),
        cost_estimate=pl.CostEstimate(flops=6 * 10**9, bytes_accessed=4 * results[0].size, transcendentals=0),
        name="right_matrices",
    )(factors, outer_weight, expand_weight, shrink_weight)


def pair_kernel(
    place_ref, *refs, seqs, cols, fold, unit, units, blocks,
):
    left_refs, refs = refs[:blocks], refs[blocks:]
    rbd_s, rbdt_s, wec_s, wt_s, et_ref, st_ref, returned_ref, pair_ref, cot_ref = refs[:9]
    bias_ref, expand_ref, shrink_ref, out_ref, gl_ref = refs[9:14]
    both_refs, (outer_s, l_s, lt_s, stage_s, glacc_s, lblk_s, both_s) = refs[14:-7], refs[-7:]
    step = pl.program_id(0)
    row_parts, each = left_refs[0].shape[:2]
    span = l_s.shape[0]
    groups = span // FACTOR_WIDTH
    wide = fold * HALF
    scaling = 1.0 / seqs
    low_half = lax.broadcasted_iota(jnp.int32, (1, LANES), 1) < HALF

    @pl.when(step == 0)
    def _prologue():
        for n, ref in enumerate(left_refs):
            lblk_s[place_ref[n]] = ref[...]
        pairs = fold // 2
        for p in range(groups * pairs):
            column, inside = divmod(p, row_parts * each)
            block = lblk_s[column, inside // each, inside % each]
            g, at = p // pairs, p % pairs * 2 * seqs
            l_s[g * FACTOR_WIDTH:(g + 1) * FACTOR_WIDTH, at:at + 2 * seqs] = (
                block.astype(jnp.float32) * scaling
            ).astype(jnp.bfloat16)
        for b in range(span // LANES):
            block = l_s[b * LANES:(b + 1) * LANES, :].astype(jnp.float32)
            lt_s[:, b * LANES:(b + 1) * LANES] = block.T.astype(jnp.bfloat16)

        def two_outers(n, carry):
            both = dot_nn(l_s[...], jnp.concatenate([rbd_s[2 * n], rbd_s[2 * n + 1]], axis=1))
            outer_s[2 * n] = both[:, :wide].astype(jnp.bfloat16)
            outer_s[2 * n + 1] = both[:, wide:].astype(jnp.bfloat16)
            return carry

        lax.fori_loop(0, FACTOR_WIDTH // 2, two_outers, 0, unroll=4)

    gap = jnp.zeros((HALF - cols, PAIR_W), jnp.bfloat16)

    def group_rows(u, n):
        g = (step * units + u) * unit + n
        return pl.ds(pl.multiple_of(g * FACTOR_WIDTH, FACTOR_WIDTH), FACTOR_WIDTH)

    def forward(u):
        outers = [
            outer_s[:, group_rows(u, n), :].reshape(FACTOR_WIDTH * FACTOR_WIDTH, wide) for n in range(unit)
        ]
        product = dot_nn(wt_s[...], jnp.concatenate(outers, axis=1)).T
        pieces = [product[k * HALF:k * HALF + cols] for k in range(unit * fold)]
        own = pl.ds((step * units + u) * unit * fold, unit * fold)
        projected = jnp.concatenate(pieces, axis=0)
        pair = pair_ref[own].reshape(-1, PAIR_W)
        middles, inverses, spreads = [], [], []
        for at in range(0, projected.shape[0], TILE):
            middle = pair[at:at + TILE] + projected[at:at + TILE] + bias_ref[...]
            average = jnp.mean(middle, axis=-1, keepdims=True)
            centred = middle - average
            variance = jnp.mean(centred * centred, axis=-1, keepdims=True)
            inverse = lax.rsqrt(variance + EPSILON)
            middles.append(middle)
            inverses.append(inverse)
            spreads.append(centred * inverse)
        spread_low = jnp.concatenate([v.astype(jnp.bfloat16) for v in spreads], axis=0)
        cotangent = cot_ref[own].reshape(-1, PAIR_W)
        before = dot_nn(spread_low, expand_ref[...])
        back_hidden = dot_nn(cotangent.astype(jnp.bfloat16), st_ref[...])
        return middles, inverses, spreads, before, cotangent, back_hidden

    def backward(u, middles, inverses, spreads, before, cotangent, back_hidden):
        own = slice(u * unit * fold, (u + 1) * unit * fold)
        rows, width = before.shape
        hidden, back_before = [], []
        for at in range(0, rows, TILE):
            hidden_parts, back_parts = [], []
            for v in range(0, width, MXU_SIDE):
                x = before[at:at + TILE, v:v + MXU_SIDE]
                phi = 0.5 * (1.0 + lax.erf(x * 0.7071067811865476))
                slope = phi + x * jnp.exp(-0.5 * x * x) * 0.3989422804014327
                hidden_parts.append((x * phi).astype(jnp.bfloat16))
                back_parts.append((back_hidden[at:at + TILE, v:v + MXU_SIDE] * slope).astype(jnp.bfloat16))
            hidden.append(jnp.concatenate(hidden_parts, axis=1))
            back_before.append(jnp.concatenate(back_parts, axis=1))
        back_spread = dot_nn(jnp.concatenate(back_before, axis=0), et_ref[...])
        change = dot_nn(jnp.concatenate(hidden, axis=0), shrink_ref[...])
        out_ref[own] = (jnp.concatenate(middles, axis=0) + change).reshape(unit * fold, cols, PAIR_W)
        back_middle = []
        for n, at in enumerate(range(0, rows, TILE)):
            back, spread = back_spread[at:at + TILE], spreads[n]
            centre_term = jnp.mean(back, axis=-1, keepdims=True)
            slope_term = jnp.mean(back * spread, axis=-1, keepdims=True)
            back = cotangent[at:at + TILE] + inverses[n] * (back - centre_term - spread * slope_term)
            back_middle.append(back.astype(jnp.bfloat16))
        back_middle = jnp.concatenate(back_middle, axis=0)
        parts = []
        for k in range(unit * fold):
            parts += [back_middle[k * cols:(k + 1) * cols], gap]
        back_outer = dot_nt(wec_s[...], jnp.concatenate(parts, axis=0)).astype(jnp.bfloat16)
        for n in range(unit):
            outer_s[:, group_rows(u, n), :] = back_outer[:, n * wide:(n + 1) * wide].reshape(
                FACTOR_WIDTH, FACTOR_WIDTH, wide
            )

    held = forward(0)
    for u in range(units):
        ahead = forward(u + 1) if u + 1 < units else None
        backward(u, *held)
        held = ahead

    @pl.when(step == pl.num_programs(0) - 1)
    def _epilogue():
        glacc_s[...] = jnp.zeros_like(glacc_s)
        batch = 4
        empty = jnp.zeros((LANES - seqs % LANES, LANES), jnp.float32) if seqs % LANES else None

        def some(n, carry):
            base = n * batch
            backs = [outer_s[base + u] for u in range(batch)]
            glacc_s[...] += dot_nn(
                jnp.concatenate(backs, axis=1),
                jnp.concatenate([rbdt_s[base + u] for u in range(batch)], axis=0),
            )
            lows, highs = [], []
            together = dot_nn(lt_s[...], jnp.concatenate(backs, axis=1))
            for u in range(batch):
                full = together[:, u * wide:(u + 1) * wide]
                low = high = None
                for k in range(fold):
                    v = k // 2
                    block = full[k * seqs:(k + 1) * seqs, v * LANES:(v + 1) * LANES]
                    if k % 2 == 0:
                        low = block if low is None else low + block
                    else:
                        high = block if high is None else high + block
                lows.append(low)
                highs.append(high)
            for u in range(0, batch, 2):
                both = jnp.where(low_half, lows[u], highs[u + 1]) + pltpu.roll(
                    jnp.where(low_half, lows[u + 1], highs[u]), HALF, axis=1
                )
                if empty is not None:
                    both = jnp.concatenate([both, empty], axis=0)
                turned = both.T
                stage_s[pl.ds(base + u, cols, stride=FACTOR_WIDTH), :] = turned[:cols]
                stage_s[pl.ds(base + u + 1, cols, stride=FACTOR_WIDTH), :] = turned[HALF:HALF + cols]
            return carry

        lax.fori_loop(0, FACTOR_WIDTH // batch, some, 0, unroll=2)
        part_seqs, width = returned_ref.shape[1:]
        both_s[:, :, :width] = returned_ref[...]
        for b in range(cols * FACTOR_WIDTH // LANES):
            block = stage_s[b * LANES:(b + 1) * LANES, :].T[:seqs].astype(jnp.bfloat16)
            both_s[:, :, width + b * LANES:width + (b + 1) * LANES] = block.reshape(row_parts, part_seqs, LANES)
        for k, ref in enumerate(both_refs):
            ref[...] = both_s[place_ref[blocks] ^ k]
        for b in range(span // LANES):
            block = glacc_s[b * LANES:(b + 1) * LANES, :].T * scaling
            for k in range(fold):
                at = k * span + b * LANES
                gl_ref[:, at:at + LANES] = block[k * seqs:(k + 1) * seqs].astype(jnp.bfloat16)


def pair_tile(place, lefts, matrices, returned, pair_features, cotangent, outer_bias, expand_weight, shrink_weight):
    seqs = lefts[0].shape[-1] // 2
    rows, cols, _ = pair_features.shape
    fold = MXU_SIDE // HALF
    groups = rows // fold
    unit = 2 if groups % 2 == 0 else 1
    units = 4 if groups % (4 * unit) == 0 else 1
    steps = groups // unit // units
    wide = fold * HALF
    span = groups * FACTOR_WIDTH
    channels = FACTOR_WIDTH * FACTOR_WIDTH
    block = pl.BlockSpec((unit * units * fold, cols, PAIR_W), lambda n, place: (n, 0, 0))
    resident = pl.BlockSpec(memory_space=pltpu.VMEM)
    operands = (
        *lefts, *matrices, returned, pair_features, cotangent, outer_bias.reshape(1, -1), expand_weight,
        shrink_weight,
    )
    results = (
        jax.ShapeDtypeStruct(pair_features.shape, jnp.float32),
        jax.ShapeDtypeStruct((seqs, rows * FACTOR_WIDTH), jnp.bfloat16),
    ) + returned.shape[0] * (
        jax.ShapeDtypeStruct((returned.shape[1], returned.shape[2] + cols * FACTOR_WIDTH), jnp.bfloat16),
    )
    padded = groups * wide
    macs = 3 * FACTOR_WIDTH * span * fold * seqs * wide + padded * (2 * channels * MXU_SIDE + 8 * MXU_SIDE * MXU_SIDE)
    return pl.pallas_call(
        functools.partial(
            pair_kernel, seqs=seqs, cols=cols, fold=fold, unit=unit, units=units, blocks=len(lefts)
        ),
        grid_spec=pltpu.PrefetchScalarGridSpec(
            num_scalar_prefetch=1,
            grid=(steps,),
            in_specs=[resident] * len(operands),
            out_specs=[block] + [resident] * (len(results) - 1),
            scratch_shapes=[
                pltpu.VMEM((FACTOR_WIDTH, span, wide), jnp.bfloat16),
                pltpu.VMEM((span, fold * seqs), jnp.bfloat16),
                pltpu.VMEM((fold * seqs, span), jnp.bfloat16),
                pltpu.VMEM((cols * FACTOR_WIDTH, max(seqs, LANES)), jnp.float32),
                pltpu.VMEM((span, fold * seqs), jnp.float32),
                pltpu.VMEM((len(lefts),) + lefts[0].shape, jnp.bfloat16),
                pltpu.VMEM(returned.shape[:1] + results[2].shape, jnp.bfloat16),
            ],
        ),
        out_shape=results,
        compiler_params=pltpu.CompilerParams(
            dimension_semantics=("arbitrary",), vmem_limit_bytes=32 * 1024 * 1024
        ),
        cost_estimate=pl.CostEstimate(
            flops=2 * macs, bytes_accessed=3 * pair_features.size * 4, transcendentals=0
        ),
        name="pair_tile",
    )(place, *operands)


def finish_kernel(place_ref, *refs, residues, fold):
    *both_refs, gl_ref, updated_ref, left_ref, right_ref, x_s = refs
    part_seqs, res_count, width = updated_ref.shape
    total = both_refs[0][:, residues * width:].astype(jnp.float32)
    for ref in both_refs[1:]:
        total = total + ref[:, residues * width:].astype(jnp.float32)
    right_ref[...] = total
    for k, ref in enumerate(both_refs):
        first = (place_ref[0] ^ k) * residues
        for r in range(residues):
            for n in range(width // LANES):
                at = r * width + n * LANES
                x_s[n, pl.ds(first + r, part_seqs, stride=res_count), :] = ref[:, at:at + LANES].astype(jnp.float32)
    for n in range(width // LANES):
        updated_ref[:, :, n * LANES:(n + 1) * LANES] = (
            x_s[n].reshape(part_seqs, res_count, LANES).astype(jnp.bfloat16)
        )
    total = gl_ref[0].astype(jnp.float32)
    for n in range(1, gl_ref.shape[0]):
        total = total + gl_ref[n].astype(jnp.float32)
    span = total.shape[1] // fold
    channel_block = lax.broadcasted_iota(jnp.int32, (1, LANES), 1) // FACTOR_WIDTH
    each = LANES // FACTOR_WIDTH
    for g in range(span // FACTOR_WIDTH):
        out = None
        for k in range(fold):
            at = k * span + g // each * LANES
            piece = total[:, at:at + LANES]
            shift = (k - g) % each * FACTOR_WIDTH
            piece = pltpu.roll(piece, shift, axis=1) if shift else piece
            out = piece if out is None else jnp.where(channel_block == k, piece, out)
        left_ref[:, g * LANES:(g + 1) * LANES] = out


def finish(place, both, gl, updated_shape):
    part_seqs, res_count, width = updated_shape
    residues = res_count // len(both)
    results = (
        jax.ShapeDtypeStruct(updated_shape, jnp.bfloat16),
        jax.ShapeDtypeStruct(gl.shape[1:], jnp.float32),
        jax.ShapeDtypeStruct((part_seqs, both[0].shape[1] - residues * width), jnp.float32),
    )
    resident = pl.BlockSpec(memory_space=pltpu.VMEM)
    return pl.pallas_call(
        functools.partial(finish_kernel, residues=residues, fold=MXU_SIDE // HALF),
        grid_spec=pltpu.PrefetchScalarGridSpec(
            num_scalar_prefetch=1,
            grid=(1,),
            in_specs=[resident] * (len(both) + 1),
            out_specs=[whole_block(v.shape) for v in results],
            scratch_shapes=[pltpu.VMEM((width // LANES, part_seqs * res_count, LANES), jnp.float32)],
        ),
        out_shape=results,
        compiler_params=pltpu.CompilerParams(
            dimension_semantics=("arbitrary",), vmem_limit_bytes=16 * 1024 * 1024
        ),
        name="finish",
    )(place, *both, gl)


def spread_out(q, count):
    return q if count % 2 else q % 2 * (count // 2) + q // 2


def local(
    alignment,
    pair_features,
    query_weight,
    key_weight,
    value_projection,
    gate_projection,
    gate_bias,
    output_projection,
    left_projection,
    right_projection,
    outer_weight,
    outer_bias,
    expand_weight,
    shrink_weight,
    cotangent,
):
    part_seqs, res_count, width = alignment.shape
    row_parts = lax.axis_size("row")
    col_parts = lax.axis_size("col")
    residues = res_count // row_parts
    own = jnp.transpose(alignment, (1, 0, 2)).reshape(row_parts, residues, part_seqs, width)
    columns = lax.all_to_all(own, "row", split_axis=0, concat_axis=0, tiled=True)
    attended, factors = attend(
        columns, query_weight, key_weight, value_projection, gate_projection, gate_bias,
        output_projection, left_projection, right_projection,
    )

    factors = lax.all_to_all(factors, "row", split_axis=0, concat_axis=0, tiled=True)
    left = factors[:, 0]
    ratio = col_parts // row_parts
    lefts, place = [], []
    for m in range(ratio):
        moves = [
            (q * col_parts + ratio * r + b, r * col_parts + ratio * spread_out(q, row_parts) + (b + m) % ratio)
            for q in range(row_parts)
            for r in range(row_parts)
            for b in range(ratio)
        ]
        lefts.append(lax.ppermute(left, ("row", "col"), moves))
        place.append((lax.axis_index("col") + ratio - m) % ratio)
    row = lax.axis_index("row")
    matrices = right_matrices(factors, outer_weight, expand_weight, shrink_weight)
    pair_out, gl, *both = pair_tile(
        jnp.stack(place + [row]).astype(jnp.int32), lefts, matrices, attended, pair_features, cotangent, outer_bias,
        expand_weight, shrink_weight,
    )
    seqs, gl_width = gl.shape
    both = both[:1] + [
        lax.ppermute(v, "row", [(r, r ^ (k + 1)) for r in range(row_parts)]) for k, v in enumerate(both[1:])
    ]
    gl = lax.all_to_all(
        gl.reshape(col_parts, seqs // col_parts, gl_width), "col", split_axis=0, concat_axis=0, tiled=True
    )
    updated, grad_left, grad_right = finish(row.astype(jnp.int32).reshape(1), both, gl, alignment.shape)
    return (updated, pair_out, grad_left, grad_right)


def solution(mesh):
    return jax.shard_map(
        local,
        mesh=mesh,
        in_specs=(P("row", "col", None), P("row", "col", None)) + (P(),) * 12 + (P("row", "col", None),),
        out_specs=(P("row", "col", None), P("row", "col", None), P("col", "row"), P("row", "col")),
        check_vma=False,
    )
```

```python
import functools

import jax
import jax.numpy as jnp
from jax import lax
from jax.experimental import pallas as pl
from jax.experimental.pallas import tpu as pltpu
from jax.sharding import PartitionSpec as P

ATTENTION_HEADS = 8
HEAD_WIDTH = 32
FACTOR_WIDTH = 32
PAIR_W = 128
EPSILON = 1e-05

LANES = 128
MXU_SIDE = 256
HALF = 64
TILE = 32
CHUNK = 4


def dot_nn(a, b):
    return lax.dot_general(a, b, (((1,), (0,)), ((), ())), preferred_element_type=jnp.float32)


def dot_nt(a, b):
    return lax.dot_general(a, b, (((1,), (1,)), ((), ())), preferred_element_type=jnp.float32)


def layer_normalise(rows):
    rows = rows.astype(jnp.float32)
    average = jnp.mean(rows, axis=-1, keepdims=True)
    centred = rows - average
    variance = jnp.mean(centred * centred, axis=-1, keepdims=True)
    return centred * lax.rsqrt(variance + EPSILON)


def attend_kernel(
    x_ref, wq_ref, wk_ref, wv_ref, wg_ref, bias_ref, wo_ref, wl_ref, wr_ref,
    upd_ref, factor_ref, q_s, k_s, v_s, g_s, a_s, w_s, bias_s, project_s, sems,
):
    parts, residues, part_seqs, width = x_ref.shape
    seqs = parts * part_seqs
    sources = (wq_ref, wk_ref, wv_ref, wg_ref, wo_ref, bias_ref, wl_ref, wr_ref)
    targets = [w_s.at[n] for n in range(5)] + [bias_s, project_s.at[0], project_s.at[1]]
    copies = [pltpu.make_async_copy(a, b, sems.at[n]) for n, (a, b) in enumerate(zip(sources, targets))]
    for copy in copies:
        copy.start()
    x = jnp.concatenate([x_ref[s, r] for r in range(residues) for s in range(parts)], axis=0)
    normed = layer_normalise(x).astype(jnp.bfloat16)
    for n, ref in enumerate((q_s, k_s, v_s)):
        copies[n].wait()
        ref[...] = dot_nn(normed, w_s[n]).astype(jnp.bfloat16)
    copies[3].wait()
    copies[5].wait()
    g_s[...] = jax.nn.sigmoid(dot_nn(normed, w_s[3]) + bias_s[...])

    head_of = lax.broadcasted_iota(jnp.int32, (1, width), 1) // HEAD_WIDTH
    masks = [(head_of == h).astype(jnp.float32) for h in range(ATTENTION_HEADS)]
    masks_low = [m.astype(jnp.bfloat16) for m in masks]

    def one_residue(r, carry):
        rows = pl.ds(pl.multiple_of(r * seqs, seqs), seqs)
        query = q_s[rows, :]
        spread_query = jnp.concatenate([query * m for m in masks_low], axis=0)
        scores = dot_nt(spread_query, k_s[rows, :]) * HEAD_WIDTH ** (-0.5)
        raised = jnp.exp(scores - jnp.max(scores, axis=-1, keepdims=True))
        inverse = 1.0 / jnp.sum(raised, axis=-1, keepdims=True)
        blended = dot_nn(raised.astype(jnp.bfloat16), v_s[rows, :]) * inverse
        total = blended[:seqs] * masks[0]
        for h in range(1, ATTENTION_HEADS):
            total = total + blended[h * seqs:(h + 1) * seqs] * masks[h]
        a_s[rows, :] = (g_s[rows, :] * total).astype(jnp.bfloat16)
        return carry

    lax.fori_loop(0, residues, one_residue, 0, unroll=4 if residues % 4 == 0 else 2)

    copies[4].wait()
    updated = (x.astype(jnp.float32) + dot_nn(a_s[...], w_s[4])).astype(jnp.bfloat16)
    for r in range(residues):
        for s in range(parts):
            begin = r * seqs + s * part_seqs
            upd_ref[s, :, r * width:(r + 1) * width] = updated[begin:begin + part_seqs]
    factor_norm = layer_normalise(updated).astype(jnp.bfloat16)
    copies[6].wait()
    copies[7].wait()
    project = project_s[...].reshape(2 * FACTOR_WIDTH, width)
    for p in range(residues // 2):
        both = dot_nt(project, factor_norm[p * 2 * seqs:(p + 1) * 2 * seqs]).astype(jnp.bfloat16)
        for n in range(parts):
            factor_ref[n, 0, p] = both[:FACTOR_WIDTH]
            factor_ref[n, 1, p] = both[FACTOR_WIDTH:]


def whole_block(shape):
    return pl.BlockSpec(shape, lambda *_: (0,) * len(shape))


def in_hbm(*arrays):
    return [pltpu.with_memory_space_constraint(v, pltpu.HBM) for v in arrays]


def attend(x, wq, wk, wv, wg, gate_bias, wo, wl, wr):
    parts, residues, part_seqs, width = x.shape
    seqs = parts * part_seqs
    rows = residues * seqs
    operands = in_hbm(wq, wk, wv, wg, gate_bias.reshape(1, -1), wo, wl.T, wr.T)
    resident = pl.BlockSpec(memory_space=pltpu.VMEM)
    results = (
        jax.ShapeDtypeStruct((parts, part_seqs, residues * width), jnp.bfloat16),
        jax.ShapeDtypeStruct((parts, 2, residues // 2, FACTOR_WIDTH, 2 * seqs), jnp.bfloat16),
    )
    macs = rows * width * (5 * width + 2 * FACTOR_WIDTH) + 2 * rows * ATTENTION_HEADS * width * seqs
    return pl.pallas_call(
        attend_kernel,
        out_shape=results,
        in_specs=[resident] + [pl.BlockSpec(memory_space=pltpu.HBM)] * len(operands),
        out_specs=[resident] * 2,
        scratch_shapes=[
            pltpu.VMEM((rows, width), jnp.bfloat16),
            pltpu.VMEM((rows, width), jnp.bfloat16),
            pltpu.VMEM((rows, width), jnp.bfloat16),
            pltpu.VMEM((rows, width), jnp.float32),
            pltpu.VMEM((rows, width), jnp.bfloat16),
            pltpu.VMEM((5,) + wq.shape, jnp.bfloat16),
            pltpu.VMEM((1, width), jnp.float32),
            pltpu.VMEM((2, FACTOR_WIDTH, width), jnp.bfloat16),
            pltpu.SemaphoreType.DMA((len(operands),)),
        ],
        compiler_params=pltpu.CompilerParams(vmem_limit_bytes=32 * 1024 * 1024),
        cost_estimate=pl.CostEstimate(flops=2 * macs, bytes_accessed=4 * x.size * 2, transcendentals=rows * width),
        name="column_attention",
    )(x, *operands)


def first_of_four(at, cols):
    wide = MXU_SIDE // HALF * cols
    inside = jnp.where(at < wide, at, jnp.where(at < wide + HALF, at - HALF, at - wide - HALF))
    return inside // cols


def swapped(pair, wide):
    return [pair[:wide], pair[2 * wide - HALF:], pair[wide:2 * wide - HALF]]


def unswapped(pair, wide):
    return [pair[:wide], pair[wide + HALF:], pair[wide:wide + HALF]]


def right_kernel(
    factor_ref, w_ref, expand_ref, shrink_ref, rbd_ref, rbdt_ref, wec_ref, wt_ref, et_ref, st_ref, stage_s,
    *, seqs, cols, fold,
):
    each = factor_ref.shape[2]
    wide = fold * cols
    stage_lanes = stage_s.shape[1]
    low_half = lax.broadcasted_iota(jnp.int32, (1, LANES), 1) < HALF

    stage_s[:FACTOR_WIDTH * FACTOR_WIDTH, :LANES] = w_ref[...].astype(jnp.float32)
    for e in range(FACTOR_WIDTH):
        piece = stage_s[pl.ds(e, FACTOR_WIDTH, stride=FACTOR_WIDTH), :LANES]
        wec_ref[e * FACTOR_WIDTH:(e + 1) * FACTOR_WIDTH, :] = piece.astype(jnp.bfloat16)
    for b in range(FACTOR_WIDTH * FACTOR_WIDTH // LANES):
        block = wec_ref[b * LANES:(b + 1) * LANES, :].astype(jnp.float32)
        wt_ref[:, b * LANES:(b + 1) * LANES] = block.T.astype(jnp.bfloat16)
    et_ref[...] = expand_ref[...].astype(jnp.float32).T.astype(jnp.bfloat16)
    st_ref[...] = shrink_ref[...].astype(jnp.float32).T.astype(jnp.bfloat16)

    for p in range(cols // 2):
        block = factor_ref[p // each, 1, p % each].astype(jnp.float32)
        even = 2 * p * FACTOR_WIDTH
        odd = even + FACTOR_WIDTH
        if seqs % LANES == 0:
            stage_s[even:even + FACTOR_WIDTH, :] = block[:, :seqs]
            stage_s[odd:odd + FACTOR_WIDTH, :] = block[:, seqs:]
        else:
            stage_s[even:even + FACTOR_WIDTH, :] = block
            stage_s[odd:odd + FACTOR_WIDTH, :] = pltpu.roll(block, HALF, axis=1)

    row_k = first_of_four(lax.broadcasted_iota(jnp.int32, (2 * wide, 1), 0), cols)
    lane_k = first_of_four(lax.broadcasted_iota(jnp.int32, (1, 2 * wide), 1), cols)
    for e in range(0, FACTOR_WIDTH, 2):
        two = []
        for u in (e, e + 1):
            two += [stage_s[pl.ds(u, cols, stride=FACTOR_WIDTH), :]] * fold
        upright = jnp.concatenate(swapped(jnp.concatenate(two, axis=0), wide), axis=0)
        chunk, at = e // CHUNK, e % CHUNK * wide
        rolled = pltpu.roll(upright, HALF, axis=1) if seqs < LANES else None
        for v in range(fold * seqs // stage_lanes):
            if seqs < LANES:
                value = jnp.where(
                    low_half, jnp.where(row_k == 2 * v, upright, 0.0), jnp.where(row_k == 2 * v + 1, rolled, 0.0)
                )
            else:
                value = jnp.where(row_k == v, upright, 0.0)
            rbdt_ref[chunk, at:at + 2 * wide, v * stage_lanes:(v + 1) * stage_lanes] = value.astype(jnp.bfloat16)
        turned = upright.T[:seqs]
        for k in range(fold):
            value = jnp.where(lane_k == k, turned, 0.0).astype(jnp.bfloat16)
            rbd_ref[chunk, k * seqs:(k + 1) * seqs, at:at + 2 * wide] = value


def right_matrices(factors, outer_weight, expand_weight, shrink_weight):
    row_parts, _, each, _, lanes = factors.shape
    seqs, cols = lanes // 2, 2 * each * row_parts
    fold = MXU_SIDE // HALF
    channels, width = outer_weight.shape
    results = (
        jax.ShapeDtypeStruct((FACTOR_WIDTH // CHUNK, fold * seqs, CHUNK * fold * cols), jnp.bfloat16),
        jax.ShapeDtypeStruct((FACTOR_WIDTH // CHUNK, CHUNK * fold * cols, fold * seqs), jnp.bfloat16),
        jax.ShapeDtypeStruct((channels, width), jnp.bfloat16),
        jax.ShapeDtypeStruct((width, channels), jnp.bfloat16),
        jax.ShapeDtypeStruct(expand_weight.shape[::-1], jnp.bfloat16),
        jax.ShapeDtypeStruct(shrink_weight.shape[::-1], jnp.bfloat16),
    )
    resident = pl.BlockSpec(memory_space=pltpu.VMEM)
    return pl.pallas_call(
        functools.partial(right_kernel, seqs=seqs, cols=cols, fold=fold),
        out_shape=results,
        in_specs=[resident] * 4,
        out_specs=[resident] * len(results),
        scratch_shapes=[pltpu.VMEM((max(cols * FACTOR_WIDTH, channels), max(seqs, LANES)), jnp.float32)],
        compiler_params=pltpu.CompilerParams(vmem_limit_bytes=16 * 1024 * 1024),
        cost_estimate=pl.CostEstimate(flops=6 * 10**9, bytes_accessed=4 * results[0].size, transcendentals=0),
        name="right_matrices",
    )(factors, outer_weight, expand_weight, shrink_weight)


def pair_kernel(
    place_ref, *refs, seqs, cols, fold, unit, units, blocks,
):
    left_refs, refs = refs[:blocks], refs[blocks:]
    rbd_s, rbdt_s, wec_s, wt_s, et_ref, st_ref, returned_ref, pair_ref, cot_ref = refs[:9]
    bias_ref, expand_ref, shrink_ref, out_ref, gl_ref = refs[9:14]
    both_refs, (outer_s, l_s, lt_s, stage_s, glacc_s, lblk_s, both_s) = refs[14:-7], refs[-7:]
    step = pl.program_id(0)
    row_parts, each = left_refs[0].shape[:2]
    span = l_s.shape[0]
    groups = span // FACTOR_WIDTH
    wide = fold * cols
    scaling = 1.0 / seqs
    low_half = lax.broadcasted_iota(jnp.int32, (1, LANES), 1) < HALF

    @pl.when(step == 0)
    def _prologue():
        for n, ref in enumerate(left_refs):
            lblk_s[place_ref[n]] = ref[...]
        pairs = fold // 2
        for p in range(groups * pairs):
            column, inside = divmod(p, row_parts * each)
            block = lblk_s[column, inside // each, inside % each]
            g, at = p // pairs, p % pairs * 2 * seqs
            l_s[g * FACTOR_WIDTH:(g + 1) * FACTOR_WIDTH, at:at + 2 * seqs] = (
                block.astype(jnp.float32) * scaling
            ).astype(jnp.bfloat16)
        for b in range(span // LANES):
            block = l_s[b * LANES:(b + 1) * LANES, :].astype(jnp.float32)
            lt_s[:, b * LANES:(b + 1) * LANES] = block.T.astype(jnp.bfloat16)

        def some_outers(n, carry):
            outer_s[n] = dot_nn(l_s[...], rbd_s[n]).astype(jnp.bfloat16)
            return carry

        lax.fori_loop(0, outer_s.shape[0], some_outers, 0, unroll=2)

    def unit_rows(u):
        at = (step * units + u) * unit * FACTOR_WIDTH
        return pl.ds(pl.multiple_of(at, unit * FACTOR_WIDTH), unit * FACTOR_WIDTH)

    def group(block, g):
        return block[g * FACTOR_WIDTH:(g + 1) * FACTOR_WIDTH]

    def forward(u):
        stacked = []
        for e in range(0, FACTOR_WIDTH, 2):
            at = e % CHUNK * wide
            block = outer_s[e // CHUNK, unit_rows(u), at:at + 2 * wide]
            shared = block[:, LANES:2 * LANES]
            rolled = pltpu.roll(shared, HALF, axis=1)
            even, odd = [], []
            for g in range(0, unit, 2):
                a, b = block[:, :LANES], block[:, 2 * LANES:]
                even += [group(a, g), jnp.where(low_half, group(shared, g), group(rolled, g + 1)), group(a, g + 1)]
                odd += [group(b, g), jnp.where(low_half, group(rolled, g), group(shared, g + 1)), group(b, g + 1)]
            stacked += [jnp.concatenate(even, axis=1), jnp.concatenate(odd, axis=1)]
        product = dot_nn(wt_s[...], jnp.concatenate(stacked, axis=0)).T
        pieces = []
        for g in range(0, unit, 2):
            pieces += unswapped(product[g * wide:(g + 2) * wide], wide)
        own = pl.ds((step * units + u) * unit * fold, unit * fold)
        projected = jnp.concatenate(pieces, axis=0)
        pair = pair_ref[own].reshape(-1, PAIR_W)
        middles, inverses, spreads = [], [], []
        for at in range(0, projected.shape[0], TILE):
            middle = pair[at:at + TILE] + projected[at:at + TILE] + bias_ref[...]
            average = jnp.mean(middle, axis=-1, keepdims=True)
            centred = middle - average
            variance = jnp.mean(centred * centred, axis=-1, keepdims=True)
            inverse = lax.rsqrt(variance + EPSILON)
            middles.append(middle)
            inverses.append(inverse)
            spreads.append(centred * inverse)
        spread_low = jnp.concatenate([v.astype(jnp.bfloat16) for v in spreads], axis=0)
        cotangent = cot_ref[own].reshape(-1, PAIR_W)
        before = dot_nn(spread_low, expand_ref[...])
        back_hidden = dot_nn(cotangent.astype(jnp.bfloat16), st_ref[...])
        return middles, inverses, spreads, before, cotangent, back_hidden

    def backward(u, middles, inverses, spreads, before, cotangent, back_hidden):
        own = slice(u * unit * fold, (u + 1) * unit * fold)
        rows, width = before.shape
        hidden, back_before = [], []
        for at in range(0, rows, TILE):
            hidden_parts, back_parts = [], []
            for v in range(0, width, MXU_SIDE):
                x = before[at:at + TILE, v:v + MXU_SIDE]
                phi = 0.5 * (1.0 + lax.erf(x * 0.7071067811865476))
                slope = phi + x * jnp.exp(-0.5 * x * x) * 0.3989422804014327
                hidden_parts.append((x * phi).astype(jnp.bfloat16))
                back_parts.append((back_hidden[at:at + TILE, v:v + MXU_SIDE] * slope).astype(jnp.bfloat16))
            hidden.append(jnp.concatenate(hidden_parts, axis=1))
            back_before.append(jnp.concatenate(back_parts, axis=1))
        back_spread = dot_nn(jnp.concatenate(back_before, axis=0), et_ref[...])
        change = dot_nn(jnp.concatenate(hidden, axis=0), shrink_ref[...])
        out_ref[own] = (jnp.concatenate(middles, axis=0) + change).reshape(unit * fold, cols, PAIR_W)
        back_middle = []
        for n, at in enumerate(range(0, rows, TILE)):
            back, spread = back_spread[at:at + TILE], spreads[n]
            centre_term = jnp.mean(back, axis=-1, keepdims=True)
            slope_term = jnp.mean(back * spread, axis=-1, keepdims=True)
            back = cotangent[at:at + TILE] + inverses[n] * (back - centre_term - spread * slope_term)
            back_middle.append(back.astype(jnp.bfloat16))
        back_middle = jnp.concatenate(back_middle, axis=0)
        parts = []
        for g in range(0, unit, 2):
            parts += swapped(back_middle[g * wide:(g + 2) * wide], wide)
        back_outer = dot_nt(wec_s[...], jnp.concatenate(parts, axis=0)).astype(jnp.bfloat16)
        for e in range(0, FACTOR_WIDTH, 2):
            even, odd = group(back_outer, e), group(back_outer, e + 1)
            a, shared, b = [], [], []
            for g in range(0, unit, 2):
                at = g * wide
                of_even, of_odd = even[:, at + LANES:at + 2 * LANES], odd[:, at + LANES:at + 2 * LANES]
                a += [even[:, at:at + LANES], even[:, at + 2 * LANES:at + 3 * LANES]]
                b += [odd[:, at:at + LANES], odd[:, at + 2 * LANES:at + 3 * LANES]]
                shared += [
                    jnp.where(low_half, of_even, pltpu.roll(of_odd, HALF, axis=1)),
                    jnp.where(low_half, pltpu.roll(of_even, HALF, axis=1), of_odd),
                ]
            for n, pieces in enumerate((a, shared, b)):
                at = e % CHUNK * wide + n * LANES
                outer_s[e // CHUNK, unit_rows(u), at:at + LANES] = jnp.concatenate(pieces, axis=0)

    held = forward(0)
    for u in range(units):
        ahead = forward(u + 1) if u + 1 < units else None
        backward(u, *held)
        held = ahead

    @pl.when(step == pl.num_programs(0) - 1)
    def _epilogue():
        glacc_s[...] = jnp.zeros_like(glacc_s)
        empty = jnp.zeros((LANES - seqs % LANES, CHUNK * wide), jnp.float32) if seqs % LANES else None
        at = lax.broadcasted_iota(jnp.int32, (1, CHUNK * wide), 1)
        lane_k = first_of_four(lax.rem(at, 2 * wide), cols)

        def some(n, carry):
            back = outer_s[n]
            glacc_s[...] += dot_nn(back, rbdt_s[n])
            full = dot_nn(lt_s[...], back)
            compact = full[:seqs]
            for k in range(1, fold):
                compact = jnp.where(lane_k == k, full[k * seqs:(k + 1) * seqs], compact)
            if empty is not None:
                compact = jnp.concatenate([compact, empty], axis=0)
            turned = compact.T
            for p in range(CHUNK // 2):
                two = jnp.concatenate(unswapped(turned[2 * p * wide:2 * (p + 1) * wide], wide), axis=0)
                for u in range(2):
                    total = two[u * wide:u * wide + cols]
                    for k in range(1, fold):
                        total = total + two[u * wide + k * cols:u * wide + (k + 1) * cols]
                    stage_s[pl.ds(n * CHUNK + 2 * p + u, cols, stride=FACTOR_WIDTH), :] = total
            return carry

        lax.fori_loop(0, outer_s.shape[0], some, 0, unroll=2)
        part_seqs, width = returned_ref.shape[1:]
        both_s[:, :, :width] = returned_ref[...]
        for b in range(cols * FACTOR_WIDTH // LANES):
            block = stage_s[b * LANES:(b + 1) * LANES, :].T[:seqs].astype(jnp.bfloat16)
            both_s[:, :, width + b * LANES:width + (b + 1) * LANES] = block.reshape(row_parts, part_seqs, LANES)
        for k, ref in enumerate(both_refs):
            ref[...] = both_s[place_ref[blocks] ^ k]
        for b in range(span // LANES):
            block = glacc_s[b * LANES:(b + 1) * LANES, :].T * scaling
            for k in range(fold):
                at = k * span + b * LANES
                gl_ref[:, at:at + LANES] = block[k * seqs:(k + 1) * seqs].astype(jnp.bfloat16)


def pair_tile(place, lefts, matrices, returned, pair_features, cotangent, outer_bias, expand_weight, shrink_weight):
    seqs = lefts[0].shape[-1] // 2
    rows, cols, _ = pair_features.shape
    fold = MXU_SIDE // HALF
    groups = rows // fold
    unit = 4
    units = 2 if groups % (2 * unit) == 0 else 1
    steps = groups // unit // units
    wide = fold * cols
    span = groups * FACTOR_WIDTH
    channels = FACTOR_WIDTH * FACTOR_WIDTH
    block = pl.BlockSpec((unit * units * fold, cols, PAIR_W), lambda n, place: (n, 0, 0))
    resident = pl.BlockSpec(memory_space=pltpu.VMEM)
    operands = (
        *lefts, *matrices, returned, pair_features, cotangent, outer_bias.reshape(1, -1), expand_weight,
        shrink_weight,
    )
    results = (
        jax.ShapeDtypeStruct(pair_features.shape, jnp.float32),
        jax.ShapeDtypeStruct((seqs, rows * FACTOR_WIDTH), jnp.bfloat16),
    ) + returned.shape[0] * (
        jax.ShapeDtypeStruct((returned.shape[1], returned.shape[2] + cols * FACTOR_WIDTH), jnp.bfloat16),
    )
    padded = groups * wide
    macs = 3 * FACTOR_WIDTH * span * fold * seqs * wide + padded * (2 * channels * MXU_SIDE + 8 * MXU_SIDE * MXU_SIDE)
    return pl.pallas_call(
        functools.partial(
            pair_kernel, seqs=seqs, cols=cols, fold=fold, unit=unit, units=units, blocks=len(lefts)
        ),
        grid_spec=pltpu.PrefetchScalarGridSpec(
            num_scalar_prefetch=1,
            grid=(steps,),
            in_specs=[resident] * len(operands),
            out_specs=[block] + [resident] * (len(results) - 1),
            scratch_shapes=[
                pltpu.VMEM((FACTOR_WIDTH // CHUNK, span, CHUNK * wide), jnp.bfloat16),
                pltpu.VMEM((span, fold * seqs), jnp.bfloat16),
                pltpu.VMEM((fold * seqs, span), jnp.bfloat16),
                pltpu.VMEM((cols * FACTOR_WIDTH, max(seqs, LANES)), jnp.float32),
                pltpu.VMEM((span, fold * seqs), jnp.float32),
                pltpu.VMEM((len(lefts),) + lefts[0].shape, jnp.bfloat16),
                pltpu.VMEM(returned.shape[:1] + results[2].shape, jnp.bfloat16),
            ],
        ),
        out_shape=results,
        compiler_params=pltpu.CompilerParams(
            dimension_semantics=("arbitrary",), vmem_limit_bytes=36 * 1024 * 1024
        ),
        cost_estimate=pl.CostEstimate(
            flops=2 * macs, bytes_accessed=3 * pair_features.size * 4, transcendentals=0
        ),
        name="pair_tile",
    )(place, *operands)


def finish_kernel(place_ref, *refs, residues, fold):
    *both_refs, gl_ref, updated_ref, left_ref, right_ref, x_s = refs
    part_seqs, res_count, width = updated_ref.shape
    total = both_refs[0][:, residues * width:].astype(jnp.float32)
    for ref in both_refs[1:]:
        total = total + ref[:, residues * width:].astype(jnp.float32)
    right_ref[...] = total
    for k, ref in enumerate(both_refs):
        first = (place_ref[0] ^ k) * residues
        for r in range(residues):
            for n in range(width // LANES):
                at = r * width + n * LANES
                x_s[n, pl.ds(first + r, part_seqs, stride=res_count), :] = ref[:, at:at + LANES].astype(jnp.float32)
    for n in range(width // LANES):
        updated_ref[:, :, n * LANES:(n + 1) * LANES] = (
            x_s[n].reshape(part_seqs, res_count, LANES).astype(jnp.bfloat16)
        )
    total = gl_ref[0].astype(jnp.float32)
    for n in range(1, gl_ref.shape[0]):
        total = total + gl_ref[n].astype(jnp.float32)
    span = total.shape[1] // fold
    channel_block = lax.broadcasted_iota(jnp.int32, (1, LANES), 1) // FACTOR_WIDTH
    each = LANES // FACTOR_WIDTH
    for g in range(span // FACTOR_WIDTH):
        out = None
        for k in range(fold):
            at = k * span + g // each * LANES
            piece = total[:, at:at + LANES]
            shift = (k - g) % each * FACTOR_WIDTH
            piece = pltpu.roll(piece, shift, axis=1) if shift else piece
            out = piece if out is None else jnp.where(channel_block == k, piece, out)
        left_ref[:, g * LANES:(g + 1) * LANES] = out


def finish(place, both, gl, updated_shape):
    part_seqs, res_count, width = updated_shape
    residues = res_count // len(both)
    results = (
        jax.ShapeDtypeStruct(updated_shape, jnp.bfloat16),
        jax.ShapeDtypeStruct(gl.shape[1:], jnp.float32),
        jax.ShapeDtypeStruct((part_seqs, both[0].shape[1] - residues * width), jnp.float32),
    )
    resident = pl.BlockSpec(memory_space=pltpu.VMEM)
    return pl.pallas_call(
        functools.partial(finish_kernel, residues=residues, fold=MXU_SIDE // HALF),
        grid_spec=pltpu.PrefetchScalarGridSpec(
            num_scalar_prefetch=1,
            grid=(1,),
            in_specs=[resident] * (len(both) + 1),
            out_specs=[whole_block(v.shape) for v in results],
            scratch_shapes=[pltpu.VMEM((width // LANES, part_seqs * res_count, LANES), jnp.float32)],
        ),
        out_shape=results,
        compiler_params=pltpu.CompilerParams(
            dimension_semantics=("arbitrary",), vmem_limit_bytes=16 * 1024 * 1024
        ),
        name="finish",
    )(place, *both, gl)


def spread_out(q, count):
    return q if count % 2 else q % 2 * (count // 2) + q // 2


def local(
    alignment,
    pair_features,
    query_weight,
    key_weight,
    value_projection,
    gate_projection,
    gate_bias,
    output_projection,
    left_projection,
    right_projection,
    outer_weight,
    outer_bias,
    expand_weight,
    shrink_weight,
    cotangent,
):
    part_seqs, res_count, width = alignment.shape
    row_parts = lax.axis_size("row")
    col_parts = lax.axis_size("col")
    residues = res_count // row_parts
    own = jnp.transpose(alignment, (1, 0, 2)).reshape(row_parts, residues, part_seqs, width)
    columns = lax.all_to_all(own, "row", split_axis=0, concat_axis=0, tiled=True)
    attended, factors = attend(
        columns, query_weight, key_weight, value_projection, gate_projection, gate_bias,
        output_projection, left_projection, right_projection,
    )

    factors = lax.all_to_all(factors, "row", split_axis=0, concat_axis=0, tiled=True)
    left = factors[:, 0]
    ratio = col_parts // row_parts
    lefts, place = [], []
    for m in range(ratio):
        moves = [
            (q * col_parts + ratio * r + b, r * col_parts + ratio * spread_out(q, row_parts) + (b + m) % ratio)
            for q in range(row_parts)
            for r in range(row_parts)
            for b in range(ratio)
        ]
        lefts.append(lax.ppermute(left, ("row", "col"), moves))
        place.append((lax.axis_index("col") + ratio - m) % ratio)
    row = lax.axis_index("row")
    matrices = right_matrices(factors, outer_weight, expand_weight, shrink_weight)
    pair_out, gl, *both = pair_tile(
        jnp.stack(place + [row]).astype(jnp.int32), lefts, matrices, attended, pair_features, cotangent, outer_bias,
        expand_weight, shrink_weight,
    )
    seqs, gl_width = gl.shape
    both = both[:1] + [
        lax.ppermute(v, "row", [(r, r ^ (k + 1)) for r in range(row_parts)]) for k, v in enumerate(both[1:])
    ]
    gl = lax.all_to_all(
        gl.reshape(col_parts, seqs // col_parts, gl_width), "col", split_axis=0, concat_axis=0, tiled=True
    )
    updated, grad_left, grad_right = finish(row.astype(jnp.int32).reshape(1), both, gl, alignment.shape)
    return (updated, pair_out, grad_left, grad_right)


def solution(mesh):
    return jax.shard_map(
        local,
        mesh=mesh,
        in_specs=(P("row", "col", None), P("row", "col", None)) + (P(),) * 12 + (P("row", "col", None),),
        out_specs=(P("row", "col", None), P("row", "col", None), P("col", "row"), P("row", "col")),
        check_vma=False,
    )
```

```python
import functools

import jax
import jax.numpy as jnp
from jax import lax
from jax.experimental import pallas as pl
from jax.experimental.pallas import tpu as pltpu
from jax.sharding import PartitionSpec as P

ATTENTION_HEADS = 8
HEAD_WIDTH = 32
FACTOR_WIDTH = 32
PAIR_W = 128
EPSILON = 1e-05

LANES = 128
MXU_SIDE = 256
HALF = 64
TILE = 32
CHUNK = 4
UNIT = 4


def dot_nn(a, b):
    return lax.dot_general(a, b, (((1,), (0,)), ((), ())), preferred_element_type=jnp.float32)


def dot_nt(a, b):
    return lax.dot_general(a, b, (((1,), (1,)), ((), ())), preferred_element_type=jnp.float32)


def layer_normalise(rows):
    rows = rows.astype(jnp.float32)
    average = jnp.mean(rows, axis=-1, keepdims=True)
    centred = rows - average
    variance = jnp.mean(centred * centred, axis=-1, keepdims=True)
    return centred * lax.rsqrt(variance + EPSILON)


def attend_kernel(
    x_ref, wq_ref, wk_ref, wv_ref, wg_ref, bias_ref, wo_ref, wl_ref, wr_ref,
    upd_ref, factor_ref, q_s, k_s, v_s, g_s, a_s, w_s, bias_s, project_s, sems,
):
    parts, residues, part_seqs, width = x_ref.shape
    seqs = parts * part_seqs
    sources = (wq_ref, wk_ref, wv_ref, wg_ref, wo_ref, bias_ref, wl_ref, wr_ref)
    targets = [w_s.at[n] for n in range(5)] + [bias_s, project_s.at[0], project_s.at[1]]
    copies = [pltpu.make_async_copy(a, b, sems.at[n]) for n, (a, b) in enumerate(zip(sources, targets))]
    for copy in copies:
        copy.start()
    x = jnp.concatenate([x_ref[s, r] for r in range(residues) for s in range(parts)], axis=0)
    normed = layer_normalise(x).astype(jnp.bfloat16)
    for n, ref in enumerate((q_s, k_s, v_s)):
        copies[n].wait()
        ref[...] = dot_nn(normed, w_s[n]).astype(jnp.bfloat16)
    copies[3].wait()
    copies[5].wait()
    g_s[...] = jax.nn.sigmoid(dot_nn(normed, w_s[3]) + bias_s[...])

    head_of = lax.broadcasted_iota(jnp.int32, (1, width), 1) // HEAD_WIDTH
    masks = [(head_of == h).astype(jnp.float32) for h in range(ATTENTION_HEADS)]
    masks_low = [m.astype(jnp.bfloat16) for m in masks]

    def one_residue(r, carry):
        rows = pl.ds(pl.multiple_of(r * seqs, seqs), seqs)
        query = q_s[rows, :]
        spread_query = jnp.concatenate([query * m for m in masks_low], axis=0)
        scores = dot_nt(spread_query, k_s[rows, :]) * HEAD_WIDTH ** (-0.5)
        raised = jnp.exp(scores - jnp.max(scores, axis=-1, keepdims=True))
        inverse = 1.0 / jnp.sum(raised, axis=-1, keepdims=True)
        blended = dot_nn(raised.astype(jnp.bfloat16), v_s[rows, :]) * inverse
        total = blended[:seqs] * masks[0]
        for h in range(1, ATTENTION_HEADS):
            total = total + blended[h * seqs:(h + 1) * seqs] * masks[h]
        a_s[rows, :] = (g_s[rows, :] * total).astype(jnp.bfloat16)
        return carry

    lax.fori_loop(0, residues, one_residue, 0, unroll=4 if residues % 4 == 0 else 2)

    copies[4].wait()
    updated = (x.astype(jnp.float32) + dot_nn(a_s[...], w_s[4])).astype(jnp.bfloat16)
    for r in range(residues):
        for s in range(parts):
            begin = r * seqs + s * part_seqs
            upd_ref[s, :, r * width:(r + 1) * width] = updated[begin:begin + part_seqs]
    factor_norm = layer_normalise(updated).astype(jnp.bfloat16)
    copies[6].wait()
    copies[7].wait()
    project = project_s[...].reshape(2 * FACTOR_WIDTH, width)
    for p in range(residues // 2):
        both = dot_nt(project, factor_norm[p * 2 * seqs:(p + 1) * 2 * seqs]).astype(jnp.bfloat16)
        for n in range(parts):
            factor_ref[n, 0, p] = both[:FACTOR_WIDTH]
            factor_ref[n, 1, p] = both[FACTOR_WIDTH:]


def whole_block(shape):
    return pl.BlockSpec(shape, lambda *_: (0,) * len(shape))


def in_hbm(*arrays):
    return [pltpu.with_memory_space_constraint(v, pltpu.HBM) for v in arrays]


def attend(x, wq, wk, wv, wg, gate_bias, wo, wl, wr):
    parts, residues, part_seqs, width = x.shape
    seqs = parts * part_seqs
    rows = residues * seqs
    operands = in_hbm(wq, wk, wv, wg, gate_bias.reshape(1, -1), wo, wl.T, wr.T)
    resident = pl.BlockSpec(memory_space=pltpu.VMEM)
    results = (
        jax.ShapeDtypeStruct((parts, part_seqs, residues * width), jnp.bfloat16),
        jax.ShapeDtypeStruct((parts, 2, residues // 2, FACTOR_WIDTH, 2 * seqs), jnp.bfloat16),
    )
    macs = rows * width * (5 * width + 2 * FACTOR_WIDTH) + 2 * rows * ATTENTION_HEADS * width * seqs
    return pl.pallas_call(
        attend_kernel,
        out_shape=results,
        in_specs=[resident] + [pl.BlockSpec(memory_space=pltpu.HBM)] * len(operands),
        out_specs=[resident] * 2,
        scratch_shapes=[
            pltpu.VMEM((rows, width), jnp.bfloat16),
            pltpu.VMEM((rows, width), jnp.bfloat16),
            pltpu.VMEM((rows, width), jnp.bfloat16),
            pltpu.VMEM((rows, width), jnp.float32),
            pltpu.VMEM((rows, width), jnp.bfloat16),
            pltpu.VMEM((5,) + wq.shape, jnp.bfloat16),
            pltpu.VMEM((1, width), jnp.float32),
            pltpu.VMEM((2, FACTOR_WIDTH, width), jnp.bfloat16),
            pltpu.SemaphoreType.DMA((len(operands),)),
        ],
        compiler_params=pltpu.CompilerParams(vmem_limit_bytes=32 * 1024 * 1024),
        cost_estimate=pl.CostEstimate(flops=2 * macs, bytes_accessed=4 * x.size * 2, transcendentals=rows * width),
        name="column_attention",
    )(x, *operands)


def first_of_four(at, cols):
    wide = MXU_SIDE // HALF * cols
    inside = jnp.where(at < wide, at, jnp.where(at < wide + HALF, at - HALF, at - wide - HALF))
    return inside // cols


def swapped(pair, wide):
    return [pair[:wide], pair[2 * wide - HALF:], pair[wide:2 * wide - HALF]]


def unswapped(pair, wide):
    return [pair[:wide], pair[wide + HALF:], pair[wide:wide + HALF]]


def right_kernel(
    factor_ref, w_ref, expand_ref, shrink_ref, rbd_ref, rbdt_ref, wec_ref, wt_ref, et_ref, st_ref, stage_s,
    *, seqs, cols, fold,
):
    each = factor_ref.shape[2]
    wide = fold * cols
    stage_lanes = stage_s.shape[1]
    low_half = lax.broadcasted_iota(jnp.int32, (1, LANES), 1) < HALF

    stage_s[:FACTOR_WIDTH * FACTOR_WIDTH, :LANES] = w_ref[...].astype(jnp.float32)
    for e in range(FACTOR_WIDTH):
        piece = stage_s[pl.ds(e, FACTOR_WIDTH, stride=FACTOR_WIDTH), :LANES]
        wec_ref[e * FACTOR_WIDTH:(e + 1) * FACTOR_WIDTH, :] = piece.astype(jnp.bfloat16)
    for b in range(FACTOR_WIDTH * FACTOR_WIDTH // LANES):
        block = wec_ref[b * LANES:(b + 1) * LANES, :].astype(jnp.float32)
        wt_ref[:, b * LANES:(b + 1) * LANES] = block.T.astype(jnp.bfloat16)
    et_ref[...] = expand_ref[...].astype(jnp.float32).T.astype(jnp.bfloat16)
    st_ref[...] = shrink_ref[...].astype(jnp.float32).T.astype(jnp.bfloat16)

    for p in range(cols // 2):
        block = factor_ref[p // each, 1, p % each].astype(jnp.float32)
        even = 2 * p * FACTOR_WIDTH
        odd = even + FACTOR_WIDTH
        if seqs % LANES == 0:
            stage_s[even:even + FACTOR_WIDTH, :] = block[:, :seqs]
            stage_s[odd:odd + FACTOR_WIDTH, :] = block[:, seqs:]
        else:
            stage_s[even:even + FACTOR_WIDTH, :] = block
            stage_s[odd:odd + FACTOR_WIDTH, :] = pltpu.roll(block, HALF, axis=1)

    row_k = first_of_four(lax.broadcasted_iota(jnp.int32, (2 * wide, 1), 0), cols)
    lane_k = first_of_four(lax.broadcasted_iota(jnp.int32, (1, 2 * wide), 1), cols)
    for e in range(0, FACTOR_WIDTH, 2):
        two = []
        for u in (e, e + 1):
            two += [stage_s[pl.ds(u, cols, stride=FACTOR_WIDTH), :]] * fold
        upright = jnp.concatenate(swapped(jnp.concatenate(two, axis=0), wide), axis=0)
        chunk, at = e // CHUNK, e % CHUNK * wide
        rolled = pltpu.roll(upright, HALF, axis=1) if seqs < LANES else None
        for v in range(fold * seqs // stage_lanes):
            if seqs < LANES:
                value = jnp.where(
                    low_half, jnp.where(row_k == 2 * v, upright, 0.0), jnp.where(row_k == 2 * v + 1, rolled, 0.0)
                )
            else:
                value = jnp.where(row_k == v, upright, 0.0)
            rbdt_ref[chunk, at:at + 2 * wide, v * stage_lanes:(v + 1) * stage_lanes] = value.astype(jnp.bfloat16)
        turned = upright.T[:seqs]
        for k in range(fold):
            value = jnp.where(lane_k == k, turned, 0.0).astype(jnp.bfloat16)
            rbd_ref[chunk, k * seqs:(k + 1) * seqs, at:at + 2 * wide] = value


def right_matrices(factors, outer_weight, expand_weight, shrink_weight):
    row_parts, _, each, _, lanes = factors.shape
    seqs, cols = lanes // 2, 2 * each * row_parts
    fold = MXU_SIDE // HALF
    channels, width = outer_weight.shape
    results = (
        jax.ShapeDtypeStruct((FACTOR_WIDTH // CHUNK, fold * seqs, CHUNK * fold * cols), jnp.bfloat16),
        jax.ShapeDtypeStruct((FACTOR_WIDTH // CHUNK, CHUNK * fold * cols, fold * seqs), jnp.bfloat16),
        jax.ShapeDtypeStruct((channels, width), jnp.bfloat16),
        jax.ShapeDtypeStruct((width, channels), jnp.bfloat16),
        jax.ShapeDtypeStruct(expand_weight.shape[::-1], jnp.bfloat16),
        jax.ShapeDtypeStruct(shrink_weight.shape[::-1], jnp.bfloat16),
    )
    resident = pl.BlockSpec(memory_space=pltpu.VMEM)
    return pl.pallas_call(
        functools.partial(right_kernel, seqs=seqs, cols=cols, fold=fold),
        out_shape=results,
        in_specs=[resident] * 4,
        out_specs=[resident] * len(results),
        scratch_shapes=[pltpu.VMEM((max(cols * FACTOR_WIDTH, channels), max(seqs, LANES)), jnp.float32)],
        compiler_params=pltpu.CompilerParams(vmem_limit_bytes=16 * 1024 * 1024),
        cost_estimate=pl.CostEstimate(flops=6 * 10**9, bytes_accessed=4 * results[0].size, transcendentals=0),
        name="right_matrices",
    )(factors, outer_weight, expand_weight, shrink_weight)


def pair_kernel(
    place_ref, *refs, seqs, cols, fold, unit, units, blocks,
):
    left_refs, refs = refs[:blocks], refs[blocks:]
    rbd_s, rbdt_s, wec_s, wt_s, et_ref, st_ref, pair_ref, cot_ref, back_ref = refs[:9]
    returned_ref, bias_ref, expand_ref, out_ref, gl_ref = refs[9:14]
    both_refs, (outer_s, l_s, lt_s, stage_s, glacc_s, lblk_s, both_s) = refs[14:-7], refs[-7:]
    step = pl.program_id(0)
    row_parts, each = left_refs[0].shape[:2]
    span = l_s.shape[0]
    groups = span // FACTOR_WIDTH
    wide = fold * cols
    scaling = 1.0 / seqs
    low_half = lax.broadcasted_iota(jnp.int32, (1, LANES), 1) < HALF

    @pl.when(step == 0)
    def _prologue():
        for n, ref in enumerate(left_refs):
            lblk_s[place_ref[n]] = ref[...]
        pairs = fold // 2
        for p in range(groups * pairs):
            column, inside = divmod(p, row_parts * each)
            block = lblk_s[column, inside // each, inside % each]
            g, at = p // pairs, p % pairs * 2 * seqs
            l_s[g * FACTOR_WIDTH:(g + 1) * FACTOR_WIDTH, at:at + 2 * seqs] = (
                block.astype(jnp.float32) * scaling
            ).astype(jnp.bfloat16)
        for b in range(span // LANES):
            block = l_s[b * LANES:(b + 1) * LANES, :].astype(jnp.float32)
            lt_s[:, b * LANES:(b + 1) * LANES] = block.T.astype(jnp.bfloat16)

        def some_outers(n, carry):
            outer_s[n] = dot_nn(l_s[...], rbd_s[n]).astype(jnp.bfloat16)
            return carry

        lax.fori_loop(0, outer_s.shape[0], some_outers, 0, unroll=2)

    def unit_rows(u):
        at = (step * units + u) * unit * FACTOR_WIDTH
        return pl.ds(pl.multiple_of(at, unit * FACTOR_WIDTH), unit * FACTOR_WIDTH)

    def group(block, g):
        return block[g * FACTOR_WIDTH:(g + 1) * FACTOR_WIDTH]

    def forward(u):
        stacked = []
        for e in range(0, FACTOR_WIDTH, 2):
            at = e % CHUNK * wide
            block = outer_s[e // CHUNK, unit_rows(u), at:at + 2 * wide]
            shared = block[:, LANES:2 * LANES]
            rolled = pltpu.roll(shared, HALF, axis=1)
            even, odd = [], []
            for g in range(0, unit, 2):
                a, b = block[:, :LANES], block[:, 2 * LANES:]
                even += [group(a, g), jnp.where(low_half, group(shared, g), group(rolled, g + 1)), group(a, g + 1)]
                odd += [group(b, g), jnp.where(low_half, group(rolled, g), group(shared, g + 1)), group(b, g + 1)]
            stacked += [jnp.concatenate(even, axis=1), jnp.concatenate(odd, axis=1)]
        projected = dot_nn(wt_s[...], jnp.concatenate(stacked, axis=0))
        middles, inverses, spreads = [], [], []
        for at in range(0, projected.shape[1], LANES):
            middle = pair_ref[step * units + u, :, at:at + LANES] + projected[:, at:at + LANES] + bias_ref[...]
            average = jnp.mean(middle, axis=0, keepdims=True)
            centred = middle - average
            variance = jnp.mean(centred * centred, axis=0, keepdims=True)
            inverse = lax.rsqrt(variance + EPSILON)
            middles.append(middle)
            inverses.append(inverse)
            spreads.append(centred * inverse)
        spread_low = jnp.concatenate([v.astype(jnp.bfloat16) for v in spreads], axis=1)
        return middles, inverses, spreads, dot_nn(et_ref[...], spread_low)

    def backward(u, middles, inverses, spreads, before):
        rows, pairs = before.shape
        hidden, back_before = [], []
        for at in range(0, rows, TILE):
            hidden_parts, back_parts = [], []
            for v in range(0, pairs, MXU_SIDE):
                x = before[at:at + TILE, v:v + MXU_SIDE]
                back = back_ref[step * units + u, at:at + TILE, v:v + MXU_SIDE].astype(jnp.float32)
                phi = 0.5 * (1.0 + lax.erf(x * 0.7071067811865476))
                slope = phi + x * jnp.exp(-0.5 * x * x) * 0.3989422804014327
                hidden_parts.append((x * phi).astype(jnp.bfloat16))
                back_parts.append((back * slope).astype(jnp.bfloat16))
            hidden.append(jnp.concatenate(hidden_parts, axis=1))
            back_before.append(jnp.concatenate(back_parts, axis=1))
        back_spread = dot_nn(expand_ref[...], jnp.concatenate(back_before, axis=0))
        change = dot_nn(st_ref[...], jnp.concatenate(hidden, axis=0))
        back_middle = []
        for n, at in enumerate(range(0, pairs, LANES)):
            back, spread = back_spread[:, at:at + LANES], spreads[n]
            centre_term = jnp.mean(back, axis=0, keepdims=True)
            slope_term = jnp.mean(back * spread, axis=0, keepdims=True)
            back = back - centre_term - spread * slope_term
            back = cot_ref[step * units + u, :, at:at + LANES] + inverses[n] * back
            back_middle.append(back.astype(jnp.bfloat16))
        result = (jnp.concatenate(middles, axis=1) + change).T
        pieces = []
        for g in range(0, unit, 2):
            pieces += unswapped(result[g * wide:(g + 2) * wide], wide)
        out_ref[u * unit * fold:(u + 1) * unit * fold] = jnp.concatenate(pieces, axis=0).reshape(
            unit * fold, cols, PAIR_W
        )
        back_outer = dot_nn(wec_s[...], jnp.concatenate(back_middle, axis=1)).astype(jnp.bfloat16)
        for e in range(0, FACTOR_WIDTH, 2):
            even, odd = group(back_outer, e), group(back_outer, e + 1)
            a, shared, b = [], [], []
            for g in range(0, unit, 2):
                at = g * wide
                of_even, of_odd = even[:, at + LANES:at + 2 * LANES], odd[:, at + LANES:at + 2 * LANES]
                a += [even[:, at:at + LANES], even[:, at + 2 * LANES:at + 3 * LANES]]
                b += [odd[:, at:at + LANES], odd[:, at + 2 * LANES:at + 3 * LANES]]
                shared += [
                    jnp.where(low_half, of_even, pltpu.roll(of_odd, HALF, axis=1)),
                    jnp.where(low_half, pltpu.roll(of_even, HALF, axis=1), of_odd),
                ]
            for n, pieces in enumerate((a, shared, b)):
                at = e % CHUNK * wide + n * LANES
                outer_s[e // CHUNK, unit_rows(u), at:at + LANES] = jnp.concatenate(pieces, axis=0)

    held = forward(0)
    for u in range(units):
        ahead = forward(u + 1) if u + 1 < units else None
        backward(u, *held)
        held = ahead

    @pl.when(step == pl.num_programs(0) - 1)
    def _epilogue():
        glacc_s[...] = jnp.zeros_like(glacc_s)
        empty = jnp.zeros((LANES - seqs % LANES, CHUNK * wide), jnp.float32) if seqs % LANES else None
        at = lax.broadcasted_iota(jnp.int32, (1, CHUNK * wide), 1)
        lane_k = first_of_four(lax.rem(at, 2 * wide), cols)

        def some(n, carry):
            back = outer_s[n]
            glacc_s[...] += dot_nn(back, rbdt_s[n])
            full = dot_nn(lt_s[...], back)
            compact = full[:seqs]
            for k in range(1, fold):
                compact = jnp.where(lane_k == k, full[k * seqs:(k + 1) * seqs], compact)
            if empty is not None:
                compact = jnp.concatenate([compact, empty], axis=0)
            turned = compact.T
            for p in range(CHUNK // 2):
                two = jnp.concatenate(unswapped(turned[2 * p * wide:2 * (p + 1) * wide], wide), axis=0)
                for u in range(2):
                    total = two[u * wide:u * wide + cols]
                    for k in range(1, fold):
                        total = total + two[u * wide + k * cols:u * wide + (k + 1) * cols]
                    stage_s[pl.ds(n * CHUNK + 2 * p + u, cols, stride=FACTOR_WIDTH), :] = total
            return carry

        lax.fori_loop(0, outer_s.shape[0], some, 0, unroll=2)
        part_seqs, width = returned_ref.shape[1:]
        both_s[:, :, :width] = returned_ref[...]
        for b in range(cols * FACTOR_WIDTH // LANES):
            block = stage_s[b * LANES:(b + 1) * LANES, :].T[:seqs].astype(jnp.bfloat16)
            both_s[:, :, width + b * LANES:width + (b + 1) * LANES] = block.reshape(row_parts, part_seqs, LANES)
        for k, ref in enumerate(both_refs):
            ref[...] = both_s[place_ref[blocks] ^ k]
        for b in range(span // LANES):
            block = glacc_s[b * LANES:(b + 1) * LANES, :].T * scaling
            for k in range(fold):
                at = k * span + b * LANES
                gl_ref[:, at:at + LANES] = block[k * seqs:(k + 1) * seqs].astype(jnp.bfloat16)


def turn_kernel(pair_ref, cot_ref, shrink_ref, pair_out_ref, cot_out_ref, back_ref, *, wide):
    for source, target in ((pair_ref, pair_out_ref), (cot_ref, cot_out_ref)):
        rows = source[...].reshape(-1, PAIR_W)
        for at in range(0, rows.shape[0], 2 * wide):
            target[0, :, at:at + 2 * wide] = jnp.concatenate(swapped(rows[at:at + 2 * wide], wide), axis=0).T
    back_ref[0] = dot_nn(shrink_ref[...], cot_out_ref[0].astype(jnp.bfloat16)).astype(jnp.bfloat16)


def turned_pairs(pair_features, cotangent, shrink_weight):
    rows, cols, _ = pair_features.shape
    fold = MXU_SIDE // HALF
    count = rows // (UNIT * fold)
    pairs = UNIT * fold * cols
    hidden = shrink_weight.shape[0]
    results = (
        jax.ShapeDtypeStruct((count, PAIR_W, pairs), jnp.float32),
        jax.ShapeDtypeStruct((count, PAIR_W, pairs), jnp.float32),
        jax.ShapeDtypeStruct((count, hidden, pairs), jnp.bfloat16),
    )
    block = pl.BlockSpec((UNIT * fold, cols, PAIR_W), lambda n: (n, 0, 0))
    return pl.pallas_call(
        functools.partial(turn_kernel, wide=fold * cols),
        grid=(count,),
        out_shape=results,
        in_specs=[block, block, whole_block(shrink_weight.shape)],
        out_specs=[pl.BlockSpec((1,) + v.shape[1:], lambda n: (n, 0, 0)) for v in results],
        compiler_params=pltpu.CompilerParams(
            dimension_semantics=("arbitrary",), vmem_limit_bytes=24 * 1024 * 1024
        ),
        cost_estimate=pl.CostEstimate(
            flops=2 * 2 * count * pairs * hidden * PAIR_W, bytes_accessed=4 * 4 * pair_features.size, transcendentals=0
        ),
        name="turned_pairs",
    )(pair_features, cotangent, shrink_weight)


def pair_tile(place, lefts, matrices, turned, returned, shape, outer_bias, expand_weight):
    seqs = lefts[0].shape[-1] // 2
    rows, cols, _ = shape
    fold = MXU_SIDE // HALF
    groups = rows // fold
    unit = UNIT
    units = 2 if groups % (2 * unit) == 0 else 1
    steps = groups // unit // units
    wide = fold * cols
    span = groups * FACTOR_WIDTH
    channels = FACTOR_WIDTH * FACTOR_WIDTH
    block = pl.BlockSpec((unit * units * fold, cols, PAIR_W), lambda n, place: (n, 0, 0))
    resident = pl.BlockSpec(memory_space=pltpu.VMEM)
    operands = (
        *lefts, *matrices, *turned, returned, jnp.broadcast_to(outer_bias[:, None], (PAIR_W, LANES)), expand_weight,
    )
    results = (
        jax.ShapeDtypeStruct(shape, jnp.float32),
        jax.ShapeDtypeStruct((seqs, rows * FACTOR_WIDTH), jnp.bfloat16),
    ) + returned.shape[0] * (
        jax.ShapeDtypeStruct((returned.shape[1], returned.shape[2] + cols * FACTOR_WIDTH), jnp.bfloat16),
    )
    padded = groups * wide
    macs = 3 * FACTOR_WIDTH * span * fold * seqs * wide + padded * (2 * channels * MXU_SIDE + 8 * MXU_SIDE * MXU_SIDE)
    return pl.pallas_call(
        functools.partial(
            pair_kernel, seqs=seqs, cols=cols, fold=fold, unit=unit, units=units, blocks=len(lefts)
        ),
        grid_spec=pltpu.PrefetchScalarGridSpec(
            num_scalar_prefetch=1,
            grid=(steps,),
            in_specs=[resident] * len(operands),
            out_specs=[block] + [resident] * (len(results) - 1),
            scratch_shapes=[
                pltpu.VMEM((FACTOR_WIDTH // CHUNK, span, CHUNK * wide), jnp.bfloat16),
                pltpu.VMEM((span, fold * seqs), jnp.bfloat16),
                pltpu.VMEM((fold * seqs, span), jnp.bfloat16),
                pltpu.VMEM((cols * FACTOR_WIDTH, max(seqs, LANES)), jnp.float32),
                pltpu.VMEM((span, fold * seqs), jnp.float32),
                pltpu.VMEM((len(lefts),) + lefts[0].shape, jnp.bfloat16),
                pltpu.VMEM(returned.shape[:1] + results[2].shape, jnp.bfloat16),
            ],
        ),
        out_shape=results,
        compiler_params=pltpu.CompilerParams(
            dimension_semantics=("arbitrary",), vmem_limit_bytes=36 * 1024 * 1024
        ),
        cost_estimate=pl.CostEstimate(
            flops=2 * macs, bytes_accessed=rows * cols * PAIR_W * 4, transcendentals=0
        ),
        name="pair_tile",
    )(place, *operands)


def finish_kernel(place_ref, *refs, residues, fold):
    *both_refs, gl_ref, updated_ref, left_ref, right_ref, x_s = refs
    part_seqs, res_count, width = updated_ref.shape
    total = both_refs[0][:, residues * width:].astype(jnp.float32)
    for ref in both_refs[1:]:
        total = total + ref[:, residues * width:].astype(jnp.float32)
    right_ref[...] = total
    for k, ref in enumerate(both_refs):
        first = (place_ref[0] ^ k) * residues
        for r in range(residues):
            for n in range(width // LANES):
                at = r * width + n * LANES
                x_s[n, pl.ds(first + r, part_seqs, stride=res_count), :] = ref[:, at:at + LANES].astype(jnp.float32)
    for n in range(width // LANES):
        updated_ref[:, :, n * LANES:(n + 1) * LANES] = (
            x_s[n].reshape(part_seqs, res_count, LANES).astype(jnp.bfloat16)
        )
    total = gl_ref[0].astype(jnp.float32)
    for n in range(1, gl_ref.shape[0]):
        total = total + gl_ref[n].astype(jnp.float32)
    span = total.shape[1] // fold
    channel_block = lax.broadcasted_iota(jnp.int32, (1, LANES), 1) // FACTOR_WIDTH
    each = LANES // FACTOR_WIDTH
    for g in range(span // FACTOR_WIDTH):
        out = None
        for k in range(fold):
            at = k * span + g // each * LANES
            piece = total[:, at:at + LANES]
            shift = (k - g) % each * FACTOR_WIDTH
            piece = pltpu.roll(piece, shift, axis=1) if shift else piece
            out = piece if out is None else jnp.where(channel_block == k, piece, out)
        left_ref[:, g * LANES:(g + 1) * LANES] = out


def finish(place, both, gl, updated_shape):
    part_seqs, res_count, width = updated_shape
    residues = res_count // len(both)
    results = (
        jax.ShapeDtypeStruct(updated_shape, jnp.bfloat16),
        jax.ShapeDtypeStruct(gl.shape[1:], jnp.float32),
        jax.ShapeDtypeStruct((part_seqs, both[0].shape[1] - residues * width), jnp.float32),
    )
    resident = pl.BlockSpec(memory_space=pltpu.VMEM)
    return pl.pallas_call(
        functools.partial(finish_kernel, residues=residues, fold=MXU_SIDE // HALF),
        grid_spec=pltpu.PrefetchScalarGridSpec(
            num_scalar_prefetch=1,
            grid=(1,),
            in_specs=[resident] * (len(both) + 1),
            out_specs=[whole_block(v.shape) for v in results],
            scratch_shapes=[pltpu.VMEM((width // LANES, part_seqs * res_count, LANES), jnp.float32)],
        ),
        out_shape=results,
        compiler_params=pltpu.CompilerParams(
            dimension_semantics=("arbitrary",), vmem_limit_bytes=16 * 1024 * 1024
        ),
        name="finish",
    )(place, *both, gl)


def spread_out(q, count):
    return q if count % 2 else q % 2 * (count // 2) + q // 2


def local(
    alignment,
    pair_features,
    query_weight,
    key_weight,
    value_projection,
    gate_projection,
    gate_bias,
    output_projection,
    left_projection,
    right_projection,
    outer_weight,
    outer_bias,
    expand_weight,
    shrink_weight,
    cotangent,
):
    part_seqs, res_count, width = alignment.shape
    row_parts = lax.axis_size("row")
    col_parts = lax.axis_size("col")
    residues = res_count // row_parts
    turned = turned_pairs(pair_features, cotangent, shrink_weight)
    own = jnp.transpose(alignment, (1, 0, 2)).reshape(row_parts, residues, part_seqs, width)
    columns = lax.all_to_all(own, "row", split_axis=0, concat_axis=0, tiled=True)
    attended, factors = attend(
        columns, query_weight, key_weight, value_projection, gate_projection, gate_bias,
        output_projection, left_projection, right_projection,
    )

    factors = lax.all_to_all(factors, "row", split_axis=0, concat_axis=0, tiled=True)
    left = factors[:, 0]
    ratio = col_parts // row_parts
    lefts, place = [], []
    for m in range(ratio):
        moves = [
            (q * col_parts + ratio * r + b, r * col_parts + ratio * spread_out(q, row_parts) + (b + m) % ratio)
            for q in range(row_parts)
            for r in range(row_parts)
            for b in range(ratio)
        ]
        lefts.append(lax.ppermute(left, ("row", "col"), moves))
        place.append((lax.axis_index("col") + ratio - m) % ratio)
    row = lax.axis_index("row")
    matrices = right_matrices(factors, outer_weight, expand_weight, shrink_weight)
    pair_out, gl, *both = pair_tile(
        jnp.stack(place + [row]).astype(jnp.int32), lefts, matrices, turned, attended, pair_features.shape,
        outer_bias, expand_weight,
    )
    seqs, gl_width = gl.shape
    both = both[:1] + [
        lax.ppermute(v, "row", [(r, r ^ (k + 1)) for r in range(row_parts)]) for k, v in enumerate(both[1:])
    ]
    gl = lax.all_to_all(
        gl.reshape(col_parts, seqs // col_parts, gl_width), "col", split_axis=0, concat_axis=0, tiled=True
    )
    updated, grad_left, grad_right = finish(row.astype(jnp.int32).reshape(1), both, gl, alignment.shape)
    return (updated, pair_out, grad_left, grad_right)


def solution(mesh):
    return jax.shard_map(
        local,
        mesh=mesh,
        in_specs=(P("row", "col", None), P("row", "col", None)) + (P(),) * 12 + (P("row", "col", None),),
        out_specs=(P("row", "col", None), P("row", "col", None), P("col", "row"), P("row", "col")),
        check_vma=False,
    )
```

```python
import functools

import jax
import jax.numpy as jnp
from jax import lax
from jax.experimental import pallas as pl
from jax.experimental.pallas import tpu as pltpu
from jax.sharding import PartitionSpec as P

ATTENTION_HEADS = 8
HEAD_WIDTH = 32
FACTOR_WIDTH = 32
PAIR_W = 128
EPSILON = 1e-05

LANES = 128
MXU_SIDE = 256
HALF = 64
TILE = 32
CHUNK = 4
UNIT = 4


def dot_nn(a, b):
    return lax.dot_general(a, b, (((1,), (0,)), ((), ())), preferred_element_type=jnp.float32)


def dot_nt(a, b):
    return lax.dot_general(a, b, (((1,), (1,)), ((), ())), preferred_element_type=jnp.float32)


def layer_normalise(rows):
    rows = rows.astype(jnp.float32)
    average = jnp.mean(rows, axis=-1, keepdims=True)
    centred = rows - average
    variance = jnp.mean(centred * centred, axis=-1, keepdims=True)
    return centred * lax.rsqrt(variance + EPSILON)


def attend_kernel(
    x_ref, wq_ref, wk_ref, wv_ref, wg_ref, bias_ref, wo_ref, wl_ref, wr_ref,
    upd_ref, factor_ref, q_s, k_s, v_s, g_s, a_s, w_s, bias_s, project_s, upd_s, sems,
):
    parts, residues, part_seqs, width = x_ref.shape
    seqs = parts * part_seqs
    sources = (wq_ref, wk_ref, wv_ref, wg_ref, wo_ref, bias_ref, wl_ref, wr_ref)
    targets = [w_s.at[n] for n in range(5)] + [bias_s, project_s.at[0], project_s.at[1]]
    copies = [pltpu.make_async_copy(a, b, sems.at[n]) for n, (a, b) in enumerate(zip(sources, targets))]
    for copy in copies:
        copy.start()
    x = jnp.concatenate([x_ref[s, r] for r in range(residues) for s in range(parts)], axis=0)
    normed = layer_normalise(x).astype(jnp.bfloat16)
    for n, ref in enumerate((q_s, k_s, v_s)):
        copies[n].wait()
        ref[...] = dot_nn(normed, w_s[n]).astype(jnp.bfloat16)
    copies[3].wait()
    copies[5].wait()
    g_s[...] = jax.nn.sigmoid(dot_nn(normed, w_s[3]) + bias_s[...])

    head_of = lax.broadcasted_iota(jnp.int32, (1, width), 1) // HEAD_WIDTH
    masks = [(head_of == h).astype(jnp.float32) for h in range(ATTENTION_HEADS)]
    masks_low = [m.astype(jnp.bfloat16) for m in masks]

    def one_residue(r, carry):
        rows = pl.ds(pl.multiple_of(r * seqs, seqs), seqs)
        query = q_s[rows, :]
        spread_query = jnp.concatenate([query * m for m in masks_low], axis=0)
        scores = dot_nt(spread_query, k_s[rows, :]) * HEAD_WIDTH ** (-0.5)
        raised = jnp.exp(scores - jnp.max(scores, axis=-1, keepdims=True))
        inverse = 1.0 / jnp.sum(raised, axis=-1, keepdims=True)
        blended = dot_nn(raised.astype(jnp.bfloat16), v_s[rows, :]) * inverse
        total = blended[:seqs] * masks[0]
        for h in range(1, ATTENTION_HEADS):
            total = total + blended[h * seqs:(h + 1) * seqs] * masks[h]
        a_s[rows, :] = (g_s[rows, :] * total).astype(jnp.bfloat16)
        return carry

    lax.fori_loop(0, residues, one_residue, 0, unroll=4 if residues % 4 == 0 else 2)

    copies[4].wait()
    updated = (x.astype(jnp.float32) + dot_nn(a_s[...], w_s[4])).astype(jnp.bfloat16)
    for r in range(residues):
        for s in range(parts):
            begin = r * seqs + s * part_seqs
            upd_s[s, :, r * width:(r + 1) * width] = updated[begin:begin + part_seqs]
    leaving = pltpu.make_async_copy(upd_s, upd_ref, sems.at[len(sources)])
    leaving.start()
    factor_norm = layer_normalise(updated).astype(jnp.bfloat16)
    copies[6].wait()
    copies[7].wait()
    project = project_s[...].reshape(2 * FACTOR_WIDTH, width)
    for p in range(residues // 2):
        both = dot_nt(project, factor_norm[p * 2 * seqs:(p + 1) * 2 * seqs]).astype(jnp.bfloat16)
        for n in range(parts):
            factor_ref[n, 0, p] = both[:FACTOR_WIDTH]
            factor_ref[n, 1, p] = both[FACTOR_WIDTH:]
    leaving.wait()


def whole_block(shape):
    return pl.BlockSpec(shape, lambda *_: (0,) * len(shape))


def in_hbm(*arrays):
    return [pltpu.with_memory_space_constraint(v, pltpu.HBM) for v in arrays]


def attend(x, wq, wk, wv, wg, gate_bias, wo, wl, wr):
    parts, residues, part_seqs, width = x.shape
    seqs = parts * part_seqs
    rows = residues * seqs
    operands = in_hbm(wq, wk, wv, wg, gate_bias.reshape(1, -1), wo, wl.T, wr.T)
    resident = pl.BlockSpec(memory_space=pltpu.VMEM)
    results = (
        pltpu.HBM((parts, part_seqs, residues * width), jnp.bfloat16),
        jax.ShapeDtypeStruct((parts, 2, residues // 2, FACTOR_WIDTH, 2 * seqs), jnp.bfloat16),
    )
    macs = rows * width * (5 * width + 2 * FACTOR_WIDTH) + 2 * rows * ATTENTION_HEADS * width * seqs
    return pl.pallas_call(
        attend_kernel,
        out_shape=results,
        in_specs=[resident] + [pl.BlockSpec(memory_space=pltpu.HBM)] * len(operands),
        out_specs=[pl.BlockSpec(memory_space=pltpu.HBM), resident],
        scratch_shapes=[
            pltpu.VMEM((rows, width), jnp.bfloat16),
            pltpu.VMEM((rows, width), jnp.bfloat16),
            pltpu.VMEM((rows, width), jnp.bfloat16),
            pltpu.VMEM((rows, width), jnp.float32),
            pltpu.VMEM((rows, width), jnp.bfloat16),
            pltpu.VMEM((5,) + wq.shape, jnp.bfloat16),
            pltpu.VMEM((1, width), jnp.float32),
            pltpu.VMEM((2, FACTOR_WIDTH, width), jnp.bfloat16),
            pltpu.VMEM(results[0].shape, jnp.bfloat16),
            pltpu.SemaphoreType.DMA((len(operands) + 1,)),
        ],
        compiler_params=pltpu.CompilerParams(vmem_limit_bytes=32 * 1024 * 1024),
        cost_estimate=pl.CostEstimate(flops=2 * macs, bytes_accessed=4 * x.size * 2, transcendentals=rows * width),
        name="column_attention",
    )(x, *operands)


def first_of_four(at, cols):
    wide = MXU_SIDE // HALF * cols
    inside = jnp.where(at < wide, at, jnp.where(at < wide + HALF, at - HALF, at - wide - HALF))
    return inside // cols


def swapped(pair, wide):
    return [pair[:wide], pair[2 * wide - HALF:], pair[wide:2 * wide - HALF]]


def unswapped(pair, wide):
    return [pair[:wide], pair[wide + HALF:], pair[wide:wide + HALF]]


def right_kernel(
    factor_ref, w_ref, expand_ref, shrink_ref, rbd_ref, rbdt_ref, wec_ref, wt_ref, et_ref, st_ref, stage_s,
    *, seqs, cols, fold,
):
    each = factor_ref.shape[2]
    wide = fold * cols
    stage_lanes = stage_s.shape[1]
    low_half = lax.broadcasted_iota(jnp.int32, (1, LANES), 1) < HALF

    stage_s[:FACTOR_WIDTH * FACTOR_WIDTH, :LANES] = w_ref[...].astype(jnp.float32)
    for e in range(FACTOR_WIDTH):
        piece = stage_s[pl.ds(e, FACTOR_WIDTH, stride=FACTOR_WIDTH), :LANES]
        wec_ref[e * FACTOR_WIDTH:(e + 1) * FACTOR_WIDTH, :] = piece.astype(jnp.bfloat16)
    for b in range(FACTOR_WIDTH * FACTOR_WIDTH // LANES):
        block = wec_ref[b * LANES:(b + 1) * LANES, :].astype(jnp.float32)
        wt_ref[:, b * LANES:(b + 1) * LANES] = block.T.astype(jnp.bfloat16)
    et_ref[...] = expand_ref[...].astype(jnp.float32).T.astype(jnp.bfloat16)
    st_ref[...] = shrink_ref[...].astype(jnp.float32).T.astype(jnp.bfloat16)

    for p in range(cols // 2):
        block = factor_ref[p // each, 1, p % each].astype(jnp.float32)
        even = 2 * p * FACTOR_WIDTH
        odd = even + FACTOR_WIDTH
        if seqs % LANES == 0:
            stage_s[even:even + FACTOR_WIDTH, :] = block[:, :seqs]
            stage_s[odd:odd + FACTOR_WIDTH, :] = block[:, seqs:]
        else:
            stage_s[even:even + FACTOR_WIDTH, :] = block
            stage_s[odd:odd + FACTOR_WIDTH, :] = pltpu.roll(block, HALF, axis=1)

    row_k = first_of_four(lax.broadcasted_iota(jnp.int32, (2 * wide, 1), 0), cols)
    lane_k = first_of_four(lax.broadcasted_iota(jnp.int32, (1, 2 * wide), 1), cols)
    for e in range(0, FACTOR_WIDTH, 2):
        two = []
        for u in (e, e + 1):
            two += [stage_s[pl.ds(u, cols, stride=FACTOR_WIDTH), :]] * fold
        upright = jnp.concatenate(swapped(jnp.concatenate(two, axis=0), wide), axis=0)
        chunk, at = e // CHUNK, e % CHUNK * wide
        rolled = pltpu.roll(upright, HALF, axis=1) if seqs < LANES else None
        for v in range(fold * seqs // stage_lanes):
            if seqs < LANES:
                value = jnp.where(
                    low_half, jnp.where(row_k == 2 * v, upright, 0.0), jnp.where(row_k == 2 * v + 1, rolled, 0.0)
                )
            else:
                value = jnp.where(row_k == v, upright, 0.0)
            rbdt_ref[chunk, at:at + 2 * wide, v * stage_lanes:(v + 1) * stage_lanes] = value.astype(jnp.bfloat16)
        turned = upright.T[:seqs]
        for k in range(fold):
            value = jnp.where(lane_k == k, turned, 0.0).astype(jnp.bfloat16)
            rbd_ref[chunk, k * seqs:(k + 1) * seqs, at:at + 2 * wide] = value


def right_matrices(factors, outer_weight, expand_weight, shrink_weight):
    row_parts, _, each, _, lanes = factors.shape
    seqs, cols = lanes // 2, 2 * each * row_parts
    fold = MXU_SIDE // HALF
    channels, width = outer_weight.shape
    results = (
        jax.ShapeDtypeStruct((FACTOR_WIDTH // CHUNK, fold * seqs, CHUNK * fold * cols), jnp.bfloat16),
        jax.ShapeDtypeStruct((FACTOR_WIDTH // CHUNK, CHUNK * fold * cols, fold * seqs), jnp.bfloat16),
        jax.ShapeDtypeStruct((channels, width), jnp.bfloat16),
        jax.ShapeDtypeStruct((width, channels), jnp.bfloat16),
        jax.ShapeDtypeStruct(expand_weight.shape[::-1], jnp.bfloat16),
        jax.ShapeDtypeStruct(shrink_weight.shape[::-1], jnp.bfloat16),
    )
    resident = pl.BlockSpec(memory_space=pltpu.VMEM)
    return pl.pallas_call(
        functools.partial(right_kernel, seqs=seqs, cols=cols, fold=fold),
        out_shape=results,
        in_specs=[resident] * 4,
        out_specs=[resident] * len(results),
        scratch_shapes=[pltpu.VMEM((max(cols * FACTOR_WIDTH, channels), max(seqs, LANES)), jnp.float32)],
        compiler_params=pltpu.CompilerParams(vmem_limit_bytes=16 * 1024 * 1024),
        cost_estimate=pl.CostEstimate(flops=6 * 10**9, bytes_accessed=4 * results[0].size, transcendentals=0),
        name="right_matrices",
    )(factors, outer_weight, expand_weight, shrink_weight)


def pair_kernel(
    place_ref, *refs, seqs, cols, fold, unit, units, blocks,
):
    left_refs, refs = refs[:blocks], refs[blocks:]
    rbd_s, rbdt_s, wec_s, wt_s, et_ref, st_ref, pair_ref, cot_ref, back_ref = refs[:9]
    returned_ref, bias_ref, expand_ref, out_ref, gl_ref = refs[9:14]
    both_refs, (outer_s, l_s, lt_s, stage_s, glacc_s, lblk_s, both_s) = refs[14:-7], refs[-7:]
    step = pl.program_id(0)
    row_parts, each = left_refs[0].shape[:2]
    span = l_s.shape[0]
    groups = span // FACTOR_WIDTH
    wide = fold * cols
    scaling = 1.0 / seqs
    low_half = lax.broadcasted_iota(jnp.int32, (1, LANES), 1) < HALF

    @pl.when(step == 0)
    def _prologue():
        for n, ref in enumerate(left_refs):
            lblk_s[place_ref[n]] = ref[...]
        pairs = fold // 2
        for p in range(groups * pairs):
            column, inside = divmod(p, row_parts * each)
            block = lblk_s[column, inside // each, inside % each]
            g, at = p // pairs, p % pairs * 2 * seqs
            l_s[g * FACTOR_WIDTH:(g + 1) * FACTOR_WIDTH, at:at + 2 * seqs] = (
                block.astype(jnp.float32) * scaling
            ).astype(jnp.bfloat16)
        for b in range(span // LANES):
            block = l_s[b * LANES:(b + 1) * LANES, :].astype(jnp.float32)
            lt_s[:, b * LANES:(b + 1) * LANES] = block.T.astype(jnp.bfloat16)

        def some_outers(n, carry):
            outer_s[n] = dot_nn(l_s[...], rbd_s[n]).astype(jnp.bfloat16)
            return carry

        lax.fori_loop(0, outer_s.shape[0], some_outers, 0, unroll=2)

    def unit_rows(u):
        at = (step * units + u) * unit * FACTOR_WIDTH
        return pl.ds(pl.multiple_of(at, unit * FACTOR_WIDTH), unit * FACTOR_WIDTH)

    def group(block, g):
        return block[g * FACTOR_WIDTH:(g + 1) * FACTOR_WIDTH]

    def forward(u):
        stacked = []
        for e in range(0, FACTOR_WIDTH, 2):
            at = e % CHUNK * wide
            block = outer_s[e // CHUNK, unit_rows(u), at:at + 2 * wide]
            shared = block[:, LANES:2 * LANES]
            rolled = pltpu.roll(shared, HALF, axis=1)
            even, odd = [], []
            for g in range(0, unit, 2):
                a, b = block[:, :LANES], block[:, 2 * LANES:]
                even += [group(a, g), jnp.where(low_half, group(shared, g), group(rolled, g + 1)), group(a, g + 1)]
                odd += [group(b, g), jnp.where(low_half, group(rolled, g), group(shared, g + 1)), group(b, g + 1)]
            stacked += [jnp.concatenate(even, axis=1), jnp.concatenate(odd, axis=1)]
        projected = dot_nn(wt_s[...], jnp.concatenate(stacked, axis=0))
        middles, inverses, spreads = [], [], []
        for at in range(0, projected.shape[1], LANES):
            middle = pair_ref[step * units + u, :, at:at + LANES] + projected[:, at:at + LANES] + bias_ref[...]
            average = jnp.mean(middle, axis=0, keepdims=True)
            centred = middle - average
            variance = jnp.mean(centred * centred, axis=0, keepdims=True)
            inverse = lax.rsqrt(variance + EPSILON)
            middles.append(middle)
            inverses.append(inverse)
            spreads.append(centred * inverse)
        spread_low = jnp.concatenate([v.astype(jnp.bfloat16) for v in spreads], axis=1)
        return middles, inverses, spreads, dot_nn(et_ref[...], spread_low)

    def backward(u, middles, inverses, spreads, before):
        rows, pairs = before.shape
        hidden, back_before = [], []
        for at in range(0, rows, TILE):
            hidden_parts, back_parts = [], []
            for v in range(0, pairs, MXU_SIDE):
                x = before[at:at + TILE, v:v + MXU_SIDE]
                back = back_ref[step * units + u, at:at + TILE, v:v + MXU_SIDE].astype(jnp.float32)
                phi = 0.5 * (1.0 + lax.erf(x * 0.7071067811865476))
                slope = phi + x * jnp.exp(-0.5 * x * x) * 0.3989422804014327
                hidden_parts.append((x * phi).astype(jnp.bfloat16))
                back_parts.append((back * slope).astype(jnp.bfloat16))
            hidden.append(jnp.concatenate(hidden_parts, axis=1))
            back_before.append(jnp.concatenate(back_parts, axis=1))
        back_spread = dot_nn(expand_ref[...], jnp.concatenate(back_before, axis=0))
        change = dot_nn(st_ref[...], jnp.concatenate(hidden, axis=0))
        back_middle = []
        for n, at in enumerate(range(0, pairs, LANES)):
            back, spread = back_spread[:, at:at + LANES], spreads[n]
            centre_term = jnp.mean(back, axis=0, keepdims=True)
            slope_term = jnp.mean(back * spread, axis=0, keepdims=True)
            back = back - centre_term - spread * slope_term
            back = cot_ref[step * units + u, :, at:at + LANES] + inverses[n] * back
            back_middle.append(back.astype(jnp.bfloat16))
        result = (jnp.concatenate(middles, axis=1) + change).T
        pieces = []
        for g in range(0, unit, 2):
            pieces += unswapped(result[g * wide:(g + 2) * wide], wide)
        out_ref[u * unit * fold:(u + 1) * unit * fold] = jnp.concatenate(pieces, axis=0).reshape(
            unit * fold, cols, PAIR_W
        )
        back_outer = dot_nn(wec_s[...], jnp.concatenate(back_middle, axis=1)).astype(jnp.bfloat16)
        for e in range(0, FACTOR_WIDTH, 2):
            even, odd = group(back_outer, e), group(back_outer, e + 1)
            a, shared, b = [], [], []
            for g in range(0, unit, 2):
                at = g * wide
                of_even, of_odd = even[:, at + LANES:at + 2 * LANES], odd[:, at + LANES:at + 2 * LANES]
                a += [even[:, at:at + LANES], even[:, at + 2 * LANES:at + 3 * LANES]]
                b += [odd[:, at:at + LANES], odd[:, at + 2 * LANES:at + 3 * LANES]]
                shared += [
                    jnp.where(low_half, of_even, pltpu.roll(of_odd, HALF, axis=1)),
                    jnp.where(low_half, pltpu.roll(of_even, HALF, axis=1), of_odd),
                ]
            for n, pieces in enumerate((a, shared, b)):
                at = e % CHUNK * wide + n * LANES
                outer_s[e // CHUNK, unit_rows(u), at:at + LANES] = jnp.concatenate(pieces, axis=0)

    held = forward(0)
    for u in range(units):
        ahead = forward(u + 1) if u + 1 < units else None
        backward(u, *held)
        held = ahead

    @pl.when(step == pl.num_programs(0) - 1)
    def _epilogue():
        glacc_s[...] = jnp.zeros_like(glacc_s)
        empty = jnp.zeros((LANES - seqs % LANES, CHUNK * wide), jnp.float32) if seqs % LANES else None
        at = lax.broadcasted_iota(jnp.int32, (1, CHUNK * wide), 1)
        lane_k = first_of_four(lax.rem(at, 2 * wide), cols)

        def some(n, carry):
            back = outer_s[n]
            glacc_s[...] += dot_nn(back, rbdt_s[n])
            full = dot_nn(lt_s[...], back)
            compact = full[:seqs]
            for k in range(1, fold):
                compact = jnp.where(lane_k == k, full[k * seqs:(k + 1) * seqs], compact)
            if empty is not None:
                compact = jnp.concatenate([compact, empty], axis=0)
            turned = compact.T
            for p in range(CHUNK // 2):
                two = jnp.concatenate(unswapped(turned[2 * p * wide:2 * (p + 1) * wide], wide), axis=0)
                for u in range(2):
                    total = two[u * wide:u * wide + cols]
                    for k in range(1, fold):
                        total = total + two[u * wide + k * cols:u * wide + (k + 1) * cols]
                    stage_s[pl.ds(n * CHUNK + 2 * p + u, cols, stride=FACTOR_WIDTH), :] = total
            return carry

        lax.fori_loop(0, outer_s.shape[0], some, 0, unroll=2)
        part_seqs, width = returned_ref.shape[1:]
        both_s[:, :, :width] = returned_ref[...]
        for b in range(cols * FACTOR_WIDTH // LANES):
            block = stage_s[b * LANES:(b + 1) * LANES, :].T[:seqs].astype(jnp.bfloat16)
            both_s[:, :, width + b * LANES:width + (b + 1) * LANES] = block.reshape(row_parts, part_seqs, LANES)
        for k, ref in enumerate(both_refs):
            ref[...] = both_s[place_ref[blocks] ^ k]
        for b in range(span // LANES):
            block = glacc_s[b * LANES:(b + 1) * LANES, :].T * scaling
            for k in range(fold):
                at = k * span + b * LANES
                gl_ref[:, at:at + LANES] = block[k * seqs:(k + 1) * seqs].astype(jnp.bfloat16)


def turn_kernel(pair_ref, cot_ref, shrink_ref, pair_out_ref, cot_out_ref, back_ref, *, wide):
    for source, target in ((pair_ref, pair_out_ref), (cot_ref, cot_out_ref)):
        rows = source[...].reshape(-1, PAIR_W)
        for at in range(0, rows.shape[0], 2 * wide):
            target[0, :, at:at + 2 * wide] = jnp.concatenate(swapped(rows[at:at + 2 * wide], wide), axis=0).T
    back_ref[0] = dot_nn(shrink_ref[...], cot_out_ref[0].astype(jnp.bfloat16)).astype(jnp.bfloat16)


def turned_pairs(pair_features, cotangent, shrink_weight):
    rows, cols, _ = pair_features.shape
    fold = MXU_SIDE // HALF
    count = rows // (UNIT * fold)
    pairs = UNIT * fold * cols
    hidden = shrink_weight.shape[0]
    results = (
        pltpu.HBM((count, PAIR_W, pairs), jnp.float32),
        pltpu.HBM((count, PAIR_W, pairs), jnp.float32),
        pltpu.HBM((count, hidden, pairs), jnp.bfloat16),
    )
    block = pl.BlockSpec((UNIT * fold, cols, PAIR_W), lambda n: (n, 0, 0))
    return pl.pallas_call(
        functools.partial(turn_kernel, wide=fold * cols),
        grid=(count,),
        out_shape=results,
        in_specs=[block, block, whole_block(shrink_weight.shape)],
        out_specs=[pl.BlockSpec((1,) + v.shape[1:], lambda n: (n, 0, 0)) for v in results],
        compiler_params=pltpu.CompilerParams(
            dimension_semantics=("arbitrary",), vmem_limit_bytes=24 * 1024 * 1024
        ),
        cost_estimate=pl.CostEstimate(
            flops=2 * 2 * count * pairs * hidden * PAIR_W, bytes_accessed=4 * 4 * pair_features.size, transcendentals=0
        ),
        name="turned_pairs",
    )(*in_hbm(pair_features, cotangent, shrink_weight))


def pair_tile(place, lefts, matrices, turned, returned, shape, outer_bias, expand_weight):
    seqs = lefts[0].shape[-1] // 2
    rows, cols, _ = shape
    fold = MXU_SIDE // HALF
    groups = rows // fold
    unit = UNIT
    units = 2 if groups % (2 * unit) == 0 else 1
    steps = groups // unit // units
    wide = fold * cols
    span = groups * FACTOR_WIDTH
    channels = FACTOR_WIDTH * FACTOR_WIDTH
    block = pl.BlockSpec((unit * units * fold, cols, PAIR_W), lambda n, place: (n, 0, 0))
    resident = pl.BlockSpec(memory_space=pltpu.VMEM)
    operands = (
        *lefts, *matrices, *turned, returned, jnp.broadcast_to(outer_bias[:, None], (PAIR_W, LANES)), expand_weight,
    )
    results = (
        jax.ShapeDtypeStruct(shape, jnp.float32),
        jax.ShapeDtypeStruct((seqs, rows * FACTOR_WIDTH), jnp.bfloat16),
    ) + returned.shape[0] * (
        jax.ShapeDtypeStruct((returned.shape[1], returned.shape[2] + cols * FACTOR_WIDTH), jnp.bfloat16),
    )
    padded = groups * wide
    macs = 3 * FACTOR_WIDTH * span * fold * seqs * wide + padded * (2 * channels * MXU_SIDE + 8 * MXU_SIDE * MXU_SIDE)
    return pl.pallas_call(
        functools.partial(
            pair_kernel, seqs=seqs, cols=cols, fold=fold, unit=unit, units=units, blocks=len(lefts)
        ),
        grid_spec=pltpu.PrefetchScalarGridSpec(
            num_scalar_prefetch=1,
            grid=(steps,),
            in_specs=[resident] * len(operands),
            out_specs=[block] + [resident] * (len(results) - 1),
            scratch_shapes=[
                pltpu.VMEM((FACTOR_WIDTH // CHUNK, span, CHUNK * wide), jnp.bfloat16),
                pltpu.VMEM((span, fold * seqs), jnp.bfloat16),
                pltpu.VMEM((fold * seqs, span), jnp.bfloat16),
                pltpu.VMEM((cols * FACTOR_WIDTH, max(seqs, LANES)), jnp.float32),
                pltpu.VMEM((span, fold * seqs), jnp.float32),
                pltpu.VMEM((len(lefts),) + lefts[0].shape, jnp.bfloat16),
                pltpu.VMEM(returned.shape[:1] + results[2].shape, jnp.bfloat16),
            ],
        ),
        out_shape=results,
        compiler_params=pltpu.CompilerParams(
            dimension_semantics=("arbitrary",), vmem_limit_bytes=36 * 1024 * 1024
        ),
        cost_estimate=pl.CostEstimate(
            flops=2 * macs, bytes_accessed=rows * cols * PAIR_W * 4, transcendentals=0
        ),
        name="pair_tile",
    )(place, *operands)


def finish_kernel(place_ref, *refs, residues, fold):
    *both_refs, gl_ref, updated_ref, left_ref, right_ref, x_s = refs
    part_seqs, res_count, width = updated_ref.shape
    total = both_refs[0][:, residues * width:].astype(jnp.float32)
    for ref in both_refs[1:]:
        total = total + ref[:, residues * width:].astype(jnp.float32)
    right_ref[...] = total
    for k, ref in enumerate(both_refs):
        first = (place_ref[0] ^ k) * residues
        for r in range(residues):
            for n in range(width // LANES):
                at = r * width + n * LANES
                x_s[n, pl.ds(first + r, part_seqs, stride=res_count), :] = ref[:, at:at + LANES].astype(jnp.float32)
    for n in range(width // LANES):
        updated_ref[:, :, n * LANES:(n + 1) * LANES] = (
            x_s[n].reshape(part_seqs, res_count, LANES).astype(jnp.bfloat16)
        )
    total = gl_ref[0].astype(jnp.float32)
    for n in range(1, gl_ref.shape[0]):
        total = total + gl_ref[n].astype(jnp.float32)
    span = total.shape[1] // fold
    channel_block = lax.broadcasted_iota(jnp.int32, (1, LANES), 1) // FACTOR_WIDTH
    each = LANES // FACTOR_WIDTH
    for g in range(span // FACTOR_WIDTH):
        out = None
        for k in range(fold):
            at = k * span + g // each * LANES
            piece = total[:, at:at + LANES]
            shift = (k - g) % each * FACTOR_WIDTH
            piece = pltpu.roll(piece, shift, axis=1) if shift else piece
            out = piece if out is None else jnp.where(channel_block == k, piece, out)
        left_ref[:, g * LANES:(g + 1) * LANES] = out


def finish(place, both, gl, updated_shape):
    part_seqs, res_count, width = updated_shape
    residues = res_count // len(both)
    results = (
        jax.ShapeDtypeStruct(updated_shape, jnp.bfloat16),
        jax.ShapeDtypeStruct(gl.shape[1:], jnp.float32),
        jax.ShapeDtypeStruct((part_seqs, both[0].shape[1] - residues * width), jnp.float32),
    )
    resident = pl.BlockSpec(memory_space=pltpu.VMEM)
    return pl.pallas_call(
        functools.partial(finish_kernel, residues=residues, fold=MXU_SIDE // HALF),
        grid_spec=pltpu.PrefetchScalarGridSpec(
            num_scalar_prefetch=1,
            grid=(1,),
            in_specs=[resident] * (len(both) + 1),
            out_specs=[whole_block(v.shape) for v in results],
            scratch_shapes=[pltpu.VMEM((width // LANES, part_seqs * res_count, LANES), jnp.float32)],
        ),
        out_shape=results,
        compiler_params=pltpu.CompilerParams(
            dimension_semantics=("arbitrary",), vmem_limit_bytes=16 * 1024 * 1024
        ),
        name="finish",
    )(place, *both, gl)


def spread_out(q, count):
    return q if count % 2 else q % 2 * (count // 2) + q // 2


def local(
    alignment,
    pair_features,
    query_weight,
    key_weight,
    value_projection,
    gate_projection,
    gate_bias,
    output_projection,
    left_projection,
    right_projection,
    outer_weight,
    outer_bias,
    expand_weight,
    shrink_weight,
    cotangent,
):
    part_seqs, res_count, width = alignment.shape
    row_parts = lax.axis_size("row")
    col_parts = lax.axis_size("col")
    residues = res_count // row_parts
    turned = turned_pairs(pair_features, cotangent, shrink_weight)
    own = jnp.transpose(alignment, (1, 0, 2)).reshape(row_parts, residues, part_seqs, width)
    columns = lax.all_to_all(own, "row", split_axis=0, concat_axis=0, tiled=True)
    attended, factors = attend(
        columns, query_weight, key_weight, value_projection, gate_projection, gate_bias,
        output_projection, left_projection, right_projection,
    )

    factors = lax.all_to_all(factors, "row", split_axis=0, concat_axis=0, tiled=True)
    left = factors[:, 0]
    ratio = col_parts // row_parts
    lefts, place = [], []
    for m in range(ratio):
        moves = [
            (q * col_parts + ratio * r + b, r * col_parts + ratio * spread_out(q, row_parts) + (b + m) % ratio)
            for q in range(row_parts)
            for r in range(row_parts)
            for b in range(ratio)
        ]
        lefts.append(lax.ppermute(left, ("row", "col"), moves))
        place.append((lax.axis_index("col") + ratio - m) % ratio)
    row = lax.axis_index("row")
    matrices = right_matrices(factors, outer_weight, expand_weight, shrink_weight)
    pair_out, gl, *both = pair_tile(
        jnp.stack(place + [row]).astype(jnp.int32), lefts, matrices, turned, attended, pair_features.shape,
        outer_bias, expand_weight,
    )
    seqs, gl_width = gl.shape
    both = both[:1] + [
        lax.ppermute(v, "row", [(r, r ^ (k + 1)) for r in range(row_parts)]) for k, v in enumerate(both[1:])
    ]
    gl = lax.all_to_all(
        gl.reshape(col_parts, seqs // col_parts, gl_width), "col", split_axis=0, concat_axis=0, tiled=True
    )
    updated, grad_left, grad_right = finish(row.astype(jnp.int32).reshape(1), both, gl, alignment.shape)
    return (updated, pair_out, grad_left, grad_right)


def solution(mesh):
    return jax.shard_map(
        local,
        mesh=mesh,
        in_specs=(P("row", "col", None), P("row", "col", None)) + (P(),) * 12 + (P("row", "col", None),),
        out_specs=(P("row", "col", None), P("row", "col", None), P("col", "row"), P("row", "col")),
        check_vma=False,
    )
```

```python
import functools

import jax
import jax.numpy as jnp
from jax import lax
from jax.experimental import pallas as pl
from jax.experimental.pallas import tpu as pltpu
from jax.sharding import PartitionSpec as P

ATTENTION_HEADS = 8
HEAD_WIDTH = 32
FACTOR_WIDTH = 32
PAIR_W = 128
EPSILON = 1e-05

LANES = 128
MXU_SIDE = 256
HALF = 64
TILE = 32
CHUNK = 4
UNIT = 4


def dot_nn(a, b):
    return lax.dot_general(a, b, (((1,), (0,)), ((), ())), preferred_element_type=jnp.float32)


def dot_nt(a, b):
    return lax.dot_general(a, b, (((1,), (1,)), ((), ())), preferred_element_type=jnp.float32)


def layer_normalise(rows):
    rows = rows.astype(jnp.float32)
    average = jnp.mean(rows, axis=-1, keepdims=True)
    centred = rows - average
    variance = jnp.mean(centred * centred, axis=-1, keepdims=True)
    return centred * lax.rsqrt(variance + EPSILON)


def attend_kernel(
    x_ref, wq_ref, wk_ref, wv_ref, wg_ref, bias_ref, wo_ref, wl_ref, wr_ref,
    upd_ref, factor_ref, q_s, k_s, v_s, g_s, a_s, w_s, bias_s, project_s, upd_s, sems,
):
    parts, residues, part_seqs, width = x_ref.shape
    seqs = parts * part_seqs
    sources = (wq_ref, wk_ref, wv_ref, wg_ref, wo_ref, bias_ref, wl_ref, wr_ref)
    targets = [w_s.at[n] for n in range(5)] + [bias_s, project_s.at[0], project_s.at[1]]
    copies = [pltpu.make_async_copy(a, b, sems.at[n]) for n, (a, b) in enumerate(zip(sources, targets))]
    for copy in copies:
        copy.start()
    x = jnp.concatenate([x_ref[s, r] for r in range(residues) for s in range(parts)], axis=0)
    normed = layer_normalise(x).astype(jnp.bfloat16)
    for n, ref in enumerate((q_s, k_s, v_s)):
        copies[n].wait()
        ref[...] = dot_nn(normed, w_s[n]).astype(jnp.bfloat16)
    copies[3].wait()
    copies[5].wait()
    g_s[...] = jax.nn.sigmoid(dot_nn(normed, w_s[3]) + bias_s[...])

    head_of = lax.broadcasted_iota(jnp.int32, (1, width), 1) // HEAD_WIDTH
    masks = [(head_of == h).astype(jnp.bfloat16) for h in range(ATTENTION_HEADS)]
    together = max(1, LANES // seqs)
    lane_head = lax.broadcasted_iota(jnp.int32, (1, together * seqs), 1) // seqs

    def one_residue(r, carry):
        rows = pl.ds(pl.multiple_of(r * seqs, seqs), seqs)
        key, value = k_s[rows, :], v_s[rows, :]
        keys = jnp.concatenate([key * m for m in masks], axis=0)
        values = jnp.concatenate([value * m for m in masks], axis=0)
        scores = dot_nt(q_s[rows, :], keys) * HEAD_WIDTH ** (-0.5)
        weights, inverse = [], jnp.zeros((seqs, width), jnp.float32)
        for h in range(0, ATTENTION_HEADS, together):
            part = scores[:, h * seqs:(h + together) * seqs]
            highest = jnp.zeros_like(part)
            for n in range(together):
                own = jnp.where(lane_head == n, part, -jnp.inf)
                highest = jnp.where(lane_head == n, jnp.max(own, axis=-1, keepdims=True), highest)
            raised = jnp.exp(part - highest)
            for n in range(together):
                total = jnp.sum(jnp.where(lane_head == n, raised, 0.0), axis=-1, keepdims=True)
                inverse = jnp.where(head_of == h + n, 1.0 / total, inverse)
            weights.append(raised.astype(jnp.bfloat16))
        blended = dot_nn(jnp.concatenate(weights, axis=1), values) * inverse
        a_s[rows, :] = (g_s[rows, :] * blended).astype(jnp.bfloat16)
        return carry

    lax.fori_loop(0, residues, one_residue, 0, unroll=4 if residues % 4 == 0 else 2)

    copies[4].wait()
    updated = (x.astype(jnp.float32) + dot_nn(a_s[...], w_s[4])).astype(jnp.bfloat16)
    for r in range(residues):
        for s in range(parts):
            begin = r * seqs + s * part_seqs
            upd_s[s, :, r * width:(r + 1) * width] = updated[begin:begin + part_seqs]
    leaving = pltpu.make_async_copy(upd_s, upd_ref, sems.at[len(sources)])
    leaving.start()
    factor_norm = layer_normalise(updated).astype(jnp.bfloat16)
    copies[6].wait()
    copies[7].wait()
    project = project_s[...].reshape(2 * FACTOR_WIDTH, width)
    for p in range(residues // 2):
        both = dot_nt(project, factor_norm[p * 2 * seqs:(p + 1) * 2 * seqs]).astype(jnp.bfloat16)
        for n in range(parts):
            factor_ref[n, 0, p] = both[:FACTOR_WIDTH]
            factor_ref[n, 1, p] = both[FACTOR_WIDTH:]
    leaving.wait()


def whole_block(shape):
    return pl.BlockSpec(shape, lambda *_: (0,) * len(shape))


def in_hbm(*arrays):
    return [pltpu.with_memory_space_constraint(v, pltpu.HBM) for v in arrays]


def attend(x, wq, wk, wv, wg, gate_bias, wo, wl, wr):
    parts, residues, part_seqs, width = x.shape
    seqs = parts * part_seqs
    rows = residues * seqs
    operands = in_hbm(wq, wk, wv, wg, gate_bias.reshape(1, -1), wo, wl.T, wr.T)
    resident = pl.BlockSpec(memory_space=pltpu.VMEM)
    results = (
        pltpu.HBM((parts, part_seqs, residues * width), jnp.bfloat16),
        jax.ShapeDtypeStruct((parts, 2, residues // 2, FACTOR_WIDTH, 2 * seqs), jnp.bfloat16),
    )
    macs = rows * width * (5 * width + 2 * FACTOR_WIDTH) + 2 * rows * ATTENTION_HEADS * width * seqs
    return pl.pallas_call(
        attend_kernel,
        out_shape=results,
        in_specs=[resident] + [pl.BlockSpec(memory_space=pltpu.HBM)] * len(operands),
        out_specs=[pl.BlockSpec(memory_space=pltpu.HBM), resident],
        scratch_shapes=[
            pltpu.VMEM((rows, width), jnp.bfloat16),
            pltpu.VMEM((rows, width), jnp.bfloat16),
            pltpu.VMEM((rows, width), jnp.bfloat16),
            pltpu.VMEM((rows, width), jnp.float32),
            pltpu.VMEM((rows, width), jnp.bfloat16),
            pltpu.VMEM((5,) + wq.shape, jnp.bfloat16),
            pltpu.VMEM((1, width), jnp.float32),
            pltpu.VMEM((2, FACTOR_WIDTH, width), jnp.bfloat16),
            pltpu.VMEM(results[0].shape, jnp.bfloat16),
            pltpu.SemaphoreType.DMA((len(operands) + 1,)),
        ],
        compiler_params=pltpu.CompilerParams(vmem_limit_bytes=32 * 1024 * 1024),
        cost_estimate=pl.CostEstimate(flops=2 * macs, bytes_accessed=4 * x.size * 2, transcendentals=rows * width),
        name="column_attention",
    )(x, *operands)


def first_of_four(at, cols):
    wide = MXU_SIDE // HALF * cols
    inside = jnp.where(at < wide, at, jnp.where(at < wide + HALF, at - HALF, at - wide - HALF))
    return inside // cols


def swapped(pair, wide):
    return [pair[:wide], pair[2 * wide - HALF:], pair[wide:2 * wide - HALF]]


def unswapped(pair, wide):
    return [pair[:wide], pair[wide + HALF:], pair[wide:wide + HALF]]


def right_kernel(
    factor_ref, w_ref, expand_ref, shrink_ref, rbd_ref, rbdt_ref, wec_ref, wt_ref, et_ref, st_ref, stage_s,
    *, seqs, cols, fold,
):
    each = factor_ref.shape[2]
    wide = fold * cols
    stage_lanes = stage_s.shape[1]
    low_half = lax.broadcasted_iota(jnp.int32, (1, LANES), 1) < HALF

    stage_s[:FACTOR_WIDTH * FACTOR_WIDTH, :LANES] = w_ref[...].astype(jnp.float32)
    for e in range(FACTOR_WIDTH):
        piece = stage_s[pl.ds(e, FACTOR_WIDTH, stride=FACTOR_WIDTH), :LANES]
        wec_ref[e * FACTOR_WIDTH:(e + 1) * FACTOR_WIDTH, :] = piece.astype(jnp.bfloat16)
    for b in range(FACTOR_WIDTH * FACTOR_WIDTH // LANES):
        block = wec_ref[b * LANES:(b + 1) * LANES, :].astype(jnp.float32)
        wt_ref[:, b * LANES:(b + 1) * LANES] = block.T.astype(jnp.bfloat16)
    et_ref[...] = expand_ref[...].astype(jnp.float32).T.astype(jnp.bfloat16)
    st_ref[...] = shrink_ref[...].astype(jnp.float32).T.astype(jnp.bfloat16)

    for p in range(cols // 2):
        block = factor_ref[p // each, 1, p % each].astype(jnp.float32)
        even = 2 * p * FACTOR_WIDTH
        odd = even + FACTOR_WIDTH
        if seqs % LANES == 0:
            stage_s[even:even + FACTOR_WIDTH, :] = block[:, :seqs]
            stage_s[odd:odd + FACTOR_WIDTH, :] = block[:, seqs:]
        else:
            stage_s[even:even + FACTOR_WIDTH, :] = block
            stage_s[odd:odd + FACTOR_WIDTH, :] = pltpu.roll(block, HALF, axis=1)

    row_k = first_of_four(lax.broadcasted_iota(jnp.int32, (2 * wide, 1), 0), cols)
    lane_k = first_of_four(lax.broadcasted_iota(jnp.int32, (1, 2 * wide), 1), cols)
    for e in range(0, FACTOR_WIDTH, 2):
        two = []
        for u in (e, e + 1):
            two += [stage_s[pl.ds(u, cols, stride=FACTOR_WIDTH), :]] * fold
        upright = jnp.concatenate(swapped(jnp.concatenate(two, axis=0), wide), axis=0)
        chunk, at = e // CHUNK, e % CHUNK * wide
        rolled = pltpu.roll(upright, HALF, axis=1) if seqs < LANES else None
        for v in range(fold * seqs // stage_lanes):
            if seqs < LANES:
                value = jnp.where(
                    low_half, jnp.where(row_k == 2 * v, upright, 0.0), jnp.where(row_k == 2 * v + 1, rolled, 0.0)
                )
            else:
                value = jnp.where(row_k == v, upright, 0.0)
            rbdt_ref[chunk, at:at + 2 * wide, v * stage_lanes:(v + 1) * stage_lanes] = value.astype(jnp.bfloat16)
        turned = upright.T[:seqs]
        for k in range(fold):
            value = jnp.where(lane_k == k, turned, 0.0).astype(jnp.bfloat16)
            rbd_ref[chunk, k * seqs:(k + 1) * seqs, at:at + 2 * wide] = value


def right_matrices(factors, outer_weight, expand_weight, shrink_weight):
    row_parts, _, each, _, lanes = factors.shape
    seqs, cols = lanes // 2, 2 * each * row_parts
    fold = MXU_SIDE // HALF
    channels, width = outer_weight.shape
    results = (
        jax.ShapeDtypeStruct((FACTOR_WIDTH // CHUNK, fold * seqs, CHUNK * fold * cols), jnp.bfloat16),
        jax.ShapeDtypeStruct((FACTOR_WIDTH // CHUNK, CHUNK * fold * cols, fold * seqs), jnp.bfloat16),
        jax.ShapeDtypeStruct((channels, width), jnp.bfloat16),
        jax.ShapeDtypeStruct((width, channels), jnp.bfloat16),
        jax.ShapeDtypeStruct(expand_weight.shape[::-1], jnp.bfloat16),
        jax.ShapeDtypeStruct(shrink_weight.shape[::-1], jnp.bfloat16),
    )
    resident = pl.BlockSpec(memory_space=pltpu.VMEM)
    return pl.pallas_call(
        functools.partial(right_kernel, seqs=seqs, cols=cols, fold=fold),
        out_shape=results,
        in_specs=[resident] * 4,
        out_specs=[resident] * len(results),
        scratch_shapes=[pltpu.VMEM((max(cols * FACTOR_WIDTH, channels), max(seqs, LANES)), jnp.float32)],
        compiler_params=pltpu.CompilerParams(vmem_limit_bytes=16 * 1024 * 1024),
        cost_estimate=pl.CostEstimate(flops=6 * 10**9, bytes_accessed=4 * results[0].size, transcendentals=0),
        name="right_matrices",
    )(factors, outer_weight, expand_weight, shrink_weight)


def pair_kernel(
    place_ref, *refs, seqs, cols, fold, unit, units, blocks,
):
    left_refs, refs = refs[:blocks], refs[blocks:]
    rbd_s, rbdt_s, wec_s, wt_s, et_ref, st_ref, pair_ref, cot_ref, back_ref = refs[:9]
    returned_ref, bias_ref, expand_ref, out_ref, gl_ref = refs[9:14]
    both_refs, (outer_s, l_s, lt_s, stage_s, glacc_s, lblk_s, both_s) = refs[14:-7], refs[-7:]
    step = pl.program_id(0)
    row_parts, each = left_refs[0].shape[:2]
    span = l_s.shape[0]
    groups = span // FACTOR_WIDTH
    wide = fold * cols
    scaling = 1.0 / seqs
    low_half = lax.broadcasted_iota(jnp.int32, (1, LANES), 1) < HALF

    @pl.when(step == 0)
    def _prologue():
        for n, ref in enumerate(left_refs):
            lblk_s[place_ref[n]] = ref[...]
        pairs = fold // 2
        for p in range(groups * pairs):
            column, inside = divmod(p, row_parts * each)
            block = lblk_s[column, inside // each, inside % each]
            g, at = p // pairs, p % pairs * 2 * seqs
            l_s[g * FACTOR_WIDTH:(g + 1) * FACTOR_WIDTH, at:at + 2 * seqs] = (
                block.astype(jnp.float32) * scaling
            ).astype(jnp.bfloat16)
        for b in range(span // LANES):
            block = l_s[b * LANES:(b + 1) * LANES, :].astype(jnp.float32)
            lt_s[:, b * LANES:(b + 1) * LANES] = block.T.astype(jnp.bfloat16)

        def some_outers(n, carry):
            outer_s[n] = dot_nn(l_s[...], rbd_s[n]).astype(jnp.bfloat16)
            return carry

        lax.fori_loop(0, outer_s.shape[0], some_outers, 0, unroll=2)

    def unit_rows(u):
        at = (step * units + u) * unit * FACTOR_WIDTH
        return pl.ds(pl.multiple_of(at, unit * FACTOR_WIDTH), unit * FACTOR_WIDTH)

    def group(block, g):
        return block[g * FACTOR_WIDTH:(g + 1) * FACTOR_WIDTH]

    def forward(u):
        stacked = []
        for e in range(0, FACTOR_WIDTH, 2):
            at = e % CHUNK * wide
            block = outer_s[e // CHUNK, unit_rows(u), at:at + 2 * wide]
            shared = block[:, LANES:2 * LANES]
            rolled = pltpu.roll(shared, HALF, axis=1)
            even, odd = [], []
            for g in range(0, unit, 2):
                a, b = block[:, :LANES], block[:, 2 * LANES:]
                even += [group(a, g), jnp.where(low_half, group(shared, g), group(rolled, g + 1)), group(a, g + 1)]
                odd += [group(b, g), jnp.where(low_half, group(rolled, g), group(shared, g + 1)), group(b, g + 1)]
            stacked += [jnp.concatenate(even, axis=1), jnp.concatenate(odd, axis=1)]
        projected = dot_nn(wt_s[...], jnp.concatenate(stacked, axis=0))
        middles, inverses, spreads = [], [], []
        for at in range(0, projected.shape[1], LANES):
            middle = pair_ref[step * units + u, :, at:at + LANES] + projected[:, at:at + LANES] + bias_ref[...]
            average = jnp.mean(middle, axis=0, keepdims=True)
            centred = middle - average
            variance = jnp.mean(centred * centred, axis=0, keepdims=True)
            inverse = lax.rsqrt(variance + EPSILON)
            middles.append(middle)
            inverses.append(inverse)
            spreads.append(centred * inverse)
        spread_low = jnp.concatenate([v.astype(jnp.bfloat16) for v in spreads], axis=1)
        return middles, inverses, spreads, dot_nn(et_ref[...], spread_low)

    def backward(u, middles, inverses, spreads, before):
        rows, pairs = before.shape
        hidden, back_before = [], []
        for at in range(0, rows, TILE):
            hidden_parts, back_parts = [], []
            for v in range(0, pairs, MXU_SIDE):
                x = before[at:at + TILE, v:v + MXU_SIDE]
                back = back_ref[step * units + u, at:at + TILE, v:v + MXU_SIDE].astype(jnp.float32)
                phi = 0.5 * (1.0 + lax.erf(x * 0.7071067811865476))
                slope = phi + x * jnp.exp(-0.5 * x * x) * 0.3989422804014327
                hidden_parts.append((x * phi).astype(jnp.bfloat16))
                back_parts.append((back * slope).astype(jnp.bfloat16))
            hidden.append(jnp.concatenate(hidden_parts, axis=1))
            back_before.append(jnp.concatenate(back_parts, axis=1))
        back_spread = dot_nn(expand_ref[...], jnp.concatenate(back_before, axis=0))
        change = dot_nn(st_ref[...], jnp.concatenate(hidden, axis=0))
        back_middle = []
        for n, at in enumerate(range(0, pairs, LANES)):
            back, spread = back_spread[:, at:at + LANES], spreads[n]
            centre_term = jnp.mean(back, axis=0, keepdims=True)
            slope_term = jnp.mean(back * spread, axis=0, keepdims=True)
            back = back - centre_term - spread * slope_term
            back = cot_ref[step * units + u, :, at:at + LANES] + inverses[n] * back
            back_middle.append(back.astype(jnp.bfloat16))
        result = (jnp.concatenate(middles, axis=1) + change).T
        pieces = []
        for g in range(0, unit, 2):
            pieces += unswapped(result[g * wide:(g + 2) * wide], wide)
        out_ref[u * unit * fold:(u + 1) * unit * fold] = jnp.concatenate(pieces, axis=0).reshape(
            unit * fold, cols, PAIR_W
        )
        back_outer = dot_nn(wec_s[...], jnp.concatenate(back_middle, axis=1)).astype(jnp.bfloat16)
        for e in range(0, FACTOR_WIDTH, 2):
            even, odd = group(back_outer, e), group(back_outer, e + 1)
            a, shared, b = [], [], []
            for g in range(0, unit, 2):
                at = g * wide
                of_even, of_odd = even[:, at + LANES:at + 2 * LANES], odd[:, at + LANES:at + 2 * LANES]
                a += [even[:, at:at + LANES], even[:, at + 2 * LANES:at + 3 * LANES]]
                b += [odd[:, at:at + LANES], odd[:, at + 2 * LANES:at + 3 * LANES]]
                shared += [
                    jnp.where(low_half, of_even, pltpu.roll(of_odd, HALF, axis=1)),
                    jnp.where(low_half, pltpu.roll(of_even, HALF, axis=1), of_odd),
                ]
            for n, pieces in enumerate((a, shared, b)):
                at = e % CHUNK * wide + n * LANES
                outer_s[e // CHUNK, unit_rows(u), at:at + LANES] = jnp.concatenate(pieces, axis=0)

    held = forward(0)
    for u in range(units):
        ahead = forward(u + 1) if u + 1 < units else None
        backward(u, *held)
        held = ahead

    @pl.when(step == pl.num_programs(0) - 1)
    def _epilogue():
        glacc_s[...] = jnp.zeros_like(glacc_s)
        empty = jnp.zeros((LANES - seqs % LANES, CHUNK * wide), jnp.float32) if seqs % LANES else None
        at = lax.broadcasted_iota(jnp.int32, (1, CHUNK * wide), 1)
        lane_k = first_of_four(lax.rem(at, 2 * wide), cols)

        def some(n, carry):
            back = outer_s[n]
            glacc_s[...] += dot_nn(back, rbdt_s[n])
            full = dot_nn(lt_s[...], back)
            compact = full[:seqs]
            for k in range(1, fold):
                compact = jnp.where(lane_k == k, full[k * seqs:(k + 1) * seqs], compact)
            if empty is not None:
                compact = jnp.concatenate([compact, empty], axis=0)
            turned = compact.T
            for p in range(CHUNK // 2):
                two = jnp.concatenate(unswapped(turned[2 * p * wide:2 * (p + 1) * wide], wide), axis=0)
                for u in range(2):
                    total = two[u * wide:u * wide + cols]
                    for k in range(1, fold):
                        total = total + two[u * wide + k * cols:u * wide + (k + 1) * cols]
                    stage_s[pl.ds(n * CHUNK + 2 * p + u, cols, stride=FACTOR_WIDTH), :] = total
            return carry

        lax.fori_loop(0, outer_s.shape[0], some, 0, unroll=2)
        part_seqs, width = returned_ref.shape[1:]
        both_s[:, :, :width] = returned_ref[...]
        for b in range(cols * FACTOR_WIDTH // LANES):
            block = stage_s[b * LANES:(b + 1) * LANES, :].T[:seqs].astype(jnp.bfloat16)
            both_s[:, :, width + b * LANES:width + (b + 1) * LANES] = block.reshape(row_parts, part_seqs, LANES)
        for k, ref in enumerate(both_refs):
            ref[...] = both_s[place_ref[blocks] ^ k]
        for b in range(span // LANES):
            block = glacc_s[b * LANES:(b + 1) * LANES, :].T * scaling
            for k in range(fold):
                at = k * span + b * LANES
                gl_ref[:, at:at + LANES] = block[k * seqs:(k + 1) * seqs].astype(jnp.bfloat16)


def turn_kernel(pair_ref, cot_ref, shrink_ref, after_ref, pair_out_ref, cot_out_ref, back_ref, *, wide):
    for source, target in ((pair_ref, pair_out_ref), (cot_ref, cot_out_ref)):
        rows = source[...].reshape(-1, PAIR_W)
        for at in range(0, rows.shape[0], 2 * wide):
            target[0, :, at:at + 2 * wide] = jnp.concatenate(swapped(rows[at:at + 2 * wide], wide), axis=0).T
    back_ref[0] = dot_nn(shrink_ref[...], cot_out_ref[0].astype(jnp.bfloat16)).astype(jnp.bfloat16)


def turned_pairs(pair_features, cotangent, shrink_weight, after):
    rows, cols, _ = pair_features.shape
    fold = MXU_SIDE // HALF
    count = rows // (UNIT * fold)
    pairs = UNIT * fold * cols
    hidden = shrink_weight.shape[0]
    results = (
        jax.ShapeDtypeStruct((count, PAIR_W, pairs), jnp.float32),
        jax.ShapeDtypeStruct((count, PAIR_W, pairs), jnp.float32),
        jax.ShapeDtypeStruct((count, hidden, pairs), jnp.bfloat16),
    )
    block = pl.BlockSpec((UNIT * fold, cols, PAIR_W), lambda n: (n, 0, 0))
    return pl.pallas_call(
        functools.partial(turn_kernel, wide=fold * cols),
        grid=(count,),
        out_shape=results,
        in_specs=[block, block, whole_block(shrink_weight.shape), pl.BlockSpec(memory_space=pl.ANY)],
        out_specs=[pl.BlockSpec((1,) + v.shape[1:], lambda n: (n, 0, 0)) for v in results],
        compiler_params=pltpu.CompilerParams(
            dimension_semantics=("arbitrary",), vmem_limit_bytes=24 * 1024 * 1024
        ),
        cost_estimate=pl.CostEstimate(
            flops=2 * 2 * count * pairs * hidden * PAIR_W, bytes_accessed=4 * 4 * pair_features.size, transcendentals=0
        ),
        name="turned_pairs",
    )(pair_features, cotangent, shrink_weight, after)


def pair_tile(place, lefts, matrices, turned, returned, shape, outer_bias, expand_weight):
    seqs = lefts[0].shape[-1] // 2
    rows, cols, _ = shape
    fold = MXU_SIDE // HALF
    groups = rows // fold
    unit = UNIT
    units = 2 if groups % (2 * unit) == 0 else 1
    steps = groups // unit // units
    wide = fold * cols
    span = groups * FACTOR_WIDTH
    channels = FACTOR_WIDTH * FACTOR_WIDTH
    block = pl.BlockSpec((unit * units * fold, cols, PAIR_W), lambda n, place: (n, 0, 0))
    resident = pl.BlockSpec(memory_space=pltpu.VMEM)
    operands = (
        *lefts, *matrices, *turned, returned, jnp.broadcast_to(outer_bias[:, None], (PAIR_W, LANES)), expand_weight,
    )
    results = (
        jax.ShapeDtypeStruct(shape, jnp.float32),
        jax.ShapeDtypeStruct((seqs, rows * FACTOR_WIDTH), jnp.bfloat16),
    ) + returned.shape[0] * (
        jax.ShapeDtypeStruct((returned.shape[1], returned.shape[2] + cols * FACTOR_WIDTH), jnp.bfloat16),
    )
    padded = groups * wide
    macs = 3 * FACTOR_WIDTH * span * fold * seqs * wide + padded * (2 * channels * MXU_SIDE + 8 * MXU_SIDE * MXU_SIDE)
    return pl.pallas_call(
        functools.partial(
            pair_kernel, seqs=seqs, cols=cols, fold=fold, unit=unit, units=units, blocks=len(lefts)
        ),
        grid_spec=pltpu.PrefetchScalarGridSpec(
            num_scalar_prefetch=1,
            grid=(steps,),
            in_specs=[resident] * len(operands),
            out_specs=[block] + [resident] * (len(results) - 1),
            scratch_shapes=[
                pltpu.VMEM((FACTOR_WIDTH // CHUNK, span, CHUNK * wide), jnp.bfloat16),
                pltpu.VMEM((span, fold * seqs), jnp.bfloat16),
                pltpu.VMEM((fold * seqs, span), jnp.bfloat16),
                pltpu.VMEM((cols * FACTOR_WIDTH, max(seqs, LANES)), jnp.float32),
                pltpu.VMEM((span, fold * seqs), jnp.float32),
                pltpu.VMEM((len(lefts),) + lefts[0].shape, jnp.bfloat16),
                pltpu.VMEM(returned.shape[:1] + results[2].shape, jnp.bfloat16),
            ],
        ),
        out_shape=results,
        compiler_params=pltpu.CompilerParams(
            dimension_semantics=("arbitrary",), vmem_limit_bytes=36 * 1024 * 1024
        ),
        cost_estimate=pl.CostEstimate(
            flops=2 * macs, bytes_accessed=rows * cols * PAIR_W * 4, transcendentals=0
        ),
        name="pair_tile",
    )(place, *operands)


def finish_kernel(place_ref, *refs, residues, fold):
    *both_refs, gl_ref, updated_ref, left_ref, right_ref, x_s = refs
    part_seqs, res_count, width = updated_ref.shape
    total = both_refs[0][:, residues * width:].astype(jnp.float32)
    for ref in both_refs[1:]:
        total = total + ref[:, residues * width:].astype(jnp.float32)
    right_ref[...] = total
    for k, ref in enumerate(both_refs):
        first = (place_ref[0] ^ k) * residues
        for r in range(residues):
            for n in range(width // LANES):
                at = r * width + n * LANES
                x_s[n, pl.ds(first + r, part_seqs, stride=res_count), :] = ref[:, at:at + LANES].astype(jnp.float32)
    for n in range(width // LANES):
        updated_ref[:, :, n * LANES:(n + 1) * LANES] = (
            x_s[n].reshape(part_seqs, res_count, LANES).astype(jnp.bfloat16)
        )
    total = gl_ref[0].astype(jnp.float32)
    for n in range(1, gl_ref.shape[0]):
        total = total + gl_ref[n].astype(jnp.float32)
    span = total.shape[1] // fold
    channel_block = lax.broadcasted_iota(jnp.int32, (1, LANES), 1) // FACTOR_WIDTH
    each = LANES // FACTOR_WIDTH
    for g in range(span // FACTOR_WIDTH):
        out = None
        for k in range(fold):
            at = k * span + g // each * LANES
            piece = total[:, at:at + LANES]
            shift = (k - g) % each * FACTOR_WIDTH
            piece = pltpu.roll(piece, shift, axis=1) if shift else piece
            out = piece if out is None else jnp.where(channel_block == k, piece, out)
        left_ref[:, g * LANES:(g + 1) * LANES] = out


def finish(place, both, gl, updated_shape):
    part_seqs, res_count, width = updated_shape
    residues = res_count // len(both)
    results = (
        jax.ShapeDtypeStruct(updated_shape, jnp.bfloat16),
        jax.ShapeDtypeStruct(gl.shape[1:], jnp.float32),
        jax.ShapeDtypeStruct((part_seqs, both[0].shape[1] - residues * width), jnp.float32),
    )
    resident = pl.BlockSpec(memory_space=pltpu.VMEM)
    return pl.pallas_call(
        functools.partial(finish_kernel, residues=residues, fold=MXU_SIDE // HALF),
        grid_spec=pltpu.PrefetchScalarGridSpec(
            num_scalar_prefetch=1,
            grid=(1,),
            in_specs=[resident] * (len(both) + 1),
            out_specs=[whole_block(v.shape) for v in results],
            scratch_shapes=[pltpu.VMEM((width // LANES, part_seqs * res_count, LANES), jnp.float32)],
        ),
        out_shape=results,
        compiler_params=pltpu.CompilerParams(
            dimension_semantics=("arbitrary",), vmem_limit_bytes=16 * 1024 * 1024
        ),
        name="finish",
    )(place, *both, gl)


def spread_out(q, count):
    return q if count % 2 else q % 2 * (count // 2) + q // 2


def local(
    alignment,
    pair_features,
    query_weight,
    key_weight,
    value_projection,
    gate_projection,
    gate_bias,
    output_projection,
    left_projection,
    right_projection,
    outer_weight,
    outer_bias,
    expand_weight,
    shrink_weight,
    cotangent,
):
    part_seqs, res_count, width = alignment.shape
    row_parts = lax.axis_size("row")
    col_parts = lax.axis_size("col")
    residues = res_count // row_parts
    own = jnp.transpose(alignment, (1, 0, 2)).reshape(row_parts, residues, part_seqs, width)
    columns = lax.all_to_all(own, "row", split_axis=0, concat_axis=0, tiled=True)
    attended, factors = attend(
        columns, query_weight, key_weight, value_projection, gate_projection, gate_bias,
        output_projection, left_projection, right_projection,
    )

    factors = lax.all_to_all(factors, "row", split_axis=0, concat_axis=0, tiled=True)
    left = factors[:, 0]
    ratio = col_parts // row_parts
    lefts, place = [], []
    for m in range(ratio):
        moves = [
            (q * col_parts + ratio * r + b, r * col_parts + ratio * spread_out(q, row_parts) + (b + m) % ratio)
            for q in range(row_parts)
            for r in range(row_parts)
            for b in range(ratio)
        ]
        lefts.append(lax.ppermute(left, ("row", "col"), moves))
        place.append((lax.axis_index("col") + ratio - m) % ratio)
    row = lax.axis_index("row")
    matrices = right_matrices(factors, outer_weight, expand_weight, shrink_weight)
    turned = turned_pairs(pair_features, cotangent, shrink_weight, matrices[-1])
    pair_out, gl, *both = pair_tile(
        jnp.stack(place + [row]).astype(jnp.int32), lefts, matrices, turned, attended, pair_features.shape,
        outer_bias, expand_weight,
    )
    seqs, gl_width = gl.shape
    both = both[:1] + [
        lax.ppermute(v, "row", [(r, r ^ (k + 1)) for r in range(row_parts)]) for k, v in enumerate(both[1:])
    ]
    gl = lax.all_to_all(
        gl.reshape(col_parts, seqs // col_parts, gl_width), "col", split_axis=0, concat_axis=0, tiled=True
    )
    updated, grad_left, grad_right = finish(row.astype(jnp.int32).reshape(1), both, gl, alignment.shape)
    return (updated, pair_out, grad_left, grad_right)


def solution(mesh):
    return jax.shard_map(
        local,
        mesh=mesh,
        in_specs=(P("row", "col", None), P("row", "col", None)) + (P(),) * 12 + (P("row", "col", None),),
        out_specs=(P("row", "col", None), P("row", "col", None), P("col", "row"), P("row", "col")),
        check_vma=False,
    )
```

```python
import functools

import jax
import jax.numpy as jnp
from jax import lax
from jax.experimental import pallas as pl
from jax.experimental.pallas import tpu as pltpu
from jax.sharding import PartitionSpec as P

ATTENTION_HEADS = 8
HEAD_WIDTH = 32
FACTOR_WIDTH = 32
PAIR_W = 128
EPSILON = 1e-05

LANES = 128
MXU_SIDE = 256
HALF = 64
TILE = 32
CHUNK = 4
UNIT = 4


def dot_nn(a, b):
    return lax.dot_general(a, b, (((1,), (0,)), ((), ())), preferred_element_type=jnp.float32)


def dot_nt(a, b):
    return lax.dot_general(a, b, (((1,), (1,)), ((), ())), preferred_element_type=jnp.float32)


def layer_normalise(rows):
    rows = rows.astype(jnp.float32)
    average = jnp.mean(rows, axis=-1, keepdims=True)
    centred = rows - average
    variance = jnp.mean(centred * centred, axis=-1, keepdims=True)
    return centred * lax.rsqrt(variance + EPSILON)


def attend_kernel(
    x_ref, wq_ref, wk_ref, wv_ref, wg_ref, bias_ref, wo_ref, wl_ref, wr_ref,
    upd_ref, factor_ref, q_s, k_s, v_s, g_s, a_s, w_s, bias_s, project_s, upd_s, sems,
):
    parts, residues, part_seqs, width = x_ref.shape
    seqs = parts * part_seqs
    sources = (wq_ref, wk_ref, wv_ref, wg_ref, wo_ref, bias_ref, wl_ref, wr_ref)
    targets = [w_s.at[n] for n in range(5)] + [bias_s, project_s.at[0], project_s.at[1]]
    copies = [pltpu.make_async_copy(a, b, sems.at[n]) for n, (a, b) in enumerate(zip(sources, targets))]
    for copy in copies:
        copy.start()
    x = jnp.concatenate([x_ref[s, r] for r in range(residues) for s in range(parts)], axis=0)
    normed = layer_normalise(x).astype(jnp.bfloat16)
    for n, ref in enumerate((q_s, k_s, v_s)):
        copies[n].wait()
        ref[...] = dot_nn(normed, w_s[n]).astype(jnp.bfloat16)
    copies[3].wait()
    copies[5].wait()
    g_s[...] = jax.nn.sigmoid(dot_nn(normed, w_s[3]) + bias_s[...])

    head_of = lax.broadcasted_iota(jnp.int32, (1, width), 1) // HEAD_WIDTH
    masks = [(head_of == h).astype(jnp.bfloat16) for h in range(ATTENTION_HEADS)]

    def one_residue(r, carry):
        rows = pl.ds(pl.multiple_of(r * seqs, seqs), seqs)
        query = q_s[rows, :]
        queries = jnp.concatenate([query * m for m in masks], axis=0)
        scores = dot_nt(k_s[rows, :], queries) * HEAD_WIDTH ** (-0.5)
        raised = jnp.exp(scores - jnp.max(scores, axis=0, keepdims=True))
        inverse = 1.0 / jnp.sum(raised, axis=0, keepdims=True)
        value = v_s[rows, :].astype(jnp.float32).T.astype(jnp.bfloat16)
        crossed = dot_nn(value, raised.astype(jnp.bfloat16))
        blended = []
        for h in range(ATTENTION_HEADS):
            at = h * seqs // LANES * LANES
            lanes = slice(at, at + max(LANES, seqs))
            own = crossed[h * HEAD_WIDTH:(h + 1) * HEAD_WIDTH, lanes] * inverse[:, lanes]
            blended.append(pltpu.roll(own, LANES - h * seqs % LANES, axis=1) if h * seqs % LANES else own)
        blended = jnp.concatenate(blended, axis=0).T[:seqs]
        a_s[rows, :] = (g_s[rows, :] * blended).astype(jnp.bfloat16)
        return carry

    lax.fori_loop(0, residues, one_residue, 0, unroll=4 if residues % 4 == 0 else 2)

    copies[4].wait()
    updated = (x.astype(jnp.float32) + dot_nn(a_s[...], w_s[4])).astype(jnp.bfloat16)
    for r in range(residues):
        for s in range(parts):
            begin = r * seqs + s * part_seqs
            upd_s[s, :, r * width:(r + 1) * width] = updated[begin:begin + part_seqs]
    leaving = pltpu.make_async_copy(upd_s, upd_ref, sems.at[len(sources)])
    leaving.start()
    factor_norm = layer_normalise(updated).astype(jnp.bfloat16)
    copies[6].wait()
    copies[7].wait()
    project = project_s[...].reshape(2 * FACTOR_WIDTH, width)
    for p in range(residues // 2):
        both = dot_nt(project, factor_norm[p * 2 * seqs:(p + 1) * 2 * seqs]).astype(jnp.bfloat16)
        for n in range(parts):
            factor_ref[n, 0, p] = both[:FACTOR_WIDTH]
            factor_ref[n, 1, p] = both[FACTOR_WIDTH:]
    leaving.wait()


def whole_block(shape):
    return pl.BlockSpec(shape, lambda *_: (0,) * len(shape))


def in_hbm(*arrays):
    return [pltpu.with_memory_space_constraint(v, pltpu.HBM) for v in arrays]


def attend(x, wq, wk, wv, wg, gate_bias, wo, wl, wr):
    parts, residues, part_seqs, width = x.shape
    seqs = parts * part_seqs
    rows = residues * seqs
    operands = in_hbm(wq, wk, wv, wg, gate_bias.reshape(1, -1), wo, wl.T, wr.T)
    resident = pl.BlockSpec(memory_space=pltpu.VMEM)
    results = (
        pltpu.HBM((parts, part_seqs, residues * width), jnp.bfloat16),
        jax.ShapeDtypeStruct((parts, 2, residues // 2, FACTOR_WIDTH, 2 * seqs), jnp.bfloat16),
    )
    macs = rows * width * (5 * width + 2 * FACTOR_WIDTH) + 2 * rows * ATTENTION_HEADS * width * seqs
    return pl.pallas_call(
        attend_kernel,
        out_shape=results,
        in_specs=[resident] + [pl.BlockSpec(memory_space=pltpu.HBM)] * len(operands),
        out_specs=[pl.BlockSpec(memory_space=pltpu.HBM), resident],
        scratch_shapes=[
            pltpu.VMEM((rows, width), jnp.bfloat16),
            pltpu.VMEM((rows, width), jnp.bfloat16),
            pltpu.VMEM((rows, width), jnp.bfloat16),
            pltpu.VMEM((rows, width), jnp.float32),
            pltpu.VMEM((rows, width), jnp.bfloat16),
            pltpu.VMEM((5,) + wq.shape, jnp.bfloat16),
            pltpu.VMEM((1, width), jnp.float32),
            pltpu.VMEM((2, FACTOR_WIDTH, width), jnp.bfloat16),
            pltpu.VMEM(results[0].shape, jnp.bfloat16),
            pltpu.SemaphoreType.DMA((len(operands) + 1,)),
        ],
        compiler_params=pltpu.CompilerParams(vmem_limit_bytes=32 * 1024 * 1024),
        cost_estimate=pl.CostEstimate(flops=2 * macs, bytes_accessed=4 * x.size * 2, transcendentals=rows * width),
        name="column_attention",
    )(x, *operands)


def first_of_four(at, cols):
    wide = MXU_SIDE // HALF * cols
    inside = jnp.where(at < wide, at, jnp.where(at < wide + HALF, at - HALF, at - wide - HALF))
    return inside // cols


def swapped(pair, wide):
    return [pair[:wide], pair[2 * wide - HALF:], pair[wide:2 * wide - HALF]]


def unswapped(pair, wide):
    return [pair[:wide], pair[wide + HALF:], pair[wide:wide + HALF]]


def right_kernel(
    factor_ref, w_ref, expand_ref, shrink_ref, rbd_ref, rbdt_ref, wec_ref, wt_ref, et_ref, st_ref, stage_s,
    *, seqs, cols, fold,
):
    each = factor_ref.shape[2]
    wide = fold * cols
    stage_lanes = stage_s.shape[1]
    low_half = lax.broadcasted_iota(jnp.int32, (1, LANES), 1) < HALF

    stage_s[:FACTOR_WIDTH * FACTOR_WIDTH, :LANES] = w_ref[...].astype(jnp.float32)
    for e in range(FACTOR_WIDTH):
        piece = stage_s[pl.ds(e, FACTOR_WIDTH, stride=FACTOR_WIDTH), :LANES]
        wec_ref[e * FACTOR_WIDTH:(e + 1) * FACTOR_WIDTH, :] = piece.astype(jnp.bfloat16)
    for b in range(FACTOR_WIDTH * FACTOR_WIDTH // LANES):
        block = wec_ref[b * LANES:(b + 1) * LANES, :].astype(jnp.float32)
        wt_ref[:, b * LANES:(b + 1) * LANES] = block.T.astype(jnp.bfloat16)
    et_ref[...] = expand_ref[...].astype(jnp.float32).T.astype(jnp.bfloat16)
    st_ref[...] = shrink_ref[...].astype(jnp.float32).T.astype(jnp.bfloat16)

    for p in range(cols // 2):
        block = factor_ref[p // each, 1, p % each].astype(jnp.float32)
        even = 2 * p * FACTOR_WIDTH
        odd = even + FACTOR_WIDTH
        if seqs % LANES == 0:
            stage_s[even:even + FACTOR_WIDTH, :] = block[:, :seqs]
            stage_s[odd:odd + FACTOR_WIDTH, :] = block[:, seqs:]
        else:
            stage_s[even:even + FACTOR_WIDTH, :] = block
            stage_s[odd:odd + FACTOR_WIDTH, :] = pltpu.roll(block, HALF, axis=1)

    row_k = first_of_four(lax.broadcasted_iota(jnp.int32, (2 * wide, 1), 0), cols)
    lane_k = first_of_four(lax.broadcasted_iota(jnp.int32, (1, 2 * wide), 1), cols)
    for e in range(0, FACTOR_WIDTH, 2):
        two = []
        for u in (e, e + 1):
            two += [stage_s[pl.ds(u, cols, stride=FACTOR_WIDTH), :]] * fold
        upright = jnp.concatenate(swapped(jnp.concatenate(two, axis=0), wide), axis=0)
        chunk, at = e // CHUNK, e % CHUNK * wide
        rolled = pltpu.roll(upright, HALF, axis=1) if seqs < LANES else None
        for v in range(fold * seqs // stage_lanes):
            if seqs < LANES:
                value = jnp.where(
                    low_half, jnp.where(row_k == 2 * v, upright, 0.0), jnp.where(row_k == 2 * v + 1, rolled, 0.0)
                )
            else:
                value = jnp.where(row_k == v, upright, 0.0)
            rbdt_ref[chunk, at:at + 2 * wide, v * stage_lanes:(v + 1) * stage_lanes] = value.astype(jnp.bfloat16)
        turned = upright.T[:seqs]
        for k in range(fold):
            value = jnp.where(lane_k == k, turned, 0.0).astype(jnp.bfloat16)
            rbd_ref[chunk, k * seqs:(k + 1) * seqs, at:at + 2 * wide] = value


def right_matrices(factors, outer_weight, expand_weight, shrink_weight):
    row_parts, _, each, _, lanes = factors.shape
    seqs, cols = lanes // 2, 2 * each * row_parts
    fold = MXU_SIDE // HALF
    channels, width = outer_weight.shape
    results = (
        jax.ShapeDtypeStruct((FACTOR_WIDTH // CHUNK, fold * seqs, CHUNK * fold * cols), jnp.bfloat16),
        jax.ShapeDtypeStruct((FACTOR_WIDTH // CHUNK, CHUNK * fold * cols, fold * seqs), jnp.bfloat16),
        jax.ShapeDtypeStruct((channels, width), jnp.bfloat16),
        jax.ShapeDtypeStruct((width, channels), jnp.bfloat16),
        jax.ShapeDtypeStruct(expand_weight.shape[::-1], jnp.bfloat16),
        jax.ShapeDtypeStruct(shrink_weight.shape[::-1], jnp.bfloat16),
    )
    resident = pl.BlockSpec(memory_space=pltpu.VMEM)
    return pl.pallas_call(
        functools.partial(right_kernel, seqs=seqs, cols=cols, fold=fold),
        out_shape=results,
        in_specs=[resident] * 4,
        out_specs=[resident] * len(results),
        scratch_shapes=[pltpu.VMEM((max(cols * FACTOR_WIDTH, channels), max(seqs, LANES)), jnp.float32)],
        compiler_params=pltpu.CompilerParams(vmem_limit_bytes=16 * 1024 * 1024),
        cost_estimate=pl.CostEstimate(flops=6 * 10**9, bytes_accessed=4 * results[0].size, transcendentals=0),
        name="right_matrices",
    )(factors, outer_weight, expand_weight, shrink_weight)


def pair_kernel(
    place_ref, *refs, seqs, cols, fold, unit, units, blocks,
):
    left_refs, refs = refs[:blocks], refs[blocks:]
    rbd_s, rbdt_s, wec_s, wt_s, et_ref, st_ref, pair_ref, cot_ref, back_ref = refs[:9]
    bias_ref, expand_ref, out_ref, gl_ref = refs[9:13]
    gr_refs, (outer_s, l_s, lt_s, stage_s, glacc_s, lblk_s, gr_s) = refs[13:-7], refs[-7:]
    step = pl.program_id(0)
    row_parts, each = left_refs[0].shape[:2]
    span = l_s.shape[0]
    groups = span // FACTOR_WIDTH
    wide = fold * cols
    scaling = 1.0 / seqs
    low_half = lax.broadcasted_iota(jnp.int32, (1, LANES), 1) < HALF

    @pl.when(step == 0)
    def _prologue():
        for n, ref in enumerate(left_refs):
            lblk_s[place_ref[n]] = ref[...]
        pairs = fold // 2
        for p in range(groups * pairs):
            column, inside = divmod(p, row_parts * each)
            block = lblk_s[column, inside // each, inside % each]
            g, at = p // pairs, p % pairs * 2 * seqs
            l_s[g * FACTOR_WIDTH:(g + 1) * FACTOR_WIDTH, at:at + 2 * seqs] = (
                block.astype(jnp.float32) * scaling
            ).astype(jnp.bfloat16)
        for b in range(span // LANES):
            block = l_s[b * LANES:(b + 1) * LANES, :].astype(jnp.float32)
            lt_s[:, b * LANES:(b + 1) * LANES] = block.T.astype(jnp.bfloat16)

        def some_outers(n, carry):
            outer_s[n] = dot_nn(l_s[...], rbd_s[n]).astype(jnp.bfloat16)
            return carry

        lax.fori_loop(0, outer_s.shape[0], some_outers, 0, unroll=2)

    def unit_rows(u):
        at = (step * units + u) * unit * FACTOR_WIDTH
        return pl.ds(pl.multiple_of(at, unit * FACTOR_WIDTH), unit * FACTOR_WIDTH)

    def group(block, g):
        return block[g * FACTOR_WIDTH:(g + 1) * FACTOR_WIDTH]

    def forward(u):
        stacked = []
        for e in range(0, FACTOR_WIDTH, 2):
            at = e % CHUNK * wide
            block = outer_s[e // CHUNK, unit_rows(u), at:at + 2 * wide]
            shared = block[:, LANES:2 * LANES]
            rolled = pltpu.roll(shared, HALF, axis=1)
            even, odd = [], []
            for g in range(0, unit, 2):
                a, b = block[:, :LANES], block[:, 2 * LANES:]
                even += [group(a, g), jnp.where(low_half, group(shared, g), group(rolled, g + 1)), group(a, g + 1)]
                odd += [group(b, g), jnp.where(low_half, group(rolled, g), group(shared, g + 1)), group(b, g + 1)]
            stacked += [jnp.concatenate(even, axis=1), jnp.concatenate(odd, axis=1)]
        projected = dot_nn(wt_s[...], jnp.concatenate(stacked, axis=0))
        middles, inverses, spreads = [], [], []
        for at in range(0, projected.shape[1], LANES):
            middle = pair_ref[step * units + u, :, at:at + LANES] + projected[:, at:at + LANES] + bias_ref[...]
            average = jnp.mean(middle, axis=0, keepdims=True)
            centred = middle - average
            variance = jnp.mean(centred * centred, axis=0, keepdims=True)
            inverse = lax.rsqrt(variance + EPSILON)
            middles.append(middle)
            inverses.append(inverse)
            spreads.append(centred * inverse)
        spread_low = jnp.concatenate([v.astype(jnp.bfloat16) for v in spreads], axis=1)
        return middles, inverses, spreads, dot_nn(et_ref[...], spread_low)

    def backward(u, middles, inverses, spreads, before):
        rows, pairs = before.shape
        hidden, back_before = [], []
        for at in range(0, rows, TILE):
            hidden_parts, back_parts = [], []
            for v in range(0, pairs, MXU_SIDE):
                x = before[at:at + TILE, v:v + MXU_SIDE]
                back = back_ref[step * units + u, at:at + TILE, v:v + MXU_SIDE].astype(jnp.float32)
                phi = 0.5 * (1.0 + lax.erf(x * 0.7071067811865476))
                slope = phi + x * jnp.exp(-0.5 * x * x) * 0.3989422804014327
                hidden_parts.append((x * phi).astype(jnp.bfloat16))
                back_parts.append((back * slope).astype(jnp.bfloat16))
            hidden.append(jnp.concatenate(hidden_parts, axis=1))
            back_before.append(jnp.concatenate(back_parts, axis=1))
        back_spread = dot_nn(expand_ref[...], jnp.concatenate(back_before, axis=0))
        change = dot_nn(st_ref[...], jnp.concatenate(hidden, axis=0))
        back_middle = []
        for n, at in enumerate(range(0, pairs, LANES)):
            back, spread = back_spread[:, at:at + LANES], spreads[n]
            centre_term = jnp.mean(back, axis=0, keepdims=True)
            slope_term = jnp.mean(back * spread, axis=0, keepdims=True)
            back = back - centre_term - spread * slope_term
            back = cot_ref[step * units + u, :, at:at + LANES] + inverses[n] * back
            back_middle.append(back.astype(jnp.bfloat16))
        result = (jnp.concatenate(middles, axis=1) + change).T
        pieces = []
        for g in range(0, unit, 2):
            pieces += unswapped(result[g * wide:(g + 2) * wide], wide)
        out_ref[u * unit * fold:(u + 1) * unit * fold] = jnp.concatenate(pieces, axis=0).reshape(
            unit * fold, cols, PAIR_W
        )
        back_outer = dot_nn(wec_s[...], jnp.concatenate(back_middle, axis=1)).astype(jnp.bfloat16)
        for e in range(0, FACTOR_WIDTH, 2):
            even, odd = group(back_outer, e), group(back_outer, e + 1)
            a, shared, b = [], [], []
            for g in range(0, unit, 2):
                at = g * wide
                of_even, of_odd = even[:, at + LANES:at + 2 * LANES], odd[:, at + LANES:at + 2 * LANES]
                a += [even[:, at:at + LANES], even[:, at + 2 * LANES:at + 3 * LANES]]
                b += [odd[:, at:at + LANES], odd[:, at + 2 * LANES:at + 3 * LANES]]
                shared += [
                    jnp.where(low_half, of_even, pltpu.roll(of_odd, HALF, axis=1)),
                    jnp.where(low_half, pltpu.roll(of_even, HALF, axis=1), of_odd),
                ]
            for n, pieces in enumerate((a, shared, b)):
                at = e % CHUNK * wide + n * LANES
                outer_s[e // CHUNK, unit_rows(u), at:at + LANES] = jnp.concatenate(pieces, axis=0)

    held = forward(0)
    for u in range(units):
        ahead = forward(u + 1) if u + 1 < units else None
        backward(u, *held)
        held = ahead

    @pl.when(step == pl.num_programs(0) - 1)
    def _epilogue():
        glacc_s[...] = jnp.zeros_like(glacc_s)
        empty = jnp.zeros((LANES - seqs % LANES, CHUNK * wide), jnp.float32) if seqs % LANES else None
        at = lax.broadcasted_iota(jnp.int32, (1, CHUNK * wide), 1)
        lane_k = first_of_four(lax.rem(at, 2 * wide), cols)

        def some(n, carry):
            back = outer_s[n]
            glacc_s[...] += dot_nn(back, rbdt_s[n])
            full = dot_nn(lt_s[...], back)
            compact = full[:seqs]
            for k in range(1, fold):
                compact = jnp.where(lane_k == k, full[k * seqs:(k + 1) * seqs], compact)
            if empty is not None:
                compact = jnp.concatenate([compact, empty], axis=0)
            turned = compact.T
            for p in range(CHUNK // 2):
                two = jnp.concatenate(unswapped(turned[2 * p * wide:2 * (p + 1) * wide], wide), axis=0)
                for u in range(2):
                    total = two[u * wide:u * wide + cols]
                    for k in range(1, fold):
                        total = total + two[u * wide + k * cols:u * wide + (k + 1) * cols]
                    stage_s[pl.ds(n * CHUNK + 2 * p + u, cols, stride=FACTOR_WIDTH), :] = total
            return carry

        lax.fori_loop(0, outer_s.shape[0], some, 0, unroll=2)
        for b in range(cols * FACTOR_WIDTH // LANES):
            block = stage_s[b * LANES:(b + 1) * LANES, :].T[:seqs].astype(jnp.bfloat16)
            gr_s[:, :, b * LANES:(b + 1) * LANES] = block.reshape(row_parts, -1, LANES)
        for k, ref in enumerate(gr_refs):
            ref[...] = gr_s[place_ref[blocks] ^ k]
        for b in range(span // LANES):
            block = glacc_s[b * LANES:(b + 1) * LANES, :].T * scaling
            for k in range(fold):
                at = k * span + b * LANES
                gl_ref[:, at:at + LANES] = block[k * seqs:(k + 1) * seqs].astype(jnp.bfloat16)


def turn_kernel(pair_ref, cot_ref, shrink_ref, after_ref, pair_out_ref, cot_out_ref, back_ref, *, wide):
    for source, target in ((pair_ref, pair_out_ref), (cot_ref, cot_out_ref)):
        rows = source[...].reshape(-1, PAIR_W)
        for at in range(0, rows.shape[0], 2 * wide):
            target[0, :, at:at + 2 * wide] = jnp.concatenate(swapped(rows[at:at + 2 * wide], wide), axis=0).T
    back_ref[0] = dot_nn(shrink_ref[...], cot_out_ref[0].astype(jnp.bfloat16)).astype(jnp.bfloat16)


def turned_pairs(pair_features, cotangent, shrink_weight, after):
    rows, cols, _ = pair_features.shape
    fold = MXU_SIDE // HALF
    count = rows // (UNIT * fold)
    pairs = UNIT * fold * cols
    hidden = shrink_weight.shape[0]
    results = (
        jax.ShapeDtypeStruct((count, PAIR_W, pairs), jnp.float32),
        jax.ShapeDtypeStruct((count, PAIR_W, pairs), jnp.float32),
        jax.ShapeDtypeStruct((count, hidden, pairs), jnp.bfloat16),
    )
    block = pl.BlockSpec((UNIT * fold, cols, PAIR_W), lambda n: (n, 0, 0))
    return pl.pallas_call(
        functools.partial(turn_kernel, wide=fold * cols),
        grid=(count,),
        out_shape=results,
        in_specs=[block, block, whole_block(shrink_weight.shape), pl.BlockSpec(memory_space=pl.ANY)],
        out_specs=[pl.BlockSpec((1,) + v.shape[1:], lambda n: (n, 0, 0)) for v in results],
        compiler_params=pltpu.CompilerParams(
            dimension_semantics=("arbitrary",), vmem_limit_bytes=24 * 1024 * 1024
        ),
        cost_estimate=pl.CostEstimate(
            flops=2 * 2 * count * pairs * hidden * PAIR_W, bytes_accessed=4 * 4 * pair_features.size, transcendentals=0
        ),
        name="turned_pairs",
    )(pair_features, cotangent, shrink_weight, after)


def pair_tile(place, lefts, matrices, turned, shape, outer_bias, expand_weight):
    seqs = lefts[0].shape[-1] // 2
    row_parts = lefts[0].shape[0]
    rows, cols, _ = shape
    fold = MXU_SIDE // HALF
    groups = rows // fold
    unit = UNIT
    units = 2 if groups % (2 * unit) == 0 else 1
    steps = groups // unit // units
    wide = fold * cols
    span = groups * FACTOR_WIDTH
    channels = FACTOR_WIDTH * FACTOR_WIDTH
    block = pl.BlockSpec((unit * units * fold, cols, PAIR_W), lambda n, place: (n, 0, 0))
    resident = pl.BlockSpec(memory_space=pltpu.VMEM)
    operands = (
        *lefts, *matrices, *turned, jnp.broadcast_to(outer_bias[:, None], (PAIR_W, LANES)), expand_weight,
    )
    results = (
        jax.ShapeDtypeStruct(shape, jnp.float32),
        jax.ShapeDtypeStruct((seqs, rows * FACTOR_WIDTH), jnp.bfloat16),
    ) + row_parts * (jax.ShapeDtypeStruct((seqs // row_parts, cols * FACTOR_WIDTH), jnp.bfloat16),)
    padded = groups * wide
    macs = 3 * FACTOR_WIDTH * span * fold * seqs * wide + padded * (2 * channels * MXU_SIDE + 8 * MXU_SIDE * MXU_SIDE)
    return pl.pallas_call(
        functools.partial(
            pair_kernel, seqs=seqs, cols=cols, fold=fold, unit=unit, units=units, blocks=len(lefts)
        ),
        grid_spec=pltpu.PrefetchScalarGridSpec(
            num_scalar_prefetch=1,
            grid=(steps,),
            in_specs=[resident] * len(operands),
            out_specs=[block] + [resident] * (len(results) - 1),
            scratch_shapes=[
                pltpu.VMEM((FACTOR_WIDTH // CHUNK, span, CHUNK * wide), jnp.bfloat16),
                pltpu.VMEM((span, fold * seqs), jnp.bfloat16),
                pltpu.VMEM((fold * seqs, span), jnp.bfloat16),
                pltpu.VMEM((cols * FACTOR_WIDTH, max(seqs, LANES)), jnp.float32),
                pltpu.VMEM((span, fold * seqs), jnp.float32),
                pltpu.VMEM((len(lefts),) + lefts[0].shape, jnp.bfloat16),
                pltpu.VMEM((row_parts,) + results[2].shape, jnp.bfloat16),
            ],
        ),
        out_shape=results,
        compiler_params=pltpu.CompilerParams(
            dimension_semantics=("arbitrary",), vmem_limit_bytes=36 * 1024 * 1024
        ),
        cost_estimate=pl.CostEstimate(
            flops=2 * macs, bytes_accessed=rows * cols * PAIR_W * 4, transcendentals=0
        ),
        name="pair_tile",
    )(place, *operands)


def finish_kernel(place_ref, *refs, residues, fold):
    *gr_refs, gl_ref, returned_ref, updated_ref, left_ref, right_ref, x_s = refs
    part_seqs, res_count, width = updated_ref.shape
    total = gr_refs[0][...].astype(jnp.float32)
    for ref in gr_refs[1:]:
        total = total + ref[...].astype(jnp.float32)
    right_ref[...] = total
    for r in range(res_count):
        for n in range(width // LANES):
            at = r % residues * width + n * LANES
            piece = returned_ref[r // residues, 0, :, at:at + LANES]
            x_s[n, pl.ds(r, part_seqs, stride=res_count), :] = piece.astype(jnp.float32)
    for n in range(width // LANES):
        updated_ref[:, :, n * LANES:(n + 1) * LANES] = (
            x_s[n].reshape(part_seqs, res_count, LANES).astype(jnp.bfloat16)
        )
    total = gl_ref[0].astype(jnp.float32)
    for n in range(1, gl_ref.shape[0]):
        total = total + gl_ref[n].astype(jnp.float32)
    span = total.shape[1] // fold
    channel_block = lax.broadcasted_iota(jnp.int32, (1, LANES), 1) // FACTOR_WIDTH
    each = LANES // FACTOR_WIDTH
    for g in range(span // FACTOR_WIDTH):
        out = None
        for k in range(fold):
            at = k * span + g // each * LANES
            piece = total[:, at:at + LANES]
            shift = (k - g) % each * FACTOR_WIDTH
            piece = pltpu.roll(piece, shift, axis=1) if shift else piece
            out = piece if out is None else jnp.where(channel_block == k, piece, out)
        left_ref[:, g * LANES:(g + 1) * LANES] = out


def finish(place, gr, gl, returned, updated_shape):
    part_seqs, res_count, width = updated_shape
    residues = res_count // len(gr)
    own = pl.BlockSpec((returned.shape[0], 1) + returned.shape[2:], lambda n, place: (0, place[0], 0, 0))
    results = (
        jax.ShapeDtypeStruct(updated_shape, jnp.bfloat16),
        jax.ShapeDtypeStruct(gl.shape[1:], jnp.float32),
        jax.ShapeDtypeStruct(gr[0].shape, jnp.float32),
    )
    resident = pl.BlockSpec(memory_space=pltpu.VMEM)
    return pl.pallas_call(
        functools.partial(finish_kernel, residues=residues, fold=MXU_SIDE // HALF),
        grid_spec=pltpu.PrefetchScalarGridSpec(
            num_scalar_prefetch=1,
            grid=(1,),
            in_specs=[resident] * (len(gr) + 1) + [own],
            out_specs=[whole_block(v.shape) for v in results],
            scratch_shapes=[pltpu.VMEM((width // LANES, part_seqs * res_count, LANES), jnp.float32)],
        ),
        out_shape=results,
        compiler_params=pltpu.CompilerParams(
            dimension_semantics=("arbitrary",), vmem_limit_bytes=16 * 1024 * 1024
        ),
        name="finish",
    )(place, *gr, gl, returned)


def spread_out(q, count):
    return q if count % 2 else q % 2 * (count // 2) + q // 2


def local(
    alignment,
    pair_features,
    query_weight,
    key_weight,
    value_projection,
    gate_projection,
    gate_bias,
    output_projection,
    left_projection,
    right_projection,
    outer_weight,
    outer_bias,
    expand_weight,
    shrink_weight,
    cotangent,
):
    part_seqs, res_count, width = alignment.shape
    row_parts = lax.axis_size("row")
    col_parts = lax.axis_size("col")
    residues = res_count // row_parts
    own = jnp.transpose(alignment, (1, 0, 2)).reshape(row_parts, residues, part_seqs, width)
    columns = lax.all_to_all(own, "row", split_axis=0, concat_axis=0, tiled=True)
    attended, factors = attend(
        columns, query_weight, key_weight, value_projection, gate_projection, gate_bias,
        output_projection, left_projection, right_projection,
    )

    factors = lax.all_to_all(factors, "row", split_axis=0, concat_axis=0, tiled=True)
    left = factors[:, 0]
    ratio = col_parts // row_parts
    lefts, place = [], []
    for m in range(ratio):
        moves = [
            (q * col_parts + ratio * r + b, r * col_parts + ratio * spread_out(q, row_parts) + (b + m) % ratio)
            for q in range(row_parts)
            for r in range(row_parts)
            for b in range(ratio)
        ]
        lefts.append(lax.ppermute(left, ("row", "col"), moves))
        place.append((lax.axis_index("col") + ratio - m) % ratio)
    row = lax.axis_index("row")
    matrices = right_matrices(factors, outer_weight, expand_weight, shrink_weight)
    turned = turned_pairs(pair_features, cotangent, shrink_weight, matrices[-1])
    returned = lax.all_gather(lax.optimization_barrier((attended, *lefts))[0], "row", axis=0, tiled=False)
    pair_out, gl, *gr = pair_tile(
        jnp.stack(place + [row]).astype(jnp.int32), lefts, matrices, turned, pair_features.shape, outer_bias,
        expand_weight,
    )
    seqs, gl_width = gl.shape
    gr = gr[:1] + [
        lax.ppermute(v, "row", [(r, r ^ (k + 1)) for r in range(row_parts)]) for k, v in enumerate(gr[1:])
    ]
    gl = lax.all_to_all(
        gl.reshape(col_parts, seqs // col_parts, gl_width), "col", split_axis=0, concat_axis=0, tiled=True
    )
    updated, grad_left, grad_right = finish(
        row.astype(jnp.int32).reshape(1), gr, gl, returned, alignment.shape
    )
    return (updated, pair_out, grad_left, grad_right)


def solution(mesh):
    return jax.shard_map(
        local,
        mesh=mesh,
        in_specs=(P("row", "col", None), P("row", "col", None)) + (P(),) * 12 + (P("row", "col", None),),
        out_specs=(P("row", "col", None), P("row", "col", None), P("col", "row"), P("row", "col")),
        check_vma=False,
    )
```

```python
import functools

import jax
import jax.numpy as jnp
from jax import lax
from jax.experimental import pallas as pl
from jax.experimental.pallas import tpu as pltpu
from jax.sharding import PartitionSpec as P

ATTENTION_HEADS = 8
HEAD_WIDTH = 32
FACTOR_WIDTH = 32
PAIR_W = 128
EPSILON = 1e-05

LANES = 128
MXU_SIDE = 256
HALF = 64
TILE = 32
CHUNK = 4
UNIT = 4


def dot_nn(a, b):
    return lax.dot_general(a, b, (((1,), (0,)), ((), ())), preferred_element_type=jnp.float32)


def dot_nt(a, b):
    return lax.dot_general(a, b, (((1,), (1,)), ((), ())), preferred_element_type=jnp.float32)


def layer_normalise(rows):
    rows = rows.astype(jnp.float32)
    average = jnp.mean(rows, axis=-1, keepdims=True)
    centred = rows - average
    variance = jnp.mean(centred * centred, axis=-1, keepdims=True)
    return centred * lax.rsqrt(variance + EPSILON)


def attend_kernel(
    place_ref, x_ref, wq_ref, wk_ref, wv_ref, wg_ref, bias_ref, wo_ref, wl_ref, wr_ref, *refs,
):
    *upd_refs, factor_ref, q_s, k_s, v_s, g_s, a_s, w_s, bias_s, project_s, upd_s, ordered_s, sems = refs
    parts, residues, part_seqs, width = x_ref.shape
    seqs = parts * part_seqs
    sources = (wq_ref, wk_ref, wv_ref, wg_ref, wo_ref, bias_ref, wl_ref, wr_ref)
    targets = [w_s.at[n] for n in range(5)] + [bias_s, project_s.at[0], project_s.at[1]]
    copies = [pltpu.make_async_copy(a, b, sems.at[n]) for n, (a, b) in enumerate(zip(sources, targets))]
    for copy in copies:
        copy.start()
    x = jnp.concatenate([x_ref[s, r] for r in range(residues) for s in range(parts)], axis=0)
    normed = layer_normalise(x).astype(jnp.bfloat16)
    for n, ref in enumerate((q_s, k_s, v_s)):
        copies[n].wait()
        ref[...] = dot_nn(normed, w_s[n]).astype(jnp.bfloat16)
    copies[3].wait()
    copies[5].wait()
    g_s[...] = jax.nn.sigmoid(dot_nn(normed, w_s[3]) + bias_s[...])

    head_of = lax.broadcasted_iota(jnp.int32, (1, width), 1) // HEAD_WIDTH
    masks = [(head_of == h).astype(jnp.float32) for h in range(ATTENTION_HEADS)]
    masks_low = [m.astype(jnp.bfloat16) for m in masks]

    def one_residue(r, carry):
        rows = pl.ds(pl.multiple_of(r * seqs, seqs), seqs)
        query = q_s[rows, :]
        spread_query = jnp.concatenate([query * m for m in masks_low], axis=0)
        scores = dot_nt(spread_query, k_s[rows, :]) * HEAD_WIDTH ** (-0.5)
        raised = jnp.exp(scores - jnp.max(scores, axis=-1, keepdims=True))
        inverse = 1.0 / jnp.sum(raised, axis=-1, keepdims=True)
        blended = dot_nn(raised.astype(jnp.bfloat16), v_s[rows, :]) * inverse
        total = blended[:seqs] * masks[0]
        for h in range(1, ATTENTION_HEADS):
            total = total + blended[h * seqs:(h + 1) * seqs] * masks[h]
        a_s[rows, :] = (g_s[rows, :] * total).astype(jnp.bfloat16)
        return carry

    lax.fori_loop(0, residues, one_residue, 0, unroll=6 if residues % 6 == 0 else 2)

    copies[4].wait()
    updated = (x.astype(jnp.float32) + dot_nn(a_s[...], w_s[4])).astype(jnp.bfloat16)
    for r in range(residues):
        for s in range(parts):
            begin = r * seqs + s * part_seqs
            upd_s[s, :, r * width:(r + 1) * width] = updated[begin:begin + part_seqs]
    leaving = []
    for k, ref in enumerate(upd_refs):
        ordered_s[k] = upd_s[place_ref[0] ^ k]
        leaving.append(pltpu.make_async_copy(ordered_s.at[k], ref, sems.at[len(sources) + k]))
        leaving[k].start()
    factor_norm = layer_normalise(updated).astype(jnp.bfloat16)
    copies[6].wait()
    copies[7].wait()
    project = project_s[...].reshape(2 * FACTOR_WIDTH, width)
    for p in range(residues // 2):
        both = dot_nt(project, factor_norm[p * 2 * seqs:(p + 1) * 2 * seqs]).astype(jnp.bfloat16)
        for n in range(parts):
            factor_ref[n, 0, p] = both[:FACTOR_WIDTH]
            factor_ref[n, 1, p] = both[FACTOR_WIDTH:]
    for copy in leaving:
        copy.wait()


def whole_block(shape):
    return pl.BlockSpec(shape, lambda *_: (0,) * len(shape))


def in_hbm(*arrays):
    return [pltpu.with_memory_space_constraint(v, pltpu.HBM) for v in arrays]


def attend(place, x, wq, wk, wv, wg, gate_bias, wo, wl, wr):
    parts, residues, part_seqs, width = x.shape
    seqs = parts * part_seqs
    rows = residues * seqs
    operands = in_hbm(wq, wk, wv, wg, gate_bias.reshape(1, -1), wo, wl.T, wr.T)
    resident = pl.BlockSpec(memory_space=pltpu.VMEM)
    results = parts * (pltpu.HBM((part_seqs, residues * width), jnp.bfloat16),) + (
        jax.ShapeDtypeStruct((parts, 2, residues // 2, FACTOR_WIDTH, 2 * seqs), jnp.bfloat16),
    )
    macs = rows * width * (5 * width + 2 * FACTOR_WIDTH) + 2 * rows * ATTENTION_HEADS * width * seqs
    return pl.pallas_call(
        attend_kernel,
        out_shape=results,
        in_specs=[pl.BlockSpec(memory_space=pltpu.SMEM), resident]
        + [pl.BlockSpec(memory_space=pltpu.HBM)] * len(operands),
        out_specs=[pl.BlockSpec(memory_space=pltpu.HBM)] * parts + [resident],
        scratch_shapes=[
            pltpu.VMEM((rows, width), jnp.bfloat16),
            pltpu.VMEM((rows, width), jnp.bfloat16),
            pltpu.VMEM((rows, width), jnp.bfloat16),
            pltpu.VMEM((rows, width), jnp.float32),
            pltpu.VMEM((rows, width), jnp.bfloat16),
            pltpu.VMEM((5,) + wq.shape, jnp.bfloat16),
            pltpu.VMEM((1, width), jnp.float32),
            pltpu.VMEM((2, FACTOR_WIDTH, width), jnp.bfloat16),
            pltpu.VMEM((parts,) + results[0].shape, jnp.bfloat16),
            pltpu.VMEM((parts,) + results[0].shape, jnp.bfloat16),
            pltpu.SemaphoreType.DMA((len(operands) + parts,)),
        ],
        compiler_params=pltpu.CompilerParams(vmem_limit_bytes=32 * 1024 * 1024),
        cost_estimate=pl.CostEstimate(flops=2 * macs, bytes_accessed=4 * x.size * 2, transcendentals=rows * width),
        name="column_attention",
    )(place, x, *operands)


def first_of_four(at, cols):
    wide = MXU_SIDE // HALF * cols
    inside = jnp.where(at < wide, at, jnp.where(at < wide + HALF, at - HALF, at - wide - HALF))
    return inside // cols


def swapped(pair, wide):
    return [pair[:wide], pair[2 * wide - HALF:], pair[wide:2 * wide - HALF]]


def unswapped(pair, wide):
    return [pair[:wide], pair[wide + HALF:], pair[wide:wide + HALF]]


def right_kernel(
    factor_ref, w_ref, expand_ref, shrink_ref, rbd_ref, rbdt_ref, wec_ref, wt_ref, et_ref, st_ref, stage_s,
    *, seqs, cols, fold,
):
    each = factor_ref.shape[2]
    wide = fold * cols
    stage_lanes = stage_s.shape[1]
    low_half = lax.broadcasted_iota(jnp.int32, (1, LANES), 1) < HALF

    stage_s[:FACTOR_WIDTH * FACTOR_WIDTH, :LANES] = w_ref[...].astype(jnp.float32)
    for e in range(FACTOR_WIDTH):
        piece = stage_s[pl.ds(e, FACTOR_WIDTH, stride=FACTOR_WIDTH), :LANES]
        wec_ref[e * FACTOR_WIDTH:(e + 1) * FACTOR_WIDTH, :] = piece.astype(jnp.bfloat16)
    for b in range(FACTOR_WIDTH * FACTOR_WIDTH // LANES):
        block = wec_ref[b * LANES:(b + 1) * LANES, :].astype(jnp.float32)
        wt_ref[:, b * LANES:(b + 1) * LANES] = block.T.astype(jnp.bfloat16)
    et_ref[...] = expand_ref[...].astype(jnp.float32).T.astype(jnp.bfloat16)
    st_ref[...] = shrink_ref[...].astype(jnp.float32).T.astype(jnp.bfloat16)

    for p in range(cols // 2):
        block = factor_ref[p // each, 1, p % each].astype(jnp.float32)
        even = 2 * p * FACTOR_WIDTH
        odd = even + FACTOR_WIDTH
        if seqs % LANES == 0:
            stage_s[even:even + FACTOR_WIDTH, :] = block[:, :seqs]
            stage_s[odd:odd + FACTOR_WIDTH, :] = block[:, seqs:]
        else:
            stage_s[even:even + FACTOR_WIDTH, :] = block
            stage_s[odd:odd + FACTOR_WIDTH, :] = pltpu.roll(block, HALF, axis=1)

    row_k = first_of_four(lax.broadcasted_iota(jnp.int32, (2 * wide, 1), 0), cols)
    lane_k = first_of_four(lax.broadcasted_iota(jnp.int32, (1, 2 * wide), 1), cols)
    for e in range(0, FACTOR_WIDTH, 2):
        two = []
        for u in (e, e + 1):
            two += [stage_s[pl.ds(u, cols, stride=FACTOR_WIDTH), :]] * fold
        upright = jnp.concatenate(swapped(jnp.concatenate(two, axis=0), wide), axis=0)
        chunk, at = e // CHUNK, e % CHUNK * wide
        rolled = pltpu.roll(upright, HALF, axis=1) if seqs < LANES else None
        for v in range(fold * seqs // stage_lanes):
            if seqs < LANES:
                value = jnp.where(
                    low_half, jnp.where(row_k == 2 * v, upright, 0.0), jnp.where(row_k == 2 * v + 1, rolled, 0.0)
                )
            else:
                value = jnp.where(row_k == v, upright, 0.0)
            rbdt_ref[chunk, at:at + 2 * wide, v * stage_lanes:(v + 1) * stage_lanes] = value.astype(jnp.bfloat16)
        turned = upright.T[:seqs]
        for k in range(fold):
            value = jnp.where(lane_k == k, turned, 0.0).astype(jnp.bfloat16)
            rbd_ref[chunk, k * seqs:(k + 1) * seqs, at:at + 2 * wide] = value


def right_matrices(factors, outer_weight, expand_weight, shrink_weight):
    row_parts, _, each, _, lanes = factors.shape
    seqs, cols = lanes // 2, 2 * each * row_parts
    fold = MXU_SIDE // HALF
    channels, width = outer_weight.shape
    results = (
        jax.ShapeDtypeStruct((FACTOR_WIDTH // CHUNK, fold * seqs, CHUNK * fold * cols), jnp.bfloat16),
        jax.ShapeDtypeStruct((FACTOR_WIDTH // CHUNK, CHUNK * fold * cols, fold * seqs), jnp.bfloat16),
        jax.ShapeDtypeStruct((channels, width), jnp.bfloat16),
        jax.ShapeDtypeStruct((width, channels), jnp.bfloat16),
        jax.ShapeDtypeStruct(expand_weight.shape[::-1], jnp.bfloat16),
        jax.ShapeDtypeStruct(shrink_weight.shape[::-1], jnp.bfloat16),
    )
    resident = pl.BlockSpec(memory_space=pltpu.VMEM)
    return pl.pallas_call(
        functools.partial(right_kernel, seqs=seqs, cols=cols, fold=fold),
        out_shape=results,
        in_specs=[resident] * 4,
        out_specs=[resident] * len(results),
        scratch_shapes=[pltpu.VMEM((max(cols * FACTOR_WIDTH, channels), max(seqs, LANES)), jnp.float32)],
        compiler_params=pltpu.CompilerParams(vmem_limit_bytes=16 * 1024 * 1024),
        cost_estimate=pl.CostEstimate(flops=6 * 10**9, bytes_accessed=4 * results[0].size, transcendentals=0),
        name="right_matrices",
    )(factors, outer_weight, expand_weight, shrink_weight)


def pair_kernel(
    place_ref, *refs, seqs, cols, fold, unit, units, blocks,
):
    left_refs, refs = refs[:blocks], refs[blocks:]
    rbd_s, rbdt_s, wec_s, wt_s, et_ref, st_ref, pair_ref, cot_ref, back_ref = refs[:9]
    bias_ref, expand_ref, out_ref, gl_ref = refs[9:13]
    gr_refs, (outer_s, l_s, lt_s, stage_s, glacc_s, lblk_s, gr_s) = refs[13:-7], refs[-7:]
    step = pl.program_id(0)
    row_parts, each = left_refs[0].shape[:2]
    span = l_s.shape[0]
    groups = span // FACTOR_WIDTH
    wide = fold * cols
    scaling = 1.0 / seqs
    low_half = lax.broadcasted_iota(jnp.int32, (1, LANES), 1) < HALF

    @pl.when(step == 0)
    def _prologue():
        for n, ref in enumerate(left_refs):
            lblk_s[place_ref[n]] = ref[...]
        pairs = fold // 2
        for p in range(groups * pairs):
            column, inside = divmod(p, row_parts * each)
            block = lblk_s[column, inside // each, inside % each]
            g, at = p // pairs, p % pairs * 2 * seqs
            l_s[g * FACTOR_WIDTH:(g + 1) * FACTOR_WIDTH, at:at + 2 * seqs] = (
                block.astype(jnp.float32) * scaling
            ).astype(jnp.bfloat16)
        for b in range(span // LANES):
            block = l_s[b * LANES:(b + 1) * LANES, :].astype(jnp.float32)
            lt_s[:, b * LANES:(b + 1) * LANES] = block.T.astype(jnp.bfloat16)

        def some_outers(n, carry):
            outer_s[n] = dot_nn(l_s[...], rbd_s[n]).astype(jnp.bfloat16)
            return carry

        lax.fori_loop(0, outer_s.shape[0], some_outers, 0, unroll=2)

    def unit_rows(u):
        at = (step * units + u) * unit * FACTOR_WIDTH
        return pl.ds(pl.multiple_of(at, unit * FACTOR_WIDTH), unit * FACTOR_WIDTH)

    def group(block, g):
        return block[g * FACTOR_WIDTH:(g + 1) * FACTOR_WIDTH]

    def forward(u):
        stacked = []
        for e in range(0, FACTOR_WIDTH, 2):
            at = e % CHUNK * wide
            block = outer_s[e // CHUNK, unit_rows(u), at:at + 2 * wide]
            shared = block[:, LANES:2 * LANES]
            rolled = pltpu.roll(shared, HALF, axis=1)
            even, odd = [], []
            for g in range(0, unit, 2):
                a, b = block[:, :LANES], block[:, 2 * LANES:]
                even += [group(a, g), jnp.where(low_half, group(shared, g), group(rolled, g + 1)), group(a, g + 1)]
                odd += [group(b, g), jnp.where(low_half, group(rolled, g), group(shared, g + 1)), group(b, g + 1)]
            stacked += [jnp.concatenate(even, axis=1), jnp.concatenate(odd, axis=1)]
        projected = dot_nn(wt_s[...], jnp.concatenate(stacked, axis=0))
        middles, inverses, spreads = [], [], []
        for at in range(0, projected.shape[1], LANES):
            middle = pair_ref[step * units + u, :, at:at + LANES] + projected[:, at:at + LANES] + bias_ref[...]
            average = jnp.mean(middle, axis=0, keepdims=True)
            centred = middle - average
            variance = jnp.mean(centred * centred, axis=0, keepdims=True)
            inverse = lax.rsqrt(variance + EPSILON)
            middles.append(middle)
            inverses.append(inverse)
            spreads.append(centred * inverse)
        spread_low = jnp.concatenate([v.astype(jnp.bfloat16) for v in spreads], axis=1)
        return middles, inverses, spreads, dot_nn(et_ref[...], spread_low)

    def backward(u, middles, inverses, spreads, before):
        rows, pairs = before.shape
        hidden, back_before = [], []
        for at in range(0, rows, TILE):
            hidden_parts, back_parts = [], []
            for v in range(0, pairs, MXU_SIDE):
                x = before[at:at + TILE, v:v + MXU_SIDE]
                back = back_ref[step * units + u, at:at + TILE, v:v + MXU_SIDE].astype(jnp.float32)
                phi = 0.5 * (1.0 + lax.erf(x * 0.7071067811865476))
                slope = phi + x * jnp.exp(-0.5 * x * x) * 0.3989422804014327
                hidden_parts.append((x * phi).astype(jnp.bfloat16))
                back_parts.append((back * slope).astype(jnp.bfloat16))
            hidden.append(jnp.concatenate(hidden_parts, axis=1))
            back_before.append(jnp.concatenate(back_parts, axis=1))
        back_spread = dot_nn(expand_ref[...], jnp.concatenate(back_before, axis=0))
        change = dot_nn(st_ref[...], jnp.concatenate(hidden, axis=0))
        back_middle = []
        for n, at in enumerate(range(0, pairs, LANES)):
            back, spread = back_spread[:, at:at + LANES], spreads[n]
            centre_term = jnp.mean(back, axis=0, keepdims=True)
            slope_term = jnp.mean(back * spread, axis=0, keepdims=True)
            back = back - centre_term - spread * slope_term
            back = cot_ref[step * units + u, :, at:at + LANES] + inverses[n] * back
            back_middle.append(back.astype(jnp.bfloat16))
        result = (jnp.concatenate(middles, axis=1) + change).T
        pieces = []
        for g in range(0, unit, 2):
            pieces += unswapped(result[g * wide:(g + 2) * wide], wide)
        out_ref[u * unit * fold:(u + 1) * unit * fold] = jnp.concatenate(pieces, axis=0).reshape(
            unit * fold, cols, PAIR_W
        )
        back_outer = dot_nn(wec_s[...], jnp.concatenate(back_middle, axis=1)).astype(jnp.bfloat16)
        for e in range(0, FACTOR_WIDTH, 2):
            even, odd = group(back_outer, e), group(back_outer, e + 1)
            a, shared, b = [], [], []
            for g in range(0, unit, 2):
                at = g * wide
                of_even, of_odd = even[:, at + LANES:at + 2 * LANES], odd[:, at + LANES:at + 2 * LANES]
                a += [even[:, at:at + LANES], even[:, at + 2 * LANES:at + 3 * LANES]]
                b += [odd[:, at:at + LANES], odd[:, at + 2 * LANES:at + 3 * LANES]]
                shared += [
                    jnp.where(low_half, of_even, pltpu.roll(of_odd, HALF, axis=1)),
                    jnp.where(low_half, pltpu.roll(of_even, HALF, axis=1), of_odd),
                ]
            for n, pieces in enumerate((a, shared, b)):
                at = e % CHUNK * wide + n * LANES
                outer_s[e // CHUNK, unit_rows(u), at:at + LANES] = jnp.concatenate(pieces, axis=0)

    held = forward(0)
    for u in range(units):
        ahead = forward(u + 1) if u + 1 < units else None
        backward(u, *held)
        held = ahead

    @pl.when(step == pl.num_programs(0) - 1)
    def _epilogue():
        glacc_s[...] = jnp.zeros_like(glacc_s)
        empty = jnp.zeros((LANES - seqs % LANES, CHUNK * wide), jnp.float32) if seqs % LANES else None
        at = lax.broadcasted_iota(jnp.int32, (1, CHUNK * wide), 1)
        lane_k = first_of_four(lax.rem(at, 2 * wide), cols)

        def some(n, carry):
            back = outer_s[n]
            glacc_s[...] += dot_nn(back, rbdt_s[n])
            full = dot_nn(lt_s[...], back)
            compact = full[:seqs]
            for k in range(1, fold):
                compact = jnp.where(lane_k == k, full[k * seqs:(k + 1) * seqs], compact)
            if empty is not None:
                compact = jnp.concatenate([compact, empty], axis=0)
            turned = compact.T
            for p in range(CHUNK // 2):
                two = jnp.concatenate(unswapped(turned[2 * p * wide:2 * (p + 1) * wide], wide), axis=0)
                for u in range(2):
                    total = two[u * wide:u * wide + cols]
                    for k in range(1, fold):
                        total = total + two[u * wide + k * cols:u * wide + (k + 1) * cols]
                    stage_s[pl.ds(n * CHUNK + 2 * p + u, cols, stride=FACTOR_WIDTH), :] = total
            return carry

        lax.fori_loop(0, outer_s.shape[0], some, 0, unroll=2)
        for b in range(cols * FACTOR_WIDTH // LANES):
            block = stage_s[b * LANES:(b + 1) * LANES, :].T[:seqs].astype(jnp.bfloat16)
            gr_s[:, :, b * LANES:(b + 1) * LANES] = block.reshape(row_parts, -1, LANES)
        for k, ref in enumerate(gr_refs):
            ref[...] = gr_s[place_ref[blocks] ^ k]
        for b in range(span // LANES):
            block = glacc_s[b * LANES:(b + 1) * LANES, :].T * scaling
            for k in range(fold):
                at = k * span + b * LANES
                gl_ref[:, at:at + LANES] = block[k * seqs:(k + 1) * seqs].astype(jnp.bfloat16)


def turn_kernel(pair_ref, cot_ref, shrink_ref, after_ref, pair_out_ref, cot_out_ref, back_ref, *, wide):
    for source, target in ((pair_ref, pair_out_ref), (cot_ref, cot_out_ref)):
        rows = source[...].reshape(-1, PAIR_W)
        for at in range(0, rows.shape[0], 2 * wide):
            target[0, :, at:at + 2 * wide] = jnp.concatenate(swapped(rows[at:at + 2 * wide], wide), axis=0).T
    back_ref[0] = dot_nn(shrink_ref[...], cot_out_ref[0].astype(jnp.bfloat16)).astype(jnp.bfloat16)


def turned_pairs(pair_features, cotangent, shrink_weight, after):
    rows, cols, _ = pair_features.shape
    fold = MXU_SIDE // HALF
    count = rows // (UNIT * fold)
    pairs = UNIT * fold * cols
    hidden = shrink_weight.shape[0]
    results = (
        jax.ShapeDtypeStruct((count, PAIR_W, pairs), jnp.float32),
        jax.ShapeDtypeStruct((count, PAIR_W, pairs), jnp.float32),
        jax.ShapeDtypeStruct((count, hidden, pairs), jnp.bfloat16),
    )
    block = pl.BlockSpec((UNIT * fold, cols, PAIR_W), lambda n: (n, 0, 0))
    return pl.pallas_call(
        functools.partial(turn_kernel, wide=fold * cols),
        grid=(count,),
        out_shape=results,
        in_specs=[block, block, whole_block(shrink_weight.shape), pl.BlockSpec(memory_space=pl.ANY)],
        out_specs=[pl.BlockSpec((1,) + v.shape[1:], lambda n: (n, 0, 0)) for v in results],
        compiler_params=pltpu.CompilerParams(
            dimension_semantics=("arbitrary",), vmem_limit_bytes=24 * 1024 * 1024
        ),
        cost_estimate=pl.CostEstimate(
            flops=2 * 2 * count * pairs * hidden * PAIR_W, bytes_accessed=4 * 4 * pair_features.size, transcendentals=0
        ),
        name="turned_pairs",
    )(pair_features, cotangent, shrink_weight, after)


def pair_tile(place, lefts, matrices, turned, shape, outer_bias, expand_weight):
    seqs = lefts[0].shape[-1] // 2
    row_parts = lefts[0].shape[0]
    rows, cols, _ = shape
    fold = MXU_SIDE // HALF
    groups = rows // fold
    unit = UNIT
    units = 2 if groups % (2 * unit) == 0 else 1
    steps = groups // unit // units
    wide = fold * cols
    span = groups * FACTOR_WIDTH
    channels = FACTOR_WIDTH * FACTOR_WIDTH
    block = pl.BlockSpec((unit * units * fold, cols, PAIR_W), lambda n, place: (n, 0, 0))
    resident = pl.BlockSpec(memory_space=pltpu.VMEM)
    operands = (
        *lefts, *matrices, *turned, jnp.broadcast_to(outer_bias[:, None], (PAIR_W, LANES)), expand_weight,
    )
    results = (
        jax.ShapeDtypeStruct(shape, jnp.float32),
        jax.ShapeDtypeStruct((seqs, rows * FACTOR_WIDTH), jnp.bfloat16),
    ) + row_parts * (jax.ShapeDtypeStruct((seqs // row_parts, cols * FACTOR_WIDTH), jnp.bfloat16),)
    padded = groups * wide
    macs = 3 * FACTOR_WIDTH * span * fold * seqs * wide + padded * (2 * channels * MXU_SIDE + 8 * MXU_SIDE * MXU_SIDE)
    return pl.pallas_call(
        functools.partial(
            pair_kernel, seqs=seqs, cols=cols, fold=fold, unit=unit, units=units, blocks=len(lefts)
        ),
        grid_spec=pltpu.PrefetchScalarGridSpec(
            num_scalar_prefetch=1,
            grid=(steps,),
            in_specs=[resident] * len(operands),
            out_specs=[block] + [resident] * (len(results) - 1),
            scratch_shapes=[
                pltpu.VMEM((FACTOR_WIDTH // CHUNK, span, CHUNK * wide), jnp.bfloat16),
                pltpu.VMEM((span, fold * seqs), jnp.bfloat16),
                pltpu.VMEM((fold * seqs, span), jnp.bfloat16),
                pltpu.VMEM((cols * FACTOR_WIDTH, max(seqs, LANES)), jnp.float32),
                pltpu.VMEM((span, fold * seqs), jnp.float32),
                pltpu.VMEM((len(lefts),) + lefts[0].shape, jnp.bfloat16),
                pltpu.VMEM((row_parts,) + results[2].shape, jnp.bfloat16),
            ],
        ),
        out_shape=results,
        compiler_params=pltpu.CompilerParams(
            dimension_semantics=("arbitrary",), vmem_limit_bytes=36 * 1024 * 1024
        ),
        cost_estimate=pl.CostEstimate(
            flops=2 * macs, bytes_accessed=rows * cols * PAIR_W * 4, transcendentals=0
        ),
        name="pair_tile",
    )(place, *operands)


def finish_kernel(place_ref, *refs, residues, fold):
    *part_refs, gl_ref, updated_ref, left_ref, right_ref, x_s = refs
    upd_refs, gr_refs = part_refs[:len(part_refs) // 2], part_refs[len(part_refs) // 2:]
    part_seqs, res_count, width = updated_ref.shape
    total = gr_refs[0][...].astype(jnp.float32)
    for ref in gr_refs[1:]:
        total = total + ref[...].astype(jnp.float32)
    right_ref[...] = total
    for k, ref in enumerate(upd_refs):
        first = (place_ref[0] ^ k) * residues
        for r in range(residues):
            for n in range(width // LANES):
                at = r * width + n * LANES
                x_s[n, pl.ds(first + r, part_seqs, stride=res_count), :] = ref[:, at:at + LANES].astype(jnp.float32)
    for n in range(width // LANES):
        updated_ref[:, :, n * LANES:(n + 1) * LANES] = (
            x_s[n].reshape(part_seqs, res_count, LANES).astype(jnp.bfloat16)
        )
    total = gl_ref[0].astype(jnp.float32)
    for n in range(1, gl_ref.shape[0]):
        total = total + gl_ref[n].astype(jnp.float32)
    span = total.shape[1] // fold
    channel_block = lax.broadcasted_iota(jnp.int32, (1, LANES), 1) // FACTOR_WIDTH
    each = LANES // FACTOR_WIDTH
    for g in range(span // FACTOR_WIDTH):
        out = None
        for k in range(fold):
            at = k * span + g // each * LANES
            piece = total[:, at:at + LANES]
            shift = (k - g) % each * FACTOR_WIDTH
            piece = pltpu.roll(piece, shift, axis=1) if shift else piece
            out = piece if out is None else jnp.where(channel_block == k, piece, out)
        left_ref[:, g * LANES:(g + 1) * LANES] = out


def finish(place, returned, gr, gl, updated_shape):
    part_seqs, res_count, width = updated_shape
    residues = res_count // len(returned)
    results = (
        jax.ShapeDtypeStruct(updated_shape, jnp.bfloat16),
        jax.ShapeDtypeStruct(gl.shape[1:], jnp.float32),
        jax.ShapeDtypeStruct(gr[0].shape, jnp.float32),
    )
    resident = pl.BlockSpec(memory_space=pltpu.VMEM)
    return pl.pallas_call(
        functools.partial(finish_kernel, residues=residues, fold=MXU_SIDE // HALF),
        grid_spec=pltpu.PrefetchScalarGridSpec(
            num_scalar_prefetch=1,
            grid=(1,),
            in_specs=[resident] * (len(returned) + len(gr) + 1),
            out_specs=[whole_block(v.shape) for v in results],
            scratch_shapes=[pltpu.VMEM((width // LANES, part_seqs * res_count, LANES), jnp.float32)],
        ),
        out_shape=results,
        compiler_params=pltpu.CompilerParams(
            dimension_semantics=("arbitrary",), vmem_limit_bytes=16 * 1024 * 1024
        ),
        name="finish",
    )(place, *returned, *gr, gl)


def spread_out(q, count):
    return q if count % 2 else q % 2 * (count // 2) + q // 2


def local(
    alignment,
    pair_features,
    query_weight,
    key_weight,
    value_projection,
    gate_projection,
    gate_bias,
    output_projection,
    left_projection,
    right_projection,
    outer_weight,
    outer_bias,
    expand_weight,
    shrink_weight,
    cotangent,
):
    part_seqs, res_count, width = alignment.shape
    row_parts = lax.axis_size("row")
    col_parts = lax.axis_size("col")
    residues = res_count // row_parts
    own = jnp.transpose(alignment, (1, 0, 2)).reshape(row_parts, residues, part_seqs, width)
    columns = lax.all_to_all(own, "row", split_axis=0, concat_axis=0, tiled=True)
    row = lax.axis_index("row")
    own_row = row.astype(jnp.int32).reshape(1)
    *attended, factors = attend(
        own_row, columns, query_weight, key_weight, value_projection, gate_projection, gate_bias,
        output_projection, left_projection, right_projection,
    )

    factors = lax.all_to_all(factors, "row", split_axis=0, concat_axis=0, tiled=True)
    left = factors[:, 0]
    ratio = col_parts // row_parts
    lefts, place = [], []
    for m in range(ratio):
        moves = [
            (q * col_parts + ratio * r + b, r * col_parts + ratio * spread_out(q, row_parts) + (b + m) % ratio)
            for q in range(row_parts)
            for r in range(row_parts)
            for b in range(ratio)
        ]
        lefts.append(lax.ppermute(left, ("row", "col"), moves))
        place.append((lax.axis_index("col") + ratio - m) % ratio)
    matrices = right_matrices(factors, outer_weight, expand_weight, shrink_weight)
    turned = turned_pairs(pair_features, cotangent, shrink_weight, matrices[-1])

    def to_rows(values):
        return values[:1] + [
            lax.ppermute(v, "row", [(r, r ^ (k + 1)) for r in range(row_parts)]) for k, v in enumerate(values[1:])
        ]

    returned = to_rows(attended)
    lefts, returned = lax.optimization_barrier((lefts, returned))
    pair_out, gl, *gr = pair_tile(
        jnp.stack(place + [row]).astype(jnp.int32), lefts, matrices, turned, pair_features.shape, outer_bias,
        expand_weight,
    )
    seqs, gl_width = gl.shape
    gr = to_rows(gr)
    gl = lax.all_to_all(
        gl.reshape(col_parts, seqs // col_parts, gl_width), "col", split_axis=0, concat_axis=0, tiled=True
    )
    updated, grad_left, grad_right = finish(own_row, returned, gr, gl, alignment.shape)
    return (updated, pair_out, grad_left, grad_right)


def solution(mesh):
    return jax.shard_map(
        local,
        mesh=mesh,
        in_specs=(P("row", "col", None), P("row", "col", None)) + (P(),) * 12 + (P("row", "col", None),),
        out_specs=(P("row", "col", None), P("row", "col", None), P("col", "row"), P("row", "col")),
        check_vma=False,
    )
```

```python
import functools

import jax
import jax.numpy as jnp
from jax import lax
from jax.experimental import pallas as pl
from jax.experimental.pallas import tpu as pltpu
from jax.sharding import PartitionSpec as P

ATTENTION_HEADS = 8
HEAD_WIDTH = 32
FACTOR_WIDTH = 32
PAIR_W = 128
EPSILON = 1e-05

LANES = 128
MXU_SIDE = 256
HALF = 64
TILE = 32
CHUNK = 4
UNIT = 4


def dot_nn(a, b):
    return lax.dot_general(a, b, (((1,), (0,)), ((), ())), preferred_element_type=jnp.float32)


def dot_nt(a, b):
    return lax.dot_general(a, b, (((1,), (1,)), ((), ())), preferred_element_type=jnp.float32)


def layer_normalise(rows):
    rows = rows.astype(jnp.float32)
    average = jnp.mean(rows, axis=-1, keepdims=True)
    centred = rows - average
    variance = jnp.mean(centred * centred, axis=-1, keepdims=True)
    return centred * lax.rsqrt(variance + EPSILON)


def attend_kernel(
    x_ref, wq_ref, wk_ref, wv_ref, wg_ref, bias_ref, wo_ref, wl_ref, wr_ref, *refs,
):
    row = lax.axis_index("row")
    *upd_refs, factor_ref, q_s, k_s, v_s, g_s, a_s, w_s, bias_s, project_s, upd_s, ordered_s, sems = refs
    parts, residues, part_seqs, width = x_ref.shape
    seqs = parts * part_seqs
    sources = (wq_ref, wk_ref, wv_ref, wg_ref, wo_ref, bias_ref, wl_ref, wr_ref)
    targets = [w_s.at[n] for n in range(5)] + [bias_s, project_s.at[0], project_s.at[1]]
    copies = [pltpu.make_async_copy(a, b, sems.at[n]) for n, (a, b) in enumerate(zip(sources, targets))]
    for copy in copies:
        copy.start()
    x = jnp.concatenate([x_ref[s, r] for r in range(residues) for s in range(parts)], axis=0)
    normed = layer_normalise(x).astype(jnp.bfloat16)
    for n, ref in enumerate((q_s, k_s, v_s)):
        copies[n].wait()
        ref[...] = dot_nn(normed, w_s[n]).astype(jnp.bfloat16)
    copies[3].wait()
    copies[5].wait()
    g_s[...] = jax.nn.sigmoid(dot_nn(normed, w_s[3]) + bias_s[...])

    head_of = lax.broadcasted_iota(jnp.int32, (1, width), 1) // HEAD_WIDTH
    masks = [(head_of == h).astype(jnp.float32) for h in range(ATTENTION_HEADS)]
    masks_low = [m.astype(jnp.bfloat16) for m in masks]

    def one_residue(r, carry):
        rows = pl.ds(pl.multiple_of(r * seqs, seqs), seqs)
        query = q_s[rows, :]
        spread_query = jnp.concatenate([query * m for m in masks_low], axis=0)
        scores = dot_nt(spread_query, k_s[rows, :]) * HEAD_WIDTH ** (-0.5)
        raised = jnp.exp(scores - jnp.max(scores, axis=-1, keepdims=True))
        inverse = 1.0 / jnp.sum(raised, axis=-1, keepdims=True)
        blended = dot_nn(raised.astype(jnp.bfloat16), v_s[rows, :]) * inverse
        total = blended[:seqs] * masks[0]
        for h in range(1, ATTENTION_HEADS):
            total = total + blended[h * seqs:(h + 1) * seqs] * masks[h]
        a_s[rows, :] = (g_s[rows, :] * total).astype(jnp.bfloat16)
        return carry

    lax.fori_loop(0, residues, one_residue, 0, unroll=6 if residues % 6 == 0 else 2)

    copies[4].wait()
    updated = (x.astype(jnp.float32) + dot_nn(a_s[...], w_s[4])).astype(jnp.bfloat16)
    for r in range(residues):
        for s in range(parts):
            begin = r * seqs + s * part_seqs
            upd_s[s, :, r * width:(r + 1) * width] = updated[begin:begin + part_seqs]
    leaving = []
    for k, ref in enumerate(upd_refs):
        ordered_s[k] = upd_s[row ^ k]
        leaving.append(pltpu.make_async_copy(ordered_s.at[k], ref, sems.at[len(sources) + k]))
        leaving[k].start()
    factor_norm = layer_normalise(updated).astype(jnp.bfloat16)
    copies[6].wait()
    copies[7].wait()
    project = project_s[...].reshape(2 * FACTOR_WIDTH, width)
    for p in range(residues // 2):
        both = dot_nt(project, factor_norm[p * 2 * seqs:(p + 1) * 2 * seqs]).astype(jnp.bfloat16)
        for n in range(parts):
            factor_ref[n, 0, p] = both[:FACTOR_WIDTH]
            factor_ref[n, 1, p] = both[FACTOR_WIDTH:]
    for copy in leaving:
        copy.wait()


def whole_block(shape):
    return pl.BlockSpec(shape, lambda *_: (0,) * len(shape))


def in_hbm(*arrays):
    return [pltpu.with_memory_space_constraint(v, pltpu.HBM) for v in arrays]


def attend(x, wq, wk, wv, wg, gate_bias, wo, wl, wr):
    parts, residues, part_seqs, width = x.shape
    seqs = parts * part_seqs
    rows = residues * seqs
    operands = in_hbm(wq, wk, wv, wg, gate_bias.reshape(1, -1), wo, wl.T, wr.T)
    resident = pl.BlockSpec(memory_space=pltpu.VMEM)
    results = parts * (pltpu.HBM((part_seqs, residues * width), jnp.bfloat16),) + (
        jax.ShapeDtypeStruct((parts, 2, residues // 2, FACTOR_WIDTH, 2 * seqs), jnp.bfloat16),
    )
    macs = rows * width * (5 * width + 2 * FACTOR_WIDTH) + 2 * rows * ATTENTION_HEADS * width * seqs
    return pl.pallas_call(
        attend_kernel,
        out_shape=results,
        in_specs=[resident] + [pl.BlockSpec(memory_space=pltpu.HBM)] * len(operands),
        out_specs=[pl.BlockSpec(memory_space=pltpu.HBM)] * parts + [resident],
        scratch_shapes=[
            pltpu.VMEM((rows, width), jnp.bfloat16),
            pltpu.VMEM((rows, width), jnp.bfloat16),
            pltpu.VMEM((rows, width), jnp.bfloat16),
            pltpu.VMEM((rows, width), jnp.float32),
            pltpu.VMEM((rows, width), jnp.bfloat16),
            pltpu.VMEM((5,) + wq.shape, jnp.bfloat16),
            pltpu.VMEM((1, width), jnp.float32),
            pltpu.VMEM((2, FACTOR_WIDTH, width), jnp.bfloat16),
            pltpu.VMEM((parts,) + results[0].shape, jnp.bfloat16),
            pltpu.VMEM((parts,) + results[0].shape, jnp.bfloat16),
            pltpu.SemaphoreType.DMA((len(operands) + parts,)),
        ],
        compiler_params=pltpu.CompilerParams(vmem_limit_bytes=32 * 1024 * 1024),
        cost_estimate=pl.CostEstimate(flops=2 * macs, bytes_accessed=4 * x.size * 2, transcendentals=rows * width),
        name="column_attention",
    )(x, *operands)


def first_of_four(at, cols):
    wide = MXU_SIDE // HALF * cols
    inside = jnp.where(at < wide, at, jnp.where(at < wide + HALF, at - HALF, at - wide - HALF))
    return inside // cols


def swapped(pair, wide):
    return [pair[:wide], pair[2 * wide - HALF:], pair[wide:2 * wide - HALF]]


def unswapped(pair, wide):
    return [pair[:wide], pair[wide + HALF:], pair[wide:wide + HALF]]


def right_kernel(
    factor_ref, w_ref, expand_ref, shrink_ref, rbd_ref, rbdt_ref, wec_ref, wt_ref, et_ref, st_ref, stage_s,
    *, seqs, cols, fold,
):
    each = factor_ref.shape[2]
    wide = fold * cols
    stage_lanes = stage_s.shape[1]
    low_half = lax.broadcasted_iota(jnp.int32, (1, LANES), 1) < HALF

    stage_s[:FACTOR_WIDTH * FACTOR_WIDTH, :LANES] = w_ref[...].astype(jnp.float32)
    for e in range(FACTOR_WIDTH):
        piece = stage_s[pl.ds(e, FACTOR_WIDTH, stride=FACTOR_WIDTH), :LANES]
        wec_ref[e * FACTOR_WIDTH:(e + 1) * FACTOR_WIDTH, :] = piece.astype(jnp.bfloat16)
    for b in range(FACTOR_WIDTH * FACTOR_WIDTH // LANES):
        block = wec_ref[b * LANES:(b + 1) * LANES, :].astype(jnp.float32)
        wt_ref[:, b * LANES:(b + 1) * LANES] = block.T.astype(jnp.bfloat16)
    et_ref[...] = expand_ref[...].astype(jnp.float32).T.astype(jnp.bfloat16)
    st_ref[...] = shrink_ref[...].astype(jnp.float32).T.astype(jnp.bfloat16)

    for p in range(cols // 2):
        block = factor_ref[p // each, 1, p % each].astype(jnp.float32)
        even = 2 * p * FACTOR_WIDTH
        odd = even + FACTOR_WIDTH
        if seqs % LANES == 0:
            stage_s[even:even + FACTOR_WIDTH, :] = block[:, :seqs]
            stage_s[odd:odd + FACTOR_WIDTH, :] = block[:, seqs:]
        else:
            stage_s[even:even + FACTOR_WIDTH, :] = block
            stage_s[odd:odd + FACTOR_WIDTH, :] = pltpu.roll(block, HALF, axis=1)

    row_k = first_of_four(lax.broadcasted_iota(jnp.int32, (2 * wide, 1), 0), cols)
    lane_k = first_of_four(lax.broadcasted_iota(jnp.int32, (1, 2 * wide), 1), cols)
    for e in range(0, FACTOR_WIDTH, 2):
        two = []
        for u in (e, e + 1):
            two += [stage_s[pl.ds(u, cols, stride=FACTOR_WIDTH), :]] * fold
        upright = jnp.concatenate(swapped(jnp.concatenate(two, axis=0), wide), axis=0)
        chunk, at = e // CHUNK, e % CHUNK * wide
        rolled = pltpu.roll(upright, HALF, axis=1) if seqs < LANES else None
        for v in range(fold * seqs // stage_lanes):
            if seqs < LANES:
                value = jnp.where(
                    low_half, jnp.where(row_k == 2 * v, upright, 0.0), jnp.where(row_k == 2 * v + 1, rolled, 0.0)
                )
            else:
                value = jnp.where(row_k == v, upright, 0.0)
            rbdt_ref[chunk, at:at + 2 * wide, v * stage_lanes:(v + 1) * stage_lanes] = value.astype(jnp.bfloat16)
        turned = upright.T[:seqs]
        for k in range(fold):
            value = jnp.where(lane_k == k, turned, 0.0).astype(jnp.bfloat16)
            rbd_ref[chunk, k * seqs:(k + 1) * seqs, at:at + 2 * wide] = value


def right_matrices(factors, outer_weight, expand_weight, shrink_weight):
    row_parts, _, each, _, lanes = factors.shape
    seqs, cols = lanes // 2, 2 * each * row_parts
    fold = MXU_SIDE // HALF
    channels, width = outer_weight.shape
    results = (
        jax.ShapeDtypeStruct((FACTOR_WIDTH // CHUNK, fold * seqs, CHUNK * fold * cols), jnp.bfloat16),
        jax.ShapeDtypeStruct((FACTOR_WIDTH // CHUNK, CHUNK * fold * cols, fold * seqs), jnp.bfloat16),
        jax.ShapeDtypeStruct((channels, width), jnp.bfloat16),
        jax.ShapeDtypeStruct((width, channels), jnp.bfloat16),
        jax.ShapeDtypeStruct(expand_weight.shape[::-1], jnp.bfloat16),
        jax.ShapeDtypeStruct(shrink_weight.shape[::-1], jnp.bfloat16),
    )
    resident = pl.BlockSpec(memory_space=pltpu.VMEM)
    return pl.pallas_call(
        functools.partial(right_kernel, seqs=seqs, cols=cols, fold=fold),
        out_shape=results,
        in_specs=[resident] * 4,
        out_specs=[resident] * len(results),
        scratch_shapes=[pltpu.VMEM((max(cols * FACTOR_WIDTH, channels), max(seqs, LANES)), jnp.float32)],
        compiler_params=pltpu.CompilerParams(vmem_limit_bytes=16 * 1024 * 1024),
        cost_estimate=pl.CostEstimate(flops=6 * 10**9, bytes_accessed=4 * results[0].size, transcendentals=0),
        name="right_matrices",
    )(factors, outer_weight, expand_weight, shrink_weight)


def pair_kernel(
    place_ref, *refs, seqs, cols, fold, unit, units, blocks,
):
    left_refs, refs = refs[:blocks], refs[blocks:]
    rbd_s, rbdt_s, wec_s, wt_s, et_ref, st_ref, pair_ref, cot_ref, back_ref = refs[:9]
    bias_ref, expand_ref, out_ref, gl_ref = refs[9:13]
    gr_refs, (outer_s, l_s, lt_s, stage_s, glacc_s, lblk_s, gr_s) = refs[13:-7], refs[-7:]
    step = pl.program_id(0)
    row_parts, each = left_refs[0].shape[:2]
    span = l_s.shape[0]
    groups = span // FACTOR_WIDTH
    wide = fold * cols
    scaling = 1.0 / seqs
    low_half = lax.broadcasted_iota(jnp.int32, (1, LANES), 1) < HALF

    @pl.when(step == 0)
    def _prologue():
        for n, ref in enumerate(left_refs):
            lblk_s[place_ref[n]] = ref[...]
        pairs = fold // 2
        for p in range(groups * pairs):
            column, inside = divmod(p, row_parts * each)
            block = lblk_s[column, inside // each, inside % each]
            g, at = p // pairs, p % pairs * 2 * seqs
            l_s[g * FACTOR_WIDTH:(g + 1) * FACTOR_WIDTH, at:at + 2 * seqs] = (
                block.astype(jnp.float32) * scaling
            ).astype(jnp.bfloat16)
        for b in range(span // LANES):
            block = l_s[b * LANES:(b + 1) * LANES, :].astype(jnp.float32)
            lt_s[:, b * LANES:(b + 1) * LANES] = block.T.astype(jnp.bfloat16)

        def some_outers(n, carry):
            outer_s[n] = dot_nn(l_s[...], rbd_s[n]).astype(jnp.bfloat16)
            return carry

        lax.fori_loop(0, outer_s.shape[0], some_outers, 0, unroll=2)

    def unit_rows(u):
        at = (step * units + u) * unit * FACTOR_WIDTH
        return pl.ds(pl.multiple_of(at, unit * FACTOR_WIDTH), unit * FACTOR_WIDTH)

    def group(block, g):
        return block[g * FACTOR_WIDTH:(g + 1) * FACTOR_WIDTH]

    def forward(u):
        stacked = []
        for e in range(0, FACTOR_WIDTH, 2):
            at = e % CHUNK * wide
            block = outer_s[e // CHUNK, unit_rows(u), at:at + 2 * wide]
            shared = block[:, LANES:2 * LANES]
            rolled = pltpu.roll(shared, HALF, axis=1)
            even, odd = [], []
            for g in range(0, unit, 2):
                a, b = block[:, :LANES], block[:, 2 * LANES:]
                even += [group(a, g), jnp.where(low_half, group(shared, g), group(rolled, g + 1)), group(a, g + 1)]
                odd += [group(b, g), jnp.where(low_half, group(rolled, g), group(shared, g + 1)), group(b, g + 1)]
            stacked += [jnp.concatenate(even, axis=1), jnp.concatenate(odd, axis=1)]
        projected = dot_nn(wt_s[...], jnp.concatenate(stacked, axis=0))
        middles, inverses, spreads = [], [], []
        for at in range(0, projected.shape[1], LANES):
            middle = pair_ref[step * units + u, :, at:at + LANES] + projected[:, at:at + LANES] + bias_ref[...]
            average = jnp.mean(middle, axis=0, keepdims=True)
            centred = middle - average
            variance = jnp.mean(centred * centred, axis=0, keepdims=True)
            inverse = lax.rsqrt(variance + EPSILON)
            middles.append(middle)
            inverses.append(inverse)
            spreads.append(centred * inverse)
        spread_low = jnp.concatenate([v.astype(jnp.bfloat16) for v in spreads], axis=1)
        return middles, inverses, spreads, dot_nn(et_ref[...], spread_low)

    def backward(u, middles, inverses, spreads, before):
        rows, pairs = before.shape
        hidden, back_before = [], []
        for at in range(0, rows, TILE):
            hidden_parts, back_parts = [], []
            for v in range(0, pairs, MXU_SIDE):
                x = before[at:at + TILE, v:v + MXU_SIDE]
                back = back_ref[step * units + u, at:at + TILE, v:v + MXU_SIDE].astype(jnp.float32)
                phi = 0.5 * (1.0 + lax.erf(x * 0.7071067811865476))
                slope = phi + x * jnp.exp(-0.5 * x * x) * 0.3989422804014327
                hidden_parts.append((x * phi).astype(jnp.bfloat16))
                back_parts.append((back * slope).astype(jnp.bfloat16))
            hidden.append(jnp.concatenate(hidden_parts, axis=1))
            back_before.append(jnp.concatenate(back_parts, axis=1))
        back_spread = dot_nn(expand_ref[...], jnp.concatenate(back_before, axis=0))
        change = dot_nn(st_ref[...], jnp.concatenate(hidden, axis=0))
        back_middle = []
        for n, at in enumerate(range(0, pairs, LANES)):
            back, spread = back_spread[:, at:at + LANES], spreads[n]
            centre_term = jnp.mean(back, axis=0, keepdims=True)
            slope_term = jnp.mean(back * spread, axis=0, keepdims=True)
            back = back - centre_term - spread * slope_term
            back = cot_ref[step * units + u, :, at:at + LANES] + inverses[n] * back
            back_middle.append(back.astype(jnp.bfloat16))
        result = (jnp.concatenate(middles, axis=1) + change).T
        pieces = []
        for g in range(0, unit, 2):
            pieces += unswapped(result[g * wide:(g + 2) * wide], wide)
        out_ref[u * unit * fold:(u + 1) * unit * fold] = jnp.concatenate(pieces, axis=0).reshape(
            unit * fold, cols, PAIR_W
        )
        back_outer = dot_nn(wec_s[...], jnp.concatenate(back_middle, axis=1)).astype(jnp.bfloat16)
        for e in range(0, FACTOR_WIDTH, 2):
            even, odd = group(back_outer, e), group(back_outer, e + 1)
            a, shared, b = [], [], []
            for g in range(0, unit, 2):
                at = g * wide
                of_even, of_odd = even[:, at + LANES:at + 2 * LANES], odd[:, at + LANES:at + 2 * LANES]
                a += [even[:, at:at + LANES], even[:, at + 2 * LANES:at + 3 * LANES]]
                b += [odd[:, at:at + LANES], odd[:, at + 2 * LANES:at + 3 * LANES]]
                shared += [
                    jnp.where(low_half, of_even, pltpu.roll(of_odd, HALF, axis=1)),
                    jnp.where(low_half, pltpu.roll(of_even, HALF, axis=1), of_odd),
                ]
            for n, pieces in enumerate((a, shared, b)):
                at = e % CHUNK * wide + n * LANES
                outer_s[e // CHUNK, unit_rows(u), at:at + LANES] = jnp.concatenate(pieces, axis=0)

    held = forward(0)
    for u in range(units):
        ahead = forward(u + 1) if u + 1 < units else None
        backward(u, *held)
        held = ahead

    @pl.when(step == pl.num_programs(0) - 1)
    def _epilogue():
        glacc_s[...] = jnp.zeros_like(glacc_s)
        empty = jnp.zeros((LANES - seqs % LANES, CHUNK * wide), jnp.float32) if seqs % LANES else None
        at = lax.broadcasted_iota(jnp.int32, (1, CHUNK * wide), 1)
        lane_k = first_of_four(lax.rem(at, 2 * wide), cols)

        def some(n, carry):
            back = outer_s[n]
            glacc_s[...] += dot_nn(back, rbdt_s[n])
            full = dot_nn(lt_s[...], back)
            compact = full[:seqs]
            for k in range(1, fold):
                compact = jnp.where(lane_k == k, full[k * seqs:(k + 1) * seqs], compact)
            if empty is not None:
                compact = jnp.concatenate([compact, empty], axis=0)
            turned = compact.T
            for p in range(CHUNK // 2):
                two = jnp.concatenate(unswapped(turned[2 * p * wide:2 * (p + 1) * wide], wide), axis=0)
                for u in range(2):
                    total = two[u * wide:u * wide + cols]
                    for k in range(1, fold):
                        total = total + two[u * wide + k * cols:u * wide + (k + 1) * cols]
                    stage_s[pl.ds(n * CHUNK + 2 * p + u, cols, stride=FACTOR_WIDTH), :] = total
            return carry

        lax.fori_loop(0, outer_s.shape[0], some, 0, unroll=2)
        for b in range(cols * FACTOR_WIDTH // LANES):
            block = stage_s[b * LANES:(b + 1) * LANES, :].T[:seqs].astype(jnp.bfloat16)
            gr_s[:, :, b * LANES:(b + 1) * LANES] = block.reshape(row_parts, -1, LANES)
        for k, ref in enumerate(gr_refs):
            ref[...] = gr_s[place_ref[blocks] ^ k]
        for b in range(span // LANES):
            block = glacc_s[b * LANES:(b + 1) * LANES, :].T * scaling
            for k in range(fold):
                at = k * span + b * LANES
                gl_ref[:, at:at + LANES] = block[k * seqs:(k + 1) * seqs].astype(jnp.bfloat16)


def turn_kernel(pair_ref, cot_ref, shrink_ref, after_ref, pair_out_ref, cot_out_ref, back_ref, *, wide):
    for source, target in ((pair_ref, pair_out_ref), (cot_ref, cot_out_ref)):
        rows = source[...].reshape(-1, PAIR_W)
        for at in range(0, rows.shape[0], 2 * wide):
            target[0, :, at:at + 2 * wide] = jnp.concatenate(swapped(rows[at:at + 2 * wide], wide), axis=0).T
    back_ref[0] = dot_nn(shrink_ref[...], cot_out_ref[0].astype(jnp.bfloat16)).astype(jnp.bfloat16)


def turned_pairs(pair_features, cotangent, shrink_weight, after):
    rows, cols, _ = pair_features.shape
    fold = MXU_SIDE // HALF
    count = rows // (UNIT * fold)
    pairs = UNIT * fold * cols
    hidden = shrink_weight.shape[0]
    results = (
        jax.ShapeDtypeStruct((count, PAIR_W, pairs), jnp.float32),
        jax.ShapeDtypeStruct((count, PAIR_W, pairs), jnp.float32),
        jax.ShapeDtypeStruct((count, hidden, pairs), jnp.bfloat16),
    )
    block = pl.BlockSpec((UNIT * fold, cols, PAIR_W), lambda n: (n, 0, 0))
    return pl.pallas_call(
        functools.partial(turn_kernel, wide=fold * cols),
        grid=(count,),
        out_shape=results,
        in_specs=[block, block, whole_block(shrink_weight.shape), pl.BlockSpec(memory_space=pl.ANY)],
        out_specs=[pl.BlockSpec((1,) + v.shape[1:], lambda n: (n, 0, 0)) for v in results],
        compiler_params=pltpu.CompilerParams(
            dimension_semantics=("arbitrary",), vmem_limit_bytes=24 * 1024 * 1024
        ),
        cost_estimate=pl.CostEstimate(
            flops=2 * 2 * count * pairs * hidden * PAIR_W, bytes_accessed=4 * 4 * pair_features.size, transcendentals=0
        ),
        name="turned_pairs",
    )(pair_features, cotangent, shrink_weight, after)


def pair_tile(place, lefts, matrices, turned, shape, outer_bias, expand_weight):
    seqs = lefts[0].shape[-1] // 2
    row_parts = lefts[0].shape[0]
    rows, cols, _ = shape
    fold = MXU_SIDE // HALF
    groups = rows // fold
    unit = UNIT
    units = 2 if groups % (2 * unit) == 0 else 1
    steps = groups // unit // units
    wide = fold * cols
    span = groups * FACTOR_WIDTH
    channels = FACTOR_WIDTH * FACTOR_WIDTH
    block = pl.BlockSpec((unit * units * fold, cols, PAIR_W), lambda n, place: (n, 0, 0))
    resident = pl.BlockSpec(memory_space=pltpu.VMEM)
    operands = (
        *lefts, *matrices, *turned, jnp.broadcast_to(outer_bias[:, None], (PAIR_W, LANES)), expand_weight,
    )
    results = (
        jax.ShapeDtypeStruct(shape, jnp.float32),
        jax.ShapeDtypeStruct((seqs, rows * FACTOR_WIDTH), jnp.bfloat16),
    ) + row_parts * (jax.ShapeDtypeStruct((seqs // row_parts, cols * FACTOR_WIDTH), jnp.bfloat16),)
    padded = groups * wide
    macs = 3 * FACTOR_WIDTH * span * fold * seqs * wide + padded * (2 * channels * MXU_SIDE + 8 * MXU_SIDE * MXU_SIDE)
    return pl.pallas_call(
        functools.partial(
            pair_kernel, seqs=seqs, cols=cols, fold=fold, unit=unit, units=units, blocks=len(lefts)
        ),
        grid_spec=pltpu.PrefetchScalarGridSpec(
            num_scalar_prefetch=1,
            grid=(steps,),
            in_specs=[resident] * len(operands),
            out_specs=[block] + [resident] * (len(results) - 1),
            scratch_shapes=[
                pltpu.VMEM((FACTOR_WIDTH // CHUNK, span, CHUNK * wide), jnp.bfloat16),
                pltpu.VMEM((span, fold * seqs), jnp.bfloat16),
                pltpu.VMEM((fold * seqs, span), jnp.bfloat16),
                pltpu.VMEM((cols * FACTOR_WIDTH, max(seqs, LANES)), jnp.float32),
                pltpu.VMEM((span, fold * seqs), jnp.float32),
                pltpu.VMEM((len(lefts),) + lefts[0].shape, jnp.bfloat16),
                pltpu.VMEM((row_parts,) + results[2].shape, jnp.bfloat16),
            ],
        ),
        out_shape=results,
        compiler_params=pltpu.CompilerParams(
            dimension_semantics=("arbitrary",), vmem_limit_bytes=36 * 1024 * 1024
        ),
        cost_estimate=pl.CostEstimate(
            flops=2 * macs, bytes_accessed=rows * cols * PAIR_W * 4, transcendentals=0
        ),
        name="pair_tile",
    )(place, *operands)


def finish_kernel(place_ref, *refs, residues, fold):
    *part_refs, gl_ref, updated_ref, left_ref, right_ref, x_s = refs
    upd_refs, gr_refs = part_refs[:len(part_refs) // 2], part_refs[len(part_refs) // 2:]
    part_seqs, res_count, width = updated_ref.shape
    total = gr_refs[0][...].astype(jnp.float32)
    for ref in gr_refs[1:]:
        total = total + ref[...].astype(jnp.float32)
    right_ref[...] = total
    for k, ref in enumerate(upd_refs):
        first = (place_ref[0] ^ k) * residues
        for r in range(residues):
            for n in range(width // LANES):
                at = r * width + n * LANES
                x_s[n, pl.ds(first + r, part_seqs, stride=res_count), :] = ref[:, at:at + LANES].astype(jnp.float32)
    for n in range(width // LANES):
        updated_ref[:, :, n * LANES:(n + 1) * LANES] = (
            x_s[n].reshape(part_seqs, res_count, LANES).astype(jnp.bfloat16)
        )
    total = gl_ref[0].astype(jnp.float32)
    for n in range(1, gl_ref.shape[0]):
        total = total + gl_ref[n].astype(jnp.float32)
    span = total.shape[1] // fold
    channel_block = lax.broadcasted_iota(jnp.int32, (1, LANES), 1) // FACTOR_WIDTH
    each = LANES // FACTOR_WIDTH
    for g in range(span // FACTOR_WIDTH):
        out = None
        for k in range(fold):
            at = k * span + g // each * LANES
            piece = total[:, at:at + LANES]
            shift = (k - g) % each * FACTOR_WIDTH
            piece = pltpu.roll(piece, shift, axis=1) if shift else piece
            out = piece if out is None else jnp.where(channel_block == k, piece, out)
        left_ref[:, g * LANES:(g + 1) * LANES] = out


def finish(place, returned, gr, gl, updated_shape):
    part_seqs, res_count, width = updated_shape
    residues = res_count // len(returned)
    results = (
        jax.ShapeDtypeStruct(updated_shape, jnp.bfloat16),
        jax.ShapeDtypeStruct(gl.shape[1:], jnp.float32),
        jax.ShapeDtypeStruct(gr[0].shape, jnp.float32),
    )
    resident = pl.BlockSpec(memory_space=pltpu.VMEM)
    return pl.pallas_call(
        functools.partial(finish_kernel, residues=residues, fold=MXU_SIDE // HALF),
        grid_spec=pltpu.PrefetchScalarGridSpec(
            num_scalar_prefetch=1,
            grid=(1,),
            in_specs=[resident] * (len(returned) + len(gr) + 1),
            out_specs=[whole_block(v.shape) for v in results],
            scratch_shapes=[pltpu.VMEM((width // LANES, part_seqs * res_count, LANES), jnp.float32)],
        ),
        out_shape=results,
        compiler_params=pltpu.CompilerParams(
            dimension_semantics=("arbitrary",), vmem_limit_bytes=16 * 1024 * 1024
        ),
        name="finish",
    )(place, *returned, *gr, gl)


def spread_out(q, count):
    return q if count % 2 else q % 2 * (count // 2) + q // 2


def local(
    alignment,
    pair_features,
    query_weight,
    key_weight,
    value_projection,
    gate_projection,
    gate_bias,
    output_projection,
    left_projection,
    right_projection,
    outer_weight,
    outer_bias,
    expand_weight,
    shrink_weight,
    cotangent,
):
    part_seqs, res_count, width = alignment.shape
    row_parts = lax.axis_size("row")
    col_parts = lax.axis_size("col")
    residues = res_count // row_parts
    own = jnp.transpose(alignment, (1, 0, 2)).reshape(row_parts, residues, part_seqs, width)
    columns = lax.all_to_all(own, "row", split_axis=0, concat_axis=0, tiled=True)
    *attended, factors = attend(
        columns, query_weight, key_weight, value_projection, gate_projection, gate_bias,
        output_projection, left_projection, right_projection,
    )

    factors = lax.all_to_all(factors, "row", split_axis=0, concat_axis=0, tiled=True)
    left = factors[:, 0]
    ratio = col_parts // row_parts
    lefts, place = [], []
    for m in range(ratio):
        moves = [
            (q * col_parts + ratio * r + b, r * col_parts + ratio * spread_out(q, row_parts) + (b + m) % ratio)
            for q in range(row_parts)
            for r in range(row_parts)
            for b in range(ratio)
        ]
        lefts.append(lax.ppermute(left, ("row", "col"), moves))
        place.append((lax.axis_index("col") + ratio - m) % ratio)
    row = lax.axis_index("row")
    own_row = row.astype(jnp.int32).reshape(1)
    matrices = right_matrices(factors, outer_weight, expand_weight, shrink_weight)
    turned = turned_pairs(pair_features, cotangent, shrink_weight, matrices[-1])

    def to_rows(values):
        return values[:1] + [
            lax.ppermute(v, "row", [(r, r ^ (k + 1)) for r in range(row_parts)]) for k, v in enumerate(values[1:])
        ]

    returned = to_rows(attended)
    lefts, returned = lax.optimization_barrier((lefts, returned))
    pair_out, gl, *gr = pair_tile(
        jnp.stack(place + [row]).astype(jnp.int32), lefts, matrices, turned, pair_features.shape, outer_bias,
        expand_weight,
    )
    seqs, gl_width = gl.shape
    gr = to_rows(gr)
    gl = lax.all_to_all(
        gl.reshape(col_parts, seqs // col_parts, gl_width), "col", split_axis=0, concat_axis=0, tiled=True
    )
    updated, grad_left, grad_right = finish(own_row, returned, gr, gl, alignment.shape)
    return (updated, pair_out, grad_left, grad_right)


def solution(mesh):
    return jax.shard_map(
        local,
        mesh=mesh,
        in_specs=(P("row", "col", None), P("row", "col", None)) + (P(),) * 12 + (P("row", "col", None),),
        out_specs=(P("row", "col", None), P("row", "col", None), P("col", "row"), P("row", "col")),
        check_vma=False,
    )
```

```python
import functools

import jax
import jax.numpy as jnp
from jax import lax
from jax.experimental import pallas as pl
from jax.experimental.pallas import tpu as pltpu
from jax.sharding import PartitionSpec as P

ATTENTION_HEADS = 8
HEAD_WIDTH = 32
FACTOR_WIDTH = 32
PAIR_W = 128
EPSILON = 1e-05

LANES = 128
MXU_SIDE = 256
HALF = 64
TILE = 32
CHUNK = 4
UNIT = 4


def dot_nn(a, b):
    return lax.dot_general(a, b, (((1,), (0,)), ((), ())), preferred_element_type=jnp.float32)


def dot_nt(a, b):
    return lax.dot_general(a, b, (((1,), (1,)), ((), ())), preferred_element_type=jnp.float32)


def layer_normalise(rows):
    rows = rows.astype(jnp.float32)
    average = jnp.mean(rows, axis=-1, keepdims=True)
    centred = rows - average
    variance = jnp.mean(centred * centred, axis=-1, keepdims=True)
    return centred * lax.rsqrt(variance + EPSILON)


def attend_kernel(
    x_ref, wq_ref, wk_ref, wv_ref, wg_ref, bias_ref, wo_ref, wl_ref, wr_ref, *refs,
):
    row = lax.axis_index("row")
    *upd_refs, factor_ref, q_s, k_s, v_s, g_s, a_s, w_s, bias_s, project_s, upd_s, ordered_s, sems = refs
    parts, residues, part_seqs, width = x_ref.shape
    seqs = parts * part_seqs
    sources = (wq_ref, wk_ref, wv_ref, wg_ref, wo_ref, bias_ref, wl_ref, wr_ref)
    targets = [w_s.at[n] for n in range(5)] + [bias_s, project_s.at[0], project_s.at[1]]
    copies = [pltpu.make_async_copy(a, b, sems.at[n]) for n, (a, b) in enumerate(zip(sources, targets))]
    for copy in copies:
        copy.start()
    x = jnp.concatenate([x_ref[s, r] for r in range(residues) for s in range(parts)], axis=0)
    normed = layer_normalise(x).astype(jnp.bfloat16)
    for n, ref in enumerate((q_s, k_s, v_s)):
        copies[n].wait()
        ref[...] = dot_nn(normed, w_s[n]).astype(jnp.bfloat16)
    copies[3].wait()
    copies[5].wait()
    g_s[...] = jax.nn.sigmoid(dot_nn(normed, w_s[3]) + bias_s[...])

    head_of = lax.broadcasted_iota(jnp.int32, (1, width), 1) // HEAD_WIDTH
    masks = [(head_of == h).astype(jnp.float32) for h in range(ATTENTION_HEADS)]
    masks_low = [m.astype(jnp.bfloat16) for m in masks]

    def one_residue(r, carry):
        rows = pl.ds(pl.multiple_of(r * seqs, seqs), seqs)
        query = q_s[rows, :]
        spread_query = jnp.concatenate([query * m for m in masks_low], axis=0)
        scores = dot_nt(spread_query, k_s[rows, :]) * HEAD_WIDTH ** (-0.5)
        raised = jnp.exp(scores - jnp.max(scores, axis=-1, keepdims=True))
        inverse = 1.0 / jnp.sum(raised, axis=-1, keepdims=True)
        blended = dot_nn(raised.astype(jnp.bfloat16), v_s[rows, :]) * inverse
        total = blended[:seqs] * masks[0]
        for h in range(1, ATTENTION_HEADS):
            total = total + blended[h * seqs:(h + 1) * seqs] * masks[h]
        a_s[rows, :] = (g_s[rows, :] * total).astype(jnp.bfloat16)
        return carry

    lax.fori_loop(0, residues, one_residue, 0, unroll=6 if residues % 6 == 0 else 2)

    copies[4].wait()
    updated = (x.astype(jnp.float32) + dot_nn(a_s[...], w_s[4])).astype(jnp.bfloat16)
    for r in range(residues):
        for s in range(parts):
            begin = r * seqs + s * part_seqs
            upd_s[s, :, r * width:(r + 1) * width] = updated[begin:begin + part_seqs]
    leaving = []
    for k, ref in enumerate(upd_refs):
        ordered_s[k] = upd_s[row ^ k]
        leaving.append(pltpu.make_async_copy(ordered_s.at[k], ref, sems.at[len(sources) + k]))
        leaving[k].start()
    factor_norm = layer_normalise(updated).astype(jnp.bfloat16)
    copies[6].wait()
    copies[7].wait()
    project = project_s[...].reshape(2 * FACTOR_WIDTH, width)
    for p in range(residues // 2):
        both = dot_nt(project, factor_norm[p * 2 * seqs:(p + 1) * 2 * seqs]).astype(jnp.bfloat16)
        for n in range(parts):
            factor_ref[n, 0, p] = both[:FACTOR_WIDTH]
            factor_ref[n, 1, p] = both[FACTOR_WIDTH:]
    for copy in leaving:
        copy.wait()


def whole_block(shape):
    return pl.BlockSpec(shape, lambda *_: (0,) * len(shape))


def in_hbm(*arrays):
    return [pltpu.with_memory_space_constraint(v, pltpu.HBM) for v in arrays]


def attend(x, wq, wk, wv, wg, gate_bias, wo, wl, wr):
    parts, residues, part_seqs, width = x.shape
    seqs = parts * part_seqs
    rows = residues * seqs
    operands = in_hbm(wq, wk, wv, wg, gate_bias.reshape(1, -1), wo, wl.T, wr.T)
    resident = pl.BlockSpec(memory_space=pltpu.VMEM)
    results = parts * (pltpu.HBM((part_seqs, residues * width), jnp.bfloat16),) + (
        jax.ShapeDtypeStruct((parts, 2, residues // 2, FACTOR_WIDTH, 2 * seqs), jnp.bfloat16),
    )
    macs = rows * width * (5 * width + 2 * FACTOR_WIDTH) + 2 * rows * ATTENTION_HEADS * width * seqs
    return pl.pallas_call(
        attend_kernel,
        out_shape=results,
        in_specs=[resident] + [pl.BlockSpec(memory_space=pltpu.HBM)] * len(operands),
        out_specs=[pl.BlockSpec(memory_space=pltpu.HBM)] * parts + [resident],
        scratch_shapes=[
            pltpu.VMEM((rows, width), jnp.bfloat16),
            pltpu.VMEM((rows, width), jnp.bfloat16),
            pltpu.VMEM((rows, width), jnp.bfloat16),
            pltpu.VMEM((rows, width), jnp.float32),
            pltpu.VMEM((rows, width), jnp.bfloat16),
            pltpu.VMEM((5,) + wq.shape, jnp.bfloat16),
            pltpu.VMEM((1, width), jnp.float32),
            pltpu.VMEM((2, FACTOR_WIDTH, width), jnp.bfloat16),
            pltpu.VMEM((parts,) + results[0].shape, jnp.bfloat16),
            pltpu.VMEM((parts,) + results[0].shape, jnp.bfloat16),
            pltpu.SemaphoreType.DMA((len(operands) + parts,)),
        ],
        compiler_params=pltpu.CompilerParams(vmem_limit_bytes=32 * 1024 * 1024),
        cost_estimate=pl.CostEstimate(flops=2 * macs, bytes_accessed=4 * x.size * 2, transcendentals=rows * width),
        name="column_attention",
    )(x, *operands)


def first_of_four(at, cols):
    wide = MXU_SIDE // HALF * cols
    inside = jnp.where(at < wide, at, jnp.where(at < wide + HALF, at - HALF, at - wide - HALF))
    return inside // cols


def swapped(pair, wide):
    return [pair[:wide], pair[2 * wide - HALF:], pair[wide:2 * wide - HALF]]


def unswapped(pair, wide):
    return [pair[:wide], pair[wide + HALF:], pair[wide:wide + HALF]]


def right_kernel(
    factor_ref, w_ref, expand_ref, shrink_ref, rbd_ref, rbdt_ref, wec_ref, wt_ref, et_ref, st_ref, stage_s,
    *, seqs, cols, fold,
):
    each = factor_ref.shape[2]
    wide = fold * cols
    stage_lanes = stage_s.shape[1]
    low_half = lax.broadcasted_iota(jnp.int32, (1, LANES), 1) < HALF

    stage_s[:FACTOR_WIDTH * FACTOR_WIDTH, :LANES] = w_ref[...].astype(jnp.float32)
    for e in range(FACTOR_WIDTH):
        piece = stage_s[pl.ds(e, FACTOR_WIDTH, stride=FACTOR_WIDTH), :LANES]
        wec_ref[e * FACTOR_WIDTH:(e + 1) * FACTOR_WIDTH, :] = piece.astype(jnp.bfloat16)
    for b in range(FACTOR_WIDTH * FACTOR_WIDTH // LANES):
        block = wec_ref[b * LANES:(b + 1) * LANES, :].astype(jnp.float32)
        wt_ref[:, b * LANES:(b + 1) * LANES] = block.T.astype(jnp.bfloat16)
    et_ref[...] = expand_ref[...].astype(jnp.float32).T.astype(jnp.bfloat16)
    st_ref[...] = shrink_ref[...].astype(jnp.float32).T.astype(jnp.bfloat16)

    for p in range(cols // 2):
        block = factor_ref[p // each, 1, p % each].astype(jnp.float32)
        even = 2 * p * FACTOR_WIDTH
        odd = even + FACTOR_WIDTH
        if seqs % LANES == 0:
            stage_s[even:even + FACTOR_WIDTH, :] = block[:, :seqs]
            stage_s[odd:odd + FACTOR_WIDTH, :] = block[:, seqs:]
        else:
            stage_s[even:even + FACTOR_WIDTH, :] = block
            stage_s[odd:odd + FACTOR_WIDTH, :] = pltpu.roll(block, HALF, axis=1)

    row_k = first_of_four(lax.broadcasted_iota(jnp.int32, (2 * wide, 1), 0), cols)
    lane_k = first_of_four(lax.broadcasted_iota(jnp.int32, (1, 2 * wide), 1), cols)
    for e in range(0, FACTOR_WIDTH, 2):
        two = []
        for u in (e, e + 1):
            two += [stage_s[pl.ds(u, cols, stride=FACTOR_WIDTH), :]] * fold
        upright = jnp.concatenate(swapped(jnp.concatenate(two, axis=0), wide), axis=0)
        chunk, at = e // CHUNK, e % CHUNK * wide
        rolled = pltpu.roll(upright, HALF, axis=1) if seqs < LANES else None
        for v in range(fold * seqs // stage_lanes):
            if seqs < LANES:
                value = jnp.where(
                    low_half, jnp.where(row_k == 2 * v, upright, 0.0), jnp.where(row_k == 2 * v + 1, rolled, 0.0)
                )
            else:
                value = jnp.where(row_k == v, upright, 0.0)
            rbdt_ref[chunk, at:at + 2 * wide, v * stage_lanes:(v + 1) * stage_lanes] = value.astype(jnp.bfloat16)
        turned = upright.T[:seqs]
        for k in range(fold):
            value = jnp.where(lane_k == k, turned, 0.0).astype(jnp.bfloat16)
            rbd_ref[chunk, k * seqs:(k + 1) * seqs, at:at + 2 * wide] = value


def right_matrices(factors, outer_weight, expand_weight, shrink_weight):
    row_parts, _, each, _, lanes = factors.shape
    seqs, cols = lanes // 2, 2 * each * row_parts
    fold = MXU_SIDE // HALF
    channels, width = outer_weight.shape
    results = (
        jax.ShapeDtypeStruct((FACTOR_WIDTH // CHUNK, fold * seqs, CHUNK * fold * cols), jnp.bfloat16),
        jax.ShapeDtypeStruct((FACTOR_WIDTH // CHUNK, CHUNK * fold * cols, fold * seqs), jnp.bfloat16),
        jax.ShapeDtypeStruct((channels, width), jnp.bfloat16),
        jax.ShapeDtypeStruct((width, channels), jnp.bfloat16),
        jax.ShapeDtypeStruct(expand_weight.shape[::-1], jnp.bfloat16),
        jax.ShapeDtypeStruct(shrink_weight.shape[::-1], jnp.bfloat16),
    )
    resident = pl.BlockSpec(memory_space=pltpu.VMEM)
    return pl.pallas_call(
        functools.partial(right_kernel, seqs=seqs, cols=cols, fold=fold),
        out_shape=results,
        in_specs=[resident] * 4,
        out_specs=[resident] * len(results),
        scratch_shapes=[pltpu.VMEM((max(cols * FACTOR_WIDTH, channels), max(seqs, LANES)), jnp.float32)],
        compiler_params=pltpu.CompilerParams(vmem_limit_bytes=16 * 1024 * 1024),
        cost_estimate=pl.CostEstimate(flops=6 * 10**9, bytes_accessed=4 * results[0].size, transcendentals=0),
        name="right_matrices",
    )(factors, outer_weight, expand_weight, shrink_weight)


def pair_kernel(
    place_ref, *refs, seqs, cols, fold, unit, units, blocks,
):
    left_refs, refs = refs[:blocks], refs[blocks:]
    rbd_s, rbdt_s, wec_s, wt_s, et_ref, st_ref, pair_ref, cot_ref, back_ref = refs[:9]
    bias_ref, expand_ref, out_ref, gl_ref = refs[9:13]
    gr_refs, (outer_s, l_s, lt_s, stage_s, glacc_s, lblk_s, gr_s) = refs[13:-7], refs[-7:]
    step = pl.program_id(0)
    row_parts, each = left_refs[0].shape[:2]
    span = l_s.shape[0]
    groups = span // FACTOR_WIDTH
    wide = fold * cols
    scaling = 1.0 / seqs
    low_half = lax.broadcasted_iota(jnp.int32, (1, LANES), 1) < HALF

    @pl.when(step == 0)
    def _prologue():
        for n, ref in enumerate(left_refs):
            lblk_s[place_ref[n]] = ref[...]
        pairs = fold // 2
        for p in range(groups * pairs):
            column, inside = divmod(p, row_parts * each)
            block = lblk_s[column, inside // each, inside % each]
            g, at = p // pairs, p % pairs * 2 * seqs
            l_s[g * FACTOR_WIDTH:(g + 1) * FACTOR_WIDTH, at:at + 2 * seqs] = (
                block.astype(jnp.float32) * scaling
            ).astype(jnp.bfloat16)
        for b in range(span // LANES):
            block = l_s[b * LANES:(b + 1) * LANES, :].astype(jnp.float32)
            lt_s[:, b * LANES:(b + 1) * LANES] = block.T.astype(jnp.bfloat16)

        def some_outers(n, carry):
            outer_s[n] = dot_nn(l_s[...], rbd_s[n]).astype(jnp.bfloat16)
            return carry

        lax.fori_loop(0, outer_s.shape[0], some_outers, 0, unroll=2)

    def unit_rows(u):
        at = (step * units + u) * unit * FACTOR_WIDTH
        return pl.ds(pl.multiple_of(at, unit * FACTOR_WIDTH), unit * FACTOR_WIDTH)

    def group(block, g):
        return block[g * FACTOR_WIDTH:(g + 1) * FACTOR_WIDTH]

    def forward(u):
        stacked = []
        for e in range(0, FACTOR_WIDTH, 2):
            at = e % CHUNK * wide
            block = outer_s[e // CHUNK, unit_rows(u), at:at + 2 * wide]
            shared = block[:, LANES:2 * LANES]
            rolled = pltpu.roll(shared, HALF, axis=1)
            even, odd = [], []
            for g in range(0, unit, 2):
                a, b = block[:, :LANES], block[:, 2 * LANES:]
                even += [group(a, g), jnp.where(low_half, group(shared, g), group(rolled, g + 1)), group(a, g + 1)]
                odd += [group(b, g), jnp.where(low_half, group(rolled, g), group(shared, g + 1)), group(b, g + 1)]
            stacked += [jnp.concatenate(even, axis=1), jnp.concatenate(odd, axis=1)]
        projected = dot_nn(wt_s[...], jnp.concatenate(stacked, axis=0))
        middles, inverses, spreads = [], [], []
        for at in range(0, projected.shape[1], LANES):
            middle = pair_ref[step * units + u, :, at:at + LANES] + projected[:, at:at + LANES] + bias_ref[...]
            average = jnp.mean(middle, axis=0, keepdims=True)
            centred = middle - average
            variance = jnp.mean(centred * centred, axis=0, keepdims=True)
            inverse = lax.rsqrt(variance + EPSILON)
            middles.append(middle)
            inverses.append(inverse)
            spreads.append(centred * inverse)
        spread_low = jnp.concatenate([v.astype(jnp.bfloat16) for v in spreads], axis=1)
        return middles, inverses, spreads, dot_nn(et_ref[...], spread_low)

    def backward(u, middles, inverses, spreads, before):
        rows, pairs = before.shape
        hidden, back_before = [], []
        for at in range(0, rows, TILE):
            hidden_parts, back_parts = [], []
            for v in range(0, pairs, MXU_SIDE):
                x = before[at:at + TILE, v:v + MXU_SIDE]
                back = back_ref[step * units + u, at:at + TILE, v:v + MXU_SIDE].astype(jnp.float32)
                phi = 0.5 * (1.0 + lax.erf(x * 0.7071067811865476))
                slope = phi + x * jnp.exp(-0.5 * x * x) * 0.3989422804014327
                hidden_parts.append((x * phi).astype(jnp.bfloat16))
                back_parts.append((back * slope).astype(jnp.bfloat16))
            hidden.append(jnp.concatenate(hidden_parts, axis=1))
            back_before.append(jnp.concatenate(back_parts, axis=1))
        back_spread = dot_nn(expand_ref[...], jnp.concatenate(back_before, axis=0))
        change = dot_nn(st_ref[...], jnp.concatenate(hidden, axis=0))
        back_middle = []
        for n, at in enumerate(range(0, pairs, LANES)):
            back, spread = back_spread[:, at:at + LANES], spreads[n]
            centre_term = jnp.mean(back, axis=0, keepdims=True)
            slope_term = jnp.mean(back * spread, axis=0, keepdims=True)
            back = back - centre_term - spread * slope_term
            back = cot_ref[step * units + u, :, at:at + LANES] + inverses[n] * back
            back_middle.append(back.astype(jnp.bfloat16))
        result = (jnp.concatenate(middles, axis=1) + change).T
        pieces = []
        for g in range(0, unit, 2):
            pieces += unswapped(result[g * wide:(g + 2) * wide], wide)
        out_ref[u * unit * fold:(u + 1) * unit * fold] = jnp.concatenate(pieces, axis=0).reshape(
            unit * fold, cols, PAIR_W
        )
        back_outer = dot_nn(wec_s[...], jnp.concatenate(back_middle, axis=1)).astype(jnp.bfloat16)
        for e in range(0, FACTOR_WIDTH, 2):
            even, odd = group(back_outer, e), group(back_outer, e + 1)
            a, shared, b = [], [], []
            for g in range(0, unit, 2):
                at = g * wide
                of_even, of_odd = even[:, at + LANES:at + 2 * LANES], odd[:, at + LANES:at + 2 * LANES]
                a += [even[:, at:at + LANES], even[:, at + 2 * LANES:at + 3 * LANES]]
                b += [odd[:, at:at + LANES], odd[:, at + 2 * LANES:at + 3 * LANES]]
                shared += [
                    jnp.where(low_half, of_even, pltpu.roll(of_odd, HALF, axis=1)),
                    jnp.where(low_half, pltpu.roll(of_even, HALF, axis=1), of_odd),
                ]
            for n, pieces in enumerate((a, shared, b)):
                at = e % CHUNK * wide + n * LANES
                outer_s[e // CHUNK, unit_rows(u), at:at + LANES] = jnp.concatenate(pieces, axis=0)

    held = forward(0)
    for u in range(units):
        ahead = forward(u + 1) if u + 1 < units else None
        backward(u, *held)
        held = ahead

    @pl.when(step == pl.num_programs(0) - 1)
    def _epilogue():
        glacc_s[...] = jnp.zeros_like(glacc_s)
        empty = jnp.zeros((LANES - seqs % LANES, CHUNK * wide), jnp.float32) if seqs % LANES else None
        at = lax.broadcasted_iota(jnp.int32, (1, CHUNK * wide), 1)
        lane_k = first_of_four(lax.rem(at, 2 * wide), cols)

        def some(n, carry):
            back = outer_s[n]
            glacc_s[...] += dot_nn(back, rbdt_s[n])
            full = dot_nn(lt_s[...], back)
            compact = full[:seqs]
            for k in range(1, fold):
                compact = jnp.where(lane_k == k, full[k * seqs:(k + 1) * seqs], compact)
            if empty is not None:
                compact = jnp.concatenate([compact, empty], axis=0)
            turned = compact.T
            for p in range(CHUNK // 2):
                two = jnp.concatenate(unswapped(turned[2 * p * wide:2 * (p + 1) * wide], wide), axis=0)
                for u in range(2):
                    total = two[u * wide:u * wide + cols]
                    for k in range(1, fold):
                        total = total + two[u * wide + k * cols:u * wide + (k + 1) * cols]
                    stage_s[pl.ds(n * CHUNK + 2 * p + u, cols, stride=FACTOR_WIDTH), :] = total
            return carry

        lax.fori_loop(0, outer_s.shape[0], some, 0, unroll=2)
        for b in range(cols * FACTOR_WIDTH // LANES):
            block = stage_s[b * LANES:(b + 1) * LANES, :].T[:seqs].astype(jnp.bfloat16)
            gr_s[:, :, b * LANES:(b + 1) * LANES] = block.reshape(row_parts, -1, LANES)
        for k, ref in enumerate(gr_refs):
            ref[...] = gr_s[place_ref[blocks] ^ k]
        for b in range(span // LANES):
            block = glacc_s[b * LANES:(b + 1) * LANES, :].T * scaling
            for k in range(fold):
                at = k * span + b * LANES
                gl_ref[:, at:at + LANES] = block[k * seqs:(k + 1) * seqs].astype(jnp.bfloat16)


def turn_kernel(pair_ref, cot_ref, shrink_ref, after_ref, pair_out_ref, cot_out_ref, back_ref, *, wide):
    for source, target in ((pair_ref, pair_out_ref), (cot_ref, cot_out_ref)):
        rows = source[...].reshape(-1, PAIR_W)
        for at in range(0, rows.shape[0], 2 * wide):
            target[0, :, at:at + 2 * wide] = jnp.concatenate(swapped(rows[at:at + 2 * wide], wide), axis=0).T
    back_ref[0] = dot_nn(shrink_ref[...], cot_out_ref[0].astype(jnp.bfloat16)).astype(jnp.bfloat16)


def turned_pairs(pair_features, cotangent, shrink_weight, after):
    rows, cols, _ = pair_features.shape
    fold = MXU_SIDE // HALF
    count = rows // (UNIT * fold)
    pairs = UNIT * fold * cols
    hidden = shrink_weight.shape[0]
    results = (
        jax.ShapeDtypeStruct((count, PAIR_W, pairs), jnp.float32),
        jax.ShapeDtypeStruct((count, PAIR_W, pairs), jnp.float32),
        jax.ShapeDtypeStruct((count, hidden, pairs), jnp.bfloat16),
    )
    block = pl.BlockSpec((UNIT * fold, cols, PAIR_W), lambda n: (n, 0, 0))
    return pl.pallas_call(
        functools.partial(turn_kernel, wide=fold * cols),
        grid=(count,),
        out_shape=results,
        in_specs=[block, block, whole_block(shrink_weight.shape), pl.BlockSpec(memory_space=pl.ANY)],
        out_specs=[pl.BlockSpec((1,) + v.shape[1:], lambda n: (n, 0, 0)) for v in results],
        compiler_params=pltpu.CompilerParams(
            dimension_semantics=("arbitrary",), vmem_limit_bytes=24 * 1024 * 1024
        ),
        cost_estimate=pl.CostEstimate(
            flops=2 * 2 * count * pairs * hidden * PAIR_W, bytes_accessed=4 * 4 * pair_features.size, transcendentals=0
        ),
        name="turned_pairs",
    )(pair_features, cotangent, shrink_weight, after)


def pair_tile(place, lefts, matrices, turned, shape, outer_bias, expand_weight):
    seqs = lefts[0].shape[-1] // 2
    row_parts = lefts[0].shape[0]
    rows, cols, _ = shape
    fold = MXU_SIDE // HALF
    groups = rows // fold
    unit = UNIT
    units = 2 if groups % (2 * unit) == 0 else 1
    steps = groups // unit // units
    wide = fold * cols
    span = groups * FACTOR_WIDTH
    channels = FACTOR_WIDTH * FACTOR_WIDTH
    block = pl.BlockSpec((unit * units * fold, cols, PAIR_W), lambda n, place: (n, 0, 0))
    resident = pl.BlockSpec(memory_space=pltpu.VMEM)
    operands = (
        *lefts, *matrices, *turned, jnp.broadcast_to(outer_bias[:, None], (PAIR_W, LANES)), expand_weight,
    )
    results = (
        jax.ShapeDtypeStruct(shape, jnp.float32),
        jax.ShapeDtypeStruct((seqs, rows * FACTOR_WIDTH), jnp.bfloat16),
    ) + row_parts * (jax.ShapeDtypeStruct((seqs // row_parts, cols * FACTOR_WIDTH), jnp.bfloat16),)
    padded = groups * wide
    macs = 3 * FACTOR_WIDTH * span * fold * seqs * wide + padded * (2 * channels * MXU_SIDE + 8 * MXU_SIDE * MXU_SIDE)
    return pl.pallas_call(
        functools.partial(
            pair_kernel, seqs=seqs, cols=cols, fold=fold, unit=unit, units=units, blocks=len(lefts)
        ),
        grid_spec=pltpu.PrefetchScalarGridSpec(
            num_scalar_prefetch=1,
            grid=(steps,),
            in_specs=[resident] * len(operands),
            out_specs=[block] + [resident] * (len(results) - 1),
            scratch_shapes=[
                pltpu.VMEM((FACTOR_WIDTH // CHUNK, span, CHUNK * wide), jnp.bfloat16),
                pltpu.VMEM((span, fold * seqs), jnp.bfloat16),
                pltpu.VMEM((fold * seqs, span), jnp.bfloat16),
                pltpu.VMEM((cols * FACTOR_WIDTH, max(seqs, LANES)), jnp.float32),
                pltpu.VMEM((span, fold * seqs), jnp.float32),
                pltpu.VMEM((len(lefts),) + lefts[0].shape, jnp.bfloat16),
                pltpu.VMEM((row_parts,) + results[2].shape, jnp.bfloat16),
            ],
        ),
        out_shape=results,
        compiler_params=pltpu.CompilerParams(
            dimension_semantics=("arbitrary",), vmem_limit_bytes=36 * 1024 * 1024
        ),
        cost_estimate=pl.CostEstimate(
            flops=2 * macs, bytes_accessed=rows * cols * PAIR_W * 4, transcendentals=0
        ),
        name="pair_tile",
    )(place, *operands)


def finish_kernel(place_ref, *refs, residues, fold):
    *part_refs, gl_ref, updated_ref, left_ref, right_ref, x_s = refs
    upd_refs, gr_refs = part_refs[:len(part_refs) // 2], part_refs[len(part_refs) // 2:]
    part_seqs, res_count, width = updated_ref.shape
    total = gr_refs[0][...].astype(jnp.float32)
    for ref in gr_refs[1:]:
        total = total + ref[...].astype(jnp.float32)
    right_ref[...] = total
    for k, ref in enumerate(upd_refs):
        first = (place_ref[0] ^ k) * residues
        for r in range(residues):
            for n in range(width // LANES):
                at = r * width + n * LANES
                x_s[n, pl.ds(first + r, part_seqs, stride=res_count), :] = ref[:, at:at + LANES].astype(jnp.float32)
    for n in range(width // LANES):
        updated_ref[:, :, n * LANES:(n + 1) * LANES] = (
            x_s[n].reshape(part_seqs, res_count, LANES).astype(jnp.bfloat16)
        )
    total = gl_ref[0].astype(jnp.float32)
    for n in range(1, gl_ref.shape[0]):
        total = total + gl_ref[n].astype(jnp.float32)
    span = total.shape[1] // fold
    channel_block = lax.broadcasted_iota(jnp.int32, (1, LANES), 1) // FACTOR_WIDTH
    each = LANES // FACTOR_WIDTH
    for g in range(span // FACTOR_WIDTH):
        out = None
        for k in range(fold):
            at = k * span + g // each * LANES
            piece = total[:, at:at + LANES]
            shift = (k - g) % each * FACTOR_WIDTH
            piece = pltpu.roll(piece, shift, axis=1) if shift else piece
            out = piece if out is None else jnp.where(channel_block == k, piece, out)
        left_ref[:, g * LANES:(g + 1) * LANES] = out


def finish(place, returned, gr, gl, updated_shape):
    part_seqs, res_count, width = updated_shape
    residues = res_count // len(returned)
    results = (
        jax.ShapeDtypeStruct(updated_shape, jnp.bfloat16),
        jax.ShapeDtypeStruct(gl.shape[1:], jnp.float32),
        jax.ShapeDtypeStruct(gr[0].shape, jnp.float32),
    )
    resident = pl.BlockSpec(memory_space=pltpu.VMEM)
    return pl.pallas_call(
        functools.partial(finish_kernel, residues=residues, fold=MXU_SIDE // HALF),
        grid_spec=pltpu.PrefetchScalarGridSpec(
            num_scalar_prefetch=1,
            grid=(1,),
            in_specs=[resident] * (len(returned) + len(gr) + 1),
            out_specs=[whole_block(v.shape) for v in results],
            scratch_shapes=[pltpu.VMEM((width // LANES, part_seqs * res_count, LANES), jnp.float32)],
        ),
        out_shape=results,
        compiler_params=pltpu.CompilerParams(
            dimension_semantics=("arbitrary",), vmem_limit_bytes=16 * 1024 * 1024
        ),
        name="finish",
    )(place, *returned, *gr, gl)


def spread_out(q, count):
    return q if count % 2 else q % 2 * (count // 2) + q // 2


def local(
    alignment,
    pair_features,
    query_weight,
    key_weight,
    value_projection,
    gate_projection,
    gate_bias,
    output_projection,
    left_projection,
    right_projection,
    outer_weight,
    outer_bias,
    expand_weight,
    shrink_weight,
    cotangent,
):
    part_seqs, res_count, width = alignment.shape
    row_parts = lax.axis_size("row")
    col_parts = lax.axis_size("col")
    residues = res_count // row_parts
    own = jnp.transpose(alignment, (1, 0, 2)).reshape(row_parts, residues, part_seqs, width)
    columns = lax.all_to_all(own, "row", split_axis=0, concat_axis=0, tiled=True)
    *attended, factors = attend(
        columns, query_weight, key_weight, value_projection, gate_projection, gate_bias,
        output_projection, left_projection, right_projection,
    )

    factors = lax.all_to_all(factors, "row", split_axis=0, concat_axis=0, tiled=True)
    left = factors[:, 0]
    ratio = col_parts // row_parts
    lefts, place = [], []
    for m in range(ratio):
        moves = [
            (
                q * col_parts + ratio * r + b,
                r * col_parts
                + ratio * spread_out((q + r % 2 * (row_parts // 2)) % row_parts, row_parts)
                + (b + m) % ratio,
            )
            for q in range(row_parts)
            for r in range(row_parts)
            for b in range(ratio)
        ]
        lefts.append(lax.ppermute(left, ("row", "col"), moves))
        place.append((lax.axis_index("col") + ratio - m) % ratio)
    row = lax.axis_index("row")
    own_row = row.astype(jnp.int32).reshape(1)
    matrices = right_matrices(factors, outer_weight, expand_weight, shrink_weight)
    turned = turned_pairs(pair_features, cotangent, shrink_weight, matrices[-1])

    def to_rows(values):
        return values[:1] + [
            lax.ppermute(v, "row", [(r, r ^ (k + 1)) for r in range(row_parts)]) for k, v in enumerate(values[1:])
        ]

    returned = to_rows(attended)
    lefts, returned = lax.optimization_barrier((lefts, returned))
    pair_out, gl, *gr = pair_tile(
        jnp.stack(place + [row]).astype(jnp.int32), lefts, matrices, turned, pair_features.shape, outer_bias,
        expand_weight,
    )
    seqs, gl_width = gl.shape
    gr = to_rows(gr)
    gl = lax.all_to_all(
        gl.reshape(col_parts, seqs // col_parts, gl_width), "col", split_axis=0, concat_axis=0, tiled=True
    )
    updated, grad_left, grad_right = finish(own_row, returned, gr, gl, alignment.shape)
    return (updated, pair_out, grad_left, grad_right)


def solution(mesh):
    return jax.shard_map(
        local,
        mesh=mesh,
        in_specs=(P("row", "col", None), P("row", "col", None)) + (P(),) * 12 + (P("row", "col", None),),
        out_specs=(P("row", "col", None), P("row", "col", None), P("col", "row"), P("row", "col")),
        check_vma=False,
    )
```

```python
import functools

import jax
import jax.numpy as jnp
from jax import lax
from jax.experimental import pallas as pl
from jax.experimental.pallas import tpu as pltpu
from jax.sharding import PartitionSpec as P

ATTENTION_HEADS = 8
HEAD_WIDTH = 32
FACTOR_WIDTH = 32
PAIR_W = 128
EPSILON = 1e-05

LANES = 128
MXU_SIDE = 256
HALF = 64
TILE = 32
CHUNK = 4
UNIT = 4


def dot_nn(a, b):
    return lax.dot_general(a, b, (((1,), (0,)), ((), ())), preferred_element_type=jnp.float32)


def dot_nt(a, b):
    return lax.dot_general(a, b, (((1,), (1,)), ((), ())), preferred_element_type=jnp.float32)


def layer_normalise(rows):
    rows = rows.astype(jnp.float32)
    average = jnp.mean(rows, axis=-1, keepdims=True)
    centred = rows - average
    variance = jnp.mean(centred * centred, axis=-1, keepdims=True)
    return centred * lax.rsqrt(variance + EPSILON)


def attend_kernel(
    x_ref, wq_ref, wk_ref, wv_ref, wg_ref, bias_ref, wo_ref, wl_ref, wr_ref, *refs,
):
    row = lax.axis_index("row")
    *upd_refs, factor_ref, q_s, k_s, v_s, g_s, a_s, w_s, bias_s, project_s, upd_s, ordered_s, sems = refs
    parts, residues, part_seqs, width = x_ref.shape
    seqs = parts * part_seqs
    sources = (wq_ref, wk_ref, wv_ref, wg_ref, wo_ref, bias_ref, wl_ref, wr_ref)
    targets = [w_s.at[n] for n in range(5)] + [bias_s, project_s.at[0], project_s.at[1]]
    copies = [pltpu.make_async_copy(a, b, sems.at[n]) for n, (a, b) in enumerate(zip(sources, targets))]
    for copy in copies:
        copy.start()
    x = jnp.concatenate([x_ref[s, r] for r in range(residues) for s in range(parts)], axis=0)
    normed = layer_normalise(x).astype(jnp.bfloat16)
    for n, ref in enumerate((q_s, k_s, v_s)):
        copies[n].wait()
        ref[...] = dot_nn(normed, w_s[n]).astype(jnp.bfloat16)
    copies[3].wait()
    copies[5].wait()
    g_s[...] = jax.nn.sigmoid(dot_nn(normed, w_s[3]) + bias_s[...])

    head_of = lax.broadcasted_iota(jnp.int32, (1, width), 1) // HEAD_WIDTH
    masks = [(head_of == h).astype(jnp.float32) for h in range(ATTENTION_HEADS)]
    masks_low = [m.astype(jnp.bfloat16) for m in masks]

    def one_residue(r, carry):
        rows = pl.ds(pl.multiple_of(r * seqs, seqs), seqs)
        query = q_s[rows, :]
        spread_query = jnp.concatenate([query * m for m in masks_low], axis=0)
        scores = dot_nt(spread_query, k_s[rows, :]) * HEAD_WIDTH ** (-0.5)
        raised = jnp.exp(scores - jnp.max(scores, axis=-1, keepdims=True))
        inverse = 1.0 / jnp.sum(raised, axis=-1, keepdims=True)
        blended = dot_nn(raised.astype(jnp.bfloat16), v_s[rows, :]) * inverse
        total = blended[:seqs] * masks[0]
        for h in range(1, ATTENTION_HEADS):
            total = total + blended[h * seqs:(h + 1) * seqs] * masks[h]
        a_s[rows, :] = (g_s[rows, :] * total).astype(jnp.bfloat16)
        return carry

    lax.fori_loop(0, residues, one_residue, 0, unroll=min(residues, 12))

    copies[4].wait()
    updated = (x.astype(jnp.float32) + dot_nn(a_s[...], w_s[4])).astype(jnp.bfloat16)
    for r in range(residues):
        for s in range(parts):
            begin = r * seqs + s * part_seqs
            upd_s[s, :, r * width:(r + 1) * width] = updated[begin:begin + part_seqs]
    leaving = []
    for k, ref in enumerate(upd_refs):
        ordered_s[k] = upd_s[row ^ k]
        leaving.append(pltpu.make_async_copy(ordered_s.at[k], ref, sems.at[len(sources) + k]))
        leaving[k].start()
    factor_norm = layer_normalise(updated).astype(jnp.bfloat16)
    copies[6].wait()
    copies[7].wait()
    project = project_s[...].reshape(2 * FACTOR_WIDTH, width)
    for p in range(residues // 2):
        both = dot_nt(project, factor_norm[p * 2 * seqs:(p + 1) * 2 * seqs]).astype(jnp.bfloat16)
        for n in range(parts):
            factor_ref[n, 0, p] = both[:FACTOR_WIDTH]
            factor_ref[n, 1, p] = both[FACTOR_WIDTH:]
    for copy in leaving:
        copy.wait()


def whole_block(shape):
    return pl.BlockSpec(shape, lambda *_: (0,) * len(shape))


def in_hbm(*arrays):
    return [pltpu.with_memory_space_constraint(v, pltpu.HBM) for v in arrays]


def attend(x, wq, wk, wv, wg, gate_bias, wo, wl, wr):
    parts, residues, part_seqs, width = x.shape
    seqs = parts * part_seqs
    rows = residues * seqs
    operands = in_hbm(wq, wk, wv, wg, gate_bias.reshape(1, -1), wo, wl.T, wr.T)
    resident = pl.BlockSpec(memory_space=pltpu.VMEM)
    results = parts * (pltpu.HBM((part_seqs, residues * width), jnp.bfloat16),) + (
        jax.ShapeDtypeStruct((parts, 2, residues // 2, FACTOR_WIDTH, 2 * seqs), jnp.bfloat16),
    )
    macs = rows * width * (5 * width + 2 * FACTOR_WIDTH) + 2 * rows * ATTENTION_HEADS * width * seqs
    return pl.pallas_call(
        attend_kernel,
        out_shape=results,
        in_specs=[resident] + [pl.BlockSpec(memory_space=pltpu.HBM)] * len(operands),
        out_specs=[pl.BlockSpec(memory_space=pltpu.HBM)] * parts + [resident],
        scratch_shapes=[
            pltpu.VMEM((rows, width), jnp.bfloat16),
            pltpu.VMEM((rows, width), jnp.bfloat16),
            pltpu.VMEM((rows, width), jnp.bfloat16),
            pltpu.VMEM((rows, width), jnp.float32),
            pltpu.VMEM((rows, width), jnp.bfloat16),
            pltpu.VMEM((5,) + wq.shape, jnp.bfloat16),
            pltpu.VMEM((1, width), jnp.float32),
            pltpu.VMEM((2, FACTOR_WIDTH, width), jnp.bfloat16),
            pltpu.VMEM((parts,) + results[0].shape, jnp.bfloat16),
            pltpu.VMEM((parts,) + results[0].shape, jnp.bfloat16),
            pltpu.SemaphoreType.DMA((len(operands) + parts,)),
        ],
        compiler_params=pltpu.CompilerParams(vmem_limit_bytes=32 * 1024 * 1024),
        cost_estimate=pl.CostEstimate(flops=2 * macs, bytes_accessed=4 * x.size * 2, transcendentals=rows * width),
        name="column_attention",
    )(x, *operands)


def first_of_four(at, cols):
    wide = MXU_SIDE // HALF * cols
    inside = jnp.where(at < wide, at, jnp.where(at < wide + HALF, at - HALF, at - wide - HALF))
    return inside // cols


def swapped(pair, wide):
    return [pair[:wide], pair[2 * wide - HALF:], pair[wide:2 * wide - HALF]]


def unswapped(pair, wide):
    return [pair[:wide], pair[wide + HALF:], pair[wide:wide + HALF]]


def right_kernel(
    factor_ref, w_ref, expand_ref, shrink_ref, rbd_ref, rbdt_ref, wec_ref, wt_ref, et_ref, st_ref, stage_s,
    *, seqs, cols, fold,
):
    each = factor_ref.shape[2]
    wide = fold * cols
    stage_lanes = stage_s.shape[1]
    low_half = lax.broadcasted_iota(jnp.int32, (1, LANES), 1) < HALF

    stage_s[:FACTOR_WIDTH * FACTOR_WIDTH, :LANES] = w_ref[...].astype(jnp.float32)
    for e in range(FACTOR_WIDTH):
        piece = stage_s[pl.ds(e, FACTOR_WIDTH, stride=FACTOR_WIDTH), :LANES]
        wec_ref[e * FACTOR_WIDTH:(e + 1) * FACTOR_WIDTH, :] = piece.astype(jnp.bfloat16)
    for b in range(FACTOR_WIDTH * FACTOR_WIDTH // LANES):
        block = wec_ref[b * LANES:(b + 1) * LANES, :].astype(jnp.float32)
        wt_ref[:, b * LANES:(b + 1) * LANES] = block.T.astype(jnp.bfloat16)
    et_ref[...] = expand_ref[...].astype(jnp.float32).T.astype(jnp.bfloat16)
    st_ref[...] = shrink_ref[...].astype(jnp.float32).T.astype(jnp.bfloat16)

    for p in range(cols // 2):
        block = factor_ref[p // each, 1, p % each].astype(jnp.float32)
        even = 2 * p * FACTOR_WIDTH
        odd = even + FACTOR_WIDTH
        if seqs % LANES == 0:
            stage_s[even:even + FACTOR_WIDTH, :] = block[:, :seqs]
            stage_s[odd:odd + FACTOR_WIDTH, :] = block[:, seqs:]
        else:
            stage_s[even:even + FACTOR_WIDTH, :] = block
            stage_s[odd:odd + FACTOR_WIDTH, :] = pltpu.roll(block, HALF, axis=1)

    row_k = first_of_four(lax.broadcasted_iota(jnp.int32, (2 * wide, 1), 0), cols)
    lane_k = first_of_four(lax.broadcasted_iota(jnp.int32, (1, 2 * wide), 1), cols)
    for e in range(0, FACTOR_WIDTH, 2):
        two = []
        for u in (e, e + 1):
            two += [stage_s[pl.ds(u, cols, stride=FACTOR_WIDTH), :]] * fold
        upright = jnp.concatenate(swapped(jnp.concatenate(two, axis=0), wide), axis=0)
        chunk, at = e // CHUNK, e % CHUNK * wide
        rolled = pltpu.roll(upright, HALF, axis=1) if seqs < LANES else None
        for v in range(fold * seqs // stage_lanes):
            if seqs < LANES:
                value = jnp.where(
                    low_half, jnp.where(row_k == 2 * v, upright, 0.0), jnp.where(row_k == 2 * v + 1, rolled, 0.0)
                )
            else:
                value = jnp.where(row_k == v, upright, 0.0)
            rbdt_ref[chunk, at:at + 2 * wide, v * stage_lanes:(v + 1) * stage_lanes] = value.astype(jnp.bfloat16)
        turned = upright.T[:seqs]
        for k in range(fold):
            value = jnp.where(lane_k == k, turned, 0.0).astype(jnp.bfloat16)
            rbd_ref[chunk, k * seqs:(k + 1) * seqs, at:at + 2 * wide] = value


def right_matrices(factors, outer_weight, expand_weight, shrink_weight):
    row_parts, _, each, _, lanes = factors.shape
    seqs, cols = lanes // 2, 2 * each * row_parts
    fold = MXU_SIDE // HALF
    channels, width = outer_weight.shape
    results = (
        jax.ShapeDtypeStruct((FACTOR_WIDTH // CHUNK, fold * seqs, CHUNK * fold * cols), jnp.bfloat16),
        jax.ShapeDtypeStruct((FACTOR_WIDTH // CHUNK, CHUNK * fold * cols, fold * seqs), jnp.bfloat16),
        jax.ShapeDtypeStruct((channels, width), jnp.bfloat16),
        jax.ShapeDtypeStruct((width, channels), jnp.bfloat16),
        jax.ShapeDtypeStruct(expand_weight.shape[::-1], jnp.bfloat16),
        jax.ShapeDtypeStruct(shrink_weight.shape[::-1], jnp.bfloat16),
    )
    resident = pl.BlockSpec(memory_space=pltpu.VMEM)
    return pl.pallas_call(
        functools.partial(right_kernel, seqs=seqs, cols=cols, fold=fold),
        out_shape=results,
        in_specs=[resident] * 4,
        out_specs=[resident] * len(results),
        scratch_shapes=[pltpu.VMEM((max(cols * FACTOR_WIDTH, channels), max(seqs, LANES)), jnp.float32)],
        compiler_params=pltpu.CompilerParams(vmem_limit_bytes=16 * 1024 * 1024),
        cost_estimate=pl.CostEstimate(flops=6 * 10**9, bytes_accessed=4 * results[0].size, transcendentals=0),
        name="right_matrices",
    )(factors, outer_weight, expand_weight, shrink_weight)


def pair_kernel(
    place_ref, *refs, seqs, cols, fold, unit, units, blocks,
):
    left_refs, refs = refs[:blocks], refs[blocks:]
    rbd_s, rbdt_s, wec_s, wt_s, et_ref, st_ref, pair_ref, cot_ref, back_ref = refs[:9]
    bias_ref, expand_ref, out_ref, gl_ref = refs[9:13]
    gr_refs, (outer_s, l_s, lt_s, stage_s, glacc_s, lblk_s, gr_s) = refs[13:-7], refs[-7:]
    step = pl.program_id(0)
    row_parts, each = left_refs[0].shape[:2]
    span = l_s.shape[0]
    groups = span // FACTOR_WIDTH
    wide = fold * cols
    scaling = 1.0 / seqs
    low_half = lax.broadcasted_iota(jnp.int32, (1, LANES), 1) < HALF

    @pl.when(step == 0)
    def _prologue():
        for n, ref in enumerate(left_refs):
            lblk_s[place_ref[n]] = ref[...]
        pairs = fold // 2
        for p in range(groups * pairs):
            column, inside = divmod(p, row_parts * each)
            block = lblk_s[column, inside // each, inside % each]
            g, at = p // pairs, p % pairs * 2 * seqs
            l_s[g * FACTOR_WIDTH:(g + 1) * FACTOR_WIDTH, at:at + 2 * seqs] = (
                block.astype(jnp.float32) * scaling
            ).astype(jnp.bfloat16)
        for b in range(span // LANES):
            block = l_s[b * LANES:(b + 1) * LANES, :].astype(jnp.float32)
            lt_s[:, b * LANES:(b + 1) * LANES] = block.T.astype(jnp.bfloat16)

        def some_outers(n, carry):
            outer_s[n] = dot_nn(l_s[...], rbd_s[n]).astype(jnp.bfloat16)
            return carry

        lax.fori_loop(0, outer_s.shape[0], some_outers, 0, unroll=2)

    def unit_rows(u):
        at = (step * units + u) * unit * FACTOR_WIDTH
        return pl.ds(pl.multiple_of(at, unit * FACTOR_WIDTH), unit * FACTOR_WIDTH)

    def group(block, g):
        return block[g * FACTOR_WIDTH:(g + 1) * FACTOR_WIDTH]

    def forward(u):
        stacked = []
        for e in range(0, FACTOR_WIDTH, 2):
            at = e % CHUNK * wide
            block = outer_s[e // CHUNK, unit_rows(u), at:at + 2 * wide]
            shared = block[:, LANES:2 * LANES]
            rolled = pltpu.roll(shared, HALF, axis=1)
            even, odd = [], []
            for g in range(0, unit, 2):
                a, b = block[:, :LANES], block[:, 2 * LANES:]
                even += [group(a, g), jnp.where(low_half, group(shared, g), group(rolled, g + 1)), group(a, g + 1)]
                odd += [group(b, g), jnp.where(low_half, group(rolled, g), group(shared, g + 1)), group(b, g + 1)]
            stacked += [jnp.concatenate(even, axis=1), jnp.concatenate(odd, axis=1)]
        projected = dot_nn(wt_s[...], jnp.concatenate(stacked, axis=0))
        middles, inverses, spreads = [], [], []
        for at in range(0, projected.shape[1], LANES):
            middle = pair_ref[step * units + u, :, at:at + LANES] + projected[:, at:at + LANES] + bias_ref[...]
            average = jnp.mean(middle, axis=0, keepdims=True)
            centred = middle - average
            variance = jnp.mean(centred * centred, axis=0, keepdims=True)
            inverse = lax.rsqrt(variance + EPSILON)
            middles.append(middle)
            inverses.append(inverse)
            spreads.append(centred * inverse)
        spread_low = jnp.concatenate([v.astype(jnp.bfloat16) for v in spreads], axis=1)
        return middles, inverses, spreads, dot_nn(et_ref[...], spread_low)

    def backward(u, middles, inverses, spreads, before):
        rows, pairs = before.shape
        hidden, back_before = [], []
        for at in range(0, rows, TILE):
            hidden_parts, back_parts = [], []
            for v in range(0, pairs, MXU_SIDE):
                x = before[at:at + TILE, v:v + MXU_SIDE]
                back = back_ref[step * units + u, at:at + TILE, v:v + MXU_SIDE].astype(jnp.float32)
                phi = 0.5 * (1.0 + lax.erf(x * 0.7071067811865476))
                slope = phi + x * jnp.exp(-0.5 * x * x) * 0.3989422804014327
                hidden_parts.append((x * phi).astype(jnp.bfloat16))
                back_parts.append((back * slope).astype(jnp.bfloat16))
            hidden.append(jnp.concatenate(hidden_parts, axis=1))
            back_before.append(jnp.concatenate(back_parts, axis=1))
        back_spread = dot_nn(expand_ref[...], jnp.concatenate(back_before, axis=0))
        change = dot_nn(st_ref[...], jnp.concatenate(hidden, axis=0))
        back_middle = []
        for n, at in enumerate(range(0, pairs, LANES)):
            back, spread = back_spread[:, at:at + LANES], spreads[n]
            centre_term = jnp.mean(back, axis=0, keepdims=True)
            slope_term = jnp.mean(back * spread, axis=0, keepdims=True)
            back = back - centre_term - spread * slope_term
            back = cot_ref[step * units + u, :, at:at + LANES] + inverses[n] * back
            back_middle.append(back.astype(jnp.bfloat16))
        result = (jnp.concatenate(middles, axis=1) + change).T
        pieces = []
        for g in range(0, unit, 2):
            pieces += unswapped(result[g * wide:(g + 2) * wide], wide)
        out_ref[u * unit * fold:(u + 1) * unit * fold] = jnp.concatenate(pieces, axis=0).reshape(
            unit * fold, cols, PAIR_W
        )
        back_outer = dot_nn(wec_s[...], jnp.concatenate(back_middle, axis=1)).astype(jnp.bfloat16)
        for e in range(0, FACTOR_WIDTH, 2):
            even, odd = group(back_outer, e), group(back_outer, e + 1)
            a, shared, b = [], [], []
            for g in range(0, unit, 2):
                at = g * wide
                of_even, of_odd = even[:, at + LANES:at + 2 * LANES], odd[:, at + LANES:at + 2 * LANES]
                a += [even[:, at:at + LANES], even[:, at + 2 * LANES:at + 3 * LANES]]
                b += [odd[:, at:at + LANES], odd[:, at + 2 * LANES:at + 3 * LANES]]
                shared += [
                    jnp.where(low_half, of_even, pltpu.roll(of_odd, HALF, axis=1)),
                    jnp.where(low_half, pltpu.roll(of_even, HALF, axis=1), of_odd),
                ]
            for n, pieces in enumerate((a, shared, b)):
                at = e % CHUNK * wide + n * LANES
                outer_s[e // CHUNK, unit_rows(u), at:at + LANES] = jnp.concatenate(pieces, axis=0)

    held = forward(0)
    for u in range(units):
        ahead = forward(u + 1) if u + 1 < units else None
        backward(u, *held)
        held = ahead

    @pl.when(step == pl.num_programs(0) - 1)
    def _epilogue():
        glacc_s[...] = jnp.zeros_like(glacc_s)
        empty = jnp.zeros((LANES - seqs % LANES, CHUNK * wide), jnp.float32) if seqs % LANES else None
        at = lax.broadcasted_iota(jnp.int32, (1, CHUNK * wide), 1)
        lane_k = first_of_four(lax.rem(at, 2 * wide), cols)

        def some(n, carry):
            back = outer_s[n]
            glacc_s[...] += dot_nn(back, rbdt_s[n])
            full = dot_nn(lt_s[...], back)
            compact = full[:seqs]
            for k in range(1, fold):
                compact = jnp.where(lane_k == k, full[k * seqs:(k + 1) * seqs], compact)
            if empty is not None:
                compact = jnp.concatenate([compact, empty], axis=0)
            turned = compact.T
            for p in range(CHUNK // 2):
                two = jnp.concatenate(unswapped(turned[2 * p * wide:2 * (p + 1) * wide], wide), axis=0)
                for u in range(2):
                    total = two[u * wide:u * wide + cols]
                    for k in range(1, fold):
                        total = total + two[u * wide + k * cols:u * wide + (k + 1) * cols]
                    stage_s[pl.ds(n * CHUNK + 2 * p + u, cols, stride=FACTOR_WIDTH), :] = total
            return carry

        lax.fori_loop(0, outer_s.shape[0], some, 0, unroll=2)
        for b in range(cols * FACTOR_WIDTH // LANES):
            block = stage_s[b * LANES:(b + 1) * LANES, :].T[:seqs].astype(jnp.bfloat16)
            gr_s[:, :, b * LANES:(b + 1) * LANES] = block.reshape(row_parts, -1, LANES)
        for k, ref in enumerate(gr_refs):
            ref[...] = gr_s[place_ref[blocks] ^ k]
        for b in range(span // LANES):
            block = glacc_s[b * LANES:(b + 1) * LANES, :].T * scaling
            for k in range(fold):
                at = k * span + b * LANES
                gl_ref[:, at:at + LANES] = block[k * seqs:(k + 1) * seqs].astype(jnp.bfloat16)


def turn_kernel(pair_ref, cot_ref, shrink_ref, after_ref, pair_out_ref, cot_out_ref, back_ref, *, wide):
    for source, target in ((pair_ref, pair_out_ref), (cot_ref, cot_out_ref)):
        rows = source[...].reshape(-1, PAIR_W)
        for at in range(0, rows.shape[0], 2 * wide):
            target[0, :, at:at + 2 * wide] = jnp.concatenate(swapped(rows[at:at + 2 * wide], wide), axis=0).T
    back_ref[0] = dot_nn(shrink_ref[...], cot_out_ref[0].astype(jnp.bfloat16)).astype(jnp.bfloat16)


def turned_pairs(pair_features, cotangent, shrink_weight, after):
    rows, cols, _ = pair_features.shape
    fold = MXU_SIDE // HALF
    count = rows // (UNIT * fold)
    pairs = UNIT * fold * cols
    hidden = shrink_weight.shape[0]
    results = (
        jax.ShapeDtypeStruct((count, PAIR_W, pairs), jnp.float32),
        jax.ShapeDtypeStruct((count, PAIR_W, pairs), jnp.float32),
        jax.ShapeDtypeStruct((count, hidden, pairs), jnp.bfloat16),
    )
    block = pl.BlockSpec((UNIT * fold, cols, PAIR_W), lambda n: (n, 0, 0))
    return pl.pallas_call(
        functools.partial(turn_kernel, wide=fold * cols),
        grid=(count,),
        out_shape=results,
        in_specs=[block, block, whole_block(shrink_weight.shape), pl.BlockSpec(memory_space=pl.ANY)],
        out_specs=[pl.BlockSpec((1,) + v.shape[1:], lambda n: (n, 0, 0)) for v in results],
        compiler_params=pltpu.CompilerParams(
            dimension_semantics=("arbitrary",), vmem_limit_bytes=24 * 1024 * 1024
        ),
        cost_estimate=pl.CostEstimate(
            flops=2 * 2 * count * pairs * hidden * PAIR_W, bytes_accessed=4 * 4 * pair_features.size, transcendentals=0
        ),
        name="turned_pairs",
    )(pair_features, cotangent, shrink_weight, after)


def pair_tile(place, lefts, matrices, turned, shape, outer_bias, expand_weight):
    seqs = lefts[0].shape[-1] // 2
    row_parts = lefts[0].shape[0]
    rows, cols, _ = shape
    fold = MXU_SIDE // HALF
    groups = rows // fold
    unit = UNIT
    units = 3 if groups % (3 * unit) == 0 else 1
    steps = groups // unit // units
    wide = fold * cols
    span = groups * FACTOR_WIDTH
    channels = FACTOR_WIDTH * FACTOR_WIDTH
    block = pl.BlockSpec((unit * units * fold, cols, PAIR_W), lambda n, place: (n, 0, 0))
    resident = pl.BlockSpec(memory_space=pltpu.VMEM)
    operands = (
        *lefts, *matrices, *turned, jnp.broadcast_to(outer_bias[:, None], (PAIR_W, LANES)), expand_weight,
    )
    results = (
        jax.ShapeDtypeStruct(shape, jnp.float32),
        jax.ShapeDtypeStruct((seqs, rows * FACTOR_WIDTH), jnp.bfloat16),
    ) + row_parts * (jax.ShapeDtypeStruct((seqs // row_parts, cols * FACTOR_WIDTH), jnp.bfloat16),)
    padded = groups * wide
    macs = 3 * FACTOR_WIDTH * span * fold * seqs * wide + padded * (2 * channels * MXU_SIDE + 8 * MXU_SIDE * MXU_SIDE)
    return pl.pallas_call(
        functools.partial(
            pair_kernel, seqs=seqs, cols=cols, fold=fold, unit=unit, units=units, blocks=len(lefts)
        ),
        grid_spec=pltpu.PrefetchScalarGridSpec(
            num_scalar_prefetch=1,
            grid=(steps,),
            in_specs=[resident] * len(operands),
            out_specs=[block] + [resident] * (len(results) - 1),
            scratch_shapes=[
                pltpu.VMEM((FACTOR_WIDTH // CHUNK, span, CHUNK * wide), jnp.bfloat16),
                pltpu.VMEM((span, fold * seqs), jnp.bfloat16),
                pltpu.VMEM((fold * seqs, span), jnp.bfloat16),
                pltpu.VMEM((cols * FACTOR_WIDTH, max(seqs, LANES)), jnp.float32),
                pltpu.VMEM((span, fold * seqs), jnp.float32),
                pltpu.VMEM((len(lefts),) + lefts[0].shape, jnp.bfloat16),
                pltpu.VMEM((row_parts,) + results[2].shape, jnp.bfloat16),
            ],
        ),
        out_shape=results,
        compiler_params=pltpu.CompilerParams(
            dimension_semantics=("arbitrary",), vmem_limit_bytes=36 * 1024 * 1024
        ),
        cost_estimate=pl.CostEstimate(
            flops=2 * macs, bytes_accessed=rows * cols * PAIR_W * 4, transcendentals=0
        ),
        name="pair_tile",
    )(place, *operands)


def finish_kernel(place_ref, *refs, residues, fold):
    *part_refs, gl_ref, updated_ref, left_ref, right_ref, x_s = refs
    upd_refs, gr_refs = part_refs[:len(part_refs) // 2], part_refs[len(part_refs) // 2:]
    part_seqs, res_count, width = updated_ref.shape
    total = gr_refs[0][...].astype(jnp.float32)
    for ref in gr_refs[1:]:
        total = total + ref[...].astype(jnp.float32)
    right_ref[...] = total
    for k, ref in enumerate(upd_refs):
        first = (place_ref[0] ^ k) * residues
        for r in range(residues):
            for n in range(width // LANES):
                at = r * width + n * LANES
                x_s[n, pl.ds(first + r, part_seqs, stride=res_count), :] = ref[:, at:at + LANES].astype(jnp.float32)
    for n in range(width // LANES):
        updated_ref[:, :, n * LANES:(n + 1) * LANES] = (
            x_s[n].reshape(part_seqs, res_count, LANES).astype(jnp.bfloat16)
        )
    total = gl_ref[0].astype(jnp.float32)
    for n in range(1, gl_ref.shape[0]):
        total = total + gl_ref[n].astype(jnp.float32)
    span = total.shape[1] // fold
    channel_block = lax.broadcasted_iota(jnp.int32, (1, LANES), 1) // FACTOR_WIDTH
    each = LANES // FACTOR_WIDTH
    for g in range(span // FACTOR_WIDTH):
        out = None
        for k in range(fold):
            at = k * span + g // each * LANES
            piece = total[:, at:at + LANES]
            shift = (k - g) % each * FACTOR_WIDTH
            piece = pltpu.roll(piece, shift, axis=1) if shift else piece
            out = piece if out is None else jnp.where(channel_block == k, piece, out)
        left_ref[:, g * LANES:(g + 1) * LANES] = out


def finish(place, returned, gr, gl, updated_shape):
    part_seqs, res_count, width = updated_shape
    residues = res_count // len(returned)
    results = (
        jax.ShapeDtypeStruct(updated_shape, jnp.bfloat16),
        jax.ShapeDtypeStruct(gl.shape[1:], jnp.float32),
        jax.ShapeDtypeStruct(gr[0].shape, jnp.float32),
    )
    resident = pl.BlockSpec(memory_space=pltpu.VMEM)
    return pl.pallas_call(
        functools.partial(finish_kernel, residues=residues, fold=MXU_SIDE // HALF),
        grid_spec=pltpu.PrefetchScalarGridSpec(
            num_scalar_prefetch=1,
            grid=(1,),
            in_specs=[resident] * (len(returned) + len(gr) + 1),
            out_specs=[whole_block(v.shape) for v in results],
            scratch_shapes=[pltpu.VMEM((width // LANES, part_seqs * res_count, LANES), jnp.float32)],
        ),
        out_shape=results,
        compiler_params=pltpu.CompilerParams(
            dimension_semantics=("arbitrary",), vmem_limit_bytes=16 * 1024 * 1024
        ),
        name="finish",
    )(place, *returned, *gr, gl)


def spread_out(q, count):
    return q if count % 2 else q % 2 * (count // 2) + q // 2


def local(
    alignment,
    pair_features,
    query_weight,
    key_weight,
    value_projection,
    gate_projection,
    gate_bias,
    output_projection,
    left_projection,
    right_projection,
    outer_weight,
    outer_bias,
    expand_weight,
    shrink_weight,
    cotangent,
):
    part_seqs, res_count, width = alignment.shape
    row_parts = lax.axis_size("row")
    col_parts = lax.axis_size("col")
    residues = res_count // row_parts
    own = jnp.transpose(alignment, (1, 0, 2)).reshape(row_parts, residues, part_seqs, width)
    columns = lax.all_to_all(own, "row", split_axis=0, concat_axis=0, tiled=True)
    *attended, factors = attend(
        columns, query_weight, key_weight, value_projection, gate_projection, gate_bias,
        output_projection, left_projection, right_projection,
    )

    factors = lax.all_to_all(factors, "row", split_axis=0, concat_axis=0, tiled=True)
    left = factors[:, 0]
    ratio = col_parts // row_parts
    lefts, place = [], []
    for m in range(ratio):
        moves = [
            (
                q * col_parts + ratio * r + b,
                r * col_parts
                + ratio * spread_out((q + r % 2 * (row_parts // 2)) % row_parts, row_parts)
                + (b + m) % ratio,
            )
            for q in range(row_parts)
            for r in range(row_parts)
            for b in range(ratio)
        ]
        lefts.append(lax.ppermute(left, ("row", "col"), moves))
        place.append((lax.axis_index("col") + ratio - m) % ratio)
    row = lax.axis_index("row")
    own_row = row.astype(jnp.int32).reshape(1)
    matrices = right_matrices(factors, outer_weight, expand_weight, shrink_weight)
    turned = turned_pairs(pair_features, cotangent, shrink_weight, matrices[-1])

    def to_rows(values):
        return values[:1] + [
            lax.ppermute(v, "row", [(r, r ^ (k + 1)) for r in range(row_parts)]) for k, v in enumerate(values[1:])
        ]

    returned = to_rows(attended)
    lefts, returned = lax.optimization_barrier((lefts, returned))
    pair_out, gl, *gr = pair_tile(
        jnp.stack(place + [row]).astype(jnp.int32), lefts, matrices, turned, pair_features.shape, outer_bias,
        expand_weight,
    )
    seqs, gl_width = gl.shape
    gr = to_rows(gr)
    gl = lax.all_to_all(
        gl.reshape(col_parts, seqs // col_parts, gl_width), "col", split_axis=0, concat_axis=0, tiled=True
    )
    updated, grad_left, grad_right = finish(own_row, returned, gr, gl, alignment.shape)
    return (updated, pair_out, grad_left, grad_right)


def solution(mesh):
    return jax.shard_map(
        local,
        mesh=mesh,
        in_specs=(P("row", "col", None), P("row", "col", None)) + (P(),) * 12 + (P("row", "col", None),),
        out_specs=(P("row", "col", None), P("row", "col", None), P("col", "row"), P("row", "col")),
        check_vma=False,
    )
```
